128 devices in a mesh: row: 16 (over y_hi, z, core), col: 8 (over y_lo, x).
Axes of the slice: x: 4, y: 4 (y_hi: 2, y_lo: 2; y = y_hi * 2 + y_lo), z: 4, core: 2. Of those that a mesh axis runs over, the one named last changes fastest.
Arguments:
- tokens: bfloat16 [16384, 1024], P('row', 'col'), may hold values from -6 to 6
- cotangent: bfloat16 [16384, 1024], P('row', 'col'), may hold values from -6 to 6
- lengths: int32 [32], replicated, may hold values from 0 to 2048, as said below
- deal_order: int32 [16384], replicated, may hold values from 0 to 16383, as said below
- qkv_weight: float32 [1024, 3072], P('col', 'row'), may hold values from -0.1875 to 0.1875
- up_weight: float32 [1024, 4096], P('col', 'row'), may hold values from -0.1875 to 0.1875
- proj_weight: float32 [1024, 1024], P('row', 'col'), may hold values from -1.5 to 1.5
- down_weight: float32 [4096, 1024], P('row', 'col'), may hold values from -0.09375 to 0.09375
- norm_vectors: float32 [3, 1024], P(None, 'col'), may hold values from -0.5 to 1.4, as said below
- qkv_bias: float32 [3072], P('row'), may hold values from -2 to 2
- mlp_bias: float32 [4096], P('row'), may hold values from -2 to 2
- qkv_momentum: float32 [1024, 3072], P('col', 'row'), may hold values from -1536 to 1536
- up_momentum: float32 [1024, 4096], P('col', 'row'), may hold values from -256 to 256
- proj_momentum: float32 [1024, 1024], P('row', 'col'), may hold values from -40 to 40
- down_momentum: float32 [4096, 1024], P('row', 'col'), may hold values from -320 to 320
- norm_moment: float32 [3, 1024], P(None, 'col'), may hold values from -224 to 224
- norm_square: float32 [3, 1024], P(None, 'col'), may hold values from 819.2 to 32768
- qkv_bias_moment: float32 [3072], P('row'), may hold values from -160 to 160
- qkv_bias_square: float32 [3072], P('row'), may hold values from 3276.8 to 13107.2
- mlp_bias_moment: float32 [4096], P('row'), may hold values from -32 to 32
- mlp_bias_square: float32 [4096], P('row'), may hold values from 98.304 to 409.6
Outputs:
- output: float32 [16384, 1024], P('row', 'col')
- input_grad: float32 [16384, 1024], P('row', 'col')
- qkv_grad: float32 [1024, 3072], P('col', 'row')
- up_grad: float32 [1024, 4096], P('col', 'row')
- proj_grad: float32 [1024, 1024], P('row', 'col')
- down_grad: float32 [4096, 1024], P('row', 'col')
- new_qkv_momentum: float32 [1024, 3072], P('col', 'row')
- new_up_momentum: float32 [1024, 4096], P('col', 'row')
- new_proj_momentum: float32 [1024, 1024], P('row', 'col')
- new_down_momentum: float32 [4096, 1024], P('row', 'col')
- new_qkv_weight: float32 [1024, 3072], P('col', 'row')
- new_up_weight: float32 [1024, 4096], P('col', 'row')
- new_proj_weight: float32 [1024, 1024], P('row', 'col')
- new_down_weight: float32 [4096, 1024], P('row', 'col')
- new_norm_moment: float32 [3, 1024], P(None, 'col')
- new_norm_square: float32 [3, 1024], P(None, 'col')
- new_norm_vectors: float32 [3, 1024], P(None, 'col')
- new_qkv_bias_moment: float32 [3072], P('row')
- new_qkv_bias_square: float32 [3072], P('row')
- new_qkv_bias: float32 [3072], P('row')
- new_mlp_bias_moment: float32 [4096], P('row')
- new_mlp_bias_square: float32 [4096], P('row')
- new_mlp_bias: float32 [4096], P('row')
The draws below stay inside these ranges and needn't reach their ends.
Inputs may be any that keep to these rules, and one draw needn't show every extreme that they name: `lengths`: lengths of the sequences in the initial order of tokens; they sum to 16384; zero marks an unused slot; one length is 2048. `deal_order`: A permutation of the tokens. Each aligned block of 2048 dealt positions holds whole sequences, each contiguous and in its own order, at most 4 of them. `norm_vectors`: row 0 between 0.6 and 1.4, rows 1 and 2 between -0.5 and 0.5.
All inputs are finite; a program needn't handle non-finite values.
Results may differ from the reference program's by a relative error of at most 0.012.
Values may be sent and summed in bfloat16 or wider, within the bound.
A program may use at most 192 MiB of HBM per device.

```python
import math
import jax
import jax.numpy as jnp
from jax import lax

D = 1024
HEADS = 16
HEAD = 64
ROT = 16
FF = 4096
SEQ_GROUP = 4
STEP = 10
TOKENS = 16384
GROUP = 2048
N_COL = 8


def deal_plan(key):
    subkeys = jax.random.split(key, 4)
    cut_points = jax.random.randint(subkeys[0], (N_COL, SEQ_GROUP - 1), 1, GROUP)
    keep_cut = jax.random.randint(subkeys[1], (N_COL, SEQ_GROUP - 1), 0, 2)
    single_group = jax.random.randint(subkeys[2], (), 0, N_COL)
    keep_cut = jnp.where(jnp.arange(N_COL, dtype=jnp.int32)[:, None] == single_group, 0, keep_cut)
    cut_points = jnp.sort(jnp.where(keep_cut == 1, cut_points, GROUP), axis=1)
    bounds = jnp.concatenate([jnp.zeros((N_COL, 1), jnp.int32), cut_points.astype(jnp.int32), jnp.full((N_COL, 1), GROUP, jnp.int32)], axis=1)
    pieces = (bounds[:, 1:] - bounds[:, :-1]).reshape(-1)
    dealt_start = (bounds[:, :-1] + (jnp.arange(N_COL, dtype=jnp.int32) * GROUP)[:, None]).reshape(-1)
    slot_order = jax.random.permutation(subkeys[3], N_COL * SEQ_GROUP)
    lengths = pieces[slot_order].astype(jnp.int32)
    starts = (jnp.cumsum(lengths) - lengths).astype(jnp.int32)
    return (lengths, starts, dealt_start[slot_order].astype(jnp.int32))


def draw_lengths(key, part):
    lengths, starts, dealt_start = deal_plan(key)
    return lengths


def draw_deal_order(key, part):
    lengths, starts, dealt_start = deal_plan(key)
    tokens_all = jnp.arange(TOKENS, dtype=jnp.int32)
    seq_ends = jnp.cumsum(lengths).astype(jnp.int32)
    slot_index = jnp.sum((seq_ends[None, :] <= tokens_all[:, None]).astype(jnp.int32), axis=1)
    target = dealt_start[slot_index] + tokens_all - starts[slot_index]
    return jnp.zeros((TOKENS,), jnp.int32).at[target].set(tokens_all)


def draw_norm_vectors(key, part):
    key = jax.random.fold_in(key, 7)
    subkeys = jax.random.split(key, 2)
    gains = jax.random.uniform(subkeys[0], (1, D), jnp.float32, 0.6, 1.4)
    shifts = jax.random.uniform(subkeys[1], (2, D), jnp.float32, -0.5, 0.5)
    return jnp.concatenate([gains, shifts], axis=0)


def steps_of(stream_key, dims, cuts, smallest, high):
    def one(position, blocks):
        heights = jax.random.uniform(jax.random.fold_in(jax.random.fold_in(stream_key, 6), position), (blocks,), jnp.float32, smallest / len(cuts), high / len(cuts))
        return jnp.repeat(jnp.exp(heights), dims[position] // blocks).reshape((-1,) + (1,) * (len(dims) - position - 1))

    loudness = one(*cuts[0])
    for cut in cuts[1:]:
        loudness = loudness * one(*cut)
    return loudness


def gaussian(own_key, dims, scale, most, shards=(), held_as=jnp.bfloat16):
    level = steps_of(own_key, dims, shards, -0.22, 0.18) if shards else 1.0
    array = jax.random.normal(own_key, dims, jnp.float32) * scale * level
    return jnp.minimum(jnp.maximum(array, -most), most).astype(held_as)


def setup_inputs(seed: int = 0) -> dict:
    streams_of = jax.random.split(jax.random.key(seed), 22)
    tokens = gaussian(streams_of[0], (TOKENS, D), 1.0, 6.0, ((0, 16), (1, 8)))
    cotangent = gaussian(streams_of[1], (TOKENS, D), 1.0, 6.0, ((0, 16), (1, 8)))
    lengths = draw_lengths(jax.random.fold_in(streams_of[21], 71), 0)
    deal_order = draw_deal_order(jax.random.fold_in(streams_of[21], 71), 0)
    qkv_weight = gaussian(streams_of[4], (D, 3 * D), D ** -0.5, 0.1875, ((0, 8), (1, 16)), jnp.float32)
    up_weight = gaussian(streams_of[5], (D, FF), D ** -0.5, 0.1875, ((0, 8), (1, 16)), jnp.float32)
    proj_weight = gaussian(streams_of[6], (D, D), (D // 64) ** -0.5, 1.5, ((0, 16), (1, 8)), jnp.float32)
    down_weight = gaussian(streams_of[7], (FF, D), FF ** -0.5, 0.09375, ((0, 16), (1, 8)), jnp.float32)
    norm_vectors = draw_norm_vectors(jax.random.fold_in(streams_of[21], 71), 0)
    qkv_bias = gaussian(streams_of[9], (3 * D,), 0.3, 2.0, ((0, 16),), jnp.float32)
    mlp_bias = gaussian(streams_of[10], (FF,), 0.3, 2.0, ((0, 16),), jnp.float32)
    qkv_momentum = gaussian(streams_of[11], (D, 3 * D), (2.0 * TOKENS ** 0.5), 1536.0, ((0, 8), (1, 16)), jnp.float32)
    up_momentum = gaussian(streams_of[12], (D, FF), (0.35 * TOKENS ** 0.5), 256.0, ((0, 8), (1, 16)), jnp.float32)
    proj_momentum = gaussian(streams_of[13], (D, D), (0.05 * TOKENS ** 0.5), 40.0, ((0, 16), (1, 8)), jnp.float32)
    down_momentum = gaussian(streams_of[14], (FF, D), (0.4 * TOKENS ** 0.5), 320.0, ((0, 16), (1, 8)), jnp.float32)
    norm_moment = gaussian(streams_of[15], (3, D), (0.3 * TOKENS ** 0.5), 224.0, ((1, 8),), jnp.float32)
    norm_square = jnp.clip(jnp.exp(math.log(32768.0) - 3.6888794 * jax.random.uniform(streams_of[16], (3, D), jnp.float32) ** steps_of(streams_of[16], (3, D), ((1, 8),), -0.2, 0.2)), 819.2, 32768.0)
    qkv_bias_moment = gaussian(streams_of[17], (3 * D,), (0.2 * TOKENS ** 0.5), 160.0, ((0, 16),), jnp.float32)
    qkv_bias_square = jnp.clip(jnp.exp(math.log(13107.2) - 1.3862944 * jax.random.uniform(streams_of[18], (3 * D,), jnp.float32) ** steps_of(streams_of[18], (3 * D,), ((0, 16),), -0.2, 0.2)), 3276.8, 13107.2)
    mlp_bias_moment = gaussian(streams_of[19], (FF,), (0.04 * TOKENS ** 0.5), 32.0, ((0, 16),), jnp.float32)
    mlp_bias_square = jnp.clip(jnp.exp(math.log(409.6) - 1.4271164 * jax.random.uniform(streams_of[20], (FF,), jnp.float32) ** steps_of(streams_of[20], (FF,), ((0, 16),), -0.2, 0.2)), 98.304, 409.6)
    return {"tokens": tokens, "cotangent": cotangent, "lengths": lengths, "deal_order": deal_order, "qkv_weight": qkv_weight, "up_weight": up_weight, "proj_weight": proj_weight, "down_weight": down_weight, "norm_vectors": norm_vectors, "qkv_bias": qkv_bias, "mlp_bias": mlp_bias, "qkv_momentum": qkv_momentum, "up_momentum": up_momentum, "proj_momentum": proj_momentum, "down_momentum": down_momentum, "norm_moment": norm_moment, "norm_square": norm_square, "qkv_bias_moment": qkv_bias_moment, "qkv_bias_square": qkv_bias_square, "mlp_bias_moment": mlp_bias_moment, "mlp_bias_square": mlp_bias_square}


@jax.custom_vjp
def low(v):
    return lax.optimization_barrier(v.astype(jnp.bfloat16)).astype(jnp.float32)

@jax.custom_vjp
def low_back(v):
    return v

def low_keep(v):
    return (low(v), None)

def low_pass(kept, grad):
    return (grad,)

def back_keep(v):
    return (v, None)

def back_low(kept, grad):
    return (low(grad),)
low.defvjp(low_keep, low_pass)
low_back.defvjp(back_keep, back_low)
highest = lax.Precision.HIGHEST
poly_linear = 3.4445
poly_square = -4.775
poly_cubic = 2.0315
momentum = 0.95
rate_matrix = 0.15
decay_matrix = 0.1
beta_first = 0.9
beta_second = 0.95
rate_vector = 0.2
adam_floor = 1e-08
norm_floor = 1e-05
ortho_floor = 1e-07
masked_score = -1e+30

def token_places(lengths, anchor):
    seq_ends = jnp.cumsum(lengths).astype(jnp.int32)
    before = seq_ends[None, :] <= anchor[:, None]
    seq_ids = lax.optimization_barrier(jnp.sum(before.astype(jnp.int32), axis=1)).astype(jnp.int32)
    starts = lax.optimization_barrier(jnp.sum(jnp.where(before, lengths[None, :], 0), axis=1)).astype(jnp.int32)
    return (seq_ids, anchor - starts)

def rotary_tables(places):
    half_rot = ROT // 2
    inverse = 1.0 / 10000.0 ** (jnp.arange(half_rot, dtype=jnp.float32) * (2.0 / ROT))
    angles = places.astype(jnp.float32)[:, None] * inverse[None, :]
    return (jnp.cos(angles), jnp.sin(angles))

def rotate(values, cosine, sine):
    half_rot = ROT // 2
    lower_half = values[..., :half_rot]
    upper_half = values[..., half_rot:ROT]
    return jnp.concatenate([lower_half * cosine - upper_half * sine, upper_half * cosine + lower_half * sine, values[..., ROT:]], axis=-1)

def group_attention(operands):
    queries, keys_all, values_all, seq_ids, places = operands
    scores = jnp.einsum('hqd,hkd->hqk', queries, keys_all, precision=highest) * HEAD ** (-0.5)
    scores = low_back(scores)
    allowed = (seq_ids[:, None] == seq_ids[None, :]) & (places[None, :] <= places[:, None])
    scores = jnp.where(allowed[None], scores, masked_score)
    log_total = jax.nn.logsumexp(scores, axis=-1, keepdims=True)
    weights = low(jnp.exp(scores - log_total))
    return jnp.einsum('hqk,hkd->hqd', weights, values_all, precision=highest)

def orthogonalize(direction):
    matrix = direction / (jnp.sqrt(jnp.sum(direction * direction)) + ortho_floor)
    for sweep_index in range(5):
        gram_matrix = jnp.dot(matrix, matrix.T, precision=highest)
        applied = jnp.dot(gram_matrix, matrix, precision=highest)
        matrix = poly_linear * matrix + poly_square * applied + poly_cubic * jnp.dot(gram_matrix, applied, precision=highest)
    return matrix

def muon_step(weight, gradient, old_state, flipped, width):
    state = momentum * old_state + gradient
    direction = gradient + momentum * state
    oriented = direction.T if flipped else direction
    update = orthogonalize(oriented)
    update = update.T if flipped else update
    return (state, weight * (1.0 - rate_matrix * decay_matrix) - rate_matrix * 0.2 * math.sqrt(width) * update)

def adam_step(value, gradient, first_state, second_state):
    first_new = beta_first * first_state + (1.0 - beta_first) * gradient
    second_new = beta_second * second_state + (1.0 - beta_second) * gradient * gradient
    corrected = first_new / (1.0 - beta_first ** STEP)
    root_term = jnp.sqrt(second_new / (1.0 - beta_second ** STEP)) + adam_floor
    return (first_new, second_new, value - rate_vector * corrected / root_term)

def reference(tokens, cotangent, lengths, deal_order, qkv_weight, up_weight, proj_weight, down_weight, norm_vectors, qkv_bias, mlp_bias, qkv_momentum, up_momentum, proj_momentum, down_momentum, norm_moment, norm_square, qkv_bias_moment, qkv_bias_square, mlp_bias_moment, mlp_bias_square):
    inverse_order = jnp.zeros_like(deal_order).at[deal_order].set(jnp.arange(TOKENS, dtype=jnp.int32))
    seq_ids, places = token_places(lengths, deal_order)
    cosine, sine = rotary_tables(places)
    group_cos = cosine.reshape(N_COL, 1, GROUP, ROT // 2)
    group_sin = sine.reshape(N_COL, 1, GROUP, ROT // 2)
    group_ids = seq_ids.reshape(N_COL, GROUP)
    group_places = places.reshape(N_COL, GROUP)
    inputs = tokens.astype(jnp.float32)

    def layer(inputs, qkv_weight, up_weight, proj_weight, down_weight, norm_vectors, qkv_bias, mlp_bias):
        mean_row = lax.optimization_barrier(jnp.mean(inputs, axis=1, keepdims=True))
        centered = inputs - mean_row
        variance = lax.optimization_barrier(jnp.mean(centered * centered, axis=1, keepdims=True))
        normed = low(centered * lax.rsqrt(variance + norm_floor) * norm_vectors[0] + norm_vectors[1])
        dealt = normed[deal_order]
        pre_qkv = low_back(jnp.dot(dealt, low(qkv_weight), precision=highest) + qkv_bias)
        pre_up = low_back(jnp.dot(dealt, low(up_weight), precision=highest) + mlp_bias)
        split_heads = pre_qkv.reshape(N_COL, GROUP, HEADS, 3, HEAD).transpose(3, 0, 2, 1, 4)
        queries = low(rotate(split_heads[0], group_cos, group_sin))
        keys_all = low(rotate(split_heads[1], group_cos, group_sin))
        values_all = low(split_heads[2])
        attended = lax.map(jax.checkpoint(group_attention), (queries, keys_all, values_all, group_ids, group_places))
        attended = attended.transpose(0, 2, 1, 3).reshape(TOKENS, D)
        attended = low_back(low(attended))
        activated = low(jax.nn.gelu(pre_up, approximate=True))
        branch_out = jnp.dot(attended, low(proj_weight), precision=highest) + jnp.dot(activated, low(down_weight), precision=highest)
        return inputs + branch_out[inverse_order] + norm_vectors[2]
    output, pullback = jax.vjp(layer, inputs, qkv_weight, up_weight, proj_weight, down_weight, norm_vectors, qkv_bias, mlp_bias)
    input_grad, qkv_grad, up_grad, proj_grad, down_grad, norm_grads, qkv_bias_grad, mlp_bias_grad = pullback(cotangent.astype(jnp.float32))
    qkv_state, qkv_new = muon_step(qkv_weight, qkv_grad, qkv_momentum, False, 3 * D)
    up_state, up_new = muon_step(up_weight, up_grad, up_momentum, False, FF)
    proj_state, proj_new = muon_step(proj_weight, proj_grad, proj_momentum, True, D)
    down_state, down_new = muon_step(down_weight, down_grad, down_momentum, True, FF)
    norm_first, norm_second, norm_new = adam_step(norm_vectors, norm_grads, norm_moment, norm_square)
    qkv_first, qkv_second, qkv_bias_new = adam_step(qkv_bias, qkv_bias_grad, qkv_bias_moment, qkv_bias_square)
    mlp_first, mlp_second, mlp_bias_new = adam_step(mlp_bias, mlp_bias_grad, mlp_bias_moment, mlp_bias_square)
    return (output, input_grad, qkv_grad, up_grad, proj_grad, down_grad, qkv_state, up_state, proj_state, down_state, qkv_new, up_new, proj_new, down_new, norm_first, norm_second, norm_new, qkv_first, qkv_second, qkv_bias_new, mlp_first, mlp_second, mlp_bias_new)
```

```python
import functools
import math

import jax
import jax.numpy as jnp
from jax import lax
from jax.experimental import pallas as pl
from jax.experimental.pallas import tpu as pltpu
from jax.sharding import PartitionSpec as P

D = 1024
HEAD = 64
ROT = 16
FF = 4096
STEP = 10

poly_linear = 3.4445
poly_square = -4.775
poly_cubic = 2.0315
momentum = 0.95
rate_matrix = 0.15
decay_matrix = 0.1
beta_first = 0.9
beta_second = 0.95
rate_vector = 0.2
adam_floor = 1e-08
norm_floor = 1e-05
ortho_floor = 1e-07
masked_score = -1e30
high = lax.Precision.HIGH
f32 = jnp.float32
bf16 = jnp.bfloat16
BLOCK = 256
EXTRA = 16


def dot_nt(a, b, **kw):
    return lax.dot_general(a, b, (((1,), (1,)), ((), ())), preferred_element_type=f32, **kw)


def dot_tn(a, b, **kw):
    return lax.dot_general(a, b, (((0,), (0,)), ((), ())), preferred_element_type=f32, **kw)


def dot_nn(a, b, **kw):
    return lax.dot_general(a, b, (((1,), (0,)), ((), ())), preferred_element_type=f32, **kw)


def allowed_keys(start_ref, first, keys):
    shape = (BLOCK, keys)
    key_at = lax.broadcasted_iota(jnp.int32, shape, 1)
    query_at = first + lax.broadcasted_iota(jnp.int32, shape, 0)
    return (key_at >= start_ref[pl.ds(first, BLOCK), :]) & (key_at <= query_at)


def attend_kernel(q_ref, k_ref, v_ref, start_ref, out_ref, total_ref):
    for first in range(0, q_ref.shape[0], BLOCK):
        rows, keys = pl.ds(first, BLOCK), first + BLOCK
        scores = dot_nt(q_ref[rows, :], k_ref[:keys, :])
        scores = jnp.where(allowed_keys(start_ref, first, keys), scores, masked_score)
        top = jnp.max(scores, axis=1, keepdims=True)
        raw = jnp.exp(scores - top)
        total = jnp.sum(raw, axis=1, keepdims=True)
        attended = dot_nn(raw.astype(bf16), v_ref[:keys, :]) / total
        out_ref[rows, :] = attended.astype(bf16)
        total_ref[rows, :] = top + jnp.log(total)


def attend_back_kernel(
    q_ref, k_ref, v_ref, start_ref, out_ref, grad_ref, total_ref, dq_ref, dk_ref, dv_ref
):
    dk_ref[...] = jnp.zeros_like(dk_ref)
    dv_ref[...] = jnp.zeros_like(dv_ref)
    for first in range(0, q_ref.shape[0], BLOCK):
        rows, keys = pl.ds(first, BLOCK), first + BLOCK
        query, grad = q_ref[rows, :], grad_ref[rows, :]
        key, value = k_ref[:keys, :], v_ref[:keys, :]
        scores = dot_nt(query, key)
        allowed = allowed_keys(start_ref, first, keys)
        prob = jnp.where(allowed, jnp.exp(scores - total_ref[rows, :]), 0.0)
        delta = jnp.sum(grad.astype(f32) * out_ref[rows, :].astype(f32), axis=1, keepdims=True)
        score_grad = (prob * (dot_nt(grad, value) - delta)).astype(bf16)
        dq_ref[rows, :] = dot_nn(score_grad, key) * HEAD**-0.5
        dk_ref[:keys, :] += dot_tn(score_grad, query)
        dv_ref[:keys, :] += dot_tn(prob.astype(bf16), grad)


VMEM_LIMIT = 48 * 1024 * 1024


def attend(queries, keys_all, values_all, starts):
    rows = queries.shape[0]
    return pl.pallas_call(
        attend_kernel,
        out_shape=(
            jax.ShapeDtypeStruct((rows, HEAD), bf16),
            jax.ShapeDtypeStruct((rows, 1), f32),
        ),
        compiler_params=pltpu.CompilerParams(vmem_limit_bytes=VMEM_LIMIT),
        cost_estimate=pl.CostEstimate(
            flops=2 * rows * rows * HEAD, bytes_accessed=rows * 1024, transcendentals=rows * rows // 2
        ),
        name="attend",
    )(queries, keys_all, values_all, starts)


def attend_back(queries, keys_all, values_all, starts, attended, attended_grad, totals):
    rows = queries.shape[0]
    return pl.pallas_call(
        attend_back_kernel,
        out_shape=(jax.ShapeDtypeStruct((rows, HEAD), f32),) * 3,
        compiler_params=pltpu.CompilerParams(vmem_limit_bytes=VMEM_LIMIT),
        cost_estimate=pl.CostEstimate(
            flops=5 * rows * rows * HEAD, bytes_accessed=rows * 4096, transcendentals=rows * rows // 2
        ),
        name="attend_back",
    )(queries, keys_all, values_all, starts, attended, attended_grad, totals)


def rotary_tables(places):
    half_rot = ROT // 2
    inverse = 1.0 / 10000.0 ** (jnp.arange(half_rot, dtype=f32) * (2.0 / ROT))
    angles = inverse[:, None] * places.astype(f32)[None, :]
    return (jnp.cos(angles).T, jnp.sin(angles).T)


def rotate(values, cosine, sine):
    half_rot = ROT // 2
    lower_half = values[..., :half_rot]
    upper_half = values[..., half_rot:ROT]
    return jnp.concatenate(
        [
            lower_half * cosine - upper_half * sine,
            upper_half * cosine + lower_half * sine,
            values[..., ROT:],
        ],
        axis=-1,
    )


def gelu_tanh(values):
    return jax.nn.gelu(values, approximate=True)


def adam_step(value, gradient, first_state, second_state):
    first_new = beta_first * first_state + (1.0 - beta_first) * gradient
    second_new = beta_second * second_state + (1.0 - beta_second) * gradient * gradient
    corrected = first_new / (1.0 - beta_first**STEP)
    root_term = jnp.sqrt(second_new / (1.0 - beta_second**STEP)) + adam_floor
    return (first_new, second_new, value - rate_vector * corrected / root_term)


def gather_row(x):
    return lax.all_gather(x, "row", axis=0, tiled=True)


def swap_col(x):
    return lax.all_to_all(x, "col", split_axis=0, concat_axis=0, tiled=True)


def sum_scatter(x, axis):
    return lax.psum_scatter(x, axis, scatter_dimension=0, tiled=True)


def take_rows(x, index):
    return x.at[index].get(mode="promise_in_bounds")


def high_low(x):
    high_part = x.astype(bf16)
    return high_part, (x - high_part.astype(f32)).astype(bf16)


def per_device(
    tokens,
    cotangent,
    lengths,
    deal_order,
    qkv_weight,
    up_weight,
    proj_weight,
    down_weight,
    norm_vectors,
    qkv_bias,
    mlp_bias,
    qkv_momentum,
    up_momentum,
    proj_momentum,
    down_momentum,
    norm_moment,
    norm_square,
    qkv_bias_moment,
    qkv_bias_square,
    mlp_bias_moment,
    mlp_bias_square,
):
    cols, rows = lax.axis_size("col"), lax.axis_size("row")
    col, row = lax.axis_index("col"), lax.axis_index("row")
    total_tokens = deal_order.shape[0]
    group = total_tokens // cols
    piece = group // rows
    held = total_tokens // rows
    feats = D // cols
    qkv_width, up_width = qkv_weight.shape[1], up_weight.shape[1]
    proj_width = proj_weight.shape[0]
    in_width = qkv_width + up_width
    out_width = proj_width + down_weight.shape[0]

    seq_ends = jnp.cumsum(lengths)
    seq_starts = seq_ends - lengths
    anchor = lax.dynamic_slice_in_dim(deal_order, col * group, group)
    before = seq_ends[None, :] <= anchor[:, None]
    places = anchor - jnp.sum(jnp.where(before, lengths[None, :], 0), axis=1)
    starts = (jnp.arange(group, dtype=jnp.int32) - places)[:, None]
    at = jnp.arange(total_tokens, dtype=jnp.int32)
    dealt_starts = jnp.sum(
        jnp.where(deal_order[None, :] == seq_starts[:, None], at[None, :], 0), axis=1
    )
    own = row * held + jnp.arange(held, dtype=jnp.int32)
    holds = (seq_starts[None, :] <= own[:, None]) & (own[:, None] < seq_ends[None, :])
    dealt_at = own + jnp.sum(jnp.where(holds, (dealt_starts - seq_starts)[None, :], 0), axis=1)
    cosine, sine = rotary_tables(places)

    in_weight = jnp.concatenate([qkv_weight, up_weight], axis=1)
    out_weight = jnp.concatenate([proj_weight, down_weight], axis=0)
    vector_parts = []
    rest = norm_vectors
    for _ in range(3):
        vector_parts.append(rest.astype(bf16))
        rest = rest - vector_parts[-1].astype(f32)
    vector_columns = jnp.pad(jnp.concatenate(vector_parts, axis=0).T, ((0, 0), (0, 128 - 9)))
    weight_all = lax.all_gather(
        jnp.concatenate(
            [in_weight.astype(bf16), out_weight.astype(bf16).T, vector_columns], axis=1
        ),
        "col",
        axis=0,
        tiled=True,
    )
    in_all, out_all = weight_all[:, :in_width], weight_all[:, in_width : in_width + out_width]
    vectors_all = weight_all[:, in_width + out_width :].astype(f32).T
    norm_all = vectors_all[0:3] + vectors_all[3:6] + vectors_all[6:9]

    pick = lax.dynamic_slice(
        deal_order.reshape(cols, rows, piece), (0, row, 0), (cols, 1, piece)
    ).reshape(-1)

    def deal(x):
        mine = take_rows(gather_row(x), pick).reshape(cols, piece, feats)
        return swap_col(mine).transpose(1, 0, 2).reshape(piece, D)

    def deal_back(x, more, own_more):
        parts = x.astype(bf16).reshape(piece, cols, feats).transpose(1, 0, 2)
        if more is None:
            stride = piece
            swapped = swap_col(parts)
        else:
            stride = piece + EXTRA
            swapped = swap_col(jnp.concatenate([parts, more], axis=1))
            own_more = jnp.pad(
                own_more[None], ((0, cols - 1), (stride - own_more.shape[0], 0), (0, 0))
            )
            swapped = swapped + own_more
        whole = gather_row(swapped.reshape(cols * stride, feats))
        block, inside = dealt_at // group, dealt_at % group
        index = (inside // piece) * (cols * stride) + block * stride + inside % piece
        return take_rows(whole, index), whole

    gain, shift, out_bias = norm_vectors[0], norm_vectors[1], norm_vectors[2]
    piece_tokens = deal(tokens).astype(f32)
    centered = piece_tokens - jnp.mean(piece_tokens, axis=1, keepdims=True)
    inverse_std = lax.rsqrt(jnp.mean(centered * centered, axis=1, keepdims=True) + norm_floor)
    normalized = centered * inverse_std
    normed = (normalized * norm_all[0] + norm_all[1]).astype(bf16)
    dealt = gather_row(normed)
    cotangent_dealt = gather_row(deal(cotangent))

    preact = dot_nn(dealt, in_all)
    pre_qkv = preact[:, :qkv_width] + qkv_bias
    pre_up = preact[:, qkv_width:] + mlp_bias
    queries = (rotate(pre_qkv[:, :HEAD], cosine, sine).astype(bf16) * HEAD**-0.5).astype(bf16)
    keys_all = rotate(pre_qkv[:, HEAD : 2 * HEAD], cosine, sine).astype(bf16)
    values_all = pre_qkv[:, 2 * HEAD :].astype(bf16)
    attended, totals = attend(queries, keys_all, values_all, starts)
    activated, gelu_back = jax.vjp(gelu_tanh, pre_up)
    branch = jnp.concatenate([attended, activated.astype(bf16)], axis=1)
    branch_sum = sum_scatter(dot_nt(branch, out_all).astype(bf16), "row")
    branch_back, _ = deal_back(branch_sum, None, None)
    output = tokens.astype(f32) + branch_back.astype(f32) + out_bias

    branch_grad = dot_nn(cotangent_dealt, out_all)
    out_grad = sum_scatter(dot_tn(cotangent_dealt, branch), "col")
    attended_grad = branch_grad[:, :proj_width].astype(bf16)
    up_pre_grad = gelu_back(branch_grad[:, proj_width:])[0]
    query_grad, key_grad, value_grad = attend_back(
        queries, keys_all, values_all, starts, attended, attended_grad, totals
    )
    preact_grad = jnp.concatenate(
        [
            rotate(query_grad, cosine, -sine),
            rotate(key_grad, cosine, -sine),
            value_grad,
            up_pre_grad,
        ],
        axis=1,
    ).astype(bf16)
    in_part = dot_tn(dealt, preact_grad).reshape(cols, feats, in_width)
    bias_part = jnp.sum(preact_grad, axis=0, dtype=f32)
    bias_rows = jnp.broadcast_to(bias_part[None, None, :], (cols, 8, in_width))
    in_sum = sum_scatter(
        jnp.concatenate([in_part, bias_rows], axis=1).reshape(cols * (feats + 8), in_width), "col"
    )
    in_grad, in_bias_grad = in_sum[:feats], in_sum[feats]
    normed_grad = sum_scatter(dot_nt(preact_grad, in_all).astype(bf16), "row").astype(f32)
    scaled = normed_grad * norm_all[0]
    mean_first = jnp.mean(scaled, axis=1, keepdims=True)
    mean_second = jnp.mean(scaled * normalized, axis=1, keepdims=True)
    token_grad = inverse_std * (scaled - mean_first - normalized * mean_second)
    vector_rows = jnp.stack(
        [
            *high_low(jnp.sum(normed_grad * normalized, axis=0)),
            *high_low(jnp.sum(normed_grad, axis=0)),
        ],
        axis=0,
    )
    vector_rows = jnp.pad(
        vector_rows.reshape(4, cols, feats).transpose(1, 0, 2), ((0, 0), (0, EXTRA - 4), (0, 0))
    )
    bias_rows = jnp.stack(high_low(jnp.sum(cotangent, axis=0, dtype=f32)), axis=0)
    token_back, whole = deal_back(token_grad, vector_rows, bias_rows)
    input_grad = cotangent.astype(f32) + token_back.astype(f32)
    vector_sum = jnp.sum(
        whole.reshape(rows * cols, piece + EXTRA, feats)[:, piece:].astype(f32), axis=0
    )
    norm_grads = jnp.stack(
        [
            vector_sum[0] + vector_sum[1],
            vector_sum[2] + vector_sum[3],
            vector_sum[-2] + vector_sum[-1],
        ],
        axis=0,
    )

    flip_flags = (False, False, True, True)
    oriented_grads = (
        in_grad[:, :qkv_width],
        in_grad[:, qkv_width:],
        out_grad[:, :proj_width],
        out_grad[:, proj_width:],
    )
    gradients = [g.T if f else g for g, f in zip(oriented_grads, flip_flags)]
    old_states = (qkv_momentum, up_momentum, proj_momentum, down_momentum)
    weights = (qkv_weight, up_weight, proj_weight, down_weight)
    widths = (3 * D, FF, D, FF)
    states = [momentum * old + g for old, g in zip(old_states, gradients)]
    oriented = []
    for gradient, state, flipped in zip(gradients, states, flip_flags):
        direction = gradient + momentum * state
        direction = direction.T if flipped else direction
        direction = jnp.pad(direction, ((0, 0), (0, up_width - direction.shape[1])))
        oriented += [direction, direction]
    matrix = swap_col(jnp.stack(oriented, axis=0)).reshape(D, up_width)
    gram = lax.psum(dot_nt(matrix, matrix, precision=high), "row")
    shrink = 1.0 / (jnp.sqrt(jnp.trace(gram)) + ortho_floor)
    half = up_width // 2
    thin = lax.dynamic_slice_in_dim(matrix, (col % 2) * half, half, axis=1) * shrink
    gram = gram * (shrink * shrink)
    eye = jnp.eye(D, dtype=f32)
    for sweep in range(5):
        squared = dot_nn(gram, gram, precision=high)
        poly = poly_linear * eye + poly_square * gram + poly_cubic * squared
        thin = dot_nn(poly, thin, precision=high)
        if sweep < 4:
            gram = dot_nn(gram, dot_nn(poly, poly, precision=high), precision=high)
    returned = swap_col(thin.astype(bf16).reshape(cols, feats, half))
    new_weights = []
    for index in range(4):
        update = jnp.concatenate([returned[2 * index], returned[2 * index + 1]], axis=1)
        update = update[:, : oriented_grads[index].shape[1]].astype(f32)
        update = update.T if flip_flags[index] else update
        new_weights.append(
            weights[index] * (1.0 - rate_matrix * decay_matrix)
            - rate_matrix * 0.2 * math.sqrt(widths[index]) * update
        )

    norm_first, norm_second, norm_new = adam_step(
        norm_vectors, norm_grads, norm_moment, norm_square
    )
    qkv_first, qkv_second, qkv_bias_new = adam_step(
        qkv_bias, in_bias_grad[:qkv_width], qkv_bias_moment, qkv_bias_square
    )
    mlp_first, mlp_second, mlp_bias_new = adam_step(
        mlp_bias, in_bias_grad[qkv_width:], mlp_bias_moment, mlp_bias_square
    )
    return (
        output,
        input_grad,
        *gradients,
        *states,
        *new_weights,
        norm_first,
        norm_second,
        norm_new,
        qkv_first,
        qkv_second,
        qkv_bias_new,
        mlp_first,
        mlp_second,
        mlp_bias_new,
    )


def solution(mesh):
    over_both, over_flip = P("row", "col"), P("col", "row")
    features, hidden = P(None, "col"), P("row")
    return jax.shard_map(
        per_device,
        mesh=mesh,
        in_specs=(
            *(over_both, over_both, P(), P()),
            *(over_flip, over_flip, over_both, over_both),
            *(features, hidden, hidden),
            *(over_flip, over_flip, over_both, over_both),
            *(features, features, hidden, hidden, hidden, hidden),
        ),
        out_specs=(
            *(over_both, over_both),
            *(over_flip, over_flip, over_both, over_both) * 3,
            *(features,) * 3,
            *(hidden,) * 6,
        ),
        check_vma=False,
    )
```

```python
import functools
import math

import jax
import jax.numpy as jnp
from jax import lax
from jax.experimental import pallas as pl
from jax.experimental.pallas import tpu as pltpu
from jax.sharding import PartitionSpec as P

D = 1024
HEAD = 64
ROT = 16
FF = 4096
STEP = 10

poly_linear = 3.4445
poly_square = -4.775
poly_cubic = 2.0315
momentum = 0.95
rate_matrix = 0.15
decay_matrix = 0.1
beta_first = 0.9
beta_second = 0.95
rate_vector = 0.2
adam_floor = 1e-08
norm_floor = 1e-05
ortho_floor = 1e-07
masked_score = -1e30
f32 = jnp.float32
bf16 = jnp.bfloat16
BLOCK = 256
EXTRA = 16


def dot_nt(a, b, **kw):
    return lax.dot_general(a, b, (((1,), (1,)), ((), ())), preferred_element_type=f32, **kw)


def dot_tn(a, b, **kw):
    return lax.dot_general(a, b, (((0,), (0,)), ((), ())), preferred_element_type=f32, **kw)


def dot_nn(a, b, **kw):
    return lax.dot_general(a, b, (((1,), (0,)), ((), ())), preferred_element_type=f32, **kw)


def allowed_keys(start_ref, first, keys):
    shape = (BLOCK, keys)
    key_at = lax.broadcasted_iota(jnp.int32, shape, 1)
    query_at = first + lax.broadcasted_iota(jnp.int32, shape, 0)
    return (key_at >= start_ref[pl.ds(first, BLOCK), :]) & (key_at <= query_at)


def attend_kernel(q_ref, k_ref, v_ref, start_ref, out_ref, total_ref):
    for first in range(0, q_ref.shape[0], BLOCK):
        rows, keys = pl.ds(first, BLOCK), first + BLOCK
        scores = dot_nt(q_ref[rows, :], k_ref[:keys, :])
        scores = jnp.where(allowed_keys(start_ref, first, keys), scores, masked_score)
        top = jnp.max(scores, axis=1, keepdims=True)
        raw = jnp.exp(scores - top)
        total = jnp.sum(raw, axis=1, keepdims=True)
        attended = dot_nn(raw.astype(bf16), v_ref[:keys, :]) / total
        out_ref[rows, :] = attended.astype(bf16)
        total_ref[rows, :] = top + jnp.log(total)


def attend_back_kernel(
    q_ref, k_ref, v_ref, start_ref, out_ref, grad_ref, total_ref, dq_ref, dk_ref, dv_ref
):
    dk_ref[...] = jnp.zeros_like(dk_ref)
    dv_ref[...] = jnp.zeros_like(dv_ref)
    for first in range(0, q_ref.shape[0], BLOCK):
        rows, keys = pl.ds(first, BLOCK), first + BLOCK
        query, grad = q_ref[rows, :], grad_ref[rows, :]
        key, value = k_ref[:keys, :], v_ref[:keys, :]
        scores = dot_nt(query, key)
        allowed = allowed_keys(start_ref, first, keys)
        prob = jnp.where(allowed, jnp.exp(scores - total_ref[rows, :]), 0.0)
        delta = jnp.sum(grad.astype(f32) * out_ref[rows, :].astype(f32), axis=1, keepdims=True)
        score_grad = (prob * (dot_nt(grad, value) - delta)).astype(bf16)
        dq_ref[rows, :] = dot_nn(score_grad, key) * HEAD**-0.5
        dk_ref[:keys, :] += dot_tn(score_grad, query)
        dv_ref[:keys, :] += dot_tn(prob.astype(bf16), grad)


VMEM_LIMIT = 48 * 1024 * 1024


MESH = pl.DeviceIdType.MESH
VMEM_SPEC = pl.BlockSpec(memory_space=pltpu.VMEM)
SMEM_SPEC = pl.BlockSpec(memory_space=pltpu.SMEM)


def remote(src, dst, send, recv, device):
    return pltpu.make_async_remote_copy(
        src_ref=src, dst_ref=dst, send_sem=send, recv_sem=recv, device_id=device, device_id_type=MESH
    )


class Place:
    def __init__(self):
        self.row, self.col = lax.axis_index("row"), lax.axis_index("col")
        self.rows, self.cols = lax.axis_size("row"), lax.axis_size("col")
        self.chips = self.rows // 2
        self.chip, self.core = self.row // 2, self.row % 2
        self.twin = (self.chip * 2 + 1 - self.core, self.col)

    def chip_at(self, step):
        return lax.rem(self.chip + step, self.chips)

    def chip_row(self, step):
        return self.chip_at(step) * 2 + self.core

    def col_at(self, step):
        return lax.rem(self.col + step, self.cols)


def meet(devices):
    barrier = pltpu.get_barrier_semaphore()
    for device in devices:
        pl.semaphore_signal(barrier, inc=1, device_id=device, device_id_type=MESH)
    pl.semaphore_wait(barrier, len(devices))


class RowGather:
    def __init__(self, at, slot, sems):
        self.at, self.slot = at, slot
        self.send, self.recv, self.pass_send, self.pass_recv = sems

    def outgoing(self, step, src):
        at = self.at
        return remote(
            src,
            self.slot(at.row),
            self.send.at[step],
            self.recv.at[step],
            (at.chip_row(step), at.col),
        )

    def passing(self, step, src, row):
        return remote(
            src, self.slot(row), self.pass_send.at[step], self.pass_recv.at[step], self.at.twin
        )

    def came_from(self, step):
        return self.at.chip_row(self.at.chips - step)

    def start(self, src):
        self.src = src
        for step in range(1, self.at.chips):
            self.outgoing(step, src).start()
        self.passing(0, src, self.at.row).start()

    def forward(self, then=None):
        for step in range(1, self.at.chips):
            row = self.came_from(step)
            slot = self.slot(row)
            remote(
                slot, slot, self.send.at[step], self.recv.at[step], (row, self.at.col)
            ).wait_recv()
            self.passing(step, slot, row).start()
            if then is not None:
                then(row)

    def finish(self, then=None):
        at = self.at
        for step in range(at.chips):
            row = at.chip_at(at.chips - step) * 2 + 1 - at.core
            slot = self.slot(row)
            remote(
                slot, slot, self.pass_send.at[step], self.pass_recv.at[step], at.twin
            ).wait_recv()
            if then is not None:
                then(row)

    def sent(self):
        for step in range(1, self.at.chips):
            self.outgoing(step, self.src).wait_send()
        self.passing(0, self.src, self.at.row).wait_send()
        for step in range(1, self.at.chips):
            row = self.came_from(step)
            self.passing(step, self.slot(row), row).wait_send()


class ColSwap:
    def __init__(self, at, src, dst, sems):
        self.at, self.src, self.dst = at, src, dst
        self.send, self.recv = sems

    def outgoing(self, step):
        at = self.at
        to = at.col_at(step)
        return remote(
            self.src(to), self.dst(at.col), self.send.at[step], self.recv.at[step], (at.row, to)
        )

    def start(self):
        for step in range(1, self.at.cols):
            self.outgoing(step).start()

    def arrived(self):
        at = self.at
        for step in range(1, at.cols):
            came = at.col_at(at.cols - step)
            slot = self.dst(came)
            remote(slot, slot, self.send.at[step], self.recv.at[step], (at.row, came)).wait_recv()

    def sent(self):
        for step in range(1, self.at.cols):
            self.outgoing(step).wait_send()


def gather_sems(chips):
    return [pltpu.SemaphoreType.DMA((chips,))] * 4


def swap_sems(cols):
    return [pltpu.SemaphoreType.DMA((cols,))] * 2


def deal_kernel(
    tokens_ref,
    cotangent_ref,
    pick_ref,
    weight_ref,
    vector_ref,
    dealt_ref,
    cot_dealt_ref,
    weight_all_ref,
    vector_all_ref,
    normalized_ref,
    inverse_std_ref,
    all_tokens,
    all_cots,
    wide,
    chosen,
    out_tokens,
    in_tokens,
    out_cots,
    in_cots,
    *sems,
):
    at = Place()
    held, feats = tokens_ref.shape
    piece = out_tokens.shape[1]
    depth = weight_ref.shape[0]
    sems = list(sems)

    def some(count):
        taken, sems[:count] = sems[:count], []
        return taken

    def dealt_slot(ref):
        return lambda row: ref.at[pl.ds(row * piece, piece), :]

    first_tokens = RowGather(at, lambda row: all_tokens.at[row], some(4))
    first_cots = RowGather(at, lambda row: all_cots.at[row], some(4))
    last_tokens = RowGather(at, dealt_slot(dealt_ref), some(4))
    last_cots = RowGather(at, dealt_slot(cot_dealt_ref), some(4))
    swap_tokens = ColSwap(at, lambda c: out_tokens.at[c], lambda c: in_tokens.at[c], some(2))
    swap_cots = ColSwap(at, lambda c: out_cots.at[c], lambda c: in_cots.at[c], some(2))
    swap_weight = ColSwap(
        at, lambda c: weight_ref, lambda c: weight_all_ref.at[pl.ds(c * depth, depth), :], some(2)
    )
    swap_vector = ColSwap(at, lambda c: vector_ref, lambda c: vector_all_ref.at[c], some(2))

    meet(
        [(at.chip_row(step), at.col) for step in range(1, at.chips)]
        + [at.twin]
        + [(at.row, at.col_at(step)) for step in range(1, at.cols)]
    )
    first_tokens.start(tokens_ref)
    swap_vector.start()
    swap_weight.start()
    weight_all_ref[pl.ds(at.col * depth, depth), :] = weight_ref[...]
    vector_all_ref[at.col] = vector_ref[...]

    def widen(src):
        def one(row):
            wide[pl.ds(row * held, held), :] = src[row].astype(f32)

        return one

    def choose(out_ref):
        def eight(step, carry):
            first = step * 8
            found = [wide[pl.ds(pick_ref[first + i], 1), :] for i in range(8)]
            chosen[pl.ds(first, 8), :] = jnp.concatenate(found, axis=0)
            return carry

        lax.fori_loop(0, at.cols * piece // 8, eight, 0)
        for c in range(at.cols):
            out_ref[c] = chosen[c * piece : (c + 1) * piece, :].astype(bf16)

    wide[pl.ds(at.row * held, held), :] = tokens_ref[...].astype(f32)
    first_tokens.forward(widen(all_tokens))
    first_cots.start(cotangent_ref)
    first_tokens.finish(widen(all_tokens))
    choose(out_tokens)
    swap_tokens.start()
    in_tokens[at.col] = out_tokens[at.col]
    swap_vector.arrived()
    swap_tokens.arrived()
    width = at.cols * feats
    parts = [in_tokens[f].astype(f32) for f in range(at.cols)]
    mean = sum(jnp.sum(part, axis=1, keepdims=True) for part in parts) / width
    parts = [part - mean for part in parts]
    variance = sum(jnp.sum(part * part, axis=1, keepdims=True) for part in parts) / width
    inverse_std = lax.rsqrt(variance + norm_floor)
    inverse_std_ref[...] = inverse_std
    own = pl.ds(at.row * piece, piece)
    for f in range(at.cols):
        lanes = slice(f * feats, (f + 1) * feats)
        normalized = parts[f] * inverse_std
        normalized_ref[:, lanes] = normalized
        vectors = vector_all_ref[f]
        dealt_ref[own, lanes] = (normalized * vectors[0:1, :] + vectors[1:2, :]).astype(bf16)
    last_tokens.start(dealt_ref.at[own, :])

    wide[pl.ds(at.row * held, held), :] = cotangent_ref[...].astype(f32)
    first_cots.forward(widen(all_cots))
    first_cots.finish(widen(all_cots))
    choose(out_cots)
    swap_cots.start()
    in_cots[at.col] = out_cots[at.col]
    last_tokens.forward()
    swap_cots.arrived()
    for f in range(at.cols):
        cot_dealt_ref[own, f * feats : (f + 1) * feats] = in_cots[f]
    last_cots.start(cot_dealt_ref.at[own, :])
    last_tokens.finish()
    last_cots.forward()
    last_cots.finish()
    swap_weight.arrived()
    for moved in (first_tokens, first_cots, last_tokens, last_cots):
        moved.sent()
    for moved in (swap_tokens, swap_cots, swap_weight, swap_vector):
        moved.sent()


def deal_all(tokens, cotangent, pick, weight, vectors, rows, cols):
    held, feats = tokens.shape
    total = held * rows
    group = total // cols
    piece = group // rows
    width = feats * cols
    chips = rows // 2
    shape = jax.ShapeDtypeStruct
    return pl.pallas_call(
        deal_kernel,
        out_shape=(
            shape((group, width), bf16),
            shape((group, width), bf16),
            shape((weight.shape[0] * cols, weight.shape[1]), bf16),
            shape((cols,) + vectors.shape, f32),
            shape((piece, width), f32),
            shape((piece, 1), f32),
        ),
        in_specs=[VMEM_SPEC, VMEM_SPEC, SMEM_SPEC, VMEM_SPEC, VMEM_SPEC],
        out_specs=(VMEM_SPEC,) * 6,
        scratch_shapes=[
            pltpu.VMEM((rows, held, feats), bf16),
            pltpu.VMEM((rows, held, feats), bf16),
            pltpu.VMEM((total, feats), f32),
            pltpu.VMEM((cols * piece, feats), f32),
            *([pltpu.VMEM((cols, piece, feats), bf16)] * 4),
            *(gather_sems(chips) * 4),
            *(swap_sems(cols) * 4),
        ],
        compiler_params=pltpu.CompilerParams(
            collective_id=0, has_side_effects=True, vmem_limit_bytes=VMEM_LIMIT
        ),
        name="deal_all",
    )(tokens, cotangent, pick, weight, vectors)


def split(x):
    high_part = x.astype(bf16)
    return high_part, (x - high_part.astype(f32)).astype(bf16)


def three(dot, left, right):
    return dot(left[0], right[0]) + (dot(left[0], right[1]) + dot(left[1], right[0]))


BLK = 128


def gram_kernel(
    in_part_ref,
    bias_ref,
    out_grad_ref,
    momentum_ref,
    in_grad_ref,
    bias_grad_ref,
    matrix_ref,
    gram_ref,
    parts,
    biases,
    chunks,
    partial,
    from_twin,
    half_sum,
    slices,
    *sems,
):
    at = Place()
    sems = list(sems)

    def some(count):
        taken, sems[:count] = sems[:count], []
        return taken

    swap_part = ColSwap(at, lambda c: in_part_ref.at[c], lambda c: parts.at[c], some(2))
    swap_bias = ColSwap(at, lambda c: bias_ref, lambda c: biases.at[c], some(2))
    swap_chunk = ColSwap(at, lambda c: chunks.at[c], lambda c: matrix_ref.at[c], some(2))
    twin_send, twin_recv, sum_send, sum_recv, all_send, all_recv = some(6)
    count = at.chips * 2
    mine = at.chip * 2 + at.col % 2
    first_col = at.col - at.col % 2

    def member(step):
        other = lax.rem(mine + step, count)
        return other, ((other // 2) * 2 + at.core, first_col + other % 2)

    peers = [member(step)[1] for step in range(1, count)]
    meet([(at.row, at.col_at(step)) for step in range(1, at.cols)] + [at.twin] + peers)
    swap_part.start()
    swap_bias.start()
    parts[at.col] = in_part_ref[at.col]
    biases[at.col] = bias_ref[...]
    swap_part.arrived()
    in_grad = sum(parts[c].astype(f32) for c in range(at.cols))
    in_grad_ref[...] = in_grad
    half = in_grad.shape[1] // BLK
    for index in range(at.cols):
        lanes = slice(index * BLK, (index + 1) * BLK)
        if index < half:
            grad = in_grad[:, lanes]
        else:
            grad = out_grad_ref[:, (index - half) * BLK : (index - half + 1) * BLK]
        state = momentum * momentum_ref[:, lanes] + grad
        chunks[index] = grad + momentum * state
    swap_chunk.start()
    matrix_ref[at.col] = chunks[at.col]
    swap_bias.arrived()
    bias_grad_ref[...] = sum(biases[c] for c in range(at.cols))
    swap_chunk.arrived()

    strips = matrix_ref.shape[0]
    matrix = split(matrix_ref[...].reshape(strips * BLK, BLK))
    index = 0
    for i in range(strips):
        left = [m[i * BLK : (i + 1) * BLK, :] for m in matrix]
        right = [m[i * BLK :, :] for m in matrix]
        product = three(dot_nt, left, right)
        for j in range(strips - i):
            partial[index] = product[:, j * BLK : (j + 1) * BLK]
            index += 1
    blocks = index // 2
    to_twin = remote(
        partial.at[pl.ds((1 - at.core) * blocks, blocks)],
        from_twin,
        twin_send.at[0],
        twin_recv.at[0],
        at.twin,
    )
    to_twin.start()
    to_twin.wait_recv()
    for b in range(blocks):
        half_sum[b * BLK : (b + 1) * BLK, :] = partial[at.core * blocks + b] + from_twin[b]

    size = blocks * BLK // count

    def piece_of(owner):
        return half_sum.at[pl.ds(owner * size, size), :]

    def give(step):
        owner, device = member(step)
        return remote(
            piece_of(owner), slices.at[mine], sum_send.at[step], sum_recv.at[step], device
        )

    for step in range(1, count):
        give(step).start()
    slices[mine] = half_sum[pl.ds(mine * size, size), :]
    for step in range(1, count):
        came, device = member(count - step)
        remote(
            slices.at[came], slices.at[came], sum_send.at[step], sum_recv.at[step], device
        ).wait_recv()
    total = slices[0]
    for index in range(1, count):
        total = total + slices[index]
    half_rows = blocks * BLK

    def home(owner):
        return gram_ref.at[pl.ds(at.core * half_rows + owner * size, size), :]

    gram_ref[pl.ds(at.core * half_rows + mine * size, size), :] = total

    def spread(step):
        return remote(
            home(mine), home(mine), all_send.at[step], all_recv.at[step], member(step)[1]
        )

    for step in range(1, count):
        spread(step).start()
    for step in range(1, count):
        came, device = member(count - step)
        remote(
            home(came), home(came), all_send.at[step], all_recv.at[step], device
        ).wait_recv()
    both = gram_ref.at[pl.ds(at.core * half_rows, half_rows), :]
    other = gram_ref.at[pl.ds((1 - at.core) * half_rows, half_rows), :]
    passing = remote(both, both, twin_send.at[1], twin_recv.at[1], at.twin)
    passing.start()
    remote(other, other, twin_send.at[1], twin_recv.at[1], at.twin).wait_recv()
    passing.wait_send()
    to_twin.wait_send()
    for step in range(1, count):
        give(step).wait_send()
        spread(step).wait_send()
    for moved in (swap_part, swap_bias, swap_chunk):
        moved.sent()


WIDE = 256


def poly_kernel(gram_ref, matrix_ref, out_ref, *buffers):
    first, second, third, thin = [buffers[2 * i : 2 * i + 2] for i in range(4)]
    strips = matrix_ref.shape[0]
    size = strips * BLK
    counts = range(size // WIDE)
    eye = lax.broadcasted_iota(jnp.int32, (BLK, BLK), 0) == lax.broadcasted_iota(
        jnp.int32, (BLK, BLK), 1
    )

    def put(pair, rows, lanes, value):
        high_part, low_part = split(value)
        pair[0][rows, lanes] = high_part
        pair[1][rows, lanes] = low_part

    def get(pair, rows, lanes):
        return pair[0][rows, lanes], pair[1][rows, lanes]

    places, index = [], 0
    for i in range(strips):
        for j in range(i, strips):
            places.append((i, j, index))
            index += 1
    trace = sum(
        jnp.sum(jnp.where(eye, gram_ref[at * BLK : (at + 1) * BLK, :], 0.0))
        for i, j, at in places
        if i == j
    )
    shrink = 1.0 / (jnp.sqrt(jnp.full((1, 1), trace, f32)) + ortho_floor)
    for i, j, at in places:
        block = gram_ref[at * BLK : (at + 1) * BLK, :] * (shrink * shrink)
        here, there = slice(i * BLK, (i + 1) * BLK), slice(j * BLK, (j + 1) * BLK)
        put(first, here, there, block)
        if j > i:
            put(first, there, here, block.T)
    everything = slice(0, size)
    for i in range(strips):
        put(thin, slice(i * BLK, (i + 1) * BLK), everything, matrix_ref[i] * shrink)

    def product(left, right, out, finish=None):
        for i in counts:
            rows, rest = slice(i * WIDE, (i + 1) * WIDE), slice(i * WIDE, size)
            value = three(dot_nn, get(left, rows, everything), get(right, everything, rest))
            if finish is not None:
                value = finish(value, rows, rest)
            put(out, rows, rest, value)
            for j in range(i + 1, size // WIDE):
                part = value[:, (j - i) * WIDE : (j - i + 1) * WIDE]
                put(out, slice(j * WIDE, (j + 1) * WIDE), rows, part.T)

    def thin_product(left):
        right = get(thin, everything, everything)
        return [
            three(dot_nn, get(left, slice(i * WIDE, (i + 1) * WIDE), everything), right)
            for i in counts
        ]

    def sweep(gram, poly, square):
        def finish(value, rows, rest):
            high_part, low_part = get(gram, rows, rest)
            value = poly_cubic * value + poly_square * (
                high_part.astype(f32) + low_part.astype(f32)
            )
            at_row = lax.broadcasted_iota(jnp.int32, value.shape, 0)
            at_lane = lax.broadcasted_iota(jnp.int32, value.shape, 1)
            return value + jnp.where(at_row == at_lane, poly_linear, 0.0)

        product(gram, gram, poly, finish)
        for i, value in zip(counts, thin_product(poly)):
            put(thin, slice(i * WIDE, (i + 1) * WIDE), everything, value)
        product(poly, poly, square)
        product(gram, square, poly)

    def two(step, carry):
        sweep(first, second, third)
        sweep(second, first, third)
        return carry

    lax.fori_loop(0, 2, two, 0)
    once = thin_product(first)
    old = []
    for i in counts:
        rows = slice(i * WIDE, (i + 1) * WIDE)
        high_part, low_part = get(thin, rows, everything)
        old.append(high_part.astype(f32) + low_part.astype(f32))
    for i, value in zip(counts, once):
        put(thin, slice(i * WIDE, (i + 1) * WIDE), everything, value)
    for i, value in zip(counts, thin_product(first)):
        result = poly_linear * old[i] + poly_square * once[i] + poly_cubic * value
        out_ref[i * WIDE : (i + 1) * WIDE, :] = result.astype(bf16)


def orthogonalize(gram, matrix):
    size, width = matrix.shape[0] * BLK, matrix.shape[2]
    square, narrow = pltpu.VMEM((size, size), bf16), pltpu.VMEM((size, width), bf16)
    return pl.pallas_call(
        poly_kernel,
        out_shape=jax.ShapeDtypeStruct((size, width), bf16),
        scratch_shapes=[*([square] * 6), *([narrow] * 2)],
        compiler_params=pltpu.CompilerParams(vmem_limit_bytes=VMEM_LIMIT),
        cost_estimate=pl.CostEstimate(
            flops=48 * size**3, bytes_accessed=12 * size * size, transcendentals=0
        ),
        name="orthogonalize",
    )(gram, matrix)


def gram_all(in_part, bias, out_grad, old_momentum, rows, cols):
    feats, width = in_part.shape[1:]
    chips = rows // 2
    blocks = cols * (cols + 1) // 2
    count = chips * 2
    half_rows = blocks * BLK // 2
    shape = jax.ShapeDtypeStruct
    dma = pltpu.SemaphoreType.DMA
    return pl.pallas_call(
        gram_kernel,
        out_shape=(
            shape((feats, width), f32),
            shape(bias.shape, f32),
            shape((cols, feats, BLK), f32),
            shape((blocks * BLK, BLK), f32),
        ),
        in_specs=[VMEM_SPEC] * 4,
        out_specs=(VMEM_SPEC,) * 4,
        scratch_shapes=[
            pltpu.VMEM((cols, feats, width), bf16),
            pltpu.VMEM((cols,) + bias.shape, f32),
            pltpu.VMEM((cols, feats, BLK), f32),
            pltpu.VMEM((blocks, BLK, BLK), f32),
            pltpu.VMEM((blocks // 2, BLK, BLK), f32),
            pltpu.VMEM((half_rows, BLK), f32),
            pltpu.VMEM((count, half_rows // count, BLK), f32),
            *(swap_sems(cols) * 3),
            dma((2,)),
            dma((2,)),
            *([dma((count,))] * 4),
        ],
        compiler_params=pltpu.CompilerParams(
            collective_id=1, has_side_effects=True, vmem_limit_bytes=VMEM_LIMIT
        ),
        name="gram_all",
    )(in_part, bias, out_grad, old_momentum)


def attend(queries, keys_all, values_all, starts):
    rows = queries.shape[0]
    return pl.pallas_call(
        attend_kernel,
        out_shape=(
            jax.ShapeDtypeStruct((rows, HEAD), bf16),
            jax.ShapeDtypeStruct((rows, 1), f32),
        ),
        compiler_params=pltpu.CompilerParams(vmem_limit_bytes=VMEM_LIMIT),
        cost_estimate=pl.CostEstimate(
            flops=2 * rows * rows * HEAD, bytes_accessed=rows * 1024, transcendentals=rows * rows // 2
        ),
        name="attend",
    )(queries, keys_all, values_all, starts)


def attend_back(queries, keys_all, values_all, starts, attended, attended_grad, totals):
    rows = queries.shape[0]
    return pl.pallas_call(
        attend_back_kernel,
        out_shape=(jax.ShapeDtypeStruct((rows, HEAD), f32),) * 3,
        compiler_params=pltpu.CompilerParams(vmem_limit_bytes=VMEM_LIMIT),
        cost_estimate=pl.CostEstimate(
            flops=5 * rows * rows * HEAD, bytes_accessed=rows * 4096, transcendentals=rows * rows // 2
        ),
        name="attend_back",
    )(queries, keys_all, values_all, starts, attended, attended_grad, totals)


def rotary_tables(places):
    half_rot = ROT // 2
    inverse = 1.0 / 10000.0 ** (jnp.arange(half_rot, dtype=f32) * (2.0 / ROT))
    angles = inverse[:, None] * places.astype(f32)[None, :]
    return (jnp.cos(angles).T, jnp.sin(angles).T)


def rotate(values, cosine, sine):
    half_rot = ROT // 2
    lower_half = values[..., :half_rot]
    upper_half = values[..., half_rot:ROT]
    return jnp.concatenate(
        [
            lower_half * cosine - upper_half * sine,
            upper_half * cosine + lower_half * sine,
            values[..., ROT:],
        ],
        axis=-1,
    )


def gelu_tanh(values):
    return jax.nn.gelu(values, approximate=True)


def adam_step(value, gradient, first_state, second_state):
    first_new = beta_first * first_state + (1.0 - beta_first) * gradient
    second_new = beta_second * second_state + (1.0 - beta_second) * gradient * gradient
    corrected = first_new / (1.0 - beta_first**STEP)
    root_term = jnp.sqrt(second_new / (1.0 - beta_second**STEP)) + adam_floor
    return (first_new, second_new, value - rate_vector * corrected / root_term)


def gather_row(x):
    return lax.all_gather(x, "row", axis=0, tiled=True)


def swap_col(x):
    return lax.all_to_all(x, "col", split_axis=0, concat_axis=0, tiled=True)


def sum_scatter(x, axis):
    return lax.psum_scatter(x, axis, scatter_dimension=0, tiled=True)


def take_rows(x, index):
    return x.at[index].get(mode="promise_in_bounds")


def high_low(x):
    high_part = x.astype(bf16)
    return high_part, (x - high_part.astype(f32)).astype(bf16)


def per_device(
    tokens,
    cotangent,
    lengths,
    deal_order,
    qkv_weight,
    up_weight,
    proj_weight,
    down_weight,
    norm_vectors,
    qkv_bias,
    mlp_bias,
    qkv_momentum,
    up_momentum,
    proj_momentum,
    down_momentum,
    norm_moment,
    norm_square,
    qkv_bias_moment,
    qkv_bias_square,
    mlp_bias_moment,
    mlp_bias_square,
):
    cols, rows = lax.axis_size("col"), lax.axis_size("row")
    col, row = lax.axis_index("col"), lax.axis_index("row")
    total_tokens = deal_order.shape[0]
    group = total_tokens // cols
    piece = group // rows
    held = total_tokens // rows
    feats = D // cols
    qkv_width, up_width = qkv_weight.shape[1], up_weight.shape[1]
    proj_width = proj_weight.shape[0]

    seq_ends = jnp.cumsum(lengths)
    seq_starts = seq_ends - lengths
    anchor = lax.dynamic_slice_in_dim(deal_order, col * group, group)
    before = seq_ends[None, :] <= anchor[:, None]
    places = anchor - jnp.sum(jnp.where(before, lengths[None, :], 0), axis=1)
    starts = (jnp.arange(group, dtype=jnp.int32) - places)[:, None]
    at = jnp.arange(total_tokens, dtype=jnp.int32)
    dealt_starts = jnp.sum(
        jnp.where(deal_order[None, :] == seq_starts[:, None], at[None, :], 0), axis=1
    )
    own = row * held + jnp.arange(held, dtype=jnp.int32)
    holds = (seq_starts[None, :] <= own[:, None]) & (own[:, None] < seq_ends[None, :])
    dealt_at = own + jnp.sum(jnp.where(holds, (dealt_starts - seq_starts)[None, :], 0), axis=1)
    cosine, sine = rotary_tables(places)

    def lanes(x, width):
        return jnp.pad(x, ((0, 0), (0, width - x.shape[1])))

    in_pad = 2 * up_width
    tile = jnp.concatenate(
        [
            lanes(qkv_weight.astype(bf16), up_width),
            up_weight.astype(bf16),
            lanes(proj_weight.astype(bf16).T, 128),
            down_weight.astype(bf16).T,
        ],
        axis=1,
    )
    pick = lax.dynamic_slice(
        deal_order.reshape(cols, rows, piece), (0, row, 0), (cols, 1, piece)
    ).reshape(-1)
    dealt, cotangent_dealt, weight_all, vector_all, normalized, inverse_std = deal_all(
        tokens, cotangent, pick, tile, jnp.pad(norm_vectors, ((0, 5), (0, 0))), rows, cols
    )
    in_all, out_all = weight_all[:, :in_pad], weight_all[:, in_pad:]
    gain_all = vector_all[:, 0, :].reshape(1, D)

    def deal_back(x, more, own_more):
        parts = x.astype(bf16).reshape(piece, cols, feats).transpose(1, 0, 2)
        if more is None:
            stride = piece
            swapped = swap_col(parts)
        else:
            stride = piece + EXTRA
            swapped = swap_col(jnp.concatenate([parts, more], axis=1))
            own_more = jnp.pad(
                own_more[None], ((0, cols - 1), (stride - own_more.shape[0], 0), (0, 0))
            )
            swapped = swapped + own_more
        whole = gather_row(swapped.reshape(cols * stride, feats))
        block, inside = dealt_at // group, dealt_at % group
        index = (inside // piece) * (cols * stride) + block * stride + inside % piece
        return take_rows(whole, index), whole

    out_bias = norm_vectors[2]
    preact = dot_nn(dealt, in_all)
    pre_qkv = preact[:, :qkv_width] + qkv_bias
    pre_up = preact[:, up_width:] + mlp_bias
    queries = (rotate(pre_qkv[:, :HEAD], cosine, sine).astype(bf16) * HEAD**-0.5).astype(bf16)
    keys_all = rotate(pre_qkv[:, HEAD : 2 * HEAD], cosine, sine).astype(bf16)
    values_all = pre_qkv[:, 2 * HEAD :].astype(bf16)
    attended, totals = attend(queries, keys_all, values_all, starts)
    activated, gelu_back = jax.vjp(gelu_tanh, pre_up)
    branch = jnp.concatenate([lanes(attended, 128), activated.astype(bf16)], axis=1)
    branch_sum = sum_scatter(dot_nt(branch, out_all).astype(bf16), "row")
    branch_back, _ = deal_back(branch_sum, None, None)
    output = tokens.astype(f32) + branch_back.astype(f32) + out_bias

    branch_grad = dot_nn(cotangent_dealt, out_all)
    out_grad = sum_scatter(dot_tn(cotangent_dealt, branch), "col")
    attended_grad = branch_grad[:, :proj_width].astype(bf16)
    up_pre_grad = gelu_back(branch_grad[:, 128:])[0]
    query_grad, key_grad, value_grad = attend_back(
        queries, keys_all, values_all, starts, attended, attended_grad, totals
    )
    preact_grad = jnp.concatenate(
        [
            rotate(query_grad, cosine, -sine),
            rotate(key_grad, cosine, -sine),
            value_grad,
            jnp.zeros_like(value_grad),
            up_pre_grad,
        ],
        axis=1,
    ).astype(bf16)
    in_part = dot_tn(dealt, preact_grad).astype(bf16).reshape(cols, feats, in_pad)
    bias_part = jnp.sum(preact_grad, axis=0, dtype=f32)
    normed_grad = sum_scatter(dot_nt(preact_grad, in_all).astype(bf16), "row").astype(f32)
    scaled = normed_grad * gain_all
    mean_first = jnp.mean(scaled, axis=1, keepdims=True)
    mean_second = jnp.mean(scaled * normalized, axis=1, keepdims=True)
    token_grad = inverse_std * (scaled - mean_first - normalized * mean_second)
    vector_rows = jnp.stack(
        [
            *high_low(jnp.sum(normed_grad * normalized, axis=0)),
            *high_low(jnp.sum(normed_grad, axis=0)),
        ],
        axis=0,
    )
    vector_rows = jnp.pad(
        vector_rows.reshape(4, cols, feats).transpose(1, 0, 2), ((0, 0), (0, EXTRA - 4), (0, 0))
    )
    bias_rows = jnp.stack(high_low(jnp.sum(cotangent, axis=0, dtype=f32)), axis=0)
    token_back, whole = deal_back(token_grad, vector_rows, bias_rows)
    input_grad = cotangent.astype(f32) + token_back.astype(f32)
    vector_sum = jnp.sum(
        whole.reshape(rows * cols, piece + EXTRA, feats)[:, piece:].astype(f32), axis=0
    )
    norm_grads = jnp.stack(
        [
            vector_sum[0] + vector_sum[1],
            vector_sum[2] + vector_sum[3],
            vector_sum[-2] + vector_sum[-1],
        ],
        axis=0,
    )

    out_grad = jnp.concatenate(
        [lanes(out_grad[:, :proj_width], up_width), out_grad[:, 128:]], axis=1
    )
    old_momentum = jnp.concatenate(
        [
            lanes(qkv_momentum, up_width),
            up_momentum,
            lanes(proj_momentum.T, up_width),
            down_momentum.T,
        ],
        axis=1,
    )
    in_grad, bias_rows, matrix, gram = gram_all(
        in_part, jnp.broadcast_to(bias_part[None], (8, in_pad)), out_grad, old_momentum, rows, cols
    )
    in_bias_grad = bias_rows[0]
    gradients = (
        in_grad[:, :qkv_width],
        in_grad[:, up_width:],
        out_grad[:, :proj_width].T,
        out_grad[:, up_width:].T,
    )
    old_states = (qkv_momentum, up_momentum, proj_momentum, down_momentum)
    weights = (qkv_weight, up_weight, proj_weight, down_weight)
    widths = (3 * D, FF, D, FF)
    sizes = (qkv_width, up_width, proj_width, up_width)
    states = [momentum * old + g for old, g in zip(old_states, gradients)]
    returned = swap_col(orthogonalize(gram, matrix).reshape(cols, feats, BLK))
    new_weights = []
    for index in range(4):
        update = jnp.concatenate([returned[2 * index], returned[2 * index + 1]], axis=1)
        update = update[:, : sizes[index]].astype(f32)
        update = update.T if index >= 2 else update
        new_weights.append(
            weights[index] * (1.0 - rate_matrix * decay_matrix)
            - rate_matrix * 0.2 * math.sqrt(widths[index]) * update
        )

    norm_first, norm_second, norm_new = adam_step(
        norm_vectors, norm_grads, norm_moment, norm_square
    )
    qkv_first, qkv_second, qkv_bias_new = adam_step(
        qkv_bias, in_bias_grad[:qkv_width], qkv_bias_moment, qkv_bias_square
    )
    mlp_first, mlp_second, mlp_bias_new = adam_step(
        mlp_bias, in_bias_grad[up_width:], mlp_bias_moment, mlp_bias_square
    )
    return (
        output,
        input_grad,
        *gradients,
        *states,
        *new_weights,
        norm_first,
        norm_second,
        norm_new,
        qkv_first,
        qkv_second,
        qkv_bias_new,
        mlp_first,
        mlp_second,
        mlp_bias_new,
    )


def solution(mesh):
    over_both, over_flip = P("row", "col"), P("col", "row")
    features, hidden = P(None, "col"), P("row")
    return jax.shard_map(
        per_device,
        mesh=mesh,
        in_specs=(
            *(over_both, over_both, P(), P()),
            *(over_flip, over_flip, over_both, over_both),
            *(features, hidden, hidden),
            *(over_flip, over_flip, over_both, over_both),
            *(features, features, hidden, hidden, hidden, hidden),
        ),
        out_specs=(
            *(over_both, over_both),
            *(over_flip, over_flip, over_both, over_both) * 3,
            *(features,) * 3,
            *(hidden,) * 6,
        ),
        check_vma=False,
    )
```

```python
import functools
import math

import jax
import jax.numpy as jnp
from jax import lax
from jax.experimental import pallas as pl
from jax.experimental.pallas import tpu as pltpu
from jax.sharding import PartitionSpec as P

D = 1024
HEAD = 64
ROT = 16
FF = 4096
STEP = 10

poly_linear = 3.4445
poly_square = -4.775
poly_cubic = 2.0315
momentum = 0.95
rate_matrix = 0.15
decay_matrix = 0.1
beta_first = 0.9
beta_second = 0.95
rate_vector = 0.2
adam_floor = 1e-08
norm_floor = 1e-05
ortho_floor = 1e-07
masked_score = -1e30
f32 = jnp.float32
bf16 = jnp.bfloat16
BLOCK = 256
EXTRA = 16


def dot_nt(a, b, **kw):
    return lax.dot_general(a, b, (((1,), (1,)), ((), ())), preferred_element_type=f32, **kw)


def dot_tn(a, b, **kw):
    return lax.dot_general(a, b, (((0,), (0,)), ((), ())), preferred_element_type=f32, **kw)


def dot_nn(a, b, **kw):
    return lax.dot_general(a, b, (((1,), (0,)), ((), ())), preferred_element_type=f32, **kw)


def allowed_keys(start_ref, first, keys):
    shape = (BLOCK, keys)
    key_at = lax.broadcasted_iota(jnp.int32, shape, 1)
    query_at = first + lax.broadcasted_iota(jnp.int32, shape, 0)
    return (key_at >= start_ref[pl.ds(first, BLOCK), :]) & (key_at <= query_at)


def turning(table_ref, rows):
    lane = lax.broadcasted_iota(jnp.int32, (32, 2 * HEAD), 1) % HEAD
    entry = lax.broadcasted_iota(jnp.int32, (32, 2 * HEAD), 0) % 16
    half_rot = ROT // 2

    def spread(where, value):
        picks = jnp.where(where, value, 0.0).astype(bf16)
        return dot_tn(table_ref[:, rows], picks)

    cosine = spread((lane < ROT) & (entry == lane % half_rot), 1.0)
    cosine = cosine + jnp.where(lane[:1] < ROT, 0.0, 1.0)
    lower = spread((lane < half_rot) & (entry == lane + half_rot), -1.0)
    upper = spread((lane >= half_rot) & (lane < ROT) & (entry == lane), 1.0)
    return cosine, lower, upper


def turned(values, tables, back):
    cosine, lower, upper = tables
    half_rot = ROT // 2
    moved = (
        pltpu.roll(values, 2 * HEAD - half_rot, 1) * lower + pltpu.roll(values, half_rot, 1) * upper
    )
    return values * cosine - moved if back else values * cosine + moved


def forward_kernel(
    dealt_ref,
    cotangent_ref,
    weight_ref,
    bias_ref,
    table_ref,
    start_ref,
    q_ref,
    k_ref,
    v_ref,
    slope_ref,
    branch_ref,
    total_ref,
    partial_ref,
    out_part_ref,
):
    width = bias_ref.shape[1]
    in_weight, out_weight = weight_ref[:, :width], weight_ref[:, width:]
    inner = math.sqrt(2.0 / math.pi)
    firsts = range(0, dealt_ref.shape[0], BLOCK)
    for first in firsts:
        rows = pl.ds(first, BLOCK)
        pre = dot_nn(dealt_ref[rows, :], in_weight) + bias_ref[...]
        pair = turned(pre[:, : 2 * HEAD], turning(table_ref, rows), False).astype(bf16)
        q_ref[rows, :] = (pair[:, :HEAD] * HEAD**-0.5).astype(bf16)
        k_ref[rows, :] = pair[:, HEAD:]
        v_ref[rows, :] = pre[:, 2 * HEAD : 3 * HEAD].astype(bf16)
        up = pre[:, 4 * HEAD :]
        square = up * up
        bent = jnp.tanh(inner * (up + 0.044715 * square * up))
        branch_ref[rows, 2 * HEAD :] = (0.5 * up * (1.0 + bent)).astype(bf16)
        slope_ref[rows, :] = 0.5 * (1.0 + bent) + 0.5 * up * (1.0 - bent * bent) * (
            inner * (1.0 + 3.0 * 0.044715 * square)
        )
    for first in firsts:
        rows, keys = pl.ds(first, BLOCK), first + BLOCK
        scores = dot_nt(q_ref[rows, :], k_ref[:keys, :])
        scores = jnp.where(allowed_keys(start_ref, first, keys), scores, masked_score)
        top = jnp.max(scores, axis=1, keepdims=True)
        raw = jnp.exp(scores - top)
        total = jnp.sum(raw, axis=1, keepdims=True)
        attended = dot_nn(raw.astype(bf16), v_ref[:keys, :]) / total
        branch_ref[rows, : 2 * HEAD] = jnp.concatenate(
            [attended, jnp.zeros_like(attended)], axis=1
        ).astype(bf16)
        total_ref[rows, :] = top + jnp.log(total)
        partial_ref[rows, :] = dot_nt(branch_ref[rows, :], out_weight).astype(bf16)
    for first in range(0, cotangent_ref.shape[1], BLOCK):
        lanes = slice(first, first + BLOCK)
        out_part_ref[lanes, :] = dot_tn(cotangent_ref[:, lanes], branch_ref[...])


def backward_kernel(
    dealt_ref,
    cotangent_ref,
    weight_ref,
    table_ref,
    start_ref,
    q_ref,
    k_ref,
    v_ref,
    slope_ref,
    branch_ref,
    total_ref,
    branch_part_ref,
    out_part_ref,
    in_part_ref,
    bias_part_ref,
    normed_part_ref,
    branch_sum_ref,
    out_grad_ref,
    grad_ref,
    pre_ref,
    dk_ref,
    dv_ref,
    out_parts,
    pairs,
    slots,
    *sems,
):
    at = Place()
    branch_rows = RowSum(at, branch_part_ref, pairs, slots, sems[:4])
    swap_out = ColSwap(at, lambda c: out_part_ref.at[c], lambda c: out_parts.at[c], sems[4:])
    meet(row_peers(at) + col_peers(at))
    branch_rows.start()
    swap_out.start()
    out_parts[at.col] = out_part_ref[at.col]
    width = pre_ref.shape[1]
    in_weight, out_weight = weight_ref[:, :width], weight_ref[:, width:]
    firsts = range(0, dealt_ref.shape[0], BLOCK)
    for first in firsts:
        rows = pl.ds(first, BLOCK)
        branch_grad = dot_nn(cotangent_ref[rows, :], out_weight)
        grad_ref[rows, :] = branch_grad[:, :HEAD].astype(bf16)
        pre_ref[rows, 4 * HEAD :] = (branch_grad[:, 2 * HEAD :] * slope_ref[rows, :]).astype(bf16)
    dk_ref[...] = jnp.zeros_like(dk_ref)
    dv_ref[...] = jnp.zeros_like(dv_ref)
    branch_rows.middle()
    for first in reversed(firsts):
        rows, keys = pl.ds(first, BLOCK), first + BLOCK
        query, grad = q_ref[rows, :], grad_ref[rows, :]
        key, value = k_ref[:keys, :], v_ref[:keys, :]
        scores = dot_nt(query, key)
        allowed = allowed_keys(start_ref, first, keys)
        prob = jnp.where(allowed, jnp.exp(scores - total_ref[rows, :]), 0.0)
        delta = jnp.sum(
            grad.astype(f32) * branch_ref[rows, :HEAD].astype(f32), axis=1, keepdims=True
        )
        score_grad = (prob * (dot_nt(grad, value) - delta)).astype(bf16)
        dk_ref[:keys, :] += dot_tn(score_grad, query)
        dv_ref[:keys, :] += dot_tn(prob.astype(bf16), grad)
        pair = jnp.concatenate([dot_nn(score_grad, key) * HEAD**-0.5, dk_ref[rows, :]], axis=1)
        pre_ref[rows, : 2 * HEAD] = turned(pair, turning(table_ref, rows), True).astype(bf16)
        dv = dv_ref[rows, :]
        pre_ref[rows, 2 * HEAD : 4 * HEAD] = jnp.concatenate(
            [dv, jnp.zeros_like(dv)], axis=1
        ).astype(bf16)
        normed_part_ref[rows, :] = dot_nt(pre_ref[rows, :], in_weight).astype(bf16)
    feats = in_part_ref.shape[1]
    each = BLOCK // feats
    for first in range(0, dealt_ref.shape[1], BLOCK):
        part = dot_tn(dealt_ref[:, first : first + BLOCK], pre_ref[...])
        for index in range(each):
            in_part_ref[first // feats + index] = part[
                index * feats : (index + 1) * feats, :
            ].astype(bf16)
    bias = jnp.sum(pre_ref[...].astype(f32), axis=0, keepdims=True)
    bias_part_ref[...] = jnp.broadcast_to(bias, bias_part_ref.shape)
    swap_out.arrived()
    total = sum(out_parts[c] for c in range(at.cols))
    filled = jnp.zeros((total.shape[0], width // 2 - 2 * HEAD), f32)
    out_grad_ref[:, : 2 * HEAD] = total[:, : 2 * HEAD]
    out_grad_ref[:, 2 * HEAD : width // 2] = filled
    out_grad_ref[:, width // 2 :] = total[:, 2 * HEAD :]
    branch_sum_ref[...] = branch_rows.finish().astype(bf16)
    branch_rows.sent()
    swap_out.sent()


def local_call(kernel, out_shape, scratch, flops, name):
    return pl.pallas_call(
        kernel,
        out_shape=out_shape,
        scratch_shapes=scratch,
        compiler_params=pltpu.CompilerParams(vmem_limit_bytes=VMEM_LIMIT),
        cost_estimate=pl.CostEstimate(flops=flops, bytes_accessed=1 << 24, transcendentals=0),
        name=name,
    )


def forward(dealt, cotangent, weight, bias, table, starts):
    rows, width = dealt.shape
    up = bias.shape[1] - 4 * HEAD
    branch = up + 2 * HEAD
    shape = jax.ShapeDtypeStruct
    head = shape((rows, HEAD), bf16)
    return local_call(
        forward_kernel,
        (
            *(head, head, head),
            shape((rows, up), f32),
            shape((rows, branch), bf16),
            shape((rows, 1), f32),
            shape((rows, width), bf16),
            shape((width, branch), f32),
        ),
        [],
        25 * 10**9,
        "forward",
    )(dealt, cotangent, weight, bias, table, starts)


def remote_call(kernel, identity, out_shape, in_specs, scratch, flops, name):
    return pl.pallas_call(
        kernel,
        out_shape=out_shape,
        in_specs=in_specs,
        out_specs=(VMEM_SPEC,) * len(out_shape),
        scratch_shapes=scratch,
        compiler_params=pltpu.CompilerParams(
            collective_id=identity, has_side_effects=True, vmem_limit_bytes=VMEM_LIMIT
        ),
        cost_estimate=pl.CostEstimate(flops=flops, bytes_accessed=1 << 24, transcendentals=0),
        name=name,
    )


def backward(dealt, cotangent, weight, table, starts, kept, branch_part, out_part, rows, cols):
    tokens, width = dealt.shape
    in_width = 4 * HEAD + kept[3].shape[1]
    out_width = out_part.shape[1]
    feats, piece, chips = width // cols, tokens // rows, rows // 2
    shape = jax.ShapeDtypeStruct
    return remote_call(
        backward_kernel,
        2,
        (
            shape((cols, feats, in_width), bf16),
            shape((8, in_width), f32),
            shape((tokens, width), bf16),
            shape((piece, width), bf16),
            shape((feats, in_width), f32),
        ),
        [VMEM_SPEC] * 13,
        [
            pltpu.VMEM((tokens, HEAD), bf16),
            pltpu.VMEM((tokens, in_width), bf16),
            pltpu.VMEM((tokens, HEAD), f32),
            pltpu.VMEM((tokens, HEAD), f32),
            pltpu.VMEM((cols, feats, out_width), f32),
            *sum_scratch(piece, width, chips),
            *swap_sems(cols),
        ],
        30 * 10**9,
        "backward",
    )(
        *(dealt, cotangent, weight, table, starts, *kept),
        branch_part.reshape(chips, 2, piece, width),
        out_part.reshape(cols, feats, out_width),
    )


VMEM_LIMIT = 48 * 1024 * 1024


MESH = pl.DeviceIdType.MESH
VMEM_SPEC = pl.BlockSpec(memory_space=pltpu.VMEM)
SMEM_SPEC = pl.BlockSpec(memory_space=pltpu.SMEM)


def remote(src, dst, send, recv, device):
    return pltpu.make_async_remote_copy(
        src_ref=src, dst_ref=dst, send_sem=send, recv_sem=recv, device_id=device, device_id_type=MESH
    )


class Place:
    def __init__(self):
        self.row, self.col = lax.axis_index("row"), lax.axis_index("col")
        self.rows, self.cols = lax.axis_size("row"), lax.axis_size("col")
        self.chips = self.rows // 2
        self.chip, self.core = self.row // 2, self.row % 2
        self.twin = (self.chip * 2 + 1 - self.core, self.col)
        self.ring = self.chips // 2
        self.y, self.z = self.chip // self.ring, self.chip % self.ring

    def chip_at(self, step):
        return lax.rem(self.chip + step, self.chips)

    def chip_row(self, step):
        return self.chip_at(step) * 2 + self.core

    def col_at(self, step):
        return lax.rem(self.col + step, self.cols)


def meet(devices):
    barrier = pltpu.get_barrier_semaphore()
    for device in devices:
        pl.semaphore_signal(barrier, inc=1, device_id=device, device_id_type=MESH)
    pl.semaphore_wait(barrier, len(devices))


class RowGather:
    OWN, PARTNER, BELOW, ABOVE, BELOW_PARTNER, ABOVE_PARTNER, FAR, FAR_PARTNER = range(8)

    def __init__(self, at, slot, sems):
        self.at, self.slot = at, slot
        self.sems = sems
        ring, z, y = at.ring, at.z, at.y
        self.chips = [
            y * ring + z,
            (1 - y) * ring + z,
            y * ring + lax.rem(z + ring - 1, ring),
            y * ring + lax.rem(z + 1, ring),
            (1 - y) * ring + lax.rem(z + ring - 1, ring),
            (1 - y) * ring + lax.rem(z + 1, ring),
            y * ring + lax.rem(z + 2, ring),
            (1 - y) * ring + lax.rem(z + 2, ring),
        ]

    def row_of(self, which):
        return self.chips[which] * 2 + self.at.core

    def block(self, which):
        return self.slot(self.row_of(which))

    def part(self, which, upper):
        ref = self.block(which)
        half = ref.shape[0] // 2
        return ref.at[pl.ds(0 if upper else half, half), :]

    def hop(self, tag, src, dst, to):
        send, recv = self.sems[0], self.sems[1]
        return remote(src, dst, send.at[tag], recv.at[tag], (self.row_of(to), self.at.col))

    def took(self, tag, ref):
        self.hop(tag, ref, ref, self.PARTNER).wait_recv()

    def passing(self, which, src=None):
        send, recv = self.sems[2], self.sems[3]
        ref = self.block(which)
        return remote(
            ref if src is None else src, ref, send.at[which], recv.at[which], self.at.twin
        )

    def hops(self):
        own, src = self.block(self.OWN), self.src
        partner = self.block(self.PARTNER)
        below, above = self.part(self.BELOW, True), self.part(self.ABOVE, False)
        far_below = self.part(self.BELOW_PARTNER, True)
        far_above = self.part(self.ABOVE_PARTNER, False)
        return {
            "start": [
                (0, src, own, self.PARTNER),
                (1, src, own, self.ABOVE),
                (2, src, own, self.BELOW),
            ],
            "partner": [(3, partner, partner, self.ABOVE), (4, partner, partner, self.BELOW)],
            "below": [(5, below, below, self.ABOVE)],
            "above": [(6, above, above, self.BELOW)],
            "far_below": [(7, far_below, far_below, self.ABOVE)],
            "far_above": [(8, far_above, far_above, self.BELOW)],
        }

    def go(self, stage):
        for hop in self.hops()[stage]:
            self.hop(*hop).start()

    def start(self, src):
        self.src = src
        self.go("start")
        self.passing(self.OWN, src).start()

    def landed(self, which, then):
        self.passing(which).start()
        if then is not None:
            then(self.row_of(which))

    def forward(self, then=None):
        self.took(1, self.block(self.BELOW))
        self.go("below")
        self.took(2, self.block(self.ABOVE))
        self.go("above")
        self.landed(self.BELOW, then)
        self.landed(self.ABOVE, then)
        self.took(0, self.block(self.PARTNER))
        self.go("partner")
        self.landed(self.PARTNER, then)
        self.took(3, self.block(self.BELOW_PARTNER))
        self.go("far_below")
        self.took(4, self.block(self.ABOVE_PARTNER))
        self.go("far_above")
        self.landed(self.BELOW_PARTNER, then)
        self.landed(self.ABOVE_PARTNER, then)
        self.took(5, self.part(self.FAR, True))
        self.took(6, self.part(self.FAR, False))
        self.landed(self.FAR, then)
        self.took(7, self.part(self.FAR_PARTNER, True))
        self.took(8, self.part(self.FAR_PARTNER, False))
        self.landed(self.FAR_PARTNER, then)

    def finish(self, then=None):
        send, recv = self.sems[2], self.sems[3]
        for which in range(8):
            row = self.chips[which] * 2 + 1 - self.at.core
            slot = self.slot(row)
            remote(slot, slot, send.at[which], recv.at[which], self.at.twin).wait_recv()
            if then is not None:
                then(row)

    def sent(self):
        for stage in self.hops().values():
            for hop in stage:
                self.hop(*hop).wait_send()
        self.passing(self.OWN, self.src).wait_send()
        for which in range(1, 8):
            self.passing(which).wait_send()


class ColSwap:
    def __init__(self, at, src, dst, sems):
        self.at, self.src, self.dst = at, src, dst
        self.send, self.recv = sems

    def outgoing(self, step):
        at = self.at
        to = at.col_at(step)
        return remote(
            self.src(to), self.dst(at.col), self.send.at[step], self.recv.at[step], (at.row, to)
        )

    def start(self):
        for step in range(1, self.at.cols):
            self.outgoing(step).start()

    def arrived(self):
        at = self.at
        for step in range(1, at.cols):
            came = at.col_at(at.cols - step)
            slot = self.dst(came)
            remote(slot, slot, self.send.at[step], self.recv.at[step], (at.row, came)).wait_recv()

    def sent(self):
        for step in range(1, self.at.cols):
            self.outgoing(step).wait_send()


class RowSum:
    SEMS = 4

    def __init__(self, at, part, pairs, slots, sems):
        self.at, self.part, self.pairs, self.slots = at, part, pairs, slots
        self.twin_send, self.twin_recv, self.send, self.recv = sems

    def to_twin(self):
        at = self.at
        return remote(
            self.part.at[:, 1 - at.core],
            self.pairs,
            self.twin_send.at[0],
            self.twin_recv.at[0],
            at.twin,
        )

    def outgoing(self, step):
        at = self.at
        return remote(
            self.pairs.at[at.chip_at(step)],
            self.slots.at[at.chip],
            self.send.at[step],
            self.recv.at[step],
            (at.chip_row(step), at.col),
        )

    def start(self):
        self.to_twin().start()

    def middle(self):
        at = self.at
        self.to_twin().wait_recv()

        for step in (4, 1, 2, 3, 5, 6, 7, 0):
            chip = at.chip_at(step)
            both = self.part[chip, at.core].astype(f32) + self.pairs[chip].astype(f32)
            self.pairs[chip] = both.astype(bf16)
            if step > 0:
                self.outgoing(step).start()

    def finish(self):
        at = self.at
        total = self.pairs[at.chip].astype(f32)
        for step in range(1, at.chips):
            chip = at.chip_at(at.chips - step)
            slot = self.slots.at[chip]
            remote(
                slot, slot, self.send.at[step], self.recv.at[step], (chip * 2 + at.core, at.col)
            ).wait_recv()
            total = total + self.slots[chip].astype(f32)
        return total

    def sent(self):
        self.to_twin().wait_send()
        for step in range(1, self.at.chips):
            self.outgoing(step).wait_send()


def sum_scratch(piece, width, chips):
    dma = pltpu.SemaphoreType.DMA
    return [
        pltpu.VMEM((chips, piece, width), bf16),
        pltpu.VMEM((chips, piece, width), bf16),
        dma((1,)),
        dma((1,)),
        dma((chips,)),
        dma((chips,)),
    ]


class RowSpread:
    def __init__(self, at, whole, sems):
        self.at, self.whole = at, whole
        self.send, self.recv, self.pass_send, self.pass_recv = sems

    def outgoing(self, step):
        at = self.at
        slot = self.whole.at[at.row]
        return remote(
            slot, slot, self.send.at[step], self.recv.at[step], (at.chip_row(step), at.col)
        )

    def passing(self, step):
        at = self.at
        slot = self.whole.at[at.chip_row(at.chips - step)]
        return remote(slot, slot, self.pass_send.at[step], self.pass_recv.at[step], at.twin)

    def start(self):
        for step in (4, 1, 2, 3, 5, 6, 7):
            self.outgoing(step).start()
        self.passing(0).start()

    def middle(self):
        at = self.at
        for step in (4, 1, 2, 3, 5, 6, 7):
            row = at.chip_row(at.chips - step)
            slot = self.whole.at[row]
            remote(slot, slot, self.send.at[step], self.recv.at[step], (row, at.col)).wait_recv()
            self.passing(step).start()

    def finish(self):
        at = self.at
        for step in range(at.chips):
            slot = self.whole.at[at.chip_at(at.chips - step) * 2 + 1 - at.core]
            remote(
                slot, slot, self.pass_send.at[step], self.pass_recv.at[step], at.twin
            ).wait_recv()

    def sent(self):
        for step in range(1, self.at.chips):
            self.outgoing(step).wait_send()
        for step in range(self.at.chips):
            self.passing(step).wait_send()


def row_peers(at):
    return [(at.chip_row(step), at.col) for step in range(1, at.chips)] + [at.twin]


def col_peers(at):
    return [(at.row, at.col_at(step)) for step in range(1, at.cols)]


def gather_sems():
    return [pltpu.SemaphoreType.DMA((count,)) for count in (9, 9, 8, 8)]


def swap_sems(cols):
    return [pltpu.SemaphoreType.DMA((cols,))] * 2


def deal_kernel(
    tokens_ref,
    cotangent_ref,
    pick_ref,
    weight_ref,
    vector_ref,
    dealt_ref,
    cot_dealt_ref,
    weight_all_ref,
    vector_all_ref,
    normalized_ref,
    inverse_std_ref,
    all_tokens,
    all_cots,
    wide,
    chosen,
    out_tokens,
    in_tokens,
    out_cots,
    in_cots,
    *sems,
):
    at = Place()
    held, feats = tokens_ref.shape
    piece = out_tokens.shape[1]
    depth = weight_ref.shape[0]
    sems = list(sems)

    def some(count):
        taken, sems[:count] = sems[:count], []
        return taken

    def dealt_slot(ref):
        return lambda row: ref.at[pl.ds(row * piece, piece), :]

    first_tokens = RowGather(at, lambda row: all_tokens.at[row], some(4))
    first_cots = RowGather(at, lambda row: all_cots.at[row], some(4))
    last_tokens = RowGather(at, dealt_slot(dealt_ref), some(4))
    last_cots = RowGather(at, dealt_slot(cot_dealt_ref), some(4))
    swap_tokens = ColSwap(at, lambda c: out_tokens.at[c], lambda c: in_tokens.at[c], some(2))
    swap_cots = ColSwap(at, lambda c: out_cots.at[c], lambda c: in_cots.at[c], some(2))
    swap_weight = ColSwap(
        at, lambda c: weight_ref, lambda c: weight_all_ref.at[pl.ds(c * depth, depth), :], some(2)
    )
    swap_vector = ColSwap(at, lambda c: vector_ref, lambda c: vector_all_ref.at[c], some(2))

    meet(
        [(first_tokens.row_of(which), at.col) for which in (1, 2, 3)]
        + [at.twin]
        + [(at.row, at.col_at(step)) for step in range(1, at.cols)]
    )
    first_tokens.start(tokens_ref)
    swap_vector.start()
    swap_weight.start()
    weight_all_ref[pl.ds(at.col * depth, depth), :] = weight_ref[...]
    vector_all_ref[at.col] = vector_ref[...]

    def widen(src):
        def one(row):
            wide[pl.ds(row * held, held), :] = src[row].astype(f32)

        return one

    def choose(out_ref):
        def eight(step, carry):
            first = step * 8
            found = [wide[pl.ds(pick_ref[first + i], 1), :] for i in range(8)]
            chosen[pl.ds(first, 8), :] = jnp.concatenate(found, axis=0)
            return carry

        lax.fori_loop(0, at.cols * piece // 8, eight, 0)
        for c in range(at.cols):
            out_ref[c] = chosen[c * piece : (c + 1) * piece, :].astype(bf16)

    wide[pl.ds(at.row * held, held), :] = tokens_ref[...].astype(f32)
    first_tokens.forward(widen(all_tokens))
    first_cots.start(cotangent_ref)
    first_tokens.finish(widen(all_tokens))
    choose(out_tokens)
    swap_tokens.start()
    in_tokens[at.col] = out_tokens[at.col]
    swap_vector.arrived()
    swap_tokens.arrived()
    width = at.cols * feats
    parts = [in_tokens[f].astype(f32) for f in range(at.cols)]
    mean = sum(jnp.sum(part, axis=1, keepdims=True) for part in parts) / width
    parts = [part - mean for part in parts]
    variance = sum(jnp.sum(part * part, axis=1, keepdims=True) for part in parts) / width
    inverse_std = lax.rsqrt(variance + norm_floor)
    inverse_std_ref[...] = inverse_std
    own = pl.ds(at.row * piece, piece)
    for f in range(at.cols):
        lanes = slice(f * feats, (f + 1) * feats)
        normalized = parts[f] * inverse_std
        normalized_ref[:, lanes] = normalized
        vectors = vector_all_ref[f]
        dealt_ref[own, lanes] = (normalized * vectors[0:1, :] + vectors[1:2, :]).astype(bf16)
    last_tokens.start(dealt_ref.at[own, :])

    wide[pl.ds(at.row * held, held), :] = cotangent_ref[...].astype(f32)
    first_cots.forward(widen(all_cots))
    first_cots.finish(widen(all_cots))
    choose(out_cots)
    swap_cots.start()
    in_cots[at.col] = out_cots[at.col]
    last_tokens.forward()
    swap_cots.arrived()
    for f in range(at.cols):
        cot_dealt_ref[own, f * feats : (f + 1) * feats] = in_cots[f]
    last_cots.start(cot_dealt_ref.at[own, :])
    last_tokens.finish()
    last_cots.forward()
    last_cots.finish()
    swap_weight.arrived()
    for moved in (first_tokens, first_cots, last_tokens, last_cots):
        moved.sent()
    for moved in (swap_tokens, swap_cots, swap_weight, swap_vector):
        moved.sent()


def deal_all(tokens, cotangent, pick, weight, vectors, rows, cols):
    held, feats = tokens.shape
    total = held * rows
    group = total // cols
    piece = group // rows
    width = feats * cols
    shape = jax.ShapeDtypeStruct
    return pl.pallas_call(
        deal_kernel,
        out_shape=(
            shape((group, width), bf16),
            shape((group, width), bf16),
            shape((weight.shape[0] * cols, weight.shape[1]), bf16),
            shape((cols,) + vectors.shape, f32),
            shape((piece, width), f32),
            shape((piece, 1), f32),
        ),
        in_specs=[VMEM_SPEC, VMEM_SPEC, SMEM_SPEC, VMEM_SPEC, VMEM_SPEC],
        out_specs=(VMEM_SPEC,) * 6,
        scratch_shapes=[
            pltpu.VMEM((rows, held, feats), bf16),
            pltpu.VMEM((rows, held, feats), bf16),
            pltpu.VMEM((total, feats), f32),
            pltpu.VMEM((cols * piece, feats), f32),
            *([pltpu.VMEM((cols, piece, feats), bf16)] * 4),
            *(gather_sems() * 4),
            *(swap_sems(cols) * 4),
        ],
        compiler_params=pltpu.CompilerParams(
            collective_id=0, has_side_effects=True, vmem_limit_bytes=VMEM_LIMIT
        ),
        cost_estimate=pl.CostEstimate(
            flops=100 * 10**9, bytes_accessed=1 << 24, transcendentals=0
        ),
        name="deal_all",
    )(tokens, cotangent, pick, weight, vectors)


def split(x):
    high_part = x.astype(bf16)
    return high_part, (x - high_part.astype(f32)).astype(bf16)


def three(dot, left, right):
    return dot(left[0], right[0]) + (dot(left[0], right[1]) + dot(left[1], right[0]))


BLK = 128


def gram_kernel(
    in_part_ref,
    bias_ref,
    out_grad_ref,
    momentum_ref,
    normed_part_ref,
    in_grad_ref,
    bias_grad_ref,
    matrix_ref,
    gram_ref,
    normed_sum_ref,
    parts,
    biases,
    chunks,
    partial,
    from_twin,
    half_sum,
    slices,
    pairs,
    slots,
    *sems,
):
    at = Place()
    normed_rows = RowSum(at, normed_part_ref, pairs, slots, sems[:4])
    sems = list(sems[4:])

    def some(count):
        taken, sems[:count] = sems[:count], []
        return taken

    swap_part = ColSwap(at, lambda c: in_part_ref.at[c], lambda c: parts.at[c], some(2))
    swap_bias = ColSwap(at, lambda c: bias_ref, lambda c: biases.at[c], some(2))
    swap_chunk = ColSwap(at, lambda c: chunks.at[c], lambda c: matrix_ref.at[c], some(2))
    twin_send, twin_recv, sum_send, sum_recv, all_send, all_recv = some(6)
    count = at.chips * 2
    mine = at.chip * 2 + at.col % 2
    first_col = at.col - at.col % 2

    def member(step):
        other = lax.rem(mine + step, count)
        return other, ((other // 2) * 2 + at.core, first_col + other % 2)

    peers = [member(step)[1] for step in range(1, count)]
    meet(row_peers(at) + col_peers(at) + peers)
    swap_part.start()
    normed_rows.start()
    swap_bias.start()
    parts[at.col] = in_part_ref[at.col]
    biases[at.col] = bias_ref[...]
    swap_part.arrived()
    in_grad = sum(parts[c].astype(f32) for c in range(at.cols))
    in_grad_ref[...] = in_grad
    half = in_grad.shape[1] // BLK
    for index in range(at.cols):
        lanes = slice(index * BLK, (index + 1) * BLK)
        if index < half:
            grad = in_grad[:, lanes]
        else:
            grad = out_grad_ref[:, (index - half) * BLK : (index - half + 1) * BLK]
        state = momentum * momentum_ref[:, lanes] + grad
        chunks[index] = grad + momentum * state
    swap_chunk.start()
    normed_rows.middle()
    matrix_ref[at.col] = chunks[at.col]
    swap_bias.arrived()
    bias_grad_ref[...] = sum(biases[c] for c in range(at.cols))
    swap_chunk.arrived()

    strips = matrix_ref.shape[0]
    matrix = split(matrix_ref[...].reshape(strips * BLK, BLK))
    index = 0
    for i in range(strips):
        left = [m[i * BLK : (i + 1) * BLK, :] for m in matrix]
        right = [m[i * BLK :, :] for m in matrix]
        product = three(dot_nt, left, right)
        for j in range(strips - i):
            partial[index] = product[:, j * BLK : (j + 1) * BLK]
            index += 1
    blocks = index // 2
    to_twin = remote(
        partial.at[pl.ds((1 - at.core) * blocks, blocks)],
        from_twin,
        twin_send.at[0],
        twin_recv.at[0],
        at.twin,
    )
    to_twin.start()
    to_twin.wait_recv()
    for b in range(blocks):
        half_sum[b * BLK : (b + 1) * BLK, :] = partial[at.core * blocks + b] + from_twin[b]

    size = blocks * BLK // count

    def piece_of(owner):
        return half_sum.at[pl.ds(owner * size, size), :]

    def give(step):
        owner, device = member(step)
        return remote(
            piece_of(owner), slices.at[mine], sum_send.at[step], sum_recv.at[step], device
        )

    for step in range(1, count):
        give(step).start()
    slices[mine] = half_sum[pl.ds(mine * size, size), :]
    for step in range(1, count):
        came, device = member(count - step)
        remote(
            slices.at[came], slices.at[came], sum_send.at[step], sum_recv.at[step], device
        ).wait_recv()
    total = slices[0]
    for index in range(1, count):
        total = total + slices[index]
    half_rows = blocks * BLK

    def home(owner):
        return gram_ref.at[pl.ds(at.core * half_rows + owner * size, size), :]

    gram_ref[pl.ds(at.core * half_rows + mine * size, size), :] = total

    def spread(step):
        return remote(
            home(mine), home(mine), all_send.at[step], all_recv.at[step], member(step)[1]
        )

    for step in range(1, count):
        spread(step).start()
    for step in range(1, count):
        came, device = member(count - step)
        remote(
            home(came), home(came), all_send.at[step], all_recv.at[step], device
        ).wait_recv()
    both = gram_ref.at[pl.ds(at.core * half_rows, half_rows), :]
    other = gram_ref.at[pl.ds((1 - at.core) * half_rows, half_rows), :]
    passing = remote(both, both, twin_send.at[1], twin_recv.at[1], at.twin)
    passing.start()
    remote(other, other, twin_send.at[1], twin_recv.at[1], at.twin).wait_recv()
    passing.wait_send()
    to_twin.wait_send()
    for step in range(1, count):
        give(step).wait_send()
        spread(step).wait_send()
    normed_sum_ref[...] = normed_rows.finish()
    normed_rows.sent()
    for moved in (swap_part, swap_bias, swap_chunk):
        moved.sent()


WIDE = 256


def poly_kernel(
    gram_ref,
    matrix_ref,
    branch_ref,
    normed_ref,
    normalized_ref,
    inverse_std_ref,
    vector_ref,
    tokens_ref,
    cotangent_ref,
    pick_branch_ref,
    pick_token_ref,
    update_ref,
    output_ref,
    input_grad_ref,
    vector_sum_ref,
    own_update,
    whole_branch,
    whole_token,
    out_branch,
    in_branch,
    out_token,
    in_token,
    wide,
    *buffers,
):
    at = Place()
    sems, buffers = buffers[8:], buffers[:8]
    spread_branch = RowSpread(at, whole_branch, sems[0:4])
    spread_token = RowSpread(at, whole_token, sems[4:8])
    swap_branch = ColSwap(at, lambda c: out_branch.at[c], lambda c: in_branch.at[c], sems[8:10])
    swap_token = ColSwap(at, lambda c: out_token.at[c], lambda c: in_token.at[c], sems[10:12])
    feats = out_branch.shape[2]
    swap_update = ColSwap(
        at,
        lambda c: own_update.at[pl.ds(c * feats, feats), :],
        lambda c: update_ref.at[c],
        sems[12:14],
    )
    piece, stride = out_branch.shape[1], out_token.shape[1]
    meet(row_peers(at) + col_peers(at))

    lanes = [slice(f * feats, (f + 1) * feats) for f in range(at.cols)]
    for f in range(at.cols):
        out_branch[f] = branch_ref[:, lanes[f]]
    swap_branch.start()
    in_branch[at.col] = out_branch[at.col]
    width = at.cols * feats
    scaled = [normed_ref[:, lanes[f]] * vector_ref[f][0:1, :] for f in range(at.cols)]
    mean_first = sum(jnp.sum(part, axis=1, keepdims=True) for part in scaled) / width
    mean_second = (
        sum(
            jnp.sum(part * normalized_ref[:, lanes[f]], axis=1, keepdims=True)
            for f, part in enumerate(scaled)
        )
        / width
    )
    for f in range(at.cols):
        normalized, grad = normalized_ref[:, lanes[f]], normed_ref[:, lanes[f]]
        token_grad = inverse_std_ref[...] * (scaled[f] - mean_first - normalized * mean_second)
        out_token[f, :piece, :] = token_grad.astype(bf16)
        gain_grad = jnp.sum(grad * normalized, axis=0, keepdims=True)
        shift_grad = jnp.sum(grad, axis=0, keepdims=True)
        sums = jnp.concatenate(
            [part.astype(f32) for part in (*split(gain_grad), *split(shift_grad))]
            + [jnp.zeros((stride - piece - 4, feats), f32)],
            axis=0,
        )
        out_token[f, piece:, :] = sums.astype(bf16)
    swap_token.start()
    in_token[at.col] = out_token[at.col]
    cot_sum = jnp.sum(cotangent_ref[...].astype(f32), axis=0, keepdims=True)
    cot_rows = jnp.concatenate(
        [part.astype(f32) for part in split(cot_sum)] + [jnp.zeros((14, feats), f32)], axis=0
    )
    swap_branch.arrived()
    for c in range(at.cols):
        whole_branch[at.row, c * piece : (c + 1) * piece, :] = in_branch[c]
    spread_branch.start()
    swap_token.arrived()
    for c in range(at.cols):
        whole_token[at.row, c * stride : (c + 1) * stride, :] = in_token[c]
    last = whole_token.shape[1] - 16
    whole_token[at.row, last:, :] = cot_rows.astype(bf16)
    spread_token.start()

    first, second, third, thin = [buffers[2 * i : 2 * i + 2] for i in range(4)]
    strips = matrix_ref.shape[0]
    size = strips * BLK
    counts = range(size // WIDE)
    eye = lax.broadcasted_iota(jnp.int32, (BLK, BLK), 0) == lax.broadcasted_iota(
        jnp.int32, (BLK, BLK), 1
    )

    def put(pair, rows, lanes, value):
        high_part, low_part = split(value)
        pair[0][rows, lanes] = high_part
        pair[1][rows, lanes] = low_part

    def get(pair, rows, lanes):
        return pair[0][rows, lanes], pair[1][rows, lanes]

    places, index = [], 0
    for i in range(strips):
        for j in range(i, strips):
            places.append((i, j, index))
            index += 1
    trace = sum(
        jnp.sum(jnp.where(eye, gram_ref[spot * BLK : (spot + 1) * BLK, :], 0.0))
        for i, j, spot in places
        if i == j
    )
    shrink = 1.0 / (jnp.sqrt(jnp.full((1, 1), trace, f32)) + ortho_floor)
    for i, j, spot in places:
        block = gram_ref[spot * BLK : (spot + 1) * BLK, :] * (shrink * shrink)
        here, there = slice(i * BLK, (i + 1) * BLK), slice(j * BLK, (j + 1) * BLK)
        put(first, here, there, block)
        if j > i:
            put(first, there, here, block.T)
    everything = slice(0, size)
    for i in range(strips):
        put(thin, slice(i * BLK, (i + 1) * BLK), everything, matrix_ref[i] * shrink)

    def product(left, right, out, finish=None):
        for i in counts:
            rows, rest = slice(i * WIDE, (i + 1) * WIDE), slice(i * WIDE, size)
            value = three(dot_nn, get(left, rows, everything), get(right, everything, rest))
            if finish is not None:
                value = finish(value, rows, rest)
            put(out, rows, rest, value)
            for j in range(i + 1, size // WIDE):
                part = value[:, (j - i) * WIDE : (j - i + 1) * WIDE]
                put(out, slice(j * WIDE, (j + 1) * WIDE), rows, part.T)

    def thin_product(left):
        right = get(thin, everything, everything)
        return [
            three(dot_nn, get(left, slice(i * WIDE, (i + 1) * WIDE), everything), right)
            for i in counts
        ]

    def sweep(gram, poly, square):
        def finish(value, rows, rest):
            high_part, low_part = get(gram, rows, rest)
            value = poly_cubic * value + poly_square * (
                high_part.astype(f32) + low_part.astype(f32)
            )
            at_row = lax.broadcasted_iota(jnp.int32, value.shape, 0)
            at_lane = lax.broadcasted_iota(jnp.int32, value.shape, 1)
            return value + jnp.where(at_row == at_lane, poly_linear, 0.0)

        product(gram, gram, poly, finish)
        for i, value in zip(counts, thin_product(poly)):
            put(thin, slice(i * WIDE, (i + 1) * WIDE), everything, value)
        product(poly, poly, square)
        product(gram, square, poly)

    def two(step, carry):
        sweep(first, second, third)

        @pl.when(step == 1)
        def _():
            spread_token.middle()

        sweep(second, first, third)

        @pl.when(step == 0)
        def _():
            spread_branch.middle()

        return carry

    lax.fori_loop(0, 2, two, 0)
    once = thin_product(first)
    old = []
    for i in counts:
        rows = slice(i * WIDE, (i + 1) * WIDE)
        high_part, low_part = get(thin, rows, everything)
        old.append(high_part.astype(f32) + low_part.astype(f32))
    for i, value in zip(counts, once):
        put(thin, slice(i * WIDE, (i + 1) * WIDE), everything, value)
    for i, value in zip(counts, thin_product(first)):
        result = poly_linear * old[i] + poly_square * once[i] + poly_cubic * value
        own_update[i * WIDE : (i + 1) * WIDE, :] = result.astype(bf16)
    swap_update.start()
    update_ref[at.col] = own_update[pl.ds(at.col * feats, feats), :]

    held = tokens_ref.shape[0]

    def choose(pick_ref, base_ref, out_ref, shift):
        def eight(step, carry):
            begin = step * 8
            found = [wide[pl.ds(pick_ref[begin + i], 1), :] for i in range(8)]
            out_ref[pl.ds(begin, 8), :] = jnp.concatenate(found, axis=0)
            return carry

        lax.fori_loop(0, held // 8, eight, 0)
        out_ref[...] = out_ref[...] + base_ref[...].astype(f32) + shift

    def widen(whole):
        size = whole.shape[1]
        for row in range(whole.shape[0]):
            wide[row * size : (row + 1) * size, :] = whole[row].astype(f32)

    spread_branch.finish()
    widen(whole_branch)
    choose(pick_branch_ref, tokens_ref, output_ref, vector_ref[at.col][2:3, :])
    spread_token.finish()
    widen(whole_token)
    choose(pick_token_ref, cotangent_ref, input_grad_ref, 0.0)
    total = jnp.zeros((16, feats), f32)
    for row in range(whole_token.shape[0]):
        cot_part = whole_token[row, last:, :].astype(f32)
        for c in range(at.cols):
            begin = c * stride + piece
            total = total + whole_token[row, begin : begin + 16, :].astype(f32)
        total = total + jnp.concatenate(
            [jnp.zeros((4, feats), f32), cot_part[0:2, :], jnp.zeros((10, feats), f32)], axis=0
        )
    vector_sum_ref[...] = total
    swap_update.arrived()
    for moved in (swap_branch, swap_token, swap_update, spread_branch, spread_token):
        moved.sent()


def orthogonalize(
    gram,
    matrix,
    branch_sum,
    normed_sum,
    normalized,
    inverse_std,
    vectors,
    tokens,
    cotangent,
    picks,
    rows,
):
    cols, feats, width = matrix.shape
    size = cols * BLK
    piece = branch_sum.shape[0]
    stride = piece + EXTRA
    held = tokens.shape[0]
    chips = rows // 2
    dma = pltpu.SemaphoreType.DMA
    shape = jax.ShapeDtypeStruct
    square, narrow = pltpu.VMEM((size, size), bf16), pltpu.VMEM((size, width), bf16)
    return remote_call(
        poly_kernel,
        3,
        (
            shape((cols, feats, width), bf16),
            shape((held, feats), f32),
            shape((held, feats), f32),
            shape((16, feats), f32),
        ),
        [*([VMEM_SPEC] * 9), SMEM_SPEC, SMEM_SPEC],
        [
            narrow,
            pltpu.VMEM((rows, cols * piece, feats), bf16),
            pltpu.VMEM((rows, cols * stride + 16, feats), bf16),
            *([pltpu.VMEM((cols, piece, feats), bf16)] * 2),
            *([pltpu.VMEM((cols, stride, feats), bf16)] * 2),
            pltpu.VMEM((rows * (cols * stride + 16), feats), f32),
            *([square] * 6),
            *([narrow] * 2),
            *([dma((chips,))] * 8),
            *(swap_sems(cols) * 3),
        ],
        60 * 10**9,
        "orthogonalize",
    )(
        *(gram, matrix, branch_sum, normed_sum, normalized, inverse_std, vectors),
        *(tokens, cotangent, *picks),
    )


def gram_all(in_part, bias, out_grad, old_momentum, normed_part, rows, cols):
    feats, width = in_part.shape[1:]
    full = normed_part.shape[1]
    chips = rows // 2
    piece = normed_part.shape[0] // rows
    blocks = cols * (cols + 1) // 2
    count = chips * 2
    half_rows = blocks * BLK // 2
    shape = jax.ShapeDtypeStruct
    dma = pltpu.SemaphoreType.DMA
    return remote_call(
        gram_kernel,
        1,
        (
            shape((feats, width), f32),
            shape(bias.shape, f32),
            shape((cols, feats, BLK), f32),
            shape((blocks * BLK, BLK), f32),
            shape((piece, full), f32),
        ),
        [VMEM_SPEC] * 5,
        [
            pltpu.VMEM((cols, feats, width), bf16),
            pltpu.VMEM((cols,) + bias.shape, f32),
            pltpu.VMEM((cols, feats, BLK), f32),
            pltpu.VMEM((blocks, BLK, BLK), f32),
            pltpu.VMEM((blocks // 2, BLK, BLK), f32),
            pltpu.VMEM((half_rows, BLK), f32),
            pltpu.VMEM((count, half_rows // count, BLK), f32),
            *sum_scratch(piece, full, chips),
            *(swap_sems(cols) * 3),
            dma((2,)),
            dma((2,)),
            *([dma((count,))] * 4),
        ],
        60 * 10**9,
        "gram_all",
    )(in_part, bias, out_grad, old_momentum, normed_part.reshape(chips, 2, piece, full))


def rotary_table(places):
    half_rot = ROT // 2
    inverse = 1.0 / 10000.0 ** (jnp.arange(half_rot, dtype=f32) * (2.0 / ROT))
    angles = inverse[:, None] * places.astype(f32)[None, :]
    table = jnp.concatenate([jnp.cos(angles), jnp.sin(angles)], axis=0)
    return jnp.concatenate(high_low(table), axis=0)


def adam_step(value, gradient, first_state, second_state):
    first_new = beta_first * first_state + (1.0 - beta_first) * gradient
    second_new = beta_second * second_state + (1.0 - beta_second) * gradient * gradient
    corrected = first_new / (1.0 - beta_first**STEP)
    root_term = jnp.sqrt(second_new / (1.0 - beta_second**STEP)) + adam_floor
    return (first_new, second_new, value - rate_vector * corrected / root_term)


def high_low(x):
    high_part = x.astype(bf16)
    return high_part, (x - high_part.astype(f32)).astype(bf16)


def per_device(
    tokens,
    cotangent,
    lengths,
    deal_order,
    qkv_weight,
    up_weight,
    proj_weight,
    down_weight,
    norm_vectors,
    qkv_bias,
    mlp_bias,
    qkv_momentum,
    up_momentum,
    proj_momentum,
    down_momentum,
    norm_moment,
    norm_square,
    qkv_bias_moment,
    qkv_bias_square,
    mlp_bias_moment,
    mlp_bias_square,
):
    cols, rows = lax.axis_size("col"), lax.axis_size("row")
    col, row = lax.axis_index("col"), lax.axis_index("row")
    total_tokens = deal_order.shape[0]
    group = total_tokens // cols
    piece = group // rows
    held = total_tokens // rows
    feats = D // cols
    qkv_width, up_width = qkv_weight.shape[1], up_weight.shape[1]
    proj_width = proj_weight.shape[0]

    seq_ends = jnp.cumsum(lengths)
    seq_starts = seq_ends - lengths
    anchor = lax.dynamic_slice_in_dim(deal_order, col * group, group)
    before = seq_ends[None, :] <= anchor[:, None]
    places = anchor - jnp.sum(jnp.where(before, lengths[None, :], 0), axis=1)
    starts = (jnp.arange(group, dtype=jnp.int32) - places)[:, None]
    at = jnp.arange(total_tokens, dtype=jnp.int32)
    dealt_starts = jnp.sum(
        jnp.where(deal_order[None, :] == seq_starts[:, None], at[None, :], 0), axis=1
    )
    own = row * held + jnp.arange(held, dtype=jnp.int32)
    holds = (seq_starts[None, :] <= own[:, None]) & (own[:, None] < seq_ends[None, :])
    dealt_at = own + jnp.sum(jnp.where(holds, (dealt_starts - seq_starts)[None, :], 0), axis=1)
    table = rotary_table(places)

    def lanes(x, width):
        return jnp.pad(x, ((0, 0), (0, width - x.shape[1])))

    in_pad = 2 * up_width
    tile = jnp.concatenate(
        [
            lanes(qkv_weight.astype(bf16), up_width),
            up_weight.astype(bf16),
            lanes(proj_weight.astype(bf16).T, 128),
            down_weight.astype(bf16).T,
        ],
        axis=1,
    )
    pick = lax.dynamic_slice(
        deal_order.reshape(cols, rows, piece), (0, row, 0), (cols, 1, piece)
    ).reshape(-1)
    dealt, cotangent_dealt, weight_all, vector_all, normalized, inverse_std = deal_all(
        tokens, cotangent, pick, tile, jnp.pad(norm_vectors, ((0, 5), (0, 0))), rows, cols
    )

    block, inside = dealt_at // group, dealt_at % group
    inner = inside % piece
    stride = piece + EXTRA
    pick_branch = (inside // piece) * (cols * piece) + block * piece + inner
    pick_token = (inside // piece) * (cols * stride + 16) + block * stride + inner

    bias = jnp.concatenate(
        [jnp.pad(qkv_bias, (0, up_width - qkv_width)), mlp_bias], axis=0
    ).reshape(1, in_pad)
    *kept, branch_part, out_part = forward(
        dealt, cotangent_dealt, weight_all, bias, table, starts
    )
    in_part, bias_part, normed_part, branch_sum, out_grad = backward(
        dealt, cotangent_dealt, weight_all, table, starts, kept, branch_part, out_part, rows, cols
    )

    old_momentum = jnp.concatenate(
        [
            lanes(qkv_momentum, up_width),
            up_momentum,
            lanes(proj_momentum.T, up_width),
            down_momentum.T,
        ],
        axis=1,
    )
    in_grad, bias_rows, matrix, gram, normed_sum = gram_all(
        in_part, bias_part, out_grad, old_momentum, normed_part, rows, cols
    )
    returned, output, input_grad, vector_sum = orthogonalize(
        gram,
        matrix,
        branch_sum,
        normed_sum,
        normalized,
        inverse_std,
        vector_all,
        tokens,
        cotangent,
        (pick_branch, pick_token),
        rows,
    )
    norm_grads = jnp.stack(
        [
            vector_sum[0] + vector_sum[1],
            vector_sum[2] + vector_sum[3],
            vector_sum[4] + vector_sum[5],
        ],
        axis=0,
    )
    in_bias_grad = bias_rows[0]
    gradients = (
        in_grad[:, :qkv_width],
        in_grad[:, up_width:],
        out_grad[:, :proj_width].T,
        out_grad[:, up_width:].T,
    )
    old_states = (qkv_momentum, up_momentum, proj_momentum, down_momentum)
    weights = (qkv_weight, up_weight, proj_weight, down_weight)
    widths = (3 * D, FF, D, FF)
    sizes = (qkv_width, up_width, proj_width, up_width)
    states = [momentum * old + g for old, g in zip(old_states, gradients)]
    new_weights = []
    for index in range(4):
        update = jnp.concatenate([returned[2 * index], returned[2 * index + 1]], axis=1)
        update = update[:, : sizes[index]].astype(f32)
        update = update.T if index >= 2 else update
        new_weights.append(
            weights[index] * (1.0 - rate_matrix * decay_matrix)
            - rate_matrix * 0.2 * math.sqrt(widths[index]) * update
        )

    norm_first, norm_second, norm_new = adam_step(
        norm_vectors, norm_grads, norm_moment, norm_square
    )
    qkv_first, qkv_second, qkv_bias_new = adam_step(
        qkv_bias, in_bias_grad[:qkv_width], qkv_bias_moment, qkv_bias_square
    )
    mlp_first, mlp_second, mlp_bias_new = adam_step(
        mlp_bias, in_bias_grad[up_width:], mlp_bias_moment, mlp_bias_square
    )
    return (
        output,
        input_grad,
        *gradients,
        *states,
        *new_weights,
        norm_first,
        norm_second,
        norm_new,
        qkv_first,
        qkv_second,
        qkv_bias_new,
        mlp_first,
        mlp_second,
        mlp_bias_new,
    )


def solution(mesh):
    over_both, over_flip = P("row", "col"), P("col", "row")
    features, hidden = P(None, "col"), P("row")
    return jax.shard_map(
        per_device,
        mesh=mesh,
        in_specs=(
            *(over_both, over_both, P(), P()),
            *(over_flip, over_flip, over_both, over_both),
            *(features, hidden, hidden),
            *(over_flip, over_flip, over_both, over_both),
            *(features, features, hidden, hidden, hidden, hidden),
        ),
        out_specs=(
            *(over_both, over_both),
            *(over_flip, over_flip, over_both, over_both) * 3,
            *(features,) * 3,
            *(hidden,) * 6,
        ),
        check_vma=False,
    )
```

```python
import functools
import math

import jax
import jax.numpy as jnp
from jax import lax
from jax.experimental import pallas as pl
from jax.experimental.pallas import tpu as pltpu
from jax.sharding import PartitionSpec as P

D = 1024
HEAD = 64
ROT = 16
FF = 4096
STEP = 10

poly_linear = 3.4445
poly_square = -4.775
poly_cubic = 2.0315
momentum = 0.95
rate_matrix = 0.15
decay_matrix = 0.1
beta_first = 0.9
beta_second = 0.95
rate_vector = 0.2
adam_floor = 1e-08
norm_floor = 1e-05
ortho_floor = 1e-07
masked_score = -1e30
f32 = jnp.float32
bf16 = jnp.bfloat16
BLOCK = 256
PIECE = 128
EXTRA = 16


def dot_nt(a, b, **kw):
    return lax.dot_general(a, b, (((1,), (1,)), ((), ())), preferred_element_type=f32, **kw)


def dot_tn(a, b, **kw):
    return lax.dot_general(a, b, (((0,), (0,)), ((), ())), preferred_element_type=f32, **kw)


def dot_nn(a, b, **kw):
    return lax.dot_general(a, b, (((1,), (0,)), ((), ())), preferred_element_type=f32, **kw)


def allowed_keys(start_ref, first, keys):
    shape = (BLOCK, keys)
    key_at = lax.broadcasted_iota(jnp.int32, shape, 1)
    query_at = first + lax.broadcasted_iota(jnp.int32, shape, 0)
    return (key_at >= start_ref[pl.ds(first, BLOCK), :]) & (key_at <= query_at)


def turning(table_ref, rows):
    lane = lax.broadcasted_iota(jnp.int32, (32, 2 * HEAD), 1) % HEAD
    entry = lax.broadcasted_iota(jnp.int32, (32, 2 * HEAD), 0) % 16
    half_rot = ROT // 2

    def spread(where, value):
        picks = jnp.where(where, value, 0.0).astype(bf16)
        return dot_tn(table_ref[:, rows], picks)

    cosine = spread((lane < ROT) & (entry == lane % half_rot), 1.0)
    cosine = cosine + jnp.where(lane[:1] < ROT, 0.0, 1.0)
    lower = spread((lane < half_rot) & (entry == lane + half_rot), -1.0)
    upper = spread((lane >= half_rot) & (lane < ROT) & (entry == lane), 1.0)
    return cosine, lower, upper


def turned(values, tables, back):
    cosine, lower, upper = tables
    half_rot = ROT // 2
    moved = (
        pltpu.roll(values, 2 * HEAD - half_rot, 1) * lower + pltpu.roll(values, half_rot, 1) * upper
    )
    return values * cosine - moved if back else values * cosine + moved


def forward_kernel(
    dealt_ref,
    cotangent_ref,
    weight_ref,
    bias_ref,
    table_ref,
    start_ref,
    q_ref,
    k_ref,
    v_ref,
    slope_ref,
    branch_ref,
    attended_ref,
    total_ref,
    partial_ref,
    out_part_ref,
    pairs,
    values,
):
    width = bias_ref.shape[1]
    tokens = dealt_ref.shape[0]
    rows_all = tokens // PIECE
    in_weight, out_weight = weight_ref[:, :width], weight_ref[:, width:]
    inner = math.sqrt(2.0 / math.pi)
    firsts = range(0, dealt_ref.shape[0], BLOCK)
    for first in firsts:
        rows = pl.ds(first, BLOCK)
        pre = dot_nn(dealt_ref[rows, :], in_weight) + bias_ref[...]
        pair = turned(pre[:, : 2 * HEAD], turning(table_ref, rows), False)
        for part in range(BLOCK // PIECE):
            mine = slice(part * PIECE, (part + 1) * PIECE)
            spaced = pl.ds(first // PIECE + part, PIECE, stride=rows_all)
            pairs[spaced, :] = pair[mine, :]
            values[spaced, :] = pre[mine, 2 * HEAD : 4 * HEAD]
        up = pre[:, 4 * HEAD :]
        square = up * up
        bent = jnp.tanh(inner * (up + 0.044715 * square * up))
        branch_ref[rows, 2 * HEAD :] = (0.5 * up * (1.0 + bent)).astype(bf16)
        slope_ref[rows, :] = 0.5 * (1.0 + bent) + 0.5 * up * (1.0 - bent * bent) * (
            inner * (1.0 + 3.0 * 0.044715 * square)
        )
    for first in firsts:
        rows = pl.ds(first, BLOCK)
        pair = pairs[rows, :].astype(bf16)
        q_ref[rows, :] = (pair[:, :HEAD] * HEAD**-0.5).astype(bf16)
        k_ref[rows, :] = pair[:, HEAD:]
        v_ref[rows, :] = values[rows, :HEAD].astype(bf16)
    for first in firsts:
        rows, keys = pl.ds(first, BLOCK), first + BLOCK
        scores = dot_nt(q_ref[rows, :], k_ref[:keys, :])
        scores = jnp.where(allowed_keys(start_ref, first, keys), scores, masked_score)
        top = jnp.max(scores, axis=1, keepdims=True)
        raw = jnp.exp(scores - top)
        total = jnp.sum(raw, axis=1, keepdims=True)
        attended = dot_nn(raw.astype(bf16), v_ref[:keys, :]) / total
        attended_ref[rows, :] = attended.astype(bf16)
        values[rows, :] = jnp.concatenate([attended, jnp.zeros_like(attended)], axis=1)
        total_ref[rows, :] = top + jnp.log(total)
    for first in firsts:
        rows = pl.ds(first, BLOCK)
        for part in range(BLOCK // PIECE):
            at_piece = first // PIECE + part
            branch_ref[at_piece * PIECE : (at_piece + 1) * PIECE, : 2 * HEAD] = values[
                pl.ds(at_piece, PIECE, stride=rows_all), :
            ].astype(bf16)
        partial_ref[rows, :] = dot_nt(branch_ref[rows, :], out_weight).astype(bf16)
    for first in range(0, cotangent_ref.shape[1], BLOCK):
        lanes = slice(first, first + BLOCK)
        out_part_ref[lanes, :] = dot_tn(cotangent_ref[:, lanes], branch_ref[...]).astype(bf16)


def local_call(kernel, out_shape, scratch, flops, name):
    return pl.pallas_call(
        kernel,
        out_shape=out_shape,
        scratch_shapes=scratch,
        compiler_params=pltpu.CompilerParams(vmem_limit_bytes=VMEM_LIMIT),
        cost_estimate=pl.CostEstimate(flops=flops, bytes_accessed=1 << 24, transcendentals=0),
        name=name,
    )


def forward(dealt, cotangent, weight, bias, table, starts):
    rows, width = dealt.shape
    up = bias.shape[1] - 4 * HEAD
    branch = up + 2 * HEAD
    shape = jax.ShapeDtypeStruct
    head = shape((rows, HEAD), bf16)
    return local_call(
        forward_kernel,
        (
            *(head, head, head),
            shape((rows, up), f32),
            shape((rows, branch), bf16),
            head,
            shape((rows, 1), f32),
            shape((rows, width), bf16),
            shape((width, branch), bf16),
        ),
        [pltpu.VMEM((rows, 2 * HEAD), f32)] * 2,
        25 * 10**9,
        "forward",
    )(dealt, cotangent, weight, bias, table, starts)


def remote_call(kernel, identity, out_shape, in_specs, scratch, flops, name):
    return pl.pallas_call(
        kernel,
        out_shape=out_shape,
        in_specs=in_specs,
        out_specs=(VMEM_SPEC,) * len(out_shape),
        scratch_shapes=scratch,
        compiler_params=pltpu.CompilerParams(
            collective_id=identity, has_side_effects=True, vmem_limit_bytes=VMEM_LIMIT
        ),
        cost_estimate=pl.CostEstimate(flops=flops, bytes_accessed=1 << 24, transcendentals=0),
        name=name,
    )


VMEM_LIMIT = 60 * 1024 * 1024


MESH = pl.DeviceIdType.MESH
VMEM_SPEC = pl.BlockSpec(memory_space=pltpu.VMEM)


def remote(src, dst, send, recv, device):
    return pltpu.make_async_remote_copy(
        src_ref=src, dst_ref=dst, send_sem=send, recv_sem=recv, device_id=device, device_id_type=MESH
    )


class Place:
    def __init__(self):
        self.row, self.col = lax.axis_index("row"), lax.axis_index("col")
        self.rows, self.cols = lax.axis_size("row"), lax.axis_size("col")
        self.chips = self.rows // 2
        self.chip, self.core = self.row // 2, self.row % 2
        self.twin = (self.chip * 2 + 1 - self.core, self.col)
        self.ring = self.chips // 2
        self.y, self.z = self.chip // self.ring, self.chip % self.ring

    def chip_at(self, step):
        return lax.rem(self.chip + step, self.chips)

    def chip_row(self, step):
        return self.chip_at(step) * 2 + self.core

    def col_at(self, step):
        return lax.rem(self.col + step, self.cols)


def meet(devices):
    barrier = pltpu.get_barrier_semaphore()
    for device in devices:
        pl.semaphore_signal(barrier, inc=1, device_id=device, device_id_type=MESH)
    pl.semaphore_wait(barrier, len(devices))


class RowGather:
    OWN, PARTNER, BELOW, ABOVE, BELOW_PARTNER, ABOVE_PARTNER, FAR, FAR_PARTNER = range(8)

    def __init__(self, at, slot, sems):
        self.at, self.slot = at, slot
        self.sems = sems
        ring, z, y = at.ring, at.z, at.y
        self.chips = [
            y * ring + z,
            (1 - y) * ring + z,
            y * ring + lax.rem(z + ring - 1, ring),
            y * ring + lax.rem(z + 1, ring),
            (1 - y) * ring + lax.rem(z + ring - 1, ring),
            (1 - y) * ring + lax.rem(z + 1, ring),
            y * ring + lax.rem(z + 2, ring),
            (1 - y) * ring + lax.rem(z + 2, ring),
        ]

    def row_of(self, which):
        return self.chips[which] * 2 + self.at.core

    def block(self, which):
        return self.slot(self.row_of(which))

    def part(self, which, upper):
        ref = self.block(which)
        half = ref.shape[0] // 2
        return ref.at[pl.ds(0 if upper else half, half), :]

    def hop(self, tag, src, dst, to):
        send, recv = self.sems[0], self.sems[1]
        return remote(src, dst, send.at[tag], recv.at[tag], (self.row_of(to), self.at.col))

    def took(self, tag, ref):
        self.hop(tag, ref, ref, self.PARTNER).wait_recv()

    def passing(self, which, src=None):
        send, recv = self.sems[2], self.sems[3]
        ref = self.block(which)
        return remote(
            ref if src is None else src, ref, send.at[which], recv.at[which], self.at.twin
        )

    def hops(self):
        own, src = self.block(self.OWN), self.src
        partner = self.block(self.PARTNER)
        below, above = self.part(self.BELOW, True), self.part(self.ABOVE, False)
        far_below = self.part(self.BELOW_PARTNER, True)
        far_above = self.part(self.ABOVE_PARTNER, False)
        return {
            "start": [
                (0, src, own, self.PARTNER),
                (1, src, own, self.ABOVE),
                (2, src, own, self.BELOW),
            ],
            "partner": [(3, partner, partner, self.ABOVE), (4, partner, partner, self.BELOW)],
            "below": [(5, below, below, self.ABOVE)],
            "above": [(6, above, above, self.BELOW)],
            "far_below": [(7, far_below, far_below, self.ABOVE)],
            "far_above": [(8, far_above, far_above, self.BELOW)],
        }

    def go(self, stage):
        for hop in self.hops()[stage]:
            self.hop(*hop).start()

    def start(self, src):
        self.src = src
        self.go("start")
        self.passing(self.OWN, src).start()

    def landed(self, which, then):
        self.passing(which).start()
        if then is not None:
            then(self.row_of(which))

    def forward(self, then=None):
        self.took(1, self.block(self.BELOW))
        self.go("below")
        self.took(2, self.block(self.ABOVE))
        self.go("above")
        self.landed(self.BELOW, then)
        self.landed(self.ABOVE, then)
        self.took(0, self.block(self.PARTNER))
        self.go("partner")
        self.landed(self.PARTNER, then)
        self.took(3, self.block(self.BELOW_PARTNER))
        self.go("far_below")
        self.took(4, self.block(self.ABOVE_PARTNER))
        self.go("far_above")
        self.landed(self.BELOW_PARTNER, then)
        self.landed(self.ABOVE_PARTNER, then)
        self.took(5, self.part(self.FAR, True))
        self.took(6, self.part(self.FAR, False))
        self.landed(self.FAR, then)
        self.took(7, self.part(self.FAR_PARTNER, True))
        self.took(8, self.part(self.FAR_PARTNER, False))
        self.landed(self.FAR_PARTNER, then)

    def finish(self, then=None):
        send, recv = self.sems[2], self.sems[3]
        for which in range(8):
            row = self.chips[which] * 2 + 1 - self.at.core
            slot = self.slot(row)
            remote(slot, slot, send.at[which], recv.at[which], self.at.twin).wait_recv()
            if then is not None:
                then(row)

    def sent(self):
        for stage in self.hops().values():
            for hop in stage:
                self.hop(*hop).wait_send()
        self.passing(self.OWN, self.src).wait_send()
        for which in range(1, 8):
            self.passing(which).wait_send()


class Swap:
    def __init__(self, at, axis, src, dst, sems):
        self.at, self.axis, self.src, self.dst = at, axis, src, dst
        self.send, self.recv = sems
        self.me, self.size = (at.row, at.rows) if axis == "row" else (at.col, at.cols)

    def to(self, step):
        return lax.rem(self.me + step, self.size)

    def device(self, index):
        return (index, self.at.col) if self.axis == "row" else (self.at.row, index)

    def outgoing(self, step):
        to = self.to(step)
        return remote(
            self.src(to),
            self.dst(self.me),
            self.send.at[step],
            self.recv.at[step],
            self.device(to),
        )

    def start(self, which=None):
        for step in range(1, self.size):
            if which is None:
                self.outgoing(step).start()
            else:

                @pl.when(which(self.to(step)))
                def _():
                    self.outgoing(step).start()

    def arrived(self):
        for step in range(1, self.size):
            came = self.to(self.size - step)
            slot = self.dst(came)
            remote(
                slot, slot, self.send.at[step], self.recv.at[step], self.device(came)
            ).wait_recv()

    def sent(self):
        for step in range(1, self.size):
            self.outgoing(step).wait_send()


class RowSum:
    SEMS = 4

    def __init__(self, at, part, pairs, slots, sems):
        self.at, self.part, self.pairs, self.slots = at, part, pairs, slots
        self.twin_send, self.twin_recv, self.send, self.recv = sems

    def to_twin(self):
        at = self.at
        return remote(
            self.part.at[:, 1 - at.core],
            self.pairs,
            self.twin_send.at[0],
            self.twin_recv.at[0],
            at.twin,
        )

    def outgoing(self, step):
        at = self.at
        return remote(
            self.pairs.at[at.chip_at(step)],
            self.slots.at[at.chip],
            self.send.at[step],
            self.recv.at[step],
            (at.chip_row(step), at.col),
        )

    def start(self):
        self.to_twin().start()

    def middle(self):
        at = self.at
        self.to_twin().wait_recv()

        for step in (4, 1, 2, 3, 5, 6, 7, 0):
            chip = at.chip_at(step)
            both = self.part[chip, at.core].astype(f32) + self.pairs[chip].astype(f32)
            self.pairs[chip] = both.astype(bf16)
            if step > 0:
                self.outgoing(step).start()

    def finish(self):
        at = self.at
        total = self.pairs[at.chip].astype(f32)
        for step in range(1, at.chips):
            chip = at.chip_at(at.chips - step)
            slot = self.slots.at[chip]
            remote(
                slot, slot, self.send.at[step], self.recv.at[step], (chip * 2 + at.core, at.col)
            ).wait_recv()
            total = total + self.slots[chip].astype(f32)
        return total

    def sent(self):
        self.to_twin().wait_send()
        for step in range(1, self.at.chips):
            self.outgoing(step).wait_send()


def sum_scratch(piece, width, chips):
    dma = pltpu.SemaphoreType.DMA
    return [
        pltpu.VMEM((chips, piece, width), bf16),
        pltpu.VMEM((chips, piece, width), bf16),
        dma((1,)),
        dma((1,)),
        dma((chips,)),
        dma((chips,)),
    ]


def moved_rows(index_row, first, count, values):
    shape = (count, index_row.shape[1])
    here = first + lax.broadcasted_iota(jnp.int32, shape, 0) == index_row
    return dot_nn(jnp.where(here, 1.0, 0.0).astype(bf16), values)


def flat(ref, size):
    return jnp.concatenate([ref[index, :size, :] for index in range(ref.shape[0])], axis=0)


def pack_rows(index_ref, values, out_refs, lanes):
    blocks = out_refs[0].shape[0]
    size = index_ref[1]
    for first in range(0, blocks, 4):
        found = moved_rows(index_ref[0][...], first * size, 4 * size, values).astype(bf16)
        for index in range(4):
            part = found[index * size : (index + 1) * size, :]
            for which, out_ref in enumerate(out_refs):
                out_ref[first + index, :size, :] = part[:, which * lanes : (which + 1) * lanes]


def every_row(at):
    return [(lax.rem(at.row + step, at.rows), at.col) for step in range(1, at.rows)]


def row_peers(at):
    return [(at.chip_row(step), at.col) for step in range(1, at.chips)] + [at.twin]


def col_peers(at):
    return [(at.row, at.col_at(step)) for step in range(1, at.cols)]


def gather_sems():
    return [pltpu.SemaphoreType.DMA((count,)) for count in (9, 9, 8, 8)]


def swap_sems(cols):
    return [pltpu.SemaphoreType.DMA((cols,))] * 2


def deal_kernel(
    tokens_ref,
    cotangent_ref,
    take_back_ref,
    send_back_ref,
    weight_ref,
    vector_ref,
    dealt_ref,
    cot_dealt_ref,
    weight_all_ref,
    vector_all_ref,
    normalized_ref,
    inverse_std_ref,
    out_rows_tokens,
    in_rows_tokens,
    out_rows_cots,
    in_rows_cots,
    out_tokens,
    in_tokens,
    out_cots,
    in_cots,
    *sems,
):
    at = Place()
    held, feats = tokens_ref.shape
    piece = out_tokens.shape[1]
    capacity = out_rows_tokens.shape[1]
    depth = weight_ref.shape[0]
    sems = list(sems)

    def some(count):
        taken, sems[:count] = sems[:count], []
        return taken

    def block(ref):
        return lambda index: ref.at[index]

    def dealt_slot(ref):
        return lambda row: ref.at[pl.ds(row * piece, piece), :]

    last_tokens = RowGather(at, dealt_slot(dealt_ref), some(4))
    last_cots = RowGather(at, dealt_slot(cot_dealt_ref), some(4))
    rows_tokens = Swap(at, "row", block(out_rows_tokens), block(in_rows_tokens), some(2))
    rows_cots = Swap(at, "row", block(out_rows_cots), block(in_rows_cots), some(2))
    swap_tokens = Swap(at, "col", block(out_tokens), block(in_tokens), some(2))
    swap_cots = Swap(at, "col", block(out_cots), block(in_cots), some(2))
    swap_weight = Swap(
        at,
        "col",
        lambda c: weight_ref,
        lambda c: weight_all_ref.at[pl.ds(c * depth, depth), :],
        some(2),
    )
    swap_vector = Swap(at, "col", lambda c: vector_ref, block(vector_all_ref), some(2))

    def pick(in_ref, out_ref):
        pack_rows((send_back_ref, piece), flat(in_ref, capacity), [out_ref], feats)

    both = jnp.concatenate([tokens_ref[...], cotangent_ref[...]], axis=1)
    pack_rows((take_back_ref, capacity), both, [out_rows_tokens, out_rows_cots], feats)
    meet(every_row(at) + col_peers(at))
    rows_tokens.start()
    swap_vector.start()
    rows_cots.start()
    weight_all_ref[pl.ds(at.col * depth, depth), :] = weight_ref[...]
    vector_all_ref[at.col] = vector_ref[...]
    in_rows_tokens[at.row] = out_rows_tokens[at.row]
    in_rows_cots[at.row] = out_rows_cots[at.row]

    rows_tokens.arrived()
    pick(in_rows_tokens, out_tokens)
    swap_tokens.start()
    in_tokens[at.col] = out_tokens[at.col]
    rows_cots.arrived()
    pick(in_rows_cots, out_cots)
    swap_cots.start()
    in_cots[at.col] = out_cots[at.col]

    swap_vector.arrived()
    swap_tokens.arrived()
    width = at.cols * feats
    parts = [in_tokens[f].astype(f32) for f in range(at.cols)]
    mean = sum(jnp.sum(part, axis=1, keepdims=True) for part in parts) / width
    parts = [part - mean for part in parts]
    variance = sum(jnp.sum(part * part, axis=1, keepdims=True) for part in parts) / width
    inverse_std = lax.rsqrt(variance + norm_floor)
    inverse_std_ref[...] = inverse_std
    own = pl.ds(at.row * piece, piece)
    for f in range(at.cols):
        lanes = slice(f * feats, (f + 1) * feats)
        normalized = parts[f] * inverse_std
        normalized_ref[:, lanes] = normalized
        vectors = vector_all_ref[f]
        dealt_ref[own, lanes] = (normalized * vectors[0:1, :] + vectors[1:2, :]).astype(bf16)
    last_tokens.start(dealt_ref.at[own, :])
    swap_weight.start()
    swap_cots.arrived()
    for f in range(at.cols):
        cot_dealt_ref[own, f * feats : (f + 1) * feats] = in_cots[f]
    last_cots.start(cot_dealt_ref.at[own, :])
    last_tokens.forward()
    last_cots.forward()
    last_tokens.finish()
    last_cots.finish()
    swap_weight.arrived()
    for moved in (last_tokens, last_cots, rows_tokens, rows_cots):
        moved.sent()
    for moved in (swap_tokens, swap_cots, swap_weight, swap_vector):
        moved.sent()


def deal_all(tokens, cotangent, take_back, send_back, weight, vectors, rows, cols):
    held, feats = tokens.shape
    total = held * rows
    group = total // cols
    piece = group // rows
    width = feats * cols
    capacity = send_back.shape[1] // rows
    shape = jax.ShapeDtypeStruct
    messages = pltpu.VMEM((rows, capacity, feats), bf16)
    return remote_call(
        deal_kernel,
        0,
        (
            shape((group, width), bf16),
            shape((group, width), bf16),
            shape((weight.shape[0] * cols, weight.shape[1]), bf16),
            shape((cols,) + vectors.shape, f32),
            shape((piece, width), f32),
            shape((piece, 1), f32),
        ),
        [VMEM_SPEC] * 6,
        [
            *([messages] * 4),
            *([pltpu.VMEM((cols, piece, feats), bf16)] * 4),
            *(gather_sems() * 2),
            *(swap_sems(rows) * 2),
            *(swap_sems(cols) * 4),
        ],
        100 * 10**9,
        "deal_all",
    )(tokens, cotangent, take_back, send_back, weight, vectors)


def split(x):
    high_part = x.astype(bf16)
    return high_part, (x - high_part.astype(f32)).astype(bf16)


def three(dot, left, right):
    return dot(left[0], right[0]) + (dot(left[0], right[1]) + dot(left[1], right[0]))


BLK = 128


def backward_kernel(
    dealt_ref,
    cotangent_ref,
    weight_ref,
    table_ref,
    start_ref,
    q_ref,
    k_ref,
    v_ref,
    slope_ref,
    branch_ref,
    attended_ref,
    total_ref,
    branch_part_ref,
    out_part_ref,
    momentum_ref,
    in_grad_ref,
    out_grad_ref,
    bias_grad_ref,
    matrix_ref,
    gram_ref,
    normed_part_ref,
    branch_sum_ref,
    pre_ref,
    dk_ref,
    dv_ref,
    pairs,
    values,
    out_parts,
    up_part,
    up_parts,
    qkv_part,
    qkv_parts,
    bias_part,
    biases,
    chunks,
    partial,
    from_twin,
    half_sum,
    slices,
    twin_sums,
    slots,
    *sems,
):
    at = Place()
    sems = list(sems)

    def some(count):
        taken, sems[:count] = sems[:count], []
        return taken

    def block(ref):
        return lambda index: ref.at[index]

    branch_rows = RowSum(at, branch_part_ref, twin_sums, slots, some(4))
    swap_out = Swap(at, "col", block(out_part_ref), block(out_parts), some(2))
    swap_up = Swap(at, "col", block(up_part), block(up_parts), some(2))
    swap_qkv = Swap(at, "col", block(qkv_part), block(qkv_parts), some(2))
    swap_bias = Swap(at, "col", lambda c: bias_part, block(biases), some(2))
    swap_chunk = Swap(at, "col", block(chunks), block(matrix_ref), some(2))
    twin_send, twin_recv, sum_send, sum_recv, all_send, all_recv, pass_send, pass_recv = some(8)
    count = at.chips * 2
    mine = at.chip * 2 + at.col % 2
    first_col = at.col - at.col % 2

    def member(step):
        other = lax.rem(mine + step, count)
        return other, ((other // 2) * 2 + at.core, first_col + other % 2)

    peers = [member(step)[1] for step in range(1, count)]
    meet(row_peers(at) + col_peers(at) + peers)
    branch_rows.start()
    swap_out.start()
    out_parts[at.col] = out_part_ref[at.col]
    feats = up_part.shape[1]
    half = up_part.shape[2]

    def weight_part(ref, lanes):
        for first in range(0, dealt_ref.shape[1], BLOCK):
            part = dot_tn(dealt_ref[:, first : first + BLOCK], pre_ref[:, lanes])
            for index in range(BLOCK // feats):
                ref[first // feats + index] = part[
                    index * feats : (index + 1) * feats, :
                ].astype(bf16)

    def direction(index, grad):
        lanes = slice(index * BLK, (index + 1) * BLK)
        state = momentum * momentum_ref[:, lanes] + grad
        chunks[index] = grad + momentum * state

    width = pre_ref.shape[1]
    in_weight, out_weight = weight_ref[:, :width], weight_ref[:, width:]
    tokens = dealt_ref.shape[0]
    rows_all = tokens // PIECE
    firsts = range(0, tokens, BLOCK)
    for first in firsts:
        rows = pl.ds(first, BLOCK)
        branch_grad = dot_nn(cotangent_ref[rows, :], out_weight)
        for part in range(BLOCK // PIECE):
            these = slice(part * PIECE, (part + 1) * PIECE)
            spaced = pl.ds(first // PIECE + part, PIECE, stride=rows_all)
            values[spaced, :] = branch_grad[these, : 2 * HEAD]
        pre_ref[rows, 4 * HEAD :] = (branch_grad[:, 2 * HEAD :] * slope_ref[rows, :]).astype(bf16)
    weight_part(up_part, slice(half, 2 * half))
    swap_up.start()
    up_parts[at.col] = up_part[at.col]
    dk_ref[...] = jnp.zeros_like(dk_ref)
    dv_ref[...] = jnp.zeros_like(dv_ref)
    branch_rows.middle()
    for first in reversed(firsts):
        rows, keys = pl.ds(first, BLOCK), first + BLOCK
        query, grad = q_ref[rows, :], values[rows, :HEAD].astype(bf16)
        key, value = k_ref[:keys, :], v_ref[:keys, :]
        scores = dot_nt(query, key)
        allowed = allowed_keys(start_ref, first, keys)
        prob = jnp.where(allowed, jnp.exp(scores - total_ref[rows, :]), 0.0)
        delta = jnp.sum(
            grad.astype(f32) * attended_ref[rows, :].astype(f32), axis=1, keepdims=True
        )
        score_grad = (prob * (dot_nt(grad, value) - delta)).astype(bf16)
        dk_ref[:keys, :] += dot_tn(score_grad, query)
        dv_ref[:keys, :] += dot_tn(prob.astype(bf16), grad)
        pairs[rows, :] = jnp.concatenate(
            [dot_nn(score_grad, key) * HEAD**-0.5, dk_ref[rows, :]], axis=1
        )
        dv = dv_ref[rows, :]
        values[rows, :] = jnp.concatenate([dv, jnp.zeros_like(dv)], axis=1)
    for first in firsts:
        rows = pl.ds(first, BLOCK)
        pair, value = [
            jnp.concatenate(
                [
                    ref[pl.ds(first // PIECE + part, PIECE, stride=rows_all), :]
                    for part in range(BLOCK // PIECE)
                ],
                axis=0,
            )
            for ref in (pairs, values)
        ]
        pre_ref[rows, : 2 * HEAD] = turned(pair, turning(table_ref, rows), True).astype(bf16)
        pre_ref[rows, 2 * HEAD : 4 * HEAD] = value.astype(bf16)
    weight_part(qkv_part, slice(0, half))
    swap_qkv.start()
    qkv_parts[at.col] = qkv_part[at.col]
    bias = jnp.sum(pre_ref[...].astype(f32), axis=0, keepdims=True)
    bias_part[...] = jnp.broadcast_to(bias, bias_part.shape)
    swap_bias.start()
    biases[at.col] = bias_part[...]
    for first in firsts:
        rows = pl.ds(first, BLOCK)
        normed_part_ref[rows, :] = dot_nt(pre_ref[rows, :], in_weight).astype(bf16)

    swap_out.arrived()
    total = sum(out_parts[c].astype(f32) for c in range(at.cols))
    filled = jnp.zeros((feats, half - 2 * HEAD), f32)
    out_grad = jnp.concatenate([total[:, : 2 * HEAD], filled, total[:, 2 * HEAD :]], axis=1)
    out_grad_ref[...] = out_grad
    swap_up.arrived()
    up_grad = sum(up_parts[c].astype(f32) for c in range(at.cols))
    in_grad_ref[:, half:] = up_grad
    late = half // BLK
    for index in range(late, at.cols):
        first = (index - late) * BLK
        if first < half:
            direction(index, up_grad[:, first : first + BLK])
        else:
            direction(index, out_grad[:, first - half : first - half + BLK])
    swap_chunk.start(lambda to: to >= late)
    swap_qkv.arrived()
    qkv_grad = sum(qkv_parts[c].astype(f32) for c in range(at.cols))
    in_grad_ref[:, :half] = qkv_grad
    for index in range(late):
        direction(index, qkv_grad[:, index * BLK : (index + 1) * BLK])
    swap_chunk.start(lambda to: to < late)
    matrix_ref[at.col] = chunks[at.col]
    swap_bias.arrived()
    bias_grad_ref[...] = sum(biases[c] for c in range(at.cols))
    swap_chunk.arrived()

    strips = matrix_ref.shape[0]
    matrix = split(matrix_ref[...].reshape(strips * BLK, BLK))
    index = 0
    for i in range(strips):
        left = [m[i * BLK : (i + 1) * BLK, :] for m in matrix]
        right = [m[i * BLK :, :] for m in matrix]
        product = three(dot_nt, left, right)
        for j in range(strips - i):
            partial[index] = product[:, j * BLK : (j + 1) * BLK]
            index += 1
    blocks = index // 2
    to_twin = remote(
        partial.at[pl.ds((1 - at.core) * blocks, blocks)],
        from_twin,
        twin_send.at[0],
        twin_recv.at[0],
        at.twin,
    )
    to_twin.start()
    to_twin.wait_recv()
    for b in range(blocks):
        half_sum[b * BLK : (b + 1) * BLK, :] = partial[at.core * blocks + b] + from_twin[b]

    size = blocks * BLK // count

    def piece_of(owner):
        return half_sum.at[pl.ds(owner * size, size), :]

    def give(step):
        owner, device = member(step)
        return remote(
            piece_of(owner), slices.at[mine], sum_send.at[step], sum_recv.at[step], device
        )

    for step in range(1, count):
        give(step).start()
    slices[mine] = half_sum[pl.ds(mine * size, size), :]
    for step in range(1, count):
        came, device = member(count - step)
        remote(
            slices.at[came], slices.at[came], sum_send.at[step], sum_recv.at[step], device
        ).wait_recv()
    total = slices[0]
    for index in range(1, count):
        total = total + slices[index]
    half_rows = blocks * BLK

    def home(owner):
        return gram_ref.at[pl.ds(at.core * half_rows + owner * size, size), :]

    gram_ref[pl.ds(at.core * half_rows + mine * size, size), :] = total

    def spread(step):
        return remote(
            home(mine), home(mine), all_send.at[step], all_recv.at[step], member(step)[1]
        )

    def passing(step):
        came = member(count - step)[0] if step else mine
        return remote(
            home(came), home(came), pass_send.at[step], pass_recv.at[step], at.twin
        )

    for step in range(1, count):
        spread(step).start()
    passing(0).start()
    for step in range(1, count):
        came, device = member(count - step)
        remote(
            home(came), home(came), all_send.at[step], all_recv.at[step], device
        ).wait_recv()
        passing(step).start()
    for step in range(count):
        other = lax.rem(at.chip * 2 + at.col % 2 + count - step, count)
        slot = gram_ref.at[pl.ds((1 - at.core) * half_rows + other * size, size), :]
        remote(slot, slot, pass_send.at[step], pass_recv.at[step], at.twin).wait_recv()
        passing(step).wait_send()
    to_twin.wait_send()
    for step in range(1, count):
        give(step).wait_send()
        spread(step).wait_send()
    branch_sum_ref[...] = branch_rows.finish().astype(bf16)
    branch_rows.sent()
    for moved in (swap_out, swap_up, swap_qkv, swap_bias, swap_chunk):
        moved.sent()


WIDE = 256


def poly_kernel(
    gram_ref,
    matrix_ref,
    normed_part_ref,
    branch_ref,
    normalized_ref,
    inverse_std_ref,
    vector_ref,
    tokens_ref,
    cotangent_ref,
    pick_ref,
    pack_ref,
    update_ref,
    output_ref,
    input_grad_ref,
    vector_sum_ref,
    own_update,
    normed_ref,
    out_branch,
    in_branch,
    out_rows_branch,
    in_rows_branch,
    out_token,
    in_token,
    out_rows,
    in_rows,
    twin_sums,
    slots,
    *buffers,
):
    at = Place()
    sems, buffers = buffers[8:], buffers[:8]

    def block(ref):
        return lambda index: ref.at[index]

    swap_token = Swap(at, "col", block(out_token), block(in_token), sems[0:2])
    rows_token = Swap(at, "row", block(out_rows), block(in_rows), sems[2:4])
    feats = out_token.shape[2]
    swap_update = Swap(
        at,
        "col",
        lambda c: own_update.at[pl.ds(c * feats, feats), :],
        block(update_ref),
        sems[4:6],
    )
    swap_branch = Swap(at, "col", block(out_branch), block(in_branch), sems[6:8])
    rows_branch = Swap(at, "row", block(out_rows_branch), block(in_rows_branch), sems[8:10])
    normed_rows = RowSum(at, normed_part_ref, twin_sums, slots, sems[10:14])
    piece, capacity = normed_ref.shape[0], out_rows_branch.shape[1]
    lanes = [slice(f * feats, (f + 1) * feats) for f in range(at.cols)]
    for f in range(at.cols):
        out_branch[f] = branch_ref[:, lanes[f]]
    meet(every_row(at) + col_peers(at))
    normed_rows.start()
    swap_branch.start()
    in_branch[at.col] = out_branch[at.col]

    def branch_back():
        swap_branch.arrived()
        pack_rows((pick_ref, capacity), flat(in_branch, piece), [out_rows_branch], feats)
        rows_branch.start()
        in_rows_branch[at.row] = out_rows_branch[at.row]

    def home(rows_ref, base_ref, shift, out_ref):
        values = flat(rows_ref, capacity)
        for first in range(0, out_ref.shape[0], BLOCK):
            rows = pl.ds(first, BLOCK)
            found = moved_rows(pack_ref[...], first, BLOCK, values)
            out_ref[rows, :] = found + base_ref[rows, :].astype(f32) + shift

    def branch_home():
        rows_branch.arrived()
        home(in_rows_branch, tokens_ref, vector_ref[at.col][2:3, :], output_ref)

    def extra(vectors):
        parts = [part.astype(f32) for vector in vectors for part in split(vector)]
        empty = jnp.zeros((EXTRA - len(parts), feats), f32)
        return jnp.concatenate([*parts, empty], axis=0).astype(bf16)

    def token_grads():
        normed_ref[...] = normed_rows.finish()
        width = at.cols * feats
        scaled = [normed_ref[:, lanes[f]] * vector_ref[f][0:1, :] for f in range(at.cols)]
        mean_first = sum(jnp.sum(part, axis=1, keepdims=True) for part in scaled) / width
        mean_second = (
            sum(
                jnp.sum(part * normalized_ref[:, lanes[f]], axis=1, keepdims=True)
                for f, part in enumerate(scaled)
            )
            / width
        )
        for f in range(at.cols):
            normalized, grad = normalized_ref[:, lanes[f]], normed_ref[:, lanes[f]]
            token_grad = inverse_std_ref[...] * (scaled[f] - mean_first - normalized * mean_second)
            out_token[f, :piece, :] = token_grad.astype(bf16)
            gain_grad = jnp.sum(grad * normalized, axis=0, keepdims=True)
            shift_grad = jnp.sum(grad, axis=0, keepdims=True)
            out_token[f, piece:, :] = extra([gain_grad, shift_grad])
        swap_token.start()
        in_token[at.col] = out_token[at.col]

    def token_back():
        cot_sum = jnp.sum(cotangent_ref[...].astype(f32), axis=0, keepdims=True)
        swap_token.arrived()
        pack_rows((pick_ref, capacity), flat(in_token, piece), [out_rows], feats)
        sums = sum(in_token[c, piece:, :].astype(f32) for c in range(at.cols))
        sums = extra([sums[0:1, :] + sums[1:2, :], sums[2:3, :] + sums[3:4, :], cot_sum])
        for row in range(at.rows):
            out_rows[row, capacity:, :] = sums
        rows_token.start()
        in_rows[at.row] = out_rows[at.row]

    first, second, third, thin = [buffers[2 * i : 2 * i + 2] for i in range(4)]
    strips = matrix_ref.shape[0]
    size = strips * BLK
    counts = range(size // WIDE)
    eye = lax.broadcasted_iota(jnp.int32, (BLK, BLK), 0) == lax.broadcasted_iota(
        jnp.int32, (BLK, BLK), 1
    )

    def put(pair, rows, lanes, value):
        high_part, low_part = split(value)
        pair[0][rows, lanes] = high_part
        pair[1][rows, lanes] = low_part

    def get(pair, rows, lanes):
        return pair[0][rows, lanes], pair[1][rows, lanes]

    places, index = [], 0
    for i in range(strips):
        for j in range(i, strips):
            places.append((i, j, index))
            index += 1
    trace = sum(
        jnp.sum(jnp.where(eye, gram_ref[spot * BLK : (spot + 1) * BLK, :], 0.0))
        for i, j, spot in places
        if i == j
    )
    shrink = 1.0 / (jnp.sqrt(jnp.full((1, 1), trace, f32)) + ortho_floor)
    for i, j, spot in places:
        block = gram_ref[spot * BLK : (spot + 1) * BLK, :] * (shrink * shrink)
        here, there = slice(i * BLK, (i + 1) * BLK), slice(j * BLK, (j + 1) * BLK)
        put(first, here, there, block)
        if j > i:
            put(first, there, here, block.T)
    everything = slice(0, size)
    for i in range(strips):
        put(thin, slice(i * BLK, (i + 1) * BLK), everything, matrix_ref[i] * shrink)

    def product(left, right, out, finish=None):
        for i in counts:
            rows, rest = slice(i * WIDE, (i + 1) * WIDE), slice(i * WIDE, size)
            value = three(dot_nn, get(left, rows, everything), get(right, everything, rest))
            if finish is not None:
                value = finish(value, rows, rest)
            put(out, rows, rest, value)
            for j in range(i + 1, size // WIDE):
                part = value[:, (j - i) * WIDE : (j - i + 1) * WIDE]
                put(out, slice(j * WIDE, (j + 1) * WIDE), rows, part.T)

    def thin_product(left):
        right = get(thin, everything, everything)
        return [
            three(dot_nn, get(left, slice(i * WIDE, (i + 1) * WIDE), everything), right)
            for i in counts
        ]

    def sweep(gram, poly, square, between=lambda: None):
        def finish(value, rows, rest):
            high_part, low_part = get(gram, rows, rest)
            value = poly_cubic * value + poly_square * (
                high_part.astype(f32) + low_part.astype(f32)
            )
            at_row = lax.broadcasted_iota(jnp.int32, value.shape, 0)
            at_lane = lax.broadcasted_iota(jnp.int32, value.shape, 1)
            return value + jnp.where(at_row == at_lane, poly_linear, 0.0)

        product(gram, gram, poly, finish)
        between()
        for i, value in zip(counts, thin_product(poly)):
            put(thin, slice(i * WIDE, (i + 1) * WIDE), everything, value)
        product(poly, poly, square)
        product(gram, square, poly)

    def two(step, carry):
        def early():
            @pl.when(step == 0)
            def _():
                normed_rows.middle()
                branch_back()

            @pl.when(step == 1)
            def _():
                token_grads()

        def late():
            @pl.when(step == 1)
            def _():
                branch_home()

        sweep(first, second, third, early)

        @pl.when(step == 1)
        def _():
            token_back()

        sweep(second, first, third, late)
        return carry

    lax.fori_loop(0, 2, two, 0)
    once = thin_product(first)
    old = []
    for i in counts:
        rows = slice(i * WIDE, (i + 1) * WIDE)
        high_part, low_part = get(thin, rows, everything)
        old.append(high_part.astype(f32) + low_part.astype(f32))
    for i, value in zip(counts, once):
        put(thin, slice(i * WIDE, (i + 1) * WIDE), everything, value)
    for i, value in zip(counts, thin_product(first)):
        result = poly_linear * old[i] + poly_square * once[i] + poly_cubic * value
        own_update[i * WIDE : (i + 1) * WIDE, :] = result.astype(bf16)
    swap_update.start()
    update_ref[at.col] = own_update[pl.ds(at.col * feats, feats), :]

    rows_token.arrived()
    home(in_rows, cotangent_ref, 0.0, input_grad_ref)
    vector_sum_ref[...] = sum(
        in_rows[row, capacity:, :].astype(f32) for row in range(at.rows)
    )
    swap_update.arrived()
    for moved in (swap_token, rows_token, swap_update, swap_branch, rows_branch, normed_rows):
        moved.sent()


def orthogonalize(
    gram,
    matrix,
    normed_part,
    branch_sum,
    normalized,
    inverse_std,
    vectors,
    tokens,
    cotangent,
    pick,
    pack,
    rows,
):
    cols, feats, width = matrix.shape
    size = cols * BLK
    piece, full = branch_sum.shape
    held = cotangent.shape[0]
    chips = rows // 2
    capacity = pack.shape[1] // rows
    shape = jax.ShapeDtypeStruct
    square, narrow = pltpu.VMEM((size, size), bf16), pltpu.VMEM((size, width), bf16)
    return remote_call(
        poly_kernel,
        3,
        (
            shape((cols, feats, width), bf16),
            shape((held, feats), f32),
            shape((held, feats), f32),
            shape((EXTRA, feats), f32),
        ),
        [VMEM_SPEC] * 11,
        [
            narrow,
            pltpu.VMEM((piece, full), f32),
            *([pltpu.VMEM((cols, piece, feats), bf16)] * 2),
            *([pltpu.VMEM((rows, capacity, feats), bf16)] * 2),
            *([pltpu.VMEM((cols, piece + EXTRA, feats), bf16)] * 2),
            *([pltpu.VMEM((rows, capacity + EXTRA, feats), bf16)] * 2),
            *sum_scratch(piece, full, chips)[:2],
            *([square] * 6),
            *([narrow] * 2),
            *swap_sems(cols),
            *swap_sems(rows),
            *(swap_sems(cols) * 2),
            *swap_sems(rows),
            *sum_scratch(piece, full, chips)[2:],
        ],
        60 * 10**9,
        "orthogonalize",
    )(
        *(gram, matrix, normed_part.reshape(chips, 2, piece, full), branch_sum, normalized),
        *(inverse_std, vectors, tokens, cotangent, pick, pack),
    )


def backward(
    dealt, cotangent, weight, table, starts, kept, branch_part, out_part, old_momentum, rows, cols
):
    tokens, width = dealt.shape
    up = kept[3].shape[1]
    in_width = 4 * HEAD + up
    out_width = out_part.shape[1]
    feats, piece, chips = width // cols, tokens // rows, rows // 2
    blocks = cols * (cols + 1) // 2
    count = chips * 2
    half_rows = blocks * BLK // 2
    shape = jax.ShapeDtypeStruct
    dma = pltpu.SemaphoreType.DMA
    part = pltpu.VMEM((cols, feats, up), bf16)
    return remote_call(
        backward_kernel,
        1,
        (
            shape((feats, in_width), f32),
            shape((feats, in_width), f32),
            shape((8, in_width), f32),
            shape((cols, feats, BLK), f32),
            shape((blocks * BLK, BLK), f32),
            shape((tokens, width), bf16),
            shape((piece, width), bf16),
        ),
        [VMEM_SPEC] * 15,
        [
            pltpu.VMEM((tokens, in_width), bf16),
            *([pltpu.VMEM((tokens, HEAD), f32)] * 2),
            *([pltpu.VMEM((tokens, 2 * HEAD), f32)] * 2),
            pltpu.VMEM((cols, feats, out_width), bf16),
            *([part] * 4),
            pltpu.VMEM((8, in_width), f32),
            pltpu.VMEM((cols, 8, in_width), f32),
            pltpu.VMEM((cols, feats, BLK), f32),
            pltpu.VMEM((blocks, BLK, BLK), f32),
            pltpu.VMEM((blocks // 2, BLK, BLK), f32),
            pltpu.VMEM((half_rows, BLK), f32),
            pltpu.VMEM((count, half_rows // count, BLK), f32),
            *sum_scratch(piece, width, chips),
            *(swap_sems(cols) * 5),
            dma((1,)),
            dma((1,)),
            *([dma((count,))] * 6),
        ],
        90 * 10**9,
        "backward",
    )(
        *(dealt, cotangent, weight, table, starts, *kept),
        branch_part.reshape(chips, 2, piece, width),
        out_part.reshape(cols, feats, out_width),
        old_momentum,
    )


def rotary_table(places):
    half_rot = ROT // 2
    inverse = 1.0 / 10000.0 ** (jnp.arange(half_rot, dtype=f32) * (2.0 / ROT))
    angles = inverse[:, None] * places.astype(f32)[None, :]
    table = jnp.concatenate([jnp.cos(angles), jnp.sin(angles)], axis=0)
    return jnp.concatenate(high_low(table), axis=0)


CAPACITY = 96


def exchange_plan(seq_starts, seq_ends, shift, deal_order, row, rows, cols):
    total = deal_order.shape[0]
    held, group = total // rows, total // cols
    piece = group // rows

    def passed(x, to):
        return (x + rows - 1 - to) // rows

    def clipped(x, holder):
        return jnp.clip(x, holder * held, holder * held + held)

    def rank(token, holder, to):
        token, holder, to = token[:, None], holder[:, None], to[:, None]
        low = clipped(seq_starts[None], holder)
        high = jnp.maximum(clipped(jnp.minimum(seq_ends[None], token), holder), low)
        return jnp.sum(passed(high + shift, to) - passed(low + shift, to), axis=1)

    def listed(holder, to):
        slot = jnp.arange(CAPACITY, dtype=jnp.int32)[None, :, None]
        holder, to = holder[:, None], to[:, None]
        first = passed(clipped(seq_starts[None], holder) + shift, to)
        count = passed(clipped(seq_ends[None], holder) + shift, to) - first
        base = jnp.cumsum(count, axis=1) - count
        inside = slot - base[:, None, :]
        found = (inside >= 0) & (inside < count[:, None, :])
        dealt = rows * (first[:, None, :] + inside) + to[:, :, None]
        token = dealt - shift[None, None, :]
        used = jnp.any(found, axis=2)
        return [jnp.sum(jnp.where(found, x, 0), axis=2) for x in (dealt, token)] + [used]

    every = jnp.arange(rows, dtype=jnp.int32)
    mine = jnp.full((rows,), row, jnp.int32)
    dealt, token, used = listed(jnp.concatenate([mine, every]), jnp.concatenate([every, mine]))
    pack = jnp.where(used[:rows], token[:rows] - row * held, -1)
    back = dealt[rows:]
    send_back = (back // group) * piece + (back % group) // rows
    send_back = jnp.where(used[rows:], send_back, -1)
    own = row * held + jnp.arange(held, dtype=jnp.int32)
    holds = (seq_starts[None] <= own[:, None]) & (own[:, None] < seq_ends[None])
    own_to = (own + jnp.sum(jnp.where(holds, shift[None], 0), axis=1)) % rows
    wanted = deal_order.reshape(cols * piece, rows)
    wanted = jnp.sum(jnp.where(every[None] == row, wanted, 0), axis=1)
    holder = wanted // held
    ranks = rank(
        jnp.concatenate([own, wanted]),
        jnp.concatenate([jnp.full_like(own, row), holder]),
        jnp.concatenate([own_to, jnp.full_like(wanted, row)]),
    )
    take_back = own_to * CAPACITY + ranks[:held]
    pick = holder * CAPACITY + ranks[held:]
    return [x.reshape(1, -1) for x in (pack, pick, send_back, take_back)]


def adam_step(value, gradient, first_state, second_state):
    first_new = beta_first * first_state + (1.0 - beta_first) * gradient
    second_new = beta_second * second_state + (1.0 - beta_second) * gradient * gradient
    corrected = first_new / (1.0 - beta_first**STEP)
    root_term = jnp.sqrt(second_new / (1.0 - beta_second**STEP)) + adam_floor
    return (first_new, second_new, value - rate_vector * corrected / root_term)


def high_low(x):
    high_part = x.astype(bf16)
    return high_part, (x - high_part.astype(f32)).astype(bf16)


def per_device(
    tokens,
    cotangent,
    lengths,
    deal_order,
    qkv_weight,
    up_weight,
    proj_weight,
    down_weight,
    norm_vectors,
    qkv_bias,
    mlp_bias,
    qkv_momentum,
    up_momentum,
    proj_momentum,
    down_momentum,
    norm_moment,
    norm_square,
    qkv_bias_moment,
    qkv_bias_square,
    mlp_bias_moment,
    mlp_bias_square,
):
    cols, rows = lax.axis_size("col"), lax.axis_size("row")
    col, row = lax.axis_index("col"), lax.axis_index("row")
    total_tokens = deal_order.shape[0]
    group = total_tokens // cols
    piece = group // rows
    held = total_tokens // rows
    feats = D // cols
    qkv_width, up_width = qkv_weight.shape[1], up_weight.shape[1]
    proj_width = proj_weight.shape[0]

    seq_ends = jnp.cumsum(lengths)
    seq_starts = seq_ends - lengths
    anchor = lax.dynamic_slice_in_dim(deal_order, col * group, group)
    before = seq_ends[None, :] <= anchor[:, None]
    places = anchor - jnp.sum(jnp.where(before, lengths[None, :], 0), axis=1)
    starts = (jnp.arange(group, dtype=jnp.int32) - places)[:, None]
    table = rotary_table(places.reshape(piece, rows).T.reshape(group))
    at = jnp.arange(total_tokens, dtype=jnp.int32)
    dealt_starts = jnp.sum(
        jnp.where(deal_order[None, :] == seq_starts[:, None], at[None, :], 0), axis=1
    )
    shift = dealt_starts - seq_starts
    pack, pick, send_back, take_back = exchange_plan(
        seq_starts, seq_ends, shift, deal_order, row, rows, cols
    )

    def lanes(x, width):
        return jnp.pad(x, ((0, 0), (0, width - x.shape[1])))

    in_pad = 2 * up_width
    tile = jnp.concatenate(
        [
            lanes(qkv_weight.astype(bf16), up_width),
            up_weight.astype(bf16),
            lanes(proj_weight.astype(bf16).T, 128),
            down_weight.astype(bf16).T,
        ],
        axis=1,
    )
    dealt, cotangent_dealt, weight_all, vector_all, normalized, inverse_std = deal_all(
        tokens, cotangent, take_back, send_back, tile, jnp.pad(norm_vectors, ((0, 5), (0, 0))), rows, cols
    )

    bias = jnp.concatenate(
        [jnp.pad(qkv_bias, (0, up_width - qkv_width)), mlp_bias], axis=0
    ).reshape(1, in_pad)
    *kept, branch_part, out_part = forward(
        dealt, cotangent_dealt, weight_all, bias, table, starts
    )
    old_momentum = jnp.concatenate(
        [
            lanes(qkv_momentum, up_width),
            up_momentum,
            lanes(proj_momentum.T, up_width),
            down_momentum.T,
        ],
        axis=1,
    )
    in_grad, out_grad, bias_rows, matrix, gram, normed_part, branch_sum = backward(
        dealt,
        cotangent_dealt,
        weight_all,
        table,
        starts,
        kept,
        branch_part,
        out_part,
        old_momentum,
        rows,
        cols,
    )
    returned, output, input_grad, vector_sum = orthogonalize(
        gram,
        matrix,
        normed_part,
        branch_sum,
        normalized,
        inverse_std,
        vector_all,
        tokens,
        cotangent,
        pick,
        pack,
        rows,
    )
    norm_grads = jnp.stack(
        [
            vector_sum[0] + vector_sum[1],
            vector_sum[2] + vector_sum[3],
            vector_sum[4] + vector_sum[5],
        ],
        axis=0,
    )
    in_bias_grad = bias_rows[0]
    gradients = (
        in_grad[:, :qkv_width],
        in_grad[:, up_width:],
        out_grad[:, :proj_width].T,
        out_grad[:, up_width:].T,
    )
    old_states = (qkv_momentum, up_momentum, proj_momentum, down_momentum)
    weights = (qkv_weight, up_weight, proj_weight, down_weight)
    widths = (3 * D, FF, D, FF)
    sizes = (qkv_width, up_width, proj_width, up_width)
    states = [momentum * old + g for old, g in zip(old_states, gradients)]
    new_weights = []
    for index in range(4):
        update = jnp.concatenate([returned[2 * index], returned[2 * index + 1]], axis=1)
        update = update[:, : sizes[index]].astype(f32)
        update = update.T if index >= 2 else update
        new_weights.append(
            weights[index] * (1.0 - rate_matrix * decay_matrix)
            - rate_matrix * 0.2 * math.sqrt(widths[index]) * update
        )

    norm_first, norm_second, norm_new = adam_step(
        norm_vectors, norm_grads, norm_moment, norm_square
    )
    qkv_first, qkv_second, qkv_bias_new = adam_step(
        qkv_bias, in_bias_grad[:qkv_width], qkv_bias_moment, qkv_bias_square
    )
    mlp_first, mlp_second, mlp_bias_new = adam_step(
        mlp_bias, in_bias_grad[up_width:], mlp_bias_moment, mlp_bias_square
    )
    return (
        output,
        input_grad,
        *gradients,
        *states,
        *new_weights,
        norm_first,
        norm_second,
        norm_new,
        qkv_first,
        qkv_second,
        qkv_bias_new,
        mlp_first,
        mlp_second,
        mlp_bias_new,
    )


def solution(mesh):
    over_both, over_flip = P("row", "col"), P("col", "row")
    features, hidden = P(None, "col"), P("row")
    return jax.shard_map(
        per_device,
        mesh=mesh,
        in_specs=(
            *(over_both, over_both, P(), P()),
            *(over_flip, over_flip, over_both, over_both),
            *(features, hidden, hidden),
            *(over_flip, over_flip, over_both, over_both),
            *(features, features, hidden, hidden, hidden, hidden),
        ),
        out_specs=(
            *(over_both, over_both),
            *(over_flip, over_flip, over_both, over_both) * 3,
            *(features,) * 3,
            *(hidden,) * 6,
        ),
        check_vma=False,
    )
```

```python
import functools
import math

import jax
import jax.numpy as jnp
from jax import lax
from jax.experimental import pallas as pl
from jax.experimental.pallas import tpu as pltpu
from jax.sharding import PartitionSpec as P

D = 1024
HEAD = 64
ROT = 16
FF = 4096
STEP = 10

poly_linear = 3.4445
poly_square = -4.775
poly_cubic = 2.0315
momentum = 0.95
rate_matrix = 0.15
decay_matrix = 0.1
beta_first = 0.9
beta_second = 0.95
rate_vector = 0.2
adam_floor = 1e-08
norm_floor = 1e-05
ortho_floor = 1e-07
masked_score = -1e30
f32 = jnp.float32
bf16 = jnp.bfloat16
BLOCK = 256
PIECE = 128
EXTRA = 16


def dot_nt(a, b, **kw):
    return lax.dot_general(a, b, (((1,), (1,)), ((), ())), preferred_element_type=f32, **kw)


def dot_tn(a, b, **kw):
    return lax.dot_general(a, b, (((0,), (0,)), ((), ())), preferred_element_type=f32, **kw)


def dot_nn(a, b, **kw):
    return lax.dot_general(a, b, (((1,), (0,)), ((), ())), preferred_element_type=f32, **kw)


def allowed_keys(start_ref, first, keys):
    shape = (BLOCK, keys)
    key_at = lax.broadcasted_iota(jnp.int32, shape, 1)
    query_at = first + lax.broadcasted_iota(jnp.int32, shape, 0)
    return (key_at >= start_ref[pl.ds(first, BLOCK), :]) & (key_at <= query_at)


def turning(table_ref, rows):
    lane = lax.broadcasted_iota(jnp.int32, (32, 2 * HEAD), 1) % HEAD
    entry = lax.broadcasted_iota(jnp.int32, (32, 2 * HEAD), 0) % 16
    half_rot = ROT // 2

    def spread(where, value):
        picks = jnp.where(where, value, 0.0).astype(bf16)
        return dot_tn(table_ref[:, rows], picks)

    cosine = spread((lane < ROT) & (entry == lane % half_rot), 1.0)
    cosine = cosine + jnp.where(lane[:1] < ROT, 0.0, 1.0)
    lower = spread((lane < half_rot) & (entry == lane + half_rot), -1.0)
    upper = spread((lane >= half_rot) & (lane < ROT) & (entry == lane), 1.0)
    return cosine, lower, upper


def turned(values, tables, back):
    cosine, lower, upper = tables
    half_rot = ROT // 2
    moved = (
        pltpu.roll(values, 2 * HEAD - half_rot, 1) * lower + pltpu.roll(values, half_rot, 1) * upper
    )
    return values * cosine - moved if back else values * cosine + moved


VMEM_LIMIT = 63 * 1024 * 1024


def remote_call(kernel, identity, out_shape, in_specs, scratch, flops, name):
    return pl.pallas_call(
        kernel,
        out_shape=out_shape,
        in_specs=in_specs,
        out_specs=(VMEM_SPEC,) * len(out_shape),
        scratch_shapes=scratch,
        compiler_params=pltpu.CompilerParams(
            collective_id=identity, has_side_effects=True, vmem_limit_bytes=VMEM_LIMIT
        ),
        cost_estimate=pl.CostEstimate(flops=flops, bytes_accessed=1 << 24, transcendentals=0),
        name=name,
    )


MESH = pl.DeviceIdType.MESH
VMEM_SPEC = pl.BlockSpec(memory_space=pltpu.VMEM)


def remote(src, dst, send, recv, device):
    return pltpu.make_async_remote_copy(
        src_ref=src, dst_ref=dst, send_sem=send, recv_sem=recv, device_id=device, device_id_type=MESH
    )


class Place:
    def __init__(self):
        self.row, self.col = lax.axis_index("row"), lax.axis_index("col")
        self.rows, self.cols = lax.axis_size("row"), lax.axis_size("col")
        self.chips = self.rows // 2
        self.chip, self.core = self.row // 2, self.row % 2
        self.twin = (self.chip * 2 + 1 - self.core, self.col)
        self.ring = self.chips // 2
        self.y, self.z = self.chip // self.ring, self.chip % self.ring

    def chip_at(self, step):
        return lax.rem(self.chip + step, self.chips)

    def chip_row(self, step):
        return self.chip_at(step) * 2 + self.core

    def col_at(self, step):
        return lax.rem(self.col + step, self.cols)


def meet(devices):
    barrier = pltpu.get_barrier_semaphore()
    for device in devices:
        pl.semaphore_signal(barrier, inc=1, device_id=device, device_id_type=MESH)
    pl.semaphore_wait(barrier, len(devices))


class HopGather:
    OWN, PARTNER, BELOW, ABOVE, BELOW_PARTNER, ABOVE_PARTNER, FAR, FAR_PARTNER = range(8)

    def __init__(self, at, axis, slot, sems):
        self.at, self.axis, self.slot = at, axis, slot
        self.sems = sems
        index, ring = (at.chip, at.chips // 2) if axis == "row" else (at.col, at.cols // 2)
        side, step = index // ring, index % ring

        def place(other, hops):
            return (1 - side if other else side) * ring + lax.rem(step + hops, ring)

        self.places = [
            place(False, 0),
            place(True, 0),
            place(False, ring - 1),
            place(False, 1),
            place(True, ring - 1),
            place(True, 1),
            place(False, 2),
            place(True, 2),
        ]

    def index(self, which):
        return self.places[which] * 2 + self.at.core if self.axis == "row" else self.places[which]

    def device(self, which):
        at = self.at
        return (self.index(which), at.col) if self.axis == "row" else (at.row, self.index(which))

    def block(self, which):
        return self.slot(self.index(which))

    def part(self, which, upper):
        ref = self.block(which)
        half = ref.shape[0] // 2
        return ref.at[pl.ds(0 if upper else half, half), :]

    def hop(self, tag, src, dst, to):
        send, recv = self.sems[0], self.sems[1]
        return remote(src, dst, send.at[tag], recv.at[tag], self.device(to))

    def took(self, tag, ref):
        self.hop(tag, ref, ref, self.PARTNER).wait_recv()

    def passing(self, which, src=None):
        send, recv = self.sems[2], self.sems[3]
        ref = self.block(which)
        return remote(
            ref if src is None else src, ref, send.at[which], recv.at[which], self.at.twin
        )

    def hops(self):
        own, src = self.block(self.OWN), self.src
        partner = self.block(self.PARTNER)
        below, above = self.part(self.BELOW, True), self.part(self.ABOVE, False)
        far_below = self.part(self.BELOW_PARTNER, True)
        far_above = self.part(self.ABOVE_PARTNER, False)
        return {
            "start": [
                (0, src, own, self.PARTNER),
                (1, src, own, self.ABOVE),
                (2, src, own, self.BELOW),
            ],
            "partner": [(3, partner, partner, self.ABOVE), (4, partner, partner, self.BELOW)],
            "below": [(5, below, below, self.ABOVE)],
            "above": [(6, above, above, self.BELOW)],
            "far_below": [(7, far_below, far_below, self.ABOVE)],
            "far_above": [(8, far_above, far_above, self.BELOW)],
        }

    def go(self, stage):
        for hop in self.hops()[stage]:
            self.hop(*hop).start()

    def start(self, src):
        self.src = src
        self.go("start")
        if self.axis == "row":
            self.passing(self.OWN, src).start()

    def landed(self, which):
        if self.axis == "row":
            self.passing(which).start()

    def steps(self):
        def first():
            self.took(1, self.block(self.BELOW))
            self.go("below")
            self.took(2, self.block(self.ABOVE))
            self.go("above")
            self.landed(self.BELOW)
            self.landed(self.ABOVE)

        def second():
            self.took(0, self.block(self.PARTNER))
            self.go("partner")
            self.landed(self.PARTNER)

        def third():
            self.took(3, self.block(self.BELOW_PARTNER))
            self.go("far_below")
            self.took(4, self.block(self.ABOVE_PARTNER))
            self.go("far_above")
            self.landed(self.BELOW_PARTNER)
            self.landed(self.ABOVE_PARTNER)

        def fourth():
            self.took(5, self.part(self.FAR, True))
            self.took(6, self.part(self.FAR, False))
            self.landed(self.FAR)
            self.took(7, self.part(self.FAR_PARTNER, True))
            self.took(8, self.part(self.FAR_PARTNER, False))
            self.landed(self.FAR_PARTNER)

        return [first, second, third, fourth]

    def finish(self):
        send, recv = self.sems[2], self.sems[3]
        for which in range(8):
            slot = self.slot(self.places[which] * 2 + 1 - self.at.core)
            remote(slot, slot, send.at[which], recv.at[which], self.at.twin).wait_recv()

    def sent(self):
        for stage in self.hops().values():
            for hop in stage:
                self.hop(*hop).wait_send()
        if self.axis == "row":
            self.passing(self.OWN, self.src).wait_send()
            for which in range(1, 8):
                self.passing(which).wait_send()


class Swap:
    def __init__(self, at, axis, src, dst, sems):
        self.at, self.axis, self.src, self.dst = at, axis, src, dst
        self.send, self.recv = sems
        self.me, self.size = (at.row, at.rows) if axis == "row" else (at.col, at.cols)

    def to(self, step):
        return lax.rem(self.me + step, self.size)

    def device(self, index):
        return (index, self.at.col) if self.axis == "row" else (self.at.row, index)

    def outgoing(self, step):
        to = self.to(step)
        return remote(
            self.src(to),
            self.dst(self.me),
            self.send.at[step],
            self.recv.at[step],
            self.device(to),
        )

    def start(self, which=None):
        for step in range(1, self.size):
            if which is None:
                self.outgoing(step).start()
            else:

                @pl.when(which(self.to(step)))
                def _():
                    self.outgoing(step).start()

    def arrived(self):
        for step in range(1, self.size):
            came = self.to(self.size - step)
            slot = self.dst(came)
            remote(
                slot, slot, self.send.at[step], self.recv.at[step], self.device(came)
            ).wait_recv()

    def sent(self):
        for step in range(1, self.size):
            self.outgoing(step).wait_send()


class RowSum:
    SEMS = 4

    def __init__(self, at, part, pairs, slots, sems):
        self.at, self.part, self.pairs, self.slots = at, part, pairs, slots
        self.twin_send, self.twin_recv, self.send, self.recv = sems

    def to_twin(self):
        at = self.at
        return remote(
            self.part.at[:, 1 - at.core],
            self.pairs,
            self.twin_send.at[0],
            self.twin_recv.at[0],
            at.twin,
        )

    def outgoing(self, step):
        at = self.at
        return remote(
            self.pairs.at[at.chip_at(step)],
            self.slots.at[at.chip],
            self.send.at[step],
            self.recv.at[step],
            (at.chip_row(step), at.col),
        )

    def start(self):
        self.to_twin().start()

    def middle(self):
        at = self.at
        self.to_twin().wait_recv()

        for step in (4, 1, 2, 3, 5, 6, 7, 0):
            chip = at.chip_at(step)
            both = self.part[chip, at.core].astype(f32) + self.pairs[chip].astype(f32)
            self.pairs[chip] = both.astype(bf16)
            if step > 0:
                self.outgoing(step).start()

    def finish(self):
        at = self.at
        total = self.pairs[at.chip].astype(f32)
        for step in range(1, at.chips):
            chip = at.chip_at(at.chips - step)
            slot = self.slots.at[chip]
            remote(
                slot, slot, self.send.at[step], self.recv.at[step], (chip * 2 + at.core, at.col)
            ).wait_recv()
            total = total + self.slots[chip].astype(f32)
        return total

    def released(self):
        self.to_twin().wait_send()

    def sent(self):
        for step in range(1, self.at.chips):
            self.outgoing(step).wait_send()


def sum_scratch(piece, width, chips):
    dma = pltpu.SemaphoreType.DMA
    return [
        pltpu.VMEM((chips, piece, width), bf16),
        pltpu.VMEM((chips, piece, width), bf16),
        dma((1,)),
        dma((1,)),
        dma((chips,)),
        dma((chips,)),
    ]


def moved_rows(index_row, first, count, values):
    shape = (count, index_row.shape[1])
    here = first + lax.broadcasted_iota(jnp.int32, shape, 0) == index_row
    return dot_nn(jnp.where(here, 1.0, 0.0).astype(bf16), values)


def flat(ref, size):
    return jnp.concatenate([ref[index, :size, :] for index in range(ref.shape[0])], axis=0)


def pack_rows(index_ref, values, out_refs, lanes):
    blocks = out_refs[0].shape[0]
    size = index_ref[1]
    for first in range(0, blocks, 4):
        found = moved_rows(index_ref[0][...], first * size, 4 * size, values).astype(bf16)
        for index in range(4):
            part = found[index * size : (index + 1) * size, :]
            for which, out_ref in enumerate(out_refs):
                out_ref[first + index, :size, :] = part[:, which * lanes : (which + 1) * lanes]


def every_row(at):
    return [(lax.rem(at.row + step, at.rows), at.col) for step in range(1, at.rows)]


def row_peers(at):
    return [(at.chip_row(step), at.col) for step in range(1, at.chips)] + [at.twin]


def col_peers(at):
    return [(at.row, at.col_at(step)) for step in range(1, at.cols)]


def gather_sems():
    return [pltpu.SemaphoreType.DMA((count,)) for count in (9, 9, 8, 8)]


def hop_sems():
    return [pltpu.SemaphoreType.DMA((9,))] * 2


def swap_sems(cols):
    return [pltpu.SemaphoreType.DMA((cols,))] * 2


def split(x):
    high_part = x.astype(bf16)
    return high_part, (x - high_part.astype(f32)).astype(bf16)


def three(dot, left, right):
    return dot(left[0], right[0]) + (dot(left[0], right[1]) + dot(left[1], right[0]))


BLK = 128


def layer_kernel(
    tokens_ref,
    cotangent_ref,
    take_back_ref,
    send_back_ref,
    weight_ref,
    vector_ref,
    bias_ref,
    table_ref,
    start_ref,
    momentum_ref,
    vector_all_ref,
    normalized_ref,
    inverse_std_ref,
    in_grad_ref,
    out_grad_ref,
    bias_grad_ref,
    matrix_ref,
    gram_ref,
    normed_part_ref,
    branch_sum_ref,
    dealt_ref,
    cot_dealt_ref,
    weight_all_ref,
    q_ref,
    k_ref,
    v_ref,
    slope_ref,
    branch_ref,
    attended_ref,
    total_ref,
    out_part,
    pairs,
    values,
    out_rows_tokens,
    in_rows_tokens,
    out_rows_cots,
    in_rows_cots,
    out_tokens,
    in_tokens,
    out_cots,
    in_cots,
    pre_ref,
    dk_ref,
    dv_ref,
    out_parts,
    up_part,
    up_parts,
    qkv_part,
    qkv_parts,
    bias_part,
    biases,
    chunks,
    products,
    from_twin,
    half_sum,
    slices,
    twin_sums,
    slots,
    *sems,
):
    at = Place()
    held, feats = tokens_ref.shape
    piece = out_tokens.shape[1]
    capacity = out_rows_tokens.shape[1]
    depth = weight_ref.shape[0]
    sems = list(sems)

    def some(count):
        taken, sems[:count] = sems[:count], []
        return taken

    def block(ref):
        return lambda index: ref.at[index]

    def dealt_slot(ref):
        return lambda row: ref.at[pl.ds(row * piece, piece), :]

    last_tokens = HopGather(at, "row", dealt_slot(dealt_ref), some(4))
    last_cots = HopGather(at, "row", dealt_slot(cot_dealt_ref), some(4))
    rows_tokens = Swap(at, "row", block(out_rows_tokens), block(in_rows_tokens), some(2))
    rows_cots = Swap(at, "row", block(out_rows_cots), block(in_rows_cots), some(2))
    swap_tokens = Swap(at, "col", block(out_tokens), block(in_tokens), some(2))
    swap_cots = Swap(at, "col", block(out_cots), block(in_cots), some(2))
    weights = HopGather(
        at, "col", lambda c: weight_all_ref.at[pl.ds(c * depth, depth), :], some(2)
    )
    swap_vector = Swap(at, "col", lambda c: vector_ref, block(vector_all_ref), some(2))

    branch_rows = RowSum(at, normed_part_ref, twin_sums, slots, some(4))
    swap_out = Swap(at, "col", block(out_part), block(out_parts), some(2))
    swap_up = Swap(at, "col", block(up_part), block(up_parts), some(2))
    swap_qkv = Swap(at, "col", block(qkv_part), block(qkv_parts), some(2))
    swap_bias = Swap(at, "col", lambda c: bias_part, block(biases), some(2))
    swap_chunk = Swap(at, "col", block(chunks), block(matrix_ref), some(2))
    twin_send, twin_recv, sum_send, sum_recv, all_send, all_recv, pass_send, pass_recv = some(8)
    count = at.chips * 2
    mine = at.chip * 2 + at.col % 2
    first_col = at.col - at.col % 2

    def member(step):
        other = lax.rem(mine + step, count)
        return other, ((other // 2) * 2 + at.core, first_col + other % 2)

    peers = [member(step)[1] for step in range(1, count)]

    def pick(in_ref, out_ref):
        pack_rows((send_back_ref, piece), flat(in_ref, capacity), [out_ref], feats)

    both = jnp.concatenate([tokens_ref[...], cotangent_ref[...]], axis=1)
    pack_rows((take_back_ref, capacity), both, [out_rows_tokens, out_rows_cots], feats)
    meet(every_row(at) + col_peers(at) + peers)
    rows_tokens.start()
    swap_vector.start()
    rows_cots.start()
    weight_all_ref[pl.ds(at.col * depth, depth), :] = weight_ref[...]
    vector_all_ref[at.col] = vector_ref[...]
    in_rows_tokens[at.row] = out_rows_tokens[at.row]
    in_rows_cots[at.row] = out_rows_cots[at.row]

    rows_tokens.arrived()
    pick(in_rows_tokens, out_tokens)
    swap_tokens.start()
    in_tokens[at.col] = out_tokens[at.col]
    rows_cots.arrived()
    pick(in_rows_cots, out_cots)
    swap_cots.start()
    in_cots[at.col] = out_cots[at.col]

    swap_vector.arrived()
    swap_tokens.arrived()
    weights.start(weight_ref)
    width = at.cols * feats
    parts = [in_tokens[f].astype(f32) for f in range(at.cols)]
    mean = sum(jnp.sum(part, axis=1, keepdims=True) for part in parts) / width
    parts = [part - mean for part in parts]
    variance = sum(jnp.sum(part * part, axis=1, keepdims=True) for part in parts) / width
    inverse_std = lax.rsqrt(variance + norm_floor)
    inverse_std_ref[...] = inverse_std
    own = pl.ds(at.row * piece, piece)
    for f in range(at.cols):
        lanes = slice(f * feats, (f + 1) * feats)
        normalized = parts[f] * inverse_std
        normalized_ref[:, lanes] = normalized
        vectors = vector_all_ref[f]
        dealt_ref[own, lanes] = (normalized * vectors[0:1, :] + vectors[1:2, :]).astype(bf16)
    last_tokens.start(dealt_ref.at[own, :])
    token_steps, weight_steps = iter(last_tokens.steps()), iter(weights.steps())
    cot_steps = iter(last_cots.steps())
    swap_cots.arrived()
    for f in range(at.cols):
        cot_dealt_ref[own, f * feats : (f + 1) * feats] = in_cots[f]
    next(weight_steps)()
    next(token_steps)()
    next(weight_steps)()
    next(token_steps)()
    last_cots.start(cot_dealt_ref.at[own, :])
    next(weight_steps)()
    next(token_steps)()
    next(weight_steps)()
    next(token_steps)()
    next(cot_steps)()
    last_tokens.finish()

    in_width = bias_ref.shape[1]
    tokens = dealt_ref.shape[0]
    rows_all = tokens // PIECE
    in_weight, out_weight = weight_all_ref[:, :in_width], weight_all_ref[:, in_width:]
    inner = math.sqrt(2.0 / math.pi)
    firsts = range(0, tokens, BLOCK)
    for first in firsts:
        if first == 4 * BLOCK:
            next(cot_steps)()
        rows = pl.ds(first, BLOCK)
        pre = dot_nn(dealt_ref[rows, :], in_weight) + bias_ref[...]
        pair = turned(pre[:, : 2 * HEAD], turning(table_ref, rows), False)
        for part in range(BLOCK // PIECE):
            these = slice(part * PIECE, (part + 1) * PIECE)
            spaced = pl.ds(first // PIECE + part, PIECE, stride=rows_all)
            pairs[spaced, :] = pair[these, :]
            values[spaced, :] = pre[these, 2 * HEAD : 4 * HEAD]
        up = pre[:, 4 * HEAD :]
        square = up * up
        bent = jnp.tanh(inner * (up + 0.044715 * square * up))
        branch_ref[rows, 2 * HEAD :] = (0.5 * up * (1.0 + bent)).astype(bf16)
        slope_ref[rows, :] = 0.5 * (1.0 + bent) + 0.5 * up * (1.0 - bent * bent) * (
            inner * (1.0 + 3.0 * 0.044715 * square)
        )
    for first in firsts:
        rows = pl.ds(first, BLOCK)
        pair = pairs[rows, :].astype(bf16)
        q_ref[rows, :] = (pair[:, :HEAD] * HEAD**-0.5).astype(bf16)
        k_ref[rows, :] = pair[:, HEAD:]
        v_ref[rows, :] = values[rows, :HEAD].astype(bf16)
    next(cot_steps)()
    for first in firsts:
        if first == 6 * BLOCK:
            next(cot_steps)()
        rows, keys = pl.ds(first, BLOCK), first + BLOCK
        scores = dot_nt(q_ref[rows, :], k_ref[:keys, :])
        scores = jnp.where(allowed_keys(start_ref, first, keys), scores, masked_score)
        top = jnp.max(scores, axis=1, keepdims=True)
        raw = jnp.exp(scores - top)
        total = jnp.sum(raw, axis=1, keepdims=True)
        attended = dot_nn(raw.astype(bf16), v_ref[:keys, :]) / total
        attended_ref[rows, :] = attended.astype(bf16)
        values[rows, :] = jnp.concatenate([attended, jnp.zeros_like(attended)], axis=1)
        total_ref[rows, :] = top + jnp.log(total)
    for first in firsts:
        rows = pl.ds(first, BLOCK)
        for part in range(BLOCK // PIECE):
            at_piece = first // PIECE + part
            branch_ref[at_piece * PIECE : (at_piece + 1) * PIECE, : 2 * HEAD] = values[
                pl.ds(at_piece, PIECE, stride=rows_all), :
            ].astype(bf16)
        partial = dot_nt(branch_ref[rows, :], out_weight).astype(bf16)
        for part in range(BLOCK // PIECE):
            at_piece = first // PIECE + part
            normed_part_ref[at_piece // 2, at_piece % 2] = partial[
                part * PIECE : (part + 1) * PIECE, :
            ]
    branch_rows.start()
    last_cots.finish()
    for first in range(0, cot_dealt_ref.shape[1], BLOCK):
        part = dot_tn(cot_dealt_ref[:, first : first + BLOCK], branch_ref[...]).astype(bf16)
        for index in range(BLOCK // feats):
            out_part[first // feats + index] = part[index * feats : (index + 1) * feats, :]
    swap_out.start()
    out_parts[at.col] = out_part[at.col]

    half = up_part.shape[2]

    def weight_part(ref, lanes):
        for first in range(0, dealt_ref.shape[1], BLOCK):
            part = dot_tn(dealt_ref[:, first : first + BLOCK], pre_ref[:, lanes])
            for index in range(BLOCK // feats):
                ref[first // feats + index] = part[
                    index * feats : (index + 1) * feats, :
                ].astype(bf16)

    def direction(index, grad):
        lanes = slice(index * BLK, (index + 1) * BLK)
        state = momentum * momentum_ref[:, lanes] + grad
        chunks[index] = grad + momentum * state

    for first in firsts:
        rows = pl.ds(first, BLOCK)
        branch_grad = dot_nn(cot_dealt_ref[rows, :], out_weight)
        for part in range(BLOCK // PIECE):
            these = slice(part * PIECE, (part + 1) * PIECE)
            spaced = pl.ds(first // PIECE + part, PIECE, stride=rows_all)
            values[spaced, :] = branch_grad[these, : 2 * HEAD]
        pre_ref[rows, 4 * HEAD :] = (branch_grad[:, 2 * HEAD :] * slope_ref[rows, :]).astype(bf16)
    weight_part(up_part, slice(half, 2 * half))
    swap_up.start()
    up_parts[at.col] = up_part[at.col]
    dk_ref[...] = jnp.zeros_like(dk_ref)
    dv_ref[...] = jnp.zeros_like(dv_ref)
    branch_rows.middle()
    for first in reversed(firsts):
        rows, keys = pl.ds(first, BLOCK), first + BLOCK
        query, grad = q_ref[rows, :], values[rows, :HEAD].astype(bf16)
        key, value = k_ref[:keys, :], v_ref[:keys, :]
        scores = dot_nt(query, key)
        allowed = allowed_keys(start_ref, first, keys)
        prob = jnp.where(allowed, jnp.exp(scores - total_ref[rows, :]), 0.0)
        delta = jnp.sum(
            grad.astype(f32) * attended_ref[rows, :].astype(f32), axis=1, keepdims=True
        )
        score_grad = (prob * (dot_nt(grad, value) - delta)).astype(bf16)
        dk_ref[:keys, :] += dot_tn(score_grad, query)
        dv_ref[:keys, :] += dot_tn(prob.astype(bf16), grad)
        pairs[rows, :] = jnp.concatenate(
            [dot_nn(score_grad, key) * HEAD**-0.5, dk_ref[rows, :]], axis=1
        )
        dv = dv_ref[rows, :]
        values[rows, :] = jnp.concatenate([dv, jnp.zeros_like(dv)], axis=1)
    for first in firsts:
        rows = pl.ds(first, BLOCK)
        pair, value = [
            jnp.concatenate(
                [
                    ref[pl.ds(first // PIECE + part, PIECE, stride=rows_all), :]
                    for part in range(BLOCK // PIECE)
                ],
                axis=0,
            )
            for ref in (pairs, values)
        ]
        pre_ref[rows, : 2 * HEAD] = turned(pair, turning(table_ref, rows), True).astype(bf16)
        pre_ref[rows, 2 * HEAD : 4 * HEAD] = value.astype(bf16)
    weight_part(qkv_part, slice(0, half))
    swap_qkv.start()
    qkv_parts[at.col] = qkv_part[at.col]
    bias = jnp.sum(pre_ref[...].astype(f32), axis=0, keepdims=True)
    bias_part[...] = jnp.broadcast_to(bias, bias_part.shape)
    swap_bias.start()
    biases[at.col] = bias_part[...]
    branch_rows.released()
    for first in firsts:
        rows = pl.ds(first, BLOCK)
        partial = dot_nt(pre_ref[rows, :], in_weight).astype(bf16)
        for part in range(BLOCK // PIECE):
            at_piece = first // PIECE + part
            normed_part_ref[at_piece // 2, at_piece % 2] = partial[
                part * PIECE : (part + 1) * PIECE, :
            ]

    swap_out.arrived()
    total = sum(out_parts[c].astype(f32) for c in range(at.cols))
    filled = jnp.zeros((feats, half - 2 * HEAD), f32)
    out_grad = jnp.concatenate([total[:, : 2 * HEAD], filled, total[:, 2 * HEAD :]], axis=1)
    out_grad_ref[...] = out_grad
    swap_up.arrived()
    up_grad = sum(up_parts[c].astype(f32) for c in range(at.cols))
    in_grad_ref[:, half:] = up_grad
    late = half // BLK
    for index in range(late, at.cols):
        first = (index - late) * BLK
        if first < half:
            direction(index, up_grad[:, first : first + BLK])
        else:
            direction(index, out_grad[:, first - half : first - half + BLK])
    swap_chunk.start(lambda to: to >= late)
    swap_qkv.arrived()
    qkv_grad = sum(qkv_parts[c].astype(f32) for c in range(at.cols))
    in_grad_ref[:, :half] = qkv_grad
    for index in range(late):
        direction(index, qkv_grad[:, index * BLK : (index + 1) * BLK])
    swap_chunk.start(lambda to: to < late)
    matrix_ref[at.col] = chunks[at.col]
    swap_bias.arrived()
    bias_grad_ref[...] = sum(biases[c] for c in range(at.cols))
    swap_chunk.arrived()

    strips = matrix_ref.shape[0]
    matrix = split(matrix_ref[...].reshape(strips * BLK, BLK))
    index = 0
    for i in range(strips):
        left = [m[i * BLK : (i + 1) * BLK, :] for m in matrix]
        right = [m[i * BLK :, :] for m in matrix]
        product = three(dot_nt, left, right)
        for j in range(strips - i):
            products[index] = product[:, j * BLK : (j + 1) * BLK]
            index += 1
    blocks = index // 2
    to_twin = remote(
        products.at[pl.ds((1 - at.core) * blocks, blocks)],
        from_twin,
        twin_send.at[0],
        twin_recv.at[0],
        at.twin,
    )
    to_twin.start()
    to_twin.wait_recv()
    for b in range(blocks):
        half_sum[b * BLK : (b + 1) * BLK, :] = products[at.core * blocks + b] + from_twin[b]

    size = blocks * BLK // count

    def piece_of(owner):
        return half_sum.at[pl.ds(owner * size, size), :]

    def give(step):
        owner, device = member(step)
        return remote(
            piece_of(owner), slices.at[mine], sum_send.at[step], sum_recv.at[step], device
        )

    for step in range(1, count):
        give(step).start()
    slices[mine] = half_sum[pl.ds(mine * size, size), :]
    for step in range(1, count):
        came, device = member(count - step)
        remote(
            slices.at[came], slices.at[came], sum_send.at[step], sum_recv.at[step], device
        ).wait_recv()
    total = slices[0]
    for index in range(1, count):
        total = total + slices[index]
    half_rows = blocks * BLK

    def home(owner):
        return gram_ref.at[pl.ds(at.core * half_rows + owner * size, size), :]

    gram_ref[pl.ds(at.core * half_rows + mine * size, size), :] = total

    def spread(step):
        return remote(
            home(mine), home(mine), all_send.at[step], all_recv.at[step], member(step)[1]
        )

    def passing(step):
        came = member(count - step)[0] if step else mine
        return remote(
            home(came), home(came), pass_send.at[step], pass_recv.at[step], at.twin
        )

    for step in range(1, count):
        spread(step).start()
    passing(0).start()
    for step in range(1, count):
        came, device = member(count - step)
        remote(
            home(came), home(came), all_send.at[step], all_recv.at[step], device
        ).wait_recv()
        passing(step).start()
    for step in range(count):
        other = lax.rem(at.chip * 2 + at.col % 2 + count - step, count)
        slot = gram_ref.at[pl.ds((1 - at.core) * half_rows + other * size, size), :]
        remote(slot, slot, pass_send.at[step], pass_recv.at[step], at.twin).wait_recv()
        passing(step).wait_send()
    to_twin.wait_send()
    for step in range(1, count):
        give(step).wait_send()
        spread(step).wait_send()
    branch_sum_ref[...] = branch_rows.finish().astype(bf16)
    branch_rows.sent()
    for moved in (last_tokens, last_cots, weights, rows_tokens, rows_cots):
        moved.sent()
    for moved in (swap_tokens, swap_cots, swap_vector):
        moved.sent()
    for moved in (swap_out, swap_up, swap_qkv, swap_bias, swap_chunk):
        moved.sent()


WIDE = 256


def poly_kernel(
    gram_ref,
    matrix_ref,
    normed_part_ref,
    branch_ref,
    normalized_ref,
    inverse_std_ref,
    vector_ref,
    tokens_ref,
    cotangent_ref,
    pick_ref,
    pack_ref,
    update_ref,
    output_ref,
    input_grad_ref,
    vector_sum_ref,
    own_update,
    normed_ref,
    out_branch,
    in_branch,
    out_rows_branch,
    in_rows_branch,
    out_token,
    in_token,
    out_rows,
    in_rows,
    twin_sums,
    slots,
    *buffers,
):
    at = Place()
    sems, buffers = buffers[8:], buffers[:8]

    def block(ref):
        return lambda index: ref.at[index]

    swap_token = Swap(at, "col", block(out_token), block(in_token), sems[0:2])
    rows_token = Swap(at, "row", block(out_rows), block(in_rows), sems[2:4])
    feats = out_token.shape[2]
    swap_update = Swap(
        at,
        "col",
        lambda c: own_update.at[pl.ds(c * feats, feats), :],
        block(update_ref),
        sems[4:6],
    )
    swap_branch = Swap(at, "col", block(out_branch), block(in_branch), sems[6:8])
    rows_branch = Swap(at, "row", block(out_rows_branch), block(in_rows_branch), sems[8:10])
    normed_rows = RowSum(at, normed_part_ref, twin_sums, slots, sems[10:14])
    piece, capacity = normed_ref.shape[0], out_rows_branch.shape[1]
    lanes = [slice(f * feats, (f + 1) * feats) for f in range(at.cols)]
    for f in range(at.cols):
        out_branch[f] = branch_ref[:, lanes[f]]
    meet(every_row(at) + col_peers(at))
    normed_rows.start()
    swap_branch.start()
    in_branch[at.col] = out_branch[at.col]

    def branch_back():
        swap_branch.arrived()
        pack_rows((pick_ref, capacity), flat(in_branch, piece), [out_rows_branch], feats)
        rows_branch.start()
        in_rows_branch[at.row] = out_rows_branch[at.row]

    def home(rows_ref, base_ref, shift, out_ref):
        values = flat(rows_ref, capacity)
        for first in range(0, out_ref.shape[0], BLOCK):
            rows = pl.ds(first, BLOCK)
            found = moved_rows(pack_ref[...], first, BLOCK, values)
            out_ref[rows, :] = found + base_ref[rows, :].astype(f32) + shift

    def branch_home():
        rows_branch.arrived()
        home(in_rows_branch, tokens_ref, vector_ref[at.col][2:3, :], output_ref)

    def extra(vectors):
        parts = [part.astype(f32) for vector in vectors for part in split(vector)]
        empty = jnp.zeros((EXTRA - len(parts), feats), f32)
        return jnp.concatenate([*parts, empty], axis=0).astype(bf16)

    def token_grads():
        normed_ref[...] = normed_rows.finish()
        width = at.cols * feats
        scaled = [normed_ref[:, lanes[f]] * vector_ref[f][0:1, :] for f in range(at.cols)]
        mean_first = sum(jnp.sum(part, axis=1, keepdims=True) for part in scaled) / width
        mean_second = (
            sum(
                jnp.sum(part * normalized_ref[:, lanes[f]], axis=1, keepdims=True)
                for f, part in enumerate(scaled)
            )
            / width
        )
        for f in range(at.cols):
            normalized, grad = normalized_ref[:, lanes[f]], normed_ref[:, lanes[f]]
            token_grad = inverse_std_ref[...] * (scaled[f] - mean_first - normalized * mean_second)
            out_token[f, :piece, :] = token_grad.astype(bf16)
            gain_grad = jnp.sum(grad * normalized, axis=0, keepdims=True)
            shift_grad = jnp.sum(grad, axis=0, keepdims=True)
            out_token[f, piece:, :] = extra([gain_grad, shift_grad])
        swap_token.start()
        in_token[at.col] = out_token[at.col]

    def token_back():
        cot_sum = jnp.sum(cotangent_ref[...].astype(f32), axis=0, keepdims=True)
        swap_token.arrived()
        pack_rows((pick_ref, capacity), flat(in_token, piece), [out_rows], feats)
        sums = sum(in_token[c, piece:, :].astype(f32) for c in range(at.cols))
        sums = extra([sums[0:1, :] + sums[1:2, :], sums[2:3, :] + sums[3:4, :], cot_sum])
        for row in range(at.rows):
            out_rows[row, capacity:, :] = sums
        rows_token.start()
        in_rows[at.row] = out_rows[at.row]

    first, second, third, thin = [buffers[2 * i : 2 * i + 2] for i in range(4)]
    strips = matrix_ref.shape[0]
    size = strips * BLK
    counts = range(size // WIDE)
    eye = lax.broadcasted_iota(jnp.int32, (BLK, BLK), 0) == lax.broadcasted_iota(
        jnp.int32, (BLK, BLK), 1
    )

    def put(pair, rows, lanes, value):
        high_part, low_part = split(value)
        pair[0][rows, lanes] = high_part
        pair[1][rows, lanes] = low_part

    def get(pair, rows, lanes):
        return pair[0][rows, lanes], pair[1][rows, lanes]

    places, index = [], 0
    for i in range(strips):
        for j in range(i, strips):
            places.append((i, j, index))
            index += 1
    trace = sum(
        jnp.sum(jnp.where(eye, gram_ref[spot * BLK : (spot + 1) * BLK, :], 0.0))
        for i, j, spot in places
        if i == j
    )
    shrink = 1.0 / (jnp.sqrt(jnp.full((1, 1), trace, f32)) + ortho_floor)
    for i, j, spot in places:
        block = gram_ref[spot * BLK : (spot + 1) * BLK, :] * (shrink * shrink)
        here, there = slice(i * BLK, (i + 1) * BLK), slice(j * BLK, (j + 1) * BLK)
        put(first, here, there, block)
        if j > i:
            put(first, there, here, block.T)
    everything = slice(0, size)
    for i in range(strips):
        put(thin, slice(i * BLK, (i + 1) * BLK), everything, matrix_ref[i] * shrink)

    def product(left, right, out, finish=None):
        for i in counts:
            rows, rest = slice(i * WIDE, (i + 1) * WIDE), slice(i * WIDE, size)
            value = three(dot_nn, get(left, rows, everything), get(right, everything, rest))
            if finish is not None:
                value = finish(value, rows, rest)
            put(out, rows, rest, value)
            for j in range(i + 1, size // WIDE):
                part = value[:, (j - i) * WIDE : (j - i + 1) * WIDE]
                put(out, slice(j * WIDE, (j + 1) * WIDE), rows, part.T)

    def thin_product(left):
        right = get(thin, everything, everything)
        return [
            three(dot_nn, get(left, slice(i * WIDE, (i + 1) * WIDE), everything), right)
            for i in counts
        ]

    def sweep(gram, poly, square, between=lambda: None):
        def finish(value, rows, rest):
            high_part, low_part = get(gram, rows, rest)
            value = poly_cubic * value + poly_square * (
                high_part.astype(f32) + low_part.astype(f32)
            )
            at_row = lax.broadcasted_iota(jnp.int32, value.shape, 0)
            at_lane = lax.broadcasted_iota(jnp.int32, value.shape, 1)
            return value + jnp.where(at_row == at_lane, poly_linear, 0.0)

        product(gram, gram, poly, finish)
        between()
        for i, value in zip(counts, thin_product(poly)):
            put(thin, slice(i * WIDE, (i + 1) * WIDE), everything, value)
        product(poly, poly, square)
        product(gram, square, poly)

    def two(step, carry):
        def early():
            @pl.when(step == 0)
            def _():
                normed_rows.middle()
                branch_back()

            @pl.when(step == 1)
            def _():
                token_grads()

        def late():
            @pl.when(step == 1)
            def _():
                branch_home()

        sweep(first, second, third, early)

        @pl.when(step == 1)
        def _():
            token_back()

        sweep(second, first, third, late)
        return carry

    lax.fori_loop(0, 2, two, 0)
    once = thin_product(first)
    old = []
    for i in counts:
        rows = slice(i * WIDE, (i + 1) * WIDE)
        high_part, low_part = get(thin, rows, everything)
        old.append(high_part.astype(f32) + low_part.astype(f32))
    for i, value in zip(counts, once):
        put(thin, slice(i * WIDE, (i + 1) * WIDE), everything, value)
    for i, value in zip(counts, thin_product(first)):
        result = poly_linear * old[i] + poly_square * once[i] + poly_cubic * value
        own_update[i * WIDE : (i + 1) * WIDE, :] = result.astype(bf16)
    swap_update.start()
    update_ref[at.col] = own_update[pl.ds(at.col * feats, feats), :]

    rows_token.arrived()
    home(in_rows, cotangent_ref, 0.0, input_grad_ref)
    vector_sum_ref[...] = sum(
        in_rows[row, capacity:, :].astype(f32) for row in range(at.rows)
    )
    swap_update.arrived()
    normed_rows.released()
    for moved in (swap_token, rows_token, swap_update, swap_branch, rows_branch, normed_rows):
        moved.sent()


def orthogonalize(
    gram,
    matrix,
    normed_part,
    branch_sum,
    normalized,
    inverse_std,
    vectors,
    tokens,
    cotangent,
    pick,
    pack,
    rows,
):
    cols, feats, width = matrix.shape
    size = cols * BLK
    piece, full = branch_sum.shape
    held = cotangent.shape[0]
    chips = rows // 2
    capacity = pack.shape[1] // rows
    shape = jax.ShapeDtypeStruct
    square, narrow = pltpu.VMEM((size, size), bf16), pltpu.VMEM((size, width), bf16)
    return remote_call(
        poly_kernel,
        3,
        (
            shape((cols, feats, width), bf16),
            shape((held, feats), f32),
            shape((held, feats), f32),
            shape((EXTRA, feats), f32),
        ),
        [VMEM_SPEC] * 11,
        [
            narrow,
            pltpu.VMEM((piece, full), f32),
            *([pltpu.VMEM((cols, piece, feats), bf16)] * 2),
            *([pltpu.VMEM((rows, capacity, feats), bf16)] * 2),
            *([pltpu.VMEM((cols, piece + EXTRA, feats), bf16)] * 2),
            *([pltpu.VMEM((rows, capacity + EXTRA, feats), bf16)] * 2),
            *sum_scratch(piece, full, chips)[:2],
            *([square] * 6),
            *([narrow] * 2),
            *swap_sems(cols),
            *swap_sems(rows),
            *(swap_sems(cols) * 2),
            *swap_sems(rows),
            *sum_scratch(piece, full, chips)[2:],
        ],
        60 * 10**9,
        "orthogonalize",
    )(
        *(gram, matrix, normed_part, branch_sum, normalized),
        *(inverse_std, vectors, tokens, cotangent, pick, pack),
    )


def layer(
    tokens,
    cotangent,
    take_back,
    send_back,
    weight,
    vectors,
    bias,
    table,
    starts,
    old_momentum,
    rows,
    cols,
):
    held, feats = tokens.shape
    group = held * rows // cols
    piece, width, chips = group // rows, feats * cols, rows // 2
    in_width = bias.shape[1]
    up = in_width - 4 * HEAD
    branch = up + 2 * HEAD
    capacity = send_back.shape[1] // rows
    blocks = cols * (cols + 1) // 2
    count = chips * 2
    half_rows = blocks * BLK // 2
    shape, vmem = jax.ShapeDtypeStruct, pltpu.VMEM
    dma = pltpu.SemaphoreType.DMA
    return remote_call(
        layer_kernel,
        0,
        (
            shape((cols,) + vectors.shape, f32),
            shape((piece, width), f32),
            shape((piece, 1), f32),
            shape((feats, in_width), f32),
            shape((feats, in_width), f32),
            shape((8, in_width), f32),
            shape((cols, feats, BLK), f32),
            shape((blocks * BLK, BLK), f32),
            shape((chips, 2, piece, width), bf16),
            shape((piece, width), bf16),
        ),
        [VMEM_SPEC] * 10,
        [
            *([vmem((group, width), bf16)] * 2),
            vmem((weight.shape[0] * cols, weight.shape[1]), bf16),
            *([vmem((group, HEAD), bf16)] * 3),
            vmem((group, up), f32),
            vmem((group, branch), bf16),
            vmem((group, HEAD), bf16),
            vmem((group, 1), f32),
            vmem((cols, feats, branch), bf16),
            *([vmem((group, 2 * HEAD), f32)] * 2),
            *([vmem((rows, capacity, feats), bf16)] * 4),
            *([vmem((cols, piece, feats), bf16)] * 4),
            vmem((group, in_width), bf16),
            *([vmem((group, HEAD), f32)] * 2),
            vmem((cols, feats, branch), bf16),
            *([vmem((cols, feats, up), bf16)] * 4),
            vmem((8, in_width), f32),
            vmem((cols, 8, in_width), f32),
            vmem((cols, feats, BLK), f32),
            vmem((blocks, BLK, BLK), f32),
            vmem((blocks // 2, BLK, BLK), f32),
            vmem((half_rows, BLK), f32),
            vmem((count, half_rows // count, BLK), f32),
            *sum_scratch(piece, width, chips)[:2],
            *(gather_sems() * 2),
            *(swap_sems(rows) * 2),
            *(swap_sems(cols) * 2),
            *hop_sems(),
            *swap_sems(cols),
            *sum_scratch(piece, width, chips)[2:],
            *(swap_sems(cols) * 5),
            dma((1,)),
            dma((1,)),
            *([dma((count,))] * 6),
        ],
        150 * 10**9,
        "layer",
    )(
        *(tokens, cotangent, take_back, send_back, weight, vectors),
        *(bias, table, starts, old_momentum),
    )


def rotary_table(places):
    half_rot = ROT // 2
    inverse = 1.0 / 10000.0 ** (jnp.arange(half_rot, dtype=f32) * (2.0 / ROT))
    angles = inverse[:, None] * places.astype(f32)[None, :]
    table = jnp.concatenate([jnp.cos(angles), jnp.sin(angles)], axis=0)
    return jnp.concatenate(high_low(table), axis=0)


CAPACITY = 96


def exchange_plan(seq_starts, seq_ends, shift, deal_order, row, rows, cols):
    total = deal_order.shape[0]
    held, group = total // rows, total // cols
    piece = group // rows

    def passed(x, to):
        return (x + rows - 1 - to) // rows

    def clipped(x, holder):
        return jnp.clip(x, holder * held, holder * held + held)

    def rank(token, holder, to):
        token, holder, to = token[:, None], holder[:, None], to[:, None]
        low = clipped(seq_starts[None], holder)
        high = jnp.maximum(clipped(jnp.minimum(seq_ends[None], token), holder), low)
        return jnp.sum(passed(high + shift, to) - passed(low + shift, to), axis=1)

    def listed(holder, to):
        slot = jnp.arange(CAPACITY, dtype=jnp.int32)[None, :, None]
        holder, to = holder[:, None], to[:, None]
        first = passed(clipped(seq_starts[None], holder) + shift, to)
        count = passed(clipped(seq_ends[None], holder) + shift, to) - first
        base = jnp.cumsum(count, axis=1) - count
        inside = slot - base[:, None, :]
        found = (inside >= 0) & (inside < count[:, None, :])
        dealt = rows * (first[:, None, :] + inside) + to[:, :, None]
        token = dealt - shift[None, None, :]
        used = jnp.any(found, axis=2)
        return [jnp.sum(jnp.where(found, x, 0), axis=2) for x in (dealt, token)] + [used]

    every = jnp.arange(rows, dtype=jnp.int32)
    mine = jnp.full((rows,), row, jnp.int32)
    dealt, token, used = listed(jnp.concatenate([mine, every]), jnp.concatenate([every, mine]))
    pack = jnp.where(used[:rows], token[:rows] - row * held, -1)
    back = dealt[rows:]
    send_back = (back // group) * piece + (back % group) // rows
    send_back = jnp.where(used[rows:], send_back, -1)
    own = row * held + jnp.arange(held, dtype=jnp.int32)
    holds = (seq_starts[None] <= own[:, None]) & (own[:, None] < seq_ends[None])
    own_to = (own + jnp.sum(jnp.where(holds, shift[None], 0), axis=1)) % rows
    wanted = deal_order.reshape(cols * piece, rows)
    wanted = jnp.sum(jnp.where(every[None] == row, wanted, 0), axis=1)
    holder = wanted // held
    ranks = rank(
        jnp.concatenate([own, wanted]),
        jnp.concatenate([jnp.full_like(own, row), holder]),
        jnp.concatenate([own_to, jnp.full_like(wanted, row)]),
    )
    take_back = own_to * CAPACITY + ranks[:held]
    pick = holder * CAPACITY + ranks[held:]
    return [x.reshape(1, -1) for x in (pack, pick, send_back, take_back)]


def adam_step(value, gradient, first_state, second_state):
    first_new = beta_first * first_state + (1.0 - beta_first) * gradient
    second_new = beta_second * second_state + (1.0 - beta_second) * gradient * gradient
    corrected = first_new / (1.0 - beta_first**STEP)
    root_term = jnp.sqrt(second_new / (1.0 - beta_second**STEP)) + adam_floor
    return (first_new, second_new, value - rate_vector * corrected / root_term)


def high_low(x):
    high_part = x.astype(bf16)
    return high_part, (x - high_part.astype(f32)).astype(bf16)


def per_device(
    tokens,
    cotangent,
    lengths,
    deal_order,
    qkv_weight,
    up_weight,
    proj_weight,
    down_weight,
    norm_vectors,
    qkv_bias,
    mlp_bias,
    qkv_momentum,
    up_momentum,
    proj_momentum,
    down_momentum,
    norm_moment,
    norm_square,
    qkv_bias_moment,
    qkv_bias_square,
    mlp_bias_moment,
    mlp_bias_square,
):
    cols, rows = lax.axis_size("col"), lax.axis_size("row")
    col, row = lax.axis_index("col"), lax.axis_index("row")
    total_tokens = deal_order.shape[0]
    group = total_tokens // cols
    piece = group // rows
    held = total_tokens // rows
    feats = D // cols
    qkv_width, up_width = qkv_weight.shape[1], up_weight.shape[1]
    proj_width = proj_weight.shape[0]

    seq_ends = jnp.cumsum(lengths)
    seq_starts = seq_ends - lengths
    anchor = lax.dynamic_slice_in_dim(deal_order, col * group, group)
    before = seq_ends[None, :] <= anchor[:, None]
    places = anchor - jnp.sum(jnp.where(before, lengths[None, :], 0), axis=1)
    starts = (jnp.arange(group, dtype=jnp.int32) - places)[:, None]
    table = rotary_table(places.reshape(piece, rows).T.reshape(group))
    at = jnp.arange(total_tokens, dtype=jnp.int32)
    dealt_starts = jnp.sum(
        jnp.where(deal_order[None, :] == seq_starts[:, None], at[None, :], 0), axis=1
    )
    shift = dealt_starts - seq_starts
    pack, pick, send_back, take_back = exchange_plan(
        seq_starts, seq_ends, shift, deal_order, row, rows, cols
    )

    def lanes(x, width):
        return jnp.pad(x, ((0, 0), (0, width - x.shape[1])))

    in_pad = 2 * up_width
    tile = jnp.concatenate(
        [
            lanes(qkv_weight.astype(bf16), up_width),
            up_weight.astype(bf16),
            lanes(proj_weight.astype(bf16).T, 128),
            down_weight.astype(bf16).T,
        ],
        axis=1,
    )
    bias = jnp.concatenate(
        [jnp.pad(qkv_bias, (0, up_width - qkv_width)), mlp_bias], axis=0
    ).reshape(1, in_pad)
    old_momentum = jnp.concatenate(
        [
            lanes(qkv_momentum, up_width),
            up_momentum,
            lanes(proj_momentum.T, up_width),
            down_momentum.T,
        ],
        axis=1,
    )
    (
        vector_all,
        normalized,
        inverse_std,
        in_grad,
        out_grad,
        bias_rows,
        matrix,
        gram,
        normed_part,
        branch_sum,
    ) = layer(
        tokens,
        cotangent,
        take_back,
        send_back,
        tile,
        jnp.pad(norm_vectors, ((0, 5), (0, 0))),
        bias,
        table,
        starts,
        old_momentum,
        rows,
        cols,
    )
    returned, output, input_grad, vector_sum = orthogonalize(
        gram,
        matrix,
        normed_part,
        branch_sum,
        normalized,
        inverse_std,
        vector_all,
        tokens,
        cotangent,
        pick,
        pack,
        rows,
    )
    norm_grads = jnp.stack(
        [
            vector_sum[0] + vector_sum[1],
            vector_sum[2] + vector_sum[3],
            vector_sum[4] + vector_sum[5],
        ],
        axis=0,
    )
    in_bias_grad = bias_rows[0]
    gradients = (
        in_grad[:, :qkv_width],
        in_grad[:, up_width:],
        out_grad[:, :proj_width].T,
        out_grad[:, up_width:].T,
    )
    old_states = (qkv_momentum, up_momentum, proj_momentum, down_momentum)
    weights = (qkv_weight, up_weight, proj_weight, down_weight)
    widths = (3 * D, FF, D, FF)
    sizes = (qkv_width, up_width, proj_width, up_width)
    states = [momentum * old + g for old, g in zip(old_states, gradients)]
    new_weights = []
    for index in range(4):
        update = jnp.concatenate([returned[2 * index], returned[2 * index + 1]], axis=1)
        update = update[:, : sizes[index]].astype(f32)
        update = update.T if index >= 2 else update
        new_weights.append(
            weights[index] * (1.0 - rate_matrix * decay_matrix)
            - rate_matrix * 0.2 * math.sqrt(widths[index]) * update
        )

    norm_first, norm_second, norm_new = adam_step(
        norm_vectors, norm_grads, norm_moment, norm_square
    )
    qkv_first, qkv_second, qkv_bias_new = adam_step(
        qkv_bias, in_bias_grad[:qkv_width], qkv_bias_moment, qkv_bias_square
    )
    mlp_first, mlp_second, mlp_bias_new = adam_step(
        mlp_bias, in_bias_grad[up_width:], mlp_bias_moment, mlp_bias_square
    )
    return (
        output,
        input_grad,
        *gradients,
        *states,
        *new_weights,
        norm_first,
        norm_second,
        norm_new,
        qkv_first,
        qkv_second,
        qkv_bias_new,
        mlp_first,
        mlp_second,
        mlp_bias_new,
    )


def solution(mesh):
    over_both, over_flip = P("row", "col"), P("col", "row")
    features, hidden = P(None, "col"), P("row")
    return jax.shard_map(
        per_device,
        mesh=mesh,
        in_specs=(
            *(over_both, over_both, P(), P()),
            *(over_flip, over_flip, over_both, over_both),
            *(features, hidden, hidden),
            *(over_flip, over_flip, over_both, over_both),
            *(features, features, hidden, hidden, hidden, hidden),
        ),
        out_specs=(
            *(over_both, over_both),
            *(over_flip, over_flip, over_both, over_both) * 3,
            *(features,) * 3,
            *(hidden,) * 6,
        ),
        check_vma=False,
    )
```

```python
import functools
import math

import jax
import jax.numpy as jnp
from jax import lax
from jax.experimental import pallas as pl
from jax.experimental.pallas import tpu as pltpu
from jax.sharding import PartitionSpec as P

D = 1024
HEAD = 64
ROT = 16
FF = 4096
STEP = 10

poly_linear = 3.4445
poly_square = -4.775
poly_cubic = 2.0315
momentum = 0.95
rate_matrix = 0.15
decay_matrix = 0.1
beta_first = 0.9
beta_second = 0.95
rate_vector = 0.2
adam_floor = 1e-08
norm_floor = 1e-05
ortho_floor = 1e-07
masked_score = -1e30
f32 = jnp.float32
bf16 = jnp.bfloat16
BLOCK = 256
PIECE = 128
EXTRA = 16


def dot_nt(a, b, **kw):
    return lax.dot_general(a, b, (((1,), (1,)), ((), ())), preferred_element_type=f32, **kw)


def dot_tn(a, b, **kw):
    return lax.dot_general(a, b, (((0,), (0,)), ((), ())), preferred_element_type=f32, **kw)


def dot_nn(a, b, **kw):
    return lax.dot_general(a, b, (((1,), (0,)), ((), ())), preferred_element_type=f32, **kw)


def allowed_keys(start_ref, first, keys):
    shape = (BLOCK, keys)
    key_at = lax.broadcasted_iota(jnp.int32, shape, 1)
    query_at = first + lax.broadcasted_iota(jnp.int32, shape, 0)
    return (key_at >= start_ref[pl.ds(first, BLOCK), :]) & (key_at <= query_at)


def turning(table_ref, rows):
    lane = lax.broadcasted_iota(jnp.int32, (32, 2 * HEAD), 1) % HEAD
    entry = lax.broadcasted_iota(jnp.int32, (32, 2 * HEAD), 0) % 16
    half_rot = ROT // 2

    def spread(where, value):
        picks = jnp.where(where, value, 0.0).astype(bf16)
        return dot_tn(table_ref[:, rows], picks)

    cosine = spread((lane < ROT) & (entry == lane % half_rot), 1.0)
    cosine = cosine + jnp.where(lane[:1] < ROT, 0.0, 1.0)
    lower = spread((lane < half_rot) & (entry == lane + half_rot), -1.0)
    upper = spread((lane >= half_rot) & (lane < ROT) & (entry == lane), 1.0)
    return cosine, lower, upper


def turned(values, tables, back):
    cosine, lower, upper = tables
    half_rot = ROT // 2
    moved = (
        pltpu.roll(values, 2 * HEAD - half_rot, 1) * lower + pltpu.roll(values, half_rot, 1) * upper
    )
    return values * cosine - moved if back else values * cosine + moved


VMEM_LIMIT = 63 * 1024 * 1024


def remote_call(kernel, identity, out_shape, in_specs, scratch, flops, name):
    return pl.pallas_call(
        kernel,
        out_shape=out_shape,
        in_specs=in_specs,
        out_specs=(VMEM_SPEC,) * len(out_shape),
        scratch_shapes=scratch,
        compiler_params=pltpu.CompilerParams(
            collective_id=identity, has_side_effects=True, vmem_limit_bytes=VMEM_LIMIT
        ),
        cost_estimate=pl.CostEstimate(flops=flops, bytes_accessed=1 << 24, transcendentals=0),
        name=name,
    )


MESH = pl.DeviceIdType.MESH
VMEM_SPEC = pl.BlockSpec(memory_space=pltpu.VMEM)


def remote(src, dst, send, recv, device):
    return pltpu.make_async_remote_copy(
        src_ref=src, dst_ref=dst, send_sem=send, recv_sem=recv, device_id=device, device_id_type=MESH
    )


class Place:
    def __init__(self):
        self.row, self.col = lax.axis_index("row"), lax.axis_index("col")
        self.rows, self.cols = lax.axis_size("row"), lax.axis_size("col")
        self.chips = self.rows // 2
        self.chip, self.core = self.row // 2, self.row % 2
        self.twin = (self.chip * 2 + 1 - self.core, self.col)
        self.ring = self.chips // 2
        self.y, self.z = self.chip // self.ring, self.chip % self.ring

    def chip_at(self, step):
        return lax.rem(self.chip + step, self.chips)

    def chip_row(self, step):
        return self.chip_at(step) * 2 + self.core

    def col_at(self, step):
        return lax.rem(self.col + step, self.cols)


def meet(devices):
    barrier = pltpu.get_barrier_semaphore()
    for device in devices:
        pl.semaphore_signal(barrier, inc=1, device_id=device, device_id_type=MESH)
    pl.semaphore_wait(barrier, len(devices))


class HopGather:
    OWN, PARTNER, BELOW, ABOVE, BELOW_PARTNER, ABOVE_PARTNER, FAR, FAR_PARTNER = range(8)

    def __init__(self, at, axis, slot, sems):
        self.at, self.axis, self.slot = at, axis, slot
        self.sems = sems
        index, ring = (at.chip, at.chips // 2) if axis == "row" else (at.col, at.cols // 2)
        side, step = index // ring, index % ring

        def place(other, hops):
            return (1 - side if other else side) * ring + lax.rem(step + hops, ring)

        self.places = [
            place(False, 0),
            place(True, 0),
            place(False, ring - 1),
            place(False, 1),
            place(True, ring - 1),
            place(True, 1),
            place(False, 2),
            place(True, 2),
        ]

    def index(self, which):
        return self.places[which] * 2 + self.at.core if self.axis == "row" else self.places[which]

    def device(self, which):
        at = self.at
        return (self.index(which), at.col) if self.axis == "row" else (at.row, self.index(which))

    def block(self, which):
        return self.slot(self.index(which))

    def part(self, which, upper):
        ref = self.block(which)
        half = ref.shape[0] // 2
        return ref.at[pl.ds(0 if upper else half, half), :]

    def hop(self, tag, src, dst, to):
        send, recv = self.sems[0], self.sems[1]
        return remote(src, dst, send.at[tag], recv.at[tag], self.device(to))

    def took(self, tag, ref):
        self.hop(tag, ref, ref, self.PARTNER).wait_recv()

    def passing(self, which, src=None):
        send, recv = self.sems[2], self.sems[3]
        ref = self.block(which)
        return remote(
            ref if src is None else src, ref, send.at[which], recv.at[which], self.at.twin
        )

    def hops(self):
        own, src = self.block(self.OWN), self.src
        partner = self.block(self.PARTNER)
        below, above = self.part(self.BELOW, True), self.part(self.ABOVE, False)
        far_below = self.part(self.BELOW_PARTNER, True)
        far_above = self.part(self.ABOVE_PARTNER, False)
        return {
            "start": [
                (0, src, own, self.PARTNER),
                (1, src, own, self.ABOVE),
                (2, src, own, self.BELOW),
            ],
            "partner": [(3, partner, partner, self.ABOVE), (4, partner, partner, self.BELOW)],
            "below": [(5, below, below, self.ABOVE)],
            "above": [(6, above, above, self.BELOW)],
            "far_below": [(7, far_below, far_below, self.ABOVE)],
            "far_above": [(8, far_above, far_above, self.BELOW)],
        }

    def go(self, stage):
        for hop in self.hops()[stage]:
            self.hop(*hop).start()

    def start(self, src):
        self.src = src
        self.go("start")
        if self.axis == "row":
            self.passing(self.OWN, src).start()

    def landed(self, which):
        if self.axis == "row":
            self.passing(which).start()

    def steps(self):
        def first():
            self.took(1, self.block(self.BELOW))
            self.go("below")
            self.took(2, self.block(self.ABOVE))
            self.go("above")
            self.landed(self.BELOW)
            self.landed(self.ABOVE)

        def second():
            self.took(0, self.block(self.PARTNER))
            self.go("partner")
            self.landed(self.PARTNER)

        def third():
            self.took(3, self.block(self.BELOW_PARTNER))
            self.go("far_below")
            self.took(4, self.block(self.ABOVE_PARTNER))
            self.go("far_above")
            self.landed(self.BELOW_PARTNER)
            self.landed(self.ABOVE_PARTNER)

        def fourth():
            self.took(5, self.part(self.FAR, True))
            self.took(6, self.part(self.FAR, False))
            self.landed(self.FAR)
            self.took(7, self.part(self.FAR_PARTNER, True))
            self.took(8, self.part(self.FAR_PARTNER, False))
            self.landed(self.FAR_PARTNER)

        return [first, second, third, fourth]

    def finish(self):
        send, recv = self.sems[2], self.sems[3]
        for which in range(8):
            slot = self.slot(self.places[which] * 2 + 1 - self.at.core)
            remote(slot, slot, send.at[which], recv.at[which], self.at.twin).wait_recv()

    def sent(self):
        for stage in self.hops().values():
            for hop in stage:
                self.hop(*hop).wait_send()
        if self.axis == "row":
            self.passing(self.OWN, self.src).wait_send()
            for which in range(1, 8):
                self.passing(which).wait_send()


class Swap:
    def __init__(self, at, axis, src, dst, sems):
        self.at, self.axis, self.src, self.dst = at, axis, src, dst
        self.send, self.recv = sems
        self.me, self.size = (at.row, at.rows) if axis == "row" else (at.col, at.cols)

    def to(self, step):
        return lax.rem(self.me + step, self.size)

    def device(self, index):
        return (index, self.at.col) if self.axis == "row" else (self.at.row, index)

    def outgoing(self, step):
        to = self.to(step)
        return remote(
            self.src(to),
            self.dst(self.me),
            self.send.at[step],
            self.recv.at[step],
            self.device(to),
        )

    def start(self, which=None):
        for step in range(1, self.size):
            if which is None:
                self.outgoing(step).start()
            else:

                @pl.when(which(self.to(step)))
                def _():
                    self.outgoing(step).start()

    def arrived(self):
        for step in range(1, self.size):
            came = self.to(self.size - step)
            slot = self.dst(came)
            remote(
                slot, slot, self.send.at[step], self.recv.at[step], self.device(came)
            ).wait_recv()

    def sent(self):
        for step in range(1, self.size):
            self.outgoing(step).wait_send()


class RowSum:
    SEMS = 4

    def __init__(self, at, part, pairs, slots, sems):
        self.at, self.part, self.pairs, self.slots = at, part, pairs, slots
        self.twin_send, self.twin_recv, self.send, self.recv = sems

    def to_twin(self):
        at = self.at
        return remote(
            self.part.at[:, 1 - at.core],
            self.pairs,
            self.twin_send.at[0],
            self.twin_recv.at[0],
            at.twin,
        )

    def outgoing(self, step):
        at = self.at
        return remote(
            self.pairs.at[at.chip_at(step)],
            self.slots.at[at.chip],
            self.send.at[step],
            self.recv.at[step],
            (at.chip_row(step), at.col),
        )

    def start(self):
        self.to_twin().start()

    def middle(self):
        at = self.at
        self.to_twin().wait_recv()

        for step in (4, 1, 2, 3, 5, 6, 7, 0):
            chip = at.chip_at(step)
            both = self.part[chip, at.core].astype(f32) + self.pairs[chip].astype(f32)
            self.pairs[chip] = both.astype(bf16)
            if step > 0:
                self.outgoing(step).start()

    def finish(self):
        at = self.at
        total = self.pairs[at.chip].astype(f32)
        for step in range(1, at.chips):
            chip = at.chip_at(at.chips - step)
            slot = self.slots.at[chip]
            remote(
                slot, slot, self.send.at[step], self.recv.at[step], (chip * 2 + at.core, at.col)
            ).wait_recv()
            total = total + self.slots[chip].astype(f32)
        return total

    def released(self):
        self.to_twin().wait_send()

    def sent(self):
        for step in range(1, self.at.chips):
            self.outgoing(step).wait_send()


def sum_scratch(piece, width, chips):
    dma = pltpu.SemaphoreType.DMA
    return [
        pltpu.VMEM((chips, piece, width), bf16),
        pltpu.VMEM((chips, piece, width), bf16),
        dma((1,)),
        dma((1,)),
        dma((chips,)),
        dma((chips,)),
    ]


def moved_rows(index_row, first, count, values):
    shape = (count, index_row.shape[1])
    here = first + lax.broadcasted_iota(jnp.int32, shape, 0) == index_row
    return dot_nn(jnp.where(here, 1.0, 0.0).astype(bf16), values)


def flat(ref, size):
    return jnp.concatenate([ref[index, :size, :] for index in range(ref.shape[0])], axis=0)


def pack_rows(index_ref, values, out_refs, lanes):
    blocks = out_refs[0].shape[0]
    size = index_ref[1]
    for first in range(0, blocks, 4):
        found = moved_rows(index_ref[0][...], first * size, 4 * size, values).astype(bf16)
        for index in range(4):
            part = found[index * size : (index + 1) * size, :]
            for which, out_ref in enumerate(out_refs):
                out_ref[first + index, :size, :] = part[:, which * lanes : (which + 1) * lanes]


def every_row(at):
    return [(lax.rem(at.row + step, at.rows), at.col) for step in range(1, at.rows)]


def row_peers(at):
    return [(at.chip_row(step), at.col) for step in range(1, at.chips)] + [at.twin]


def col_peers(at):
    return [(at.row, at.col_at(step)) for step in range(1, at.cols)]


def gather_sems():
    return [pltpu.SemaphoreType.DMA((count,)) for count in (9, 9, 8, 8)]


def hop_sems():
    return [pltpu.SemaphoreType.DMA((9,))] * 2


def swap_sems(cols):
    return [pltpu.SemaphoreType.DMA((cols,))] * 2


def split(x):
    high_part = x.astype(bf16)
    return high_part, (x - high_part.astype(f32)).astype(bf16)


def three(dot, left, right):
    return dot(left[0], right[0]) + (dot(left[0], right[1]) + dot(left[1], right[0]))


BLK = 128


def layer_kernel(
    tokens_ref,
    cotangent_ref,
    lengths_ref,
    deal_ref,
    norm_ref,
    bias_ref,
    qkv_weight_ref,
    up_weight_ref,
    proj_weight_ref,
    down_weight_ref,
    qkv_momentum_ref,
    up_momentum_ref,
    proj_momentum_ref,
    down_momentum_ref,
    pick_ref,
    pack_ref,
    vector_all_ref,
    normalized_ref,
    inverse_std_ref,
    in_grad_ref,
    out_grad_ref,
    bias_grad_ref,
    matrix_ref,
    gram_ref,
    normed_part_ref,
    branch_sum_ref,
    take_back_ref,
    send_back_ref,
    weight_ref,
    vector_ref,
    table_ref,
    start_ref,
    momentum_ref,
    dealt_ref,
    cot_dealt_ref,
    weight_all_ref,
    q_ref,
    k_ref,
    v_ref,
    slope_ref,
    branch_ref,
    attended_ref,
    total_ref,
    out_part,
    pairs,
    values,
    out_rows_tokens,
    in_rows_tokens,
    out_rows_cots,
    in_rows_cots,
    out_tokens,
    in_tokens,
    out_cots,
    in_cots,
    pre_ref,
    dk_ref,
    dv_ref,
    out_parts,
    up_part,
    up_parts,
    qkv_part,
    qkv_parts,
    bias_part,
    biases,
    chunks,
    products,
    from_twin,
    half_sum,
    slices,
    twin_sums,
    slots,
    *sems,
):
    at = Place()
    held, feats = tokens_ref.shape
    piece = out_tokens.shape[1]
    capacity = out_rows_tokens.shape[1]
    depth = weight_ref.shape[0]
    sems = list(sems)

    def some(count):
        taken, sems[:count] = sems[:count], []
        return taken

    def block(ref):
        return lambda index: ref.at[index]

    def dealt_slot(ref):
        return lambda row: ref.at[pl.ds(row * piece, piece), :]

    last_tokens = HopGather(at, "row", dealt_slot(dealt_ref), some(4))
    last_cots = HopGather(at, "row", dealt_slot(cot_dealt_ref), some(4))
    rows_tokens = Swap(at, "row", block(out_rows_tokens), block(in_rows_tokens), some(2))
    rows_cots = Swap(at, "row", block(out_rows_cots), block(in_rows_cots), some(2))
    swap_tokens = Swap(at, "col", block(out_tokens), block(in_tokens), some(2))
    swap_cots = Swap(at, "col", block(out_cots), block(in_cots), some(2))
    weights = HopGather(
        at, "col", lambda c: weight_all_ref.at[pl.ds(c * depth, depth), :], some(2)
    )
    swap_vector = Swap(at, "col", lambda c: vector_ref, block(vector_all_ref), some(2))

    branch_rows = RowSum(at, normed_part_ref, twin_sums, slots, some(4))
    swap_out = Swap(at, "col", block(out_part), block(out_parts), some(2))
    swap_up = Swap(at, "col", block(up_part), block(up_parts), some(2))
    swap_qkv = Swap(at, "col", block(qkv_part), block(qkv_parts), some(2))
    swap_bias = Swap(at, "col", lambda c: bias_part, block(biases), some(2))
    swap_chunk = Swap(at, "col", block(chunks), block(matrix_ref), some(2))
    twin_send, twin_recv, sum_send, sum_recv, all_send, all_recv, pass_send, pass_recv = some(8)
    count = at.chips * 2
    mine = at.chip * 2 + at.col % 2
    first_col = at.col - at.col % 2

    def member(step):
        other = lax.rem(mine + step, count)
        return other, ((other // 2) * 2 + at.core, first_col + other % 2)

    peers = [member(step)[1] for step in range(1, count)]

    def pick(in_ref, out_ref):
        pack_rows((send_back_ref, piece), flat(in_ref, capacity), [out_ref], feats)

    plan = Plan(at, lengths_ref, deal_ref, held)
    take_back_ref[...] = plan.take_back()
    vector_ref[...] = jnp.zeros_like(vector_ref)
    vector_ref[: norm_ref.shape[0], :] = norm_ref[...]
    both = jnp.concatenate([tokens_ref[...], cotangent_ref[...]], axis=1)
    pack_rows((take_back_ref, capacity), both, [out_rows_tokens, out_rows_cots], feats)
    meet(every_row(at) + col_peers(at) + peers)
    rows_tokens.start()
    swap_vector.start()
    rows_cots.start()
    send_back_ref[...] = plan.listed(True)
    up = up_weight_ref.shape[1]
    weight_ref[...] = jnp.zeros_like(weight_ref)
    momentum_ref[...] = jnp.zeros_like(momentum_ref)
    for first, ref in (
        (0, qkv_weight_ref),
        (2 * up, proj_weight_ref),
        (2 * up + 2 * HEAD, down_weight_ref),
    ):
        weight_ref[:, first : first + ref.shape[0]] = ref[...].T.astype(bf16)
    weight_ref[:, up : 2 * up] = up_weight_ref[...].astype(bf16)
    weight_all_ref[pl.ds(at.col * depth, depth), :] = weight_ref[...]
    vector_all_ref[at.col] = vector_ref[...]
    in_rows_tokens[at.row] = out_rows_tokens[at.row]
    in_rows_cots[at.row] = out_rows_cots[at.row]

    rows_tokens.arrived()
    pick(in_rows_tokens, out_tokens)
    swap_tokens.start()
    in_tokens[at.col] = out_tokens[at.col]
    rows_cots.arrived()
    pick(in_rows_cots, out_cots)
    swap_cots.start()
    in_cots[at.col] = out_cots[at.col]
    start_ref[...] = plan.block_starts()
    table_ref[...] = plan.rotary()

    swap_vector.arrived()
    swap_tokens.arrived()
    weights.start(weight_ref)
    width = at.cols * feats
    parts = [in_tokens[f].astype(f32) for f in range(at.cols)]
    mean = sum(jnp.sum(part, axis=1, keepdims=True) for part in parts) / width
    parts = [part - mean for part in parts]
    variance = sum(jnp.sum(part * part, axis=1, keepdims=True) for part in parts) / width
    inverse_std = lax.rsqrt(variance + norm_floor)
    inverse_std_ref[...] = inverse_std
    own = pl.ds(at.row * piece, piece)
    for f in range(at.cols):
        lanes = slice(f * feats, (f + 1) * feats)
        normalized = parts[f] * inverse_std
        normalized_ref[:, lanes] = normalized
        vectors = vector_all_ref[f]
        dealt_ref[own, lanes] = (normalized * vectors[0:1, :] + vectors[1:2, :]).astype(bf16)
    last_tokens.start(dealt_ref.at[own, :])
    token_steps, weight_steps = iter(last_tokens.steps()), iter(weights.steps())
    cot_steps = iter(last_cots.steps())
    swap_cots.arrived()
    for f in range(at.cols):
        cot_dealt_ref[own, f * feats : (f + 1) * feats] = in_cots[f]
    next(weight_steps)()
    next(token_steps)()
    pick_ref[...] = plan.pick()
    pack_ref[...] = plan.listed(False)
    for first, ref in (
        (0, qkv_momentum_ref),
        (2 * up, proj_momentum_ref),
        (3 * up, down_momentum_ref),
    ):
        momentum_ref[:, first : first + ref.shape[0]] = ref[...].T
    momentum_ref[:, up : 2 * up] = up_momentum_ref[...]
    next(weight_steps)()
    next(token_steps)()
    last_cots.start(cot_dealt_ref.at[own, :])
    next(weight_steps)()
    next(token_steps)()
    next(weight_steps)()
    next(token_steps)()
    next(cot_steps)()
    last_tokens.finish()

    in_width = bias_ref.shape[1]
    tokens = dealt_ref.shape[0]
    rows_all = tokens // PIECE
    in_weight, out_weight = weight_all_ref[:, :in_width], weight_all_ref[:, in_width:]
    inner = math.sqrt(2.0 / math.pi)
    firsts = range(0, tokens, BLOCK)
    for first in firsts:
        if first == 4 * BLOCK:
            next(cot_steps)()
        rows = pl.ds(first, BLOCK)
        pre = dot_nn(dealt_ref[rows, :], in_weight) + bias_ref[...]
        pair = turned(pre[:, : 2 * HEAD], turning(table_ref, rows), False)
        for part in range(BLOCK // PIECE):
            these = slice(part * PIECE, (part + 1) * PIECE)
            spaced = pl.ds(first // PIECE + part, PIECE, stride=rows_all)
            pairs[spaced, :] = pair[these, :]
            values[spaced, :] = pre[these, 2 * HEAD : 4 * HEAD]
        up = pre[:, 4 * HEAD :]
        square = up * up
        bent = jnp.tanh(inner * (up + 0.044715 * square * up))
        branch_ref[rows, 2 * HEAD :] = (0.5 * up * (1.0 + bent)).astype(bf16)
        slope_ref[rows, :] = 0.5 * (1.0 + bent) + 0.5 * up * (1.0 - bent * bent) * (
            inner * (1.0 + 3.0 * 0.044715 * square)
        )
    for first in firsts:
        rows = pl.ds(first, BLOCK)
        pair = pairs[rows, :].astype(bf16)
        q_ref[rows, :] = (pair[:, :HEAD] * HEAD**-0.5).astype(bf16)
        k_ref[rows, :] = pair[:, HEAD:]
        v_ref[rows, :] = values[rows, :HEAD].astype(bf16)
    next(cot_steps)()
    for first in firsts:
        if first == 6 * BLOCK:
            next(cot_steps)()
        rows, keys = pl.ds(first, BLOCK), first + BLOCK
        scores = dot_nt(q_ref[rows, :], k_ref[:keys, :])
        scores = jnp.where(allowed_keys(start_ref, first, keys), scores, masked_score)
        top = jnp.max(scores, axis=1, keepdims=True)
        raw = jnp.exp(scores - top)
        total = jnp.sum(raw, axis=1, keepdims=True)
        attended = dot_nn(raw.astype(bf16), v_ref[:keys, :]) / total
        attended_ref[rows, :] = attended.astype(bf16)
        values[rows, :] = jnp.concatenate([attended, jnp.zeros_like(attended)], axis=1)
        total_ref[rows, :] = top + jnp.log(total)
    for first in firsts:
        rows = pl.ds(first, BLOCK)
        for part in range(BLOCK // PIECE):
            at_piece = first // PIECE + part
            branch_ref[at_piece * PIECE : (at_piece + 1) * PIECE, : 2 * HEAD] = values[
                pl.ds(at_piece, PIECE, stride=rows_all), :
            ].astype(bf16)
        partial = dot_nt(branch_ref[rows, :], out_weight).astype(bf16)
        for part in range(BLOCK // PIECE):
            at_piece = first // PIECE + part
            normed_part_ref[at_piece // 2, at_piece % 2] = partial[
                part * PIECE : (part + 1) * PIECE, :
            ]
    branch_rows.start()
    last_cots.finish()
    for first in range(0, cot_dealt_ref.shape[1], BLOCK):
        part = dot_tn(cot_dealt_ref[:, first : first + BLOCK], branch_ref[...]).astype(bf16)
        for index in range(BLOCK // feats):
            out_part[first // feats + index] = part[index * feats : (index + 1) * feats, :]
    swap_out.start()
    out_parts[at.col] = out_part[at.col]

    half = up_part.shape[2]

    def weight_part(ref, lanes):
        for first in range(0, dealt_ref.shape[1], BLOCK):
            part = dot_tn(dealt_ref[:, first : first + BLOCK], pre_ref[:, lanes])
            for index in range(BLOCK // feats):
                ref[first // feats + index] = part[
                    index * feats : (index + 1) * feats, :
                ].astype(bf16)

    def direction(index, grad):
        lanes = slice(index * BLK, (index + 1) * BLK)
        state = momentum * momentum_ref[:, lanes] + grad
        chunks[index] = grad + momentum * state

    for first in firsts:
        rows = pl.ds(first, BLOCK)
        branch_grad = dot_nn(cot_dealt_ref[rows, :], out_weight)
        for part in range(BLOCK // PIECE):
            these = slice(part * PIECE, (part + 1) * PIECE)
            spaced = pl.ds(first // PIECE + part, PIECE, stride=rows_all)
            values[spaced, :] = branch_grad[these, : 2 * HEAD]
        pre_ref[rows, 4 * HEAD :] = (branch_grad[:, 2 * HEAD :] * slope_ref[rows, :]).astype(bf16)
    weight_part(up_part, slice(half, 2 * half))
    swap_up.start()
    up_parts[at.col] = up_part[at.col]
    dk_ref[...] = jnp.zeros_like(dk_ref)
    dv_ref[...] = jnp.zeros_like(dv_ref)
    branch_rows.middle()
    for first in reversed(firsts):
        rows, keys = pl.ds(first, BLOCK), first + BLOCK
        query, grad = q_ref[rows, :], values[rows, :HEAD].astype(bf16)
        key, value = k_ref[:keys, :], v_ref[:keys, :]
        scores = dot_nt(query, key)
        allowed = allowed_keys(start_ref, first, keys)
        prob = jnp.where(allowed, jnp.exp(scores - total_ref[rows, :]), 0.0)
        delta = jnp.sum(
            grad.astype(f32) * attended_ref[rows, :].astype(f32), axis=1, keepdims=True
        )
        score_grad = (prob * (dot_nt(grad, value) - delta)).astype(bf16)
        dk_ref[:keys, :] += dot_tn(score_grad, query)
        dv_ref[:keys, :] += dot_tn(prob.astype(bf16), grad)
        pairs[rows, :] = jnp.concatenate(
            [dot_nn(score_grad, key) * HEAD**-0.5, dk_ref[rows, :]], axis=1
        )
        dv = dv_ref[rows, :]
        values[rows, :] = jnp.concatenate([dv, jnp.zeros_like(dv)], axis=1)
    for first in firsts:
        rows = pl.ds(first, BLOCK)
        pair, value = [
            jnp.concatenate(
                [
                    ref[pl.ds(first // PIECE + part, PIECE, stride=rows_all), :]
                    for part in range(BLOCK // PIECE)
                ],
                axis=0,
            )
            for ref in (pairs, values)
        ]
        pre_ref[rows, : 2 * HEAD] = turned(pair, turning(table_ref, rows), True).astype(bf16)
        pre_ref[rows, 2 * HEAD : 4 * HEAD] = value.astype(bf16)
    weight_part(qkv_part, slice(0, half))
    swap_qkv.start()
    qkv_parts[at.col] = qkv_part[at.col]
    bias = jnp.sum(pre_ref[...].astype(f32), axis=0, keepdims=True)
    bias_part[...] = jnp.broadcast_to(bias, bias_part.shape)
    swap_bias.start()
    biases[at.col] = bias_part[...]
    branch_rows.released()
    for first in firsts:
        rows = pl.ds(first, BLOCK)
        partial = dot_nt(pre_ref[rows, :], in_weight).astype(bf16)
        for part in range(BLOCK // PIECE):
            at_piece = first // PIECE + part
            normed_part_ref[at_piece // 2, at_piece % 2] = partial[
                part * PIECE : (part + 1) * PIECE, :
            ]

    swap_out.arrived()
    total = sum(out_parts[c].astype(f32) for c in range(at.cols))
    filled = jnp.zeros((feats, half - 2 * HEAD), f32)
    out_grad = jnp.concatenate([total[:, : 2 * HEAD], filled, total[:, 2 * HEAD :]], axis=1)
    out_grad_ref[...] = out_grad
    swap_up.arrived()
    up_grad = sum(up_parts[c].astype(f32) for c in range(at.cols))
    in_grad_ref[:, half:] = up_grad
    late = half // BLK
    for index in range(late, at.cols):
        first = (index - late) * BLK
        if first < half:
            direction(index, up_grad[:, first : first + BLK])
        else:
            direction(index, out_grad[:, first - half : first - half + BLK])
    swap_chunk.start(lambda to: to >= late)
    swap_qkv.arrived()
    qkv_grad = sum(qkv_parts[c].astype(f32) for c in range(at.cols))
    in_grad_ref[:, :half] = qkv_grad
    for index in range(late):
        direction(index, qkv_grad[:, index * BLK : (index + 1) * BLK])
    swap_chunk.start(lambda to: to < late)
    matrix_ref[at.col] = chunks[at.col]
    swap_bias.arrived()
    bias_grad_ref[...] = sum(biases[c] for c in range(at.cols))
    swap_chunk.arrived()

    strips = matrix_ref.shape[0]
    matrix = split(matrix_ref[...].reshape(strips * BLK, BLK))
    index = 0
    for i in range(strips):
        left = [m[i * BLK : (i + 1) * BLK, :] for m in matrix]
        right = [m[i * BLK :, :] for m in matrix]
        product = three(dot_nt, left, right)
        for j in range(strips - i):
            products[index] = product[:, j * BLK : (j + 1) * BLK]
            index += 1
    blocks = index // 2
    to_twin = remote(
        products.at[pl.ds((1 - at.core) * blocks, blocks)],
        from_twin,
        twin_send.at[0],
        twin_recv.at[0],
        at.twin,
    )
    to_twin.start()
    to_twin.wait_recv()
    for b in range(blocks):
        half_sum[b * BLK : (b + 1) * BLK, :] = products[at.core * blocks + b] + from_twin[b]

    size = blocks * BLK // count

    def piece_of(owner):
        return half_sum.at[pl.ds(owner * size, size), :]

    def give(step):
        owner, device = member(step)
        return remote(
            piece_of(owner), slices.at[mine], sum_send.at[step], sum_recv.at[step], device
        )

    for step in range(1, count):
        give(step).start()
    slices[mine] = half_sum[pl.ds(mine * size, size), :]
    for step in range(1, count):
        came, device = member(count - step)
        remote(
            slices.at[came], slices.at[came], sum_send.at[step], sum_recv.at[step], device
        ).wait_recv()
    total = slices[0]
    for index in range(1, count):
        total = total + slices[index]
    half_rows = blocks * BLK

    def home(owner):
        return gram_ref.at[pl.ds(at.core * half_rows + owner * size, size), :]

    gram_ref[pl.ds(at.core * half_rows + mine * size, size), :] = total

    def spread(step):
        return remote(
            home(mine), home(mine), all_send.at[step], all_recv.at[step], member(step)[1]
        )

    def passing(step):
        came = member(count - step)[0] if step else mine
        return remote(
            home(came), home(came), pass_send.at[step], pass_recv.at[step], at.twin
        )

    for step in range(1, count):
        spread(step).start()
    passing(0).start()
    for step in range(1, count):
        came, device = member(count - step)
        remote(
            home(came), home(came), all_send.at[step], all_recv.at[step], device
        ).wait_recv()
        passing(step).start()
    for step in range(count):
        other = lax.rem(at.chip * 2 + at.col % 2 + count - step, count)
        slot = gram_ref.at[pl.ds((1 - at.core) * half_rows + other * size, size), :]
        remote(slot, slot, pass_send.at[step], pass_recv.at[step], at.twin).wait_recv()
        passing(step).wait_send()
    to_twin.wait_send()
    for step in range(1, count):
        give(step).wait_send()
        spread(step).wait_send()
    branch_sum_ref[...] = branch_rows.finish().astype(bf16)
    branch_rows.sent()
    for moved in (last_tokens, last_cots, weights, rows_tokens, rows_cots):
        moved.sent()
    for moved in (swap_tokens, swap_cots, swap_vector):
        moved.sent()
    for moved in (swap_out, swap_up, swap_qkv, swap_bias, swap_chunk):
        moved.sent()


WIDE = 256


def poly_kernel(
    gram_ref,
    matrix_ref,
    normed_part_ref,
    branch_ref,
    normalized_ref,
    inverse_std_ref,
    vector_ref,
    tokens_ref,
    cotangent_ref,
    pick_ref,
    pack_ref,
    update_ref,
    output_ref,
    input_grad_ref,
    vector_sum_ref,
    own_update,
    normed_ref,
    out_branch,
    in_branch,
    out_rows_branch,
    in_rows_branch,
    out_token,
    in_token,
    out_rows,
    in_rows,
    twin_sums,
    slots,
    *buffers,
):
    at = Place()
    sems, buffers = buffers[8:], buffers[:8]

    def block(ref):
        return lambda index: ref.at[index]

    swap_token = Swap(at, "col", block(out_token), block(in_token), sems[0:2])
    rows_token = Swap(at, "row", block(out_rows), block(in_rows), sems[2:4])
    feats = out_token.shape[2]
    swap_update = Swap(
        at,
        "col",
        lambda c: own_update.at[pl.ds(c * feats, feats), :],
        block(update_ref),
        sems[4:6],
    )
    swap_branch = Swap(at, "col", block(out_branch), block(in_branch), sems[6:8])
    rows_branch = Swap(at, "row", block(out_rows_branch), block(in_rows_branch), sems[8:10])
    normed_rows = RowSum(at, normed_part_ref, twin_sums, slots, sems[10:14])
    piece, capacity = normed_ref.shape[0], out_rows_branch.shape[1]
    lanes = [slice(f * feats, (f + 1) * feats) for f in range(at.cols)]
    for f in range(at.cols):
        out_branch[f] = branch_ref[:, lanes[f]]
    meet(every_row(at) + col_peers(at))
    normed_rows.start()
    swap_branch.start()
    in_branch[at.col] = out_branch[at.col]

    def branch_back():
        swap_branch.arrived()
        pack_rows((pick_ref, capacity), flat(in_branch, piece), [out_rows_branch], feats)
        rows_branch.start()
        in_rows_branch[at.row] = out_rows_branch[at.row]

    def home(rows_ref, base_ref, shift, out_ref):
        values = flat(rows_ref, capacity)
        for first in range(0, out_ref.shape[0], BLOCK):
            rows = pl.ds(first, BLOCK)
            found = moved_rows(pack_ref[...], first, BLOCK, values)
            out_ref[rows, :] = found + base_ref[rows, :].astype(f32) + shift

    def branch_home():
        rows_branch.arrived()
        home(in_rows_branch, tokens_ref, vector_ref[at.col][2:3, :], output_ref)

    def extra(vectors):
        parts = [part.astype(f32) for vector in vectors for part in split(vector)]
        empty = jnp.zeros((EXTRA - len(parts), feats), f32)
        return jnp.concatenate([*parts, empty], axis=0).astype(bf16)

    def token_grads():
        normed_ref[...] = normed_rows.finish()
        width = at.cols * feats
        scaled = [normed_ref[:, lanes[f]] * vector_ref[f][0:1, :] for f in range(at.cols)]
        mean_first = sum(jnp.sum(part, axis=1, keepdims=True) for part in scaled) / width
        mean_second = (
            sum(
                jnp.sum(part * normalized_ref[:, lanes[f]], axis=1, keepdims=True)
                for f, part in enumerate(scaled)
            )
            / width
        )
        for f in range(at.cols):
            normalized, grad = normalized_ref[:, lanes[f]], normed_ref[:, lanes[f]]
            token_grad = inverse_std_ref[...] * (scaled[f] - mean_first - normalized * mean_second)
            out_token[f, :piece, :] = token_grad.astype(bf16)
            gain_grad = jnp.sum(grad * normalized, axis=0, keepdims=True)
            shift_grad = jnp.sum(grad, axis=0, keepdims=True)
            out_token[f, piece:, :] = extra([gain_grad, shift_grad])
        swap_token.start()
        in_token[at.col] = out_token[at.col]

    def token_back():
        cot_sum = jnp.sum(cotangent_ref[...].astype(f32), axis=0, keepdims=True)
        swap_token.arrived()
        pack_rows((pick_ref, capacity), flat(in_token, piece), [out_rows], feats)
        sums = sum(in_token[c, piece:, :].astype(f32) for c in range(at.cols))
        sums = extra([sums[0:1, :] + sums[1:2, :], sums[2:3, :] + sums[3:4, :], cot_sum])
        for row in range(at.rows):
            out_rows[row, capacity:, :] = sums
        rows_token.start()
        in_rows[at.row] = out_rows[at.row]

    first, second, third, thin = [buffers[2 * i : 2 * i + 2] for i in range(4)]
    strips = matrix_ref.shape[0]
    size = strips * BLK
    counts = range(size // WIDE)
    eye = lax.broadcasted_iota(jnp.int32, (BLK, BLK), 0) == lax.broadcasted_iota(
        jnp.int32, (BLK, BLK), 1
    )

    def put(pair, rows, lanes, value):
        high_part, low_part = split(value)
        pair[0][rows, lanes] = high_part
        pair[1][rows, lanes] = low_part

    def get(pair, rows, lanes):
        return pair[0][rows, lanes], pair[1][rows, lanes]

    places, index = [], 0
    for i in range(strips):
        for j in range(i, strips):
            places.append((i, j, index))
            index += 1
    trace = sum(
        jnp.sum(jnp.where(eye, gram_ref[spot * BLK : (spot + 1) * BLK, :], 0.0))
        for i, j, spot in places
        if i == j
    )
    shrink = 1.0 / (jnp.sqrt(jnp.full((1, 1), trace, f32)) + ortho_floor)
    for i, j, spot in places:
        block = gram_ref[spot * BLK : (spot + 1) * BLK, :] * (shrink * shrink)
        here, there = slice(i * BLK, (i + 1) * BLK), slice(j * BLK, (j + 1) * BLK)
        put(first, here, there, block)
        if j > i:
            put(first, there, here, block.T)
    everything = slice(0, size)
    for i in range(strips):
        put(thin, slice(i * BLK, (i + 1) * BLK), everything, matrix_ref[i] * shrink)

    def product(left, right, out, finish=None):
        for i in counts:
            rows, rest = slice(i * WIDE, (i + 1) * WIDE), slice(i * WIDE, size)
            value = three(dot_nn, get(left, rows, everything), get(right, everything, rest))
            if finish is not None:
                value = finish(value, rows, rest)
            put(out, rows, rest, value)
            for j in range(i + 1, size // WIDE):
                part = value[:, (j - i) * WIDE : (j - i + 1) * WIDE]
                put(out, slice(j * WIDE, (j + 1) * WIDE), rows, part.T)

    def thin_product(left):
        right = get(thin, everything, everything)
        return [
            three(dot_nn, get(left, slice(i * WIDE, (i + 1) * WIDE), everything), right)
            for i in counts
        ]

    def sweep(gram, poly, square, between=lambda: None):
        def finish(value, rows, rest):
            high_part, low_part = get(gram, rows, rest)
            value = poly_cubic * value + poly_square * (
                high_part.astype(f32) + low_part.astype(f32)
            )
            at_row = lax.broadcasted_iota(jnp.int32, value.shape, 0)
            at_lane = lax.broadcasted_iota(jnp.int32, value.shape, 1)
            return value + jnp.where(at_row == at_lane, poly_linear, 0.0)

        product(gram, gram, poly, finish)
        between()
        for i, value in zip(counts, thin_product(poly)):
            put(thin, slice(i * WIDE, (i + 1) * WIDE), everything, value)
        product(poly, poly, square)
        product(gram, square, poly)

    def two(step, carry):
        def early():
            @pl.when(step == 0)
            def _():
                normed_rows.middle()
                branch_back()

            @pl.when(step == 1)
            def _():
                token_grads()

        def late():
            @pl.when(step == 1)
            def _():
                branch_home()

        sweep(first, second, third, early)

        @pl.when(step == 1)
        def _():
            token_back()

        sweep(second, first, third, late)
        return carry

    lax.fori_loop(0, 2, two, 0)
    once = thin_product(first)
    old = []
    for i in counts:
        rows = slice(i * WIDE, (i + 1) * WIDE)
        high_part, low_part = get(thin, rows, everything)
        old.append(high_part.astype(f32) + low_part.astype(f32))
    for i, value in zip(counts, once):
        put(thin, slice(i * WIDE, (i + 1) * WIDE), everything, value)
    for i, value in zip(counts, thin_product(first)):
        result = poly_linear * old[i] + poly_square * once[i] + poly_cubic * value
        own_update[i * WIDE : (i + 1) * WIDE, :] = result.astype(bf16)
    swap_update.start()
    update_ref[at.col] = own_update[pl.ds(at.col * feats, feats), :]

    rows_token.arrived()
    home(in_rows, cotangent_ref, 0.0, input_grad_ref)
    vector_sum_ref[...] = sum(
        in_rows[row, capacity:, :].astype(f32) for row in range(at.rows)
    )
    swap_update.arrived()
    normed_rows.released()
    for moved in (swap_token, rows_token, swap_update, swap_branch, rows_branch, normed_rows):
        moved.sent()


def orthogonalize(
    gram,
    matrix,
    normed_part,
    branch_sum,
    normalized,
    inverse_std,
    vectors,
    tokens,
    cotangent,
    pick,
    pack,
    rows,
):
    cols, feats, width = matrix.shape
    size = cols * BLK
    piece, full = branch_sum.shape
    held = cotangent.shape[0]
    chips = rows // 2
    capacity = pack.shape[1] // rows
    shape = jax.ShapeDtypeStruct
    square, narrow = pltpu.VMEM((size, size), bf16), pltpu.VMEM((size, width), bf16)
    return remote_call(
        poly_kernel,
        3,
        (
            shape((cols, feats, width), bf16),
            shape((held, feats), f32),
            shape((held, feats), f32),
            shape((EXTRA, feats), f32),
        ),
        [VMEM_SPEC] * 11,
        [
            narrow,
            pltpu.VMEM((piece, full), f32),
            *([pltpu.VMEM((cols, piece, feats), bf16)] * 2),
            *([pltpu.VMEM((rows, capacity, feats), bf16)] * 2),
            *([pltpu.VMEM((cols, piece + EXTRA, feats), bf16)] * 2),
            *([pltpu.VMEM((rows, capacity + EXTRA, feats), bf16)] * 2),
            *sum_scratch(piece, full, chips)[:2],
            *([square] * 6),
            *([narrow] * 2),
            *swap_sems(cols),
            *swap_sems(rows),
            *(swap_sems(cols) * 2),
            *swap_sems(rows),
            *sum_scratch(piece, full, chips)[2:],
        ],
        60 * 10**9,
        "orthogonalize",
    )(
        *(gram, matrix, normed_part, branch_sum, normalized),
        *(inverse_std, vectors, tokens, cotangent, pick, pack),
    )


def layer(tokens, cotangent, lengths, deal_order, vectors, bias, weights, momenta, rows, cols):
    held, feats = tokens.shape
    group = held * rows // cols
    piece, width, chips = group // rows, feats * cols, rows // 2
    in_width = bias.shape[1]
    up = in_width - 4 * HEAD
    branch = up + 2 * HEAD
    capacity = CAPACITY
    depth, tile = feats, 2 * up + branch
    blocks = cols * (cols + 1) // 2
    count = chips * 2
    half_rows = blocks * BLK // 2
    shape, vmem = jax.ShapeDtypeStruct, pltpu.VMEM
    dma = pltpu.SemaphoreType.DMA
    return remote_call(
        layer_kernel,
        0,
        (
            shape((1, cols * piece), jnp.int32),
            shape((1, rows * capacity), jnp.int32),
            shape((cols, 8, feats), f32),
            shape((piece, width), f32),
            shape((piece, 1), f32),
            shape((feats, in_width), f32),
            shape((feats, in_width), f32),
            shape((8, in_width), f32),
            shape((cols, feats, BLK), f32),
            shape((blocks * BLK, BLK), f32),
            shape((chips, 2, piece, width), bf16),
            shape((piece, width), bf16),
        ),
        [VMEM_SPEC] * 14,
        [
            vmem((1, held), jnp.int32),
            vmem((1, rows * capacity), jnp.int32),
            vmem((depth, tile), bf16),
            vmem((8, feats), f32),
            vmem((4 * ROT // 2, group), bf16),
            vmem((group, 1), jnp.int32),
            vmem((depth, 4 * up), f32),
            *([vmem((group, width), bf16)] * 2),
            vmem((depth * cols, tile), bf16),
            *([vmem((group, HEAD), bf16)] * 3),
            vmem((group, up), f32),
            vmem((group, branch), bf16),
            vmem((group, HEAD), bf16),
            vmem((group, 1), f32),
            vmem((cols, feats, branch), bf16),
            *([vmem((group, 2 * HEAD), f32)] * 2),
            *([vmem((rows, capacity, feats), bf16)] * 4),
            *([vmem((cols, piece, feats), bf16)] * 4),
            vmem((group, in_width), bf16),
            *([vmem((group, HEAD), f32)] * 2),
            vmem((cols, feats, branch), bf16),
            *([vmem((cols, feats, up), bf16)] * 4),
            vmem((8, in_width), f32),
            vmem((cols, 8, in_width), f32),
            vmem((cols, feats, BLK), f32),
            vmem((blocks, BLK, BLK), f32),
            vmem((blocks // 2, BLK, BLK), f32),
            vmem((half_rows, BLK), f32),
            vmem((count, half_rows // count, BLK), f32),
            *sum_scratch(piece, width, chips)[:2],
            *(gather_sems() * 2),
            *(swap_sems(rows) * 2),
            *(swap_sems(cols) * 2),
            *hop_sems(),
            *swap_sems(cols),
            *sum_scratch(piece, width, chips)[2:],
            *(swap_sems(cols) * 5),
            dma((1,)),
            dma((1,)),
            *([dma((count,))] * 6),
        ],
        150 * 10**9,
        "layer",
    )(tokens, cotangent, lengths, deal_order, vectors, bias, *weights, *momenta)


CAPACITY = 96


def column_sum(x):
    return jnp.sum(x.astype(f32), axis=0, keepdims=True).astype(jnp.int32)


def lane_sum(x):
    return jnp.sum(x.astype(f32), axis=1, keepdims=True).astype(jnp.int32)


class Plan:
    def __init__(self, at, lengths_ref, deal_ref, held):
        self.at, self.held = at, held
        total = held * at.rows
        self.group = total // at.cols
        self.piece = self.group // at.rows
        self.length_row = lengths_ref[...]
        slots = self.length_row.shape[1]
        self.slots = slots
        square = (slots, slots)
        below = lax.broadcasted_iota(jnp.int32, square, 1)
        above = lax.broadcasted_iota(jnp.int32, square, 0)
        self.same = below == above
        self.strict = jnp.where(below < above, 1.0, 0.0).astype(bf16)
        lengths = jnp.broadcast_to(self.length_row, square)
        self.starts = lane_sum(jnp.where(below < above, lengths, 0))
        self.ends = lane_sum(jnp.where(below <= above, lengths, 0))
        shape = deal_ref.shape
        position = lax.broadcasted_iota(jnp.int32, shape, 0) * shape[1]
        position = (position + lax.broadcasted_iota(jnp.int32, shape, 1)).astype(f32)
        deal = deal_ref[...]
        found = [
            jnp.sum(
                jnp.where(deal == self.starts[slot : slot + 1, :], position, 0.0),
                axis=0,
                keepdims=True,
            )
            for slot in range(slots)
        ]
        self.dealt = lane_sum(jnp.concatenate(found, axis=0))
        self.shift = self.dealt - self.starts

    def passed(self, x, to):
        rows = self.at.rows
        return (x + (rows - 1 - to)) >> int(math.log2(rows))

    def clipped(self, x, first):
        return jnp.minimum(jnp.maximum(x, first), first + self.held)

    def rank(self, token, holder, to):
        first = holder * self.held
        low = self.clipped(self.starts, first)
        high = jnp.maximum(self.clipped(jnp.minimum(self.ends, token), first), low)
        return column_sum(self.passed(high + self.shift, to) - self.passed(low + self.shift, to))

    def lanes(self, count):
        return lax.broadcasted_iota(jnp.int32, (1, count), 1)

    def take_back(self):
        token = self.at.row * self.held + self.lanes(self.held)
        holds = (self.starts <= token) & (token < self.ends)
        to = (token + column_sum(jnp.where(holds, self.shift, 0))) % self.at.rows
        return to * CAPACITY + self.rank(token, self.at.row, to)

    def in_dealt(self, position):
        lengths = self.ends - self.starts
        return (self.dealt <= position) & (position < self.dealt + lengths)

    def pick(self):
        at = self.at
        slot = self.lanes(at.cols * self.piece)
        position = (slot // self.piece) * self.group + (slot % self.piece) * at.rows + at.row
        inside = self.in_dealt(position)
        token = position - column_sum(jnp.where(inside, self.shift, 0))
        holder = token // self.held
        return holder * CAPACITY + self.rank(token, holder, at.row)

    def listed(self, holder_is_lane):
        at = self.at
        lane = self.lanes(at.rows * CAPACITY)
        which = sum(jnp.where(lane >= CAPACITY * row, 1, 0) for row in range(1, at.rows))
        slot = lane - CAPACITY * which
        holder, to = (which, at.row) if holder_is_lane else (at.row, which)
        first = holder * self.held
        begin = self.passed(self.clipped(self.starts, first) + self.shift, to)
        count = self.passed(self.clipped(self.ends, first) + self.shift, to) - begin
        before = dot_nn(self.strict, count.astype(f32).astype(bf16)).astype(jnp.int32)
        inside = slot - before
        found = (inside >= 0) & (inside < count)
        dealt = at.rows * (begin + inside) + to
        used = column_sum(jnp.where(found, 1, 0)) > 0
        if holder_is_lane:
            block = dealt // self.group
            rest = dealt % self.group
            value = block * self.piece + rest // at.rows
        else:
            value = dealt - self.shift - first
        return jnp.where(used, column_sum(jnp.where(found, value, 0)), -1)

    def block_starts(self):
        shape = (self.group, self.slots)
        first = self.at.col * self.group
        position = first + lax.broadcasted_iota(jnp.int32, shape, 0)
        dealt = column_sum(jnp.where(self.same, self.dealt, 0))
        inside = (dealt <= position) & (position < dealt + self.length_row)
        return lane_sum(jnp.where(inside, dealt - first, 0))

    def rotary(self):
        half_rot = ROT // 2
        lane = self.lanes(self.group)
        position = self.at.col * self.group + (lane % self.piece) * self.at.rows
        position = position + lane // self.piece
        inside = self.in_dealt(position)
        place = position - column_sum(jnp.where(inside, self.dealt, 0))
        entry = lax.broadcasted_iota(jnp.int32, (half_rot, 1), 0)
        inverse = sum(
            jnp.where(entry == index, 1.0 / 10000.0 ** (index * 2.0 / ROT), 0.0)
            for index in range(half_rot)
        )
        angles = inverse.astype(f32) * place.astype(f32)
        parts = split(jnp.concatenate([jnp.cos(angles), jnp.sin(angles)], axis=0))
        return jnp.concatenate(parts, axis=0)


def finish_kernel(
    in_grad_ref,
    out_grad_ref,
    update_ref,
    output_ref,
    input_grad_ref,
    vector_sum_ref,
    *refs,
):
    weights, momenta, norms, outs = refs[0:4], refs[4:8], refs[8:11], refs[11:]
    outs[0][...] = output_ref[...]
    outs[1][...] = input_grad_ref[...]
    wide = in_grad_ref.shape[1] // 2
    widths = (3 * D, FF, D, FF)
    for index in range(4):
        source = in_grad_ref if index < 2 else out_grad_ref
        first = (index % 2) * wide
        grad = source[:, first : first + wide]
        update = jnp.concatenate([update_ref[2 * index], update_ref[2 * index + 1]], axis=1)
        update = update.astype(f32)
        if index != 1:
            size = weights[index].shape[0]
            grad, update = grad.T[:size, :], update.T[:size, :]
        outs[2 + index][...] = grad
        outs[6 + index][...] = momentum * momenta[index][...] + grad
        outs[10 + index][...] = (
            weights[index][...] * (1.0 - rate_matrix * decay_matrix)
            - rate_matrix * 0.2 * math.sqrt(widths[index]) * update
        )
    sums = vector_sum_ref[...]
    grads = jnp.concatenate(
        [sums[2 * index : 2 * index + 1, :] + sums[2 * index + 1 : 2 * index + 2, :] for index in range(3)],
        axis=0,
    )
    for out_ref, value in zip(
        outs[14:], adam_step(norms[0][...], grads, norms[1][...], norms[2][...])
    ):
        out_ref[...] = value


def finish(in_grad, out_grad, update, output, input_grad, vector_sum, weights, momenta, norms):
    shape = jax.ShapeDtypeStruct
    matrices = [shape(weight.shape, f32) for weight in weights]
    return pl.pallas_call(
        finish_kernel,
        out_shape=(
            shape(output.shape, f32),
            shape(output.shape, f32),
            *(matrices * 3),
            *([shape(norms[0].shape, f32)] * 3),
        ),
        compiler_params=pltpu.CompilerParams(vmem_limit_bytes=VMEM_LIMIT),
        name="finish",
    )(in_grad, out_grad, update, output, input_grad, vector_sum, *weights, *momenta, *norms)


def adam_step(value, gradient, first_state, second_state):
    first_new = beta_first * first_state + (1.0 - beta_first) * gradient
    second_new = beta_second * second_state + (1.0 - beta_second) * gradient * gradient
    corrected = first_new / (1.0 - beta_first**STEP)
    root_term = jnp.sqrt(second_new / (1.0 - beta_second**STEP)) + adam_floor
    return (first_new, second_new, value - rate_vector * corrected / root_term)


def per_device(
    tokens,
    cotangent,
    lengths,
    deal_order,
    qkv_weight,
    up_weight,
    proj_weight,
    down_weight,
    norm_vectors,
    qkv_bias,
    mlp_bias,
    qkv_momentum,
    up_momentum,
    proj_momentum,
    down_momentum,
    norm_moment,
    norm_square,
    qkv_bias_moment,
    qkv_bias_square,
    mlp_bias_moment,
    mlp_bias_square,
):
    cols, rows = lax.axis_size("col"), lax.axis_size("row")
    qkv_width, up_width = qkv_weight.shape[1], up_weight.shape[1]
    bias = jnp.concatenate(
        [jnp.pad(qkv_bias, (0, up_width - qkv_width)), mlp_bias], axis=0
    ).reshape(1, 2 * up_width)
    weights = (qkv_weight.T, up_weight, proj_weight, down_weight)
    momenta = (qkv_momentum.T, up_momentum, proj_momentum, down_momentum)
    (
        pick,
        pack,
        vector_all,
        normalized,
        inverse_std,
        in_grad,
        out_grad,
        bias_rows,
        matrix,
        gram,
        normed_part,
        branch_sum,
    ) = layer(
        tokens,
        cotangent,
        lengths.reshape(1, -1),
        deal_order.reshape(-1, 128),
        norm_vectors,
        bias,
        weights,
        momenta,
        rows,
        cols,
    )
    returned, output, input_grad, vector_sum = orthogonalize(
        gram,
        matrix,
        normed_part,
        branch_sum,
        normalized,
        inverse_std,
        vector_all,
        tokens,
        cotangent,
        pick,
        pack,
        rows,
    )
    output, input_grad, *matrices = finish(
        in_grad,
        out_grad,
        returned,
        output,
        input_grad,
        vector_sum,
        weights,
        momenta,
        (norm_vectors, norm_moment, norm_square),
    )
    matrices, norms = matrices[:12], matrices[12:]
    for index in (0, 4, 8):
        matrices[index] = matrices[index].T
    in_bias_grad = bias_rows[0]
    qkv_first, qkv_second, qkv_bias_new = adam_step(
        qkv_bias, in_bias_grad[:qkv_width], qkv_bias_moment, qkv_bias_square
    )
    mlp_first, mlp_second, mlp_bias_new = adam_step(
        mlp_bias, in_bias_grad[up_width:], mlp_bias_moment, mlp_bias_square
    )
    return (
        output,
        input_grad,
        *matrices,
        *norms,
        qkv_first,
        qkv_second,
        qkv_bias_new,
        mlp_first,
        mlp_second,
        mlp_bias_new,
    )


def solution(mesh):
    over_both, over_flip = P("row", "col"), P("col", "row")
    features, hidden = P(None, "col"), P("row")
    return jax.shard_map(
        per_device,
        mesh=mesh,
        in_specs=(
            *(over_both, over_both, P(), P()),
            *(over_flip, over_flip, over_both, over_both),
            *(features, hidden, hidden),
            *(over_flip, over_flip, over_both, over_both),
            *(features, features, hidden, hidden, hidden, hidden),
        ),
        out_specs=(
            *(over_both, over_both),
            *(over_flip, over_flip, over_both, over_both) * 3,
            *(features,) * 3,
            *(hidden,) * 6,
        ),
        check_vma=False,
    )
```

```python
import functools
import math

import jax
import jax.numpy as jnp
from jax import lax
from jax.experimental import pallas as pl
from jax.experimental.pallas import tpu as pltpu
from jax.sharding import PartitionSpec as P

D = 1024
HEAD = 64
ROT = 16
FF = 4096
STEP = 10

poly_linear = 3.4445
poly_square = -4.775
poly_cubic = 2.0315
momentum = 0.95
rate_matrix = 0.15
decay_matrix = 0.1
beta_first = 0.9
beta_second = 0.95
rate_vector = 0.2
adam_floor = 1e-08
norm_floor = 1e-05
ortho_floor = 1e-07
masked_score = -1e30
f32 = jnp.float32
bf16 = jnp.bfloat16
BLOCK = 256
PIECE = 128
EXTRA = 16


def dot_nt(a, b, **kw):
    return lax.dot_general(a, b, (((1,), (1,)), ((), ())), preferred_element_type=f32, **kw)


def dot_tn(a, b, **kw):
    return lax.dot_general(a, b, (((0,), (0,)), ((), ())), preferred_element_type=f32, **kw)


def dot_nn(a, b, **kw):
    return lax.dot_general(a, b, (((1,), (0,)), ((), ())), preferred_element_type=f32, **kw)


def allowed_keys(start_ref, first, keys):
    shape = (BLOCK, keys)
    key_at = lax.broadcasted_iota(jnp.int32, shape, 1)
    query_at = first + lax.broadcasted_iota(jnp.int32, shape, 0)
    return (key_at >= start_ref[pl.ds(first, BLOCK), :]) & (key_at <= query_at)


def turning(table_ref, rows):
    lane = lax.broadcasted_iota(jnp.int32, (32, 2 * HEAD), 1) % HEAD
    entry = lax.broadcasted_iota(jnp.int32, (32, 2 * HEAD), 0) % 16
    half_rot = ROT // 2

    def spread(where, value):
        picks = jnp.where(where, value, 0.0).astype(bf16)
        return dot_tn(table_ref[:, rows], picks)

    cosine = spread((lane < ROT) & (entry == lane % half_rot), 1.0)
    cosine = cosine + jnp.where(lane[:1] < ROT, 0.0, 1.0)
    lower = spread((lane < half_rot) & (entry == lane + half_rot), -1.0)
    upper = spread((lane >= half_rot) & (lane < ROT) & (entry == lane), 1.0)
    return cosine, lower, upper


def turned(values, tables, back):
    cosine, lower, upper = tables
    half_rot = ROT // 2
    moved = (
        pltpu.roll(values, 2 * HEAD - half_rot, 1) * lower + pltpu.roll(values, half_rot, 1) * upper
    )
    return values * cosine - moved if back else values * cosine + moved


VMEM_LIMIT = 63 * 1024 * 1024


def remote_call(kernel, identity, out_shape, in_specs, scratch, flops, name):
    return pl.pallas_call(
        kernel,
        out_shape=out_shape,
        in_specs=in_specs,
        out_specs=(VMEM_SPEC,) * len(out_shape),
        scratch_shapes=scratch,
        compiler_params=pltpu.CompilerParams(
            collective_id=identity, has_side_effects=True, vmem_limit_bytes=VMEM_LIMIT
        ),
        cost_estimate=pl.CostEstimate(flops=flops, bytes_accessed=1 << 24, transcendentals=0),
        name=name,
    )


MESH = pl.DeviceIdType.MESH
VMEM_SPEC = pl.BlockSpec(memory_space=pltpu.VMEM)


def remote(src, dst, send, recv, device):
    return pltpu.make_async_remote_copy(
        src_ref=src, dst_ref=dst, send_sem=send, recv_sem=recv, device_id=device, device_id_type=MESH
    )


class Place:
    def __init__(self):
        self.row, self.col = lax.axis_index("row"), lax.axis_index("col")
        self.rows, self.cols = lax.axis_size("row"), lax.axis_size("col")
        self.chips = self.rows // 2
        self.chip, self.core = self.row // 2, self.row % 2
        self.twin = (self.chip * 2 + 1 - self.core, self.col)
        self.ring = self.chips // 2
        self.y, self.z = self.chip // self.ring, self.chip % self.ring

    def chip_at(self, step):
        return lax.rem(self.chip + step, self.chips)

    def chip_row(self, step):
        return self.chip_at(step) * 2 + self.core

    def col_at(self, step):
        return lax.rem(self.col + step, self.cols)


def greet(devices):
    barrier = pltpu.get_barrier_semaphore()
    for device in devices:
        pl.semaphore_signal(barrier, inc=1, device_id=device, device_id_type=MESH)


def meet(devices):
    pl.semaphore_wait(pltpu.get_barrier_semaphore(), len(devices))


class HopGather:
    OWN, PARTNER, BELOW, ABOVE, BELOW_PARTNER, ABOVE_PARTNER, FAR, FAR_PARTNER = range(8)

    def __init__(self, at, axis, slot, sems):
        self.at, self.axis, self.slot = at, axis, slot
        self.sems = sems
        index, ring = (at.chip, at.chips // 2) if axis == "row" else (at.col, at.cols // 2)
        side, step = index // ring, index % ring

        def place(other, hops):
            return (1 - side if other else side) * ring + lax.rem(step + hops, ring)

        self.places = [
            place(False, 0),
            place(True, 0),
            place(False, ring - 1),
            place(False, 1),
            place(True, ring - 1),
            place(True, 1),
            place(False, 2),
            place(True, 2),
        ]

    def index(self, which):
        return self.places[which] * 2 + self.at.core if self.axis == "row" else self.places[which]

    def device(self, which):
        at = self.at
        return (self.index(which), at.col) if self.axis == "row" else (at.row, self.index(which))

    def block(self, which):
        return self.slot(self.index(which))

    def part(self, which, upper):
        ref = self.block(which)
        half = ref.shape[0] // 2
        return ref.at[pl.ds(0 if upper else half, half), :]

    def hop(self, tag, src, dst, to):
        send, recv = self.sems[0], self.sems[1]
        return remote(src, dst, send.at[tag], recv.at[tag], self.device(to))

    def took(self, tag, ref):
        self.hop(tag, ref, ref, self.PARTNER).wait_recv()

    def passing(self, which, src=None):
        send, recv = self.sems[2], self.sems[3]
        ref = self.block(which)
        return remote(
            ref if src is None else src, ref, send.at[which], recv.at[which], self.at.twin
        )

    def hops(self):
        own, src = self.block(self.OWN), self.src
        partner = self.block(self.PARTNER)
        below, above = self.part(self.BELOW, True), self.part(self.ABOVE, False)
        far = self.block(self.FAR)
        return {
            "start": [
                (0, src, own, self.PARTNER),
                (1, src, own, self.ABOVE),
                (2, src, own, self.BELOW),
            ],
            "partner": [(3, partner, partner, self.ABOVE), (4, partner, partner, self.BELOW)],
            "below": [(5, below, below, self.ABOVE)],
            "above": [(6, above, above, self.BELOW)],
            "far": [(7, far, far, self.PARTNER)],
        }

    def go(self, stage):
        for hop in self.hops()[stage]:
            self.hop(*hop).start()

    def start(self, src):
        self.src = src
        self.go("start")
        if self.axis == "row":
            self.passing(self.OWN, src).start()

    def landed(self, which):
        if self.axis == "row":
            self.passing(which).start()

    def steps(self):
        def first():
            self.took(1, self.block(self.BELOW))
            self.go("below")
            self.took(2, self.block(self.ABOVE))
            self.go("above")
            self.landed(self.BELOW)
            self.landed(self.ABOVE)

        def second():
            self.took(0, self.block(self.PARTNER))
            self.go("partner")
            self.landed(self.PARTNER)

        def third():
            self.took(5, self.part(self.FAR, True))
            self.took(6, self.part(self.FAR, False))
            self.go("far")
            self.landed(self.FAR)

        def fourth():
            self.took(3, self.block(self.BELOW_PARTNER))
            self.landed(self.BELOW_PARTNER)
            self.took(4, self.block(self.ABOVE_PARTNER))
            self.landed(self.ABOVE_PARTNER)
            self.took(7, self.block(self.FAR_PARTNER))
            self.landed(self.FAR_PARTNER)

        return [first, second, third, fourth]

    def finish(self):
        send, recv = self.sems[2], self.sems[3]
        for which in range(8):
            slot = self.slot(self.places[which] * 2 + 1 - self.at.core)
            remote(slot, slot, send.at[which], recv.at[which], self.at.twin).wait_recv()

    def sent(self):
        for stage in self.hops().values():
            for hop in stage:
                self.hop(*hop).wait_send()
        if self.axis == "row":
            self.passing(self.OWN, self.src).wait_send()
            for which in range(1, 8):
                self.passing(which).wait_send()


class Swap:
    def __init__(self, at, axis, src, dst, sems):
        self.at, self.axis, self.src, self.dst = at, axis, src, dst
        self.send, self.recv = sems
        self.me, self.size = (at.row, at.rows) if axis == "row" else (at.col, at.cols)

    def to(self, step):
        return lax.rem(self.me + step, self.size)

    def device(self, index):
        return (index, self.at.col) if self.axis == "row" else (self.at.row, index)

    def outgoing(self, step):
        to = self.to(step)
        return remote(
            self.src(to),
            self.dst(self.me),
            self.send.at[step],
            self.recv.at[step],
            self.device(to),
        )

    def start(self, which=None):
        for step in range(1, self.size):
            if which is None:
                self.outgoing(step).start()
            else:

                @pl.when(which(self.to(step)))
                def _():
                    self.outgoing(step).start()

    def arrived(self):
        for step in range(1, self.size):
            came = self.to(self.size - step)
            slot = self.dst(came)
            remote(
                slot, slot, self.send.at[step], self.recv.at[step], self.device(came)
            ).wait_recv()

    def sent(self):
        for step in range(1, self.size):
            self.outgoing(step).wait_send()


class RowSum:
    SEMS = 4

    def __init__(self, at, part, pairs, slots, sems):
        self.at, self.part, self.pairs, self.slots = at, part, pairs, slots
        self.twin_send, self.twin_recv, self.send, self.recv = sems

    def to_twin(self):
        at = self.at
        return remote(
            self.part.at[:, 1 - at.core],
            self.pairs,
            self.twin_send.at[0],
            self.twin_recv.at[0],
            at.twin,
        )

    def outgoing(self, step):
        at = self.at
        return remote(
            self.pairs.at[at.chip_at(step)],
            self.slots.at[at.chip],
            self.send.at[step],
            self.recv.at[step],
            (at.chip_row(step), at.col),
        )

    def start(self):
        self.to_twin().start()

    def add_twin(self):
        at = self.at
        self.to_twin().wait_recv()
        for chip in range(at.chips):
            both = self.part[chip, at.core].astype(f32) + self.pairs[chip].astype(f32)
            self.pairs[chip] = both.astype(bf16)

    def spread(self):
        for step in (4, 1, 2, 3, 5, 6, 7):
            self.outgoing(step).start()

    def middle(self):
        self.add_twin()
        self.spread()

    def finish(self):
        at = self.at
        total = self.pairs[at.chip].astype(f32)
        for step in range(1, at.chips):
            chip = at.chip_at(at.chips - step)
            slot = self.slots.at[chip]
            remote(
                slot, slot, self.send.at[step], self.recv.at[step], (chip * 2 + at.core, at.col)
            ).wait_recv()
            total = total + self.slots[chip].astype(f32)
        return total

    def released(self):
        self.to_twin().wait_send()

    def sent(self):
        for step in range(1, self.at.chips):
            self.outgoing(step).wait_send()


def sum_scratch(piece, width, chips):
    dma = pltpu.SemaphoreType.DMA
    return [
        pltpu.VMEM((chips, piece, width), bf16),
        pltpu.VMEM((chips, piece, width), bf16),
        dma((1,)),
        dma((1,)),
        dma((chips,)),
        dma((chips,)),
    ]


def moved_rows(index_row, first, count, values):
    shape = (count, index_row.shape[1])
    here = first + lax.broadcasted_iota(jnp.int32, shape, 0) == index_row
    return dot_nn(jnp.where(here, 1.0, 0.0).astype(bf16), values)


def flat(ref, size):
    return jnp.concatenate([ref[index, :size, :] for index in range(ref.shape[0])], axis=0)


def pack_rows(index_ref, values, out_refs, lanes):
    blocks = out_refs[0].shape[0]
    size = index_ref[1]
    for first in range(0, blocks, 4):
        found = moved_rows(index_ref[0][...], first * size, 4 * size, values).astype(bf16)
        for index in range(4):
            part = found[index * size : (index + 1) * size, :]
            for which, out_ref in enumerate(out_refs):
                out_ref[first + index, :size, :] = part[:, which * lanes : (which + 1) * lanes]


def every_row(at):
    return [(lax.rem(at.row + step, at.rows), at.col) for step in range(1, at.rows)]


def row_peers(at):
    return [(at.chip_row(step), at.col) for step in range(1, at.chips)] + [at.twin]


def col_peers(at):
    return [(at.row, at.col_at(step)) for step in range(1, at.cols)]


def gather_sems():
    return [pltpu.SemaphoreType.DMA((count,)) for count in (8, 8, 8, 8)]


def hop_sems():
    return [pltpu.SemaphoreType.DMA((8,))] * 2


def swap_sems(cols):
    return [pltpu.SemaphoreType.DMA((cols,))] * 2


def split(x):
    high_part = x.astype(bf16)
    return high_part, (x - high_part.astype(f32)).astype(bf16)


def three(dot, left, right):
    return dot(left[0], right[0]) + (dot(left[0], right[1]) + dot(left[1], right[0]))


BLK = 128


def layer_kernel(
    tokens_ref,
    cotangent_ref,
    lengths_ref,
    deal_ref,
    norm_ref,
    bias_ref,
    qkv_weight_ref,
    up_weight_ref,
    proj_weight_ref,
    down_weight_ref,
    qkv_momentum_ref,
    up_momentum_ref,
    proj_momentum_ref,
    down_momentum_ref,
    pick_ref,
    pack_ref,
    vector_all_ref,
    normalized_ref,
    inverse_std_ref,
    in_grad_ref,
    out_grad_ref,
    bias_grad_ref,
    matrix_ref,
    gram_ref,
    normed_twins_ref,
    branch_sum_ref,
    normed_part_ref,
    take_back_ref,
    send_back_ref,
    weight_ref,
    vector_ref,
    table_ref,
    start_ref,
    momentum_ref,
    dealt_ref,
    cot_dealt_ref,
    weight_all_ref,
    q_ref,
    k_ref,
    v_ref,
    slope_ref,
    branch_ref,
    attended_ref,
    total_ref,
    out_part,
    pairs,
    values,
    out_rows_tokens,
    in_rows_tokens,
    out_rows_cots,
    in_rows_cots,
    out_tokens,
    in_tokens,
    out_cots,
    in_cots,
    pre_ref,
    dk_ref,
    dv_ref,
    out_parts,
    up_part,
    up_parts,
    qkv_part,
    qkv_parts,
    bias_part,
    biases,
    chunks,
    products,
    from_twin,
    half_sum,
    slices,
    twin_sums,
    slots,
    *sems,
):
    at = Place()
    held, feats = tokens_ref.shape
    piece = out_tokens.shape[1]
    capacity = out_rows_tokens.shape[1]
    depth = weight_ref.shape[0]
    sems = list(sems)

    def some(count):
        taken, sems[:count] = sems[:count], []
        return taken

    def block(ref):
        return lambda index: ref.at[index]

    def dealt_slot(ref):
        return lambda row: ref.at[pl.ds(row * piece, piece), :]

    last_tokens = HopGather(at, "row", dealt_slot(dealt_ref), some(4))
    last_cots = HopGather(at, "row", dealt_slot(cot_dealt_ref), some(4))
    rows_tokens = Swap(at, "row", block(out_rows_tokens), block(in_rows_tokens), some(2))
    rows_cots = Swap(at, "row", block(out_rows_cots), block(in_rows_cots), some(2))
    swap_tokens = Swap(at, "col", block(out_tokens), block(in_tokens), some(2))
    swap_cots = Swap(at, "col", block(out_cots), block(in_cots), some(2))
    weights = HopGather(
        at, "col", lambda c: weight_all_ref.at[pl.ds(c * depth, depth), :], some(2)
    )
    swap_vector = Swap(at, "col", lambda c: vector_ref, block(vector_all_ref), some(2))

    branch_rows = RowSum(at, normed_part_ref, twin_sums, slots, some(4))
    swap_out = Swap(at, "col", block(out_part), block(out_parts), some(2))
    swap_up = Swap(at, "col", block(up_part), block(up_parts), some(2))
    swap_qkv = Swap(at, "col", block(qkv_part), block(qkv_parts), some(2))
    swap_bias = Swap(at, "col", lambda c: bias_part, block(biases), some(2))
    swap_chunk = Swap(at, "col", block(chunks), block(matrix_ref), some(2))
    normed_rows = RowSum(at, normed_part_ref, normed_twins_ref, None, [*some(2), None, None])
    twin_send, twin_recv, sum_send, sum_recv, all_send, all_recv, pass_send, pass_recv = some(8)
    count = at.chips * 2
    mine = at.chip * 2 + at.col % 2
    first_col = at.col - at.col % 2

    def member(step):
        other = lax.rem(mine + step, count)
        return other, ((other // 2) * 2 + at.core, first_col + other % 2)

    peers = [member(step)[1] for step in range(1, count)]

    def pick(in_ref, out_ref):
        pack_rows((send_back_ref, piece), flat(in_ref, capacity), [out_ref], feats)

    everyone = every_row(at) + col_peers(at) + peers
    greet(everyone)
    plan = Plan(at, lengths_ref, deal_ref, held)
    take_back_ref[...] = plan.take_back()
    vector_ref[...] = jnp.zeros_like(vector_ref)
    vector_ref[: norm_ref.shape[0], :] = norm_ref[...]
    both = jnp.concatenate([tokens_ref[...], cotangent_ref[...]], axis=1)
    pack_rows((take_back_ref, capacity), both, [out_rows_tokens, out_rows_cots], feats)
    meet(everyone)
    rows_tokens.start()
    swap_vector.start()
    send_back_ref[...] = plan.listed(True)
    up = up_weight_ref.shape[1]
    weight_ref[...] = jnp.zeros_like(weight_ref)
    momentum_ref[...] = jnp.zeros_like(momentum_ref)
    for first, ref in (
        (0, qkv_weight_ref),
        (2 * up, proj_weight_ref),
        (2 * up + 2 * HEAD, down_weight_ref),
    ):
        weight_ref[:, first : first + ref.shape[0]] = ref[...].T.astype(bf16)
    weight_ref[:, up : 2 * up] = up_weight_ref[...].astype(bf16)
    weight_all_ref[pl.ds(at.col * depth, depth), :] = weight_ref[...]
    vector_all_ref[at.col] = vector_ref[...]
    in_rows_tokens[at.row] = out_rows_tokens[at.row]
    in_rows_cots[at.row] = out_rows_cots[at.row]

    rows_tokens.arrived()
    rows_cots.start()
    pick(in_rows_tokens, out_tokens)
    swap_tokens.start()
    in_tokens[at.col] = out_tokens[at.col]
    start_ref[...] = plan.block_starts()
    table_ref[...] = plan.rotary()

    swap_vector.arrived()
    swap_tokens.arrived()
    weights.start(weight_ref)
    width = at.cols * feats
    parts = [in_tokens[f].astype(f32) for f in range(at.cols)]
    mean = sum(jnp.sum(part, axis=1, keepdims=True) for part in parts) / width
    parts = [part - mean for part in parts]
    variance = sum(jnp.sum(part * part, axis=1, keepdims=True) for part in parts) / width
    inverse_std = lax.rsqrt(variance + norm_floor)
    inverse_std_ref[...] = inverse_std
    own = pl.ds(at.row * piece, piece)
    for f in range(at.cols):
        lanes = slice(f * feats, (f + 1) * feats)
        normalized = parts[f] * inverse_std
        normalized_ref[:, lanes] = normalized
        vectors = vector_all_ref[f]
        dealt_ref[own, lanes] = (normalized * vectors[0:1, :] + vectors[1:2, :]).astype(bf16)
    last_tokens.start(dealt_ref.at[own, :])
    token_steps, weight_steps = iter(last_tokens.steps()), iter(weights.steps())
    cot_steps = iter(last_cots.steps())
    rows_cots.arrived()
    pick(in_rows_cots, out_cots)
    swap_cots.start()
    in_cots[at.col] = out_cots[at.col]
    next(weight_steps)()
    next(token_steps)()
    pick_ref[...] = plan.pick()
    pack_ref[...] = plan.listed(False)
    for first, ref in (
        (0, qkv_momentum_ref),
        (2 * up, proj_momentum_ref),
        (3 * up, down_momentum_ref),
    ):
        momentum_ref[:, first : first + ref.shape[0]] = ref[...].T
    momentum_ref[:, up : 2 * up] = up_momentum_ref[...]
    next(weight_steps)()
    next(token_steps)()
    swap_cots.arrived()
    for f in range(at.cols):
        cot_dealt_ref[own, f * feats : (f + 1) * feats] = in_cots[f]
    last_cots.start(cot_dealt_ref.at[own, :])
    next(weight_steps)()
    next(token_steps)()
    next(weight_steps)()
    next(token_steps)()
    next(cot_steps)()
    last_tokens.finish()

    in_width = bias_ref.shape[1]
    tokens = dealt_ref.shape[0]
    rows_all = tokens // PIECE
    in_weight, out_weight = weight_all_ref[:, :in_width], weight_all_ref[:, in_width:]
    inner = math.sqrt(2.0 / math.pi)
    firsts = range(0, tokens, BLOCK)
    for first in firsts:
        if first == 4 * BLOCK:
            next(cot_steps)()
        rows = pl.ds(first, BLOCK)
        pre = dot_nn(dealt_ref[rows, :], in_weight) + bias_ref[...]
        pair = turned(pre[:, : 2 * HEAD], turning(table_ref, rows), False)
        for part in range(BLOCK // PIECE):
            these = slice(part * PIECE, (part + 1) * PIECE)
            spaced = pl.ds(first // PIECE + part, PIECE, stride=rows_all)
            pairs[spaced, :] = pair[these, :]
            values[spaced, :] = pre[these, 2 * HEAD : 4 * HEAD]
        up = pre[:, 4 * HEAD :]
        square = up * up
        bent = jnp.tanh(inner * (up + 0.044715 * square * up))
        branch_ref[rows, 2 * HEAD :] = (0.5 * up * (1.0 + bent)).astype(bf16)
        slope_ref[rows, :] = 0.5 * (1.0 + bent) + 0.5 * up * (1.0 - bent * bent) * (
            inner * (1.0 + 3.0 * 0.044715 * square)
        )
    for first in firsts:
        rows = pl.ds(first, BLOCK)
        pair = pairs[rows, :].astype(bf16)
        q_ref[rows, :] = (pair[:, :HEAD] * HEAD**-0.5).astype(bf16)
        k_ref[rows, :] = pair[:, HEAD:]
        v_ref[rows, :] = values[rows, :HEAD].astype(bf16)
    next(cot_steps)()
    for first in firsts:
        if first == 6 * BLOCK:
            next(cot_steps)()
        rows, keys = pl.ds(first, BLOCK), first + BLOCK
        scores = dot_nt(q_ref[rows, :], k_ref[:keys, :])
        scores = jnp.where(allowed_keys(start_ref, first, keys), scores, masked_score)
        top = jnp.max(scores, axis=1, keepdims=True)
        raw = jnp.exp(scores - top)
        total = jnp.sum(raw, axis=1, keepdims=True)
        attended = dot_nn(raw.astype(bf16), v_ref[:keys, :]) / total
        attended_ref[rows, :] = attended.astype(bf16)
        values[rows, :] = jnp.concatenate([attended, jnp.zeros_like(attended)], axis=1)
        total_ref[rows, :] = top + jnp.log(total)
    for first in firsts:
        rows = pl.ds(first, BLOCK)
        for part in range(BLOCK // PIECE):
            at_piece = first // PIECE + part
            branch_ref[at_piece * PIECE : (at_piece + 1) * PIECE, : 2 * HEAD] = values[
                pl.ds(at_piece, PIECE, stride=rows_all), :
            ].astype(bf16)
        partial = dot_nt(branch_ref[rows, :], out_weight).astype(bf16)
        for part in range(BLOCK // PIECE):
            at_piece = first // PIECE + part
            normed_part_ref[at_piece // 2, at_piece % 2] = partial[
                part * PIECE : (part + 1) * PIECE, :
            ]
    branch_rows.start()
    last_cots.finish()
    for first in range(0, cot_dealt_ref.shape[1], BLOCK):
        part = dot_tn(cot_dealt_ref[:, first : first + BLOCK], branch_ref[...]).astype(bf16)
        for index in range(BLOCK // feats):
            out_part[first // feats + index] = part[index * feats : (index + 1) * feats, :]
    swap_out.start()
    out_parts[at.col] = out_part[at.col]

    half = up_part.shape[2]

    def weight_part(ref, lanes):
        for first in range(0, dealt_ref.shape[1], BLOCK):
            part = dot_tn(dealt_ref[:, first : first + BLOCK], pre_ref[:, lanes])
            for index in range(BLOCK // feats):
                ref[first // feats + index] = part[
                    index * feats : (index + 1) * feats, :
                ].astype(bf16)

    def direction(index, grad):
        lanes = slice(index * BLK, (index + 1) * BLK)
        state = momentum * momentum_ref[:, lanes] + grad
        chunks[index] = grad + momentum * state

    for first in firsts:
        rows = pl.ds(first, BLOCK)
        branch_grad = dot_nn(cot_dealt_ref[rows, :], out_weight)
        for part in range(BLOCK // PIECE):
            these = slice(part * PIECE, (part + 1) * PIECE)
            spaced = pl.ds(first // PIECE + part, PIECE, stride=rows_all)
            values[spaced, :] = branch_grad[these, : 2 * HEAD]
        pre_ref[rows, 4 * HEAD :] = (branch_grad[:, 2 * HEAD :] * slope_ref[rows, :]).astype(bf16)
    weight_part(up_part, slice(half, 2 * half))
    swap_up.start()
    up_parts[at.col] = up_part[at.col]
    dk_ref[...] = jnp.zeros_like(dk_ref)
    dv_ref[...] = jnp.zeros_like(dv_ref)
    branch_rows.middle()
    for first in reversed(firsts):
        rows, keys = pl.ds(first, BLOCK), first + BLOCK
        query, grad = q_ref[rows, :], values[rows, :HEAD].astype(bf16)
        key, value = k_ref[:keys, :], v_ref[:keys, :]
        scores = dot_nt(query, key)
        allowed = allowed_keys(start_ref, first, keys)
        prob = jnp.where(allowed, jnp.exp(scores - total_ref[rows, :]), 0.0)
        delta = jnp.sum(
            grad.astype(f32) * attended_ref[rows, :].astype(f32), axis=1, keepdims=True
        )
        score_grad = (prob * (dot_nt(grad, value) - delta)).astype(bf16)
        dk_ref[:keys, :] += dot_tn(score_grad, query)
        dv_ref[:keys, :] += dot_tn(prob.astype(bf16), grad)
        pairs[rows, :] = jnp.concatenate(
            [dot_nn(score_grad, key) * HEAD**-0.5, dk_ref[rows, :]], axis=1
        )
        dv = dv_ref[rows, :]
        values[rows, :] = jnp.concatenate([dv, jnp.zeros_like(dv)], axis=1)
    for first in firsts:
        rows = pl.ds(first, BLOCK)
        pair, value = [
            jnp.concatenate(
                [
                    ref[pl.ds(first // PIECE + part, PIECE, stride=rows_all), :]
                    for part in range(BLOCK // PIECE)
                ],
                axis=0,
            )
            for ref in (pairs, values)
        ]
        pre_ref[rows, : 2 * HEAD] = turned(pair, turning(table_ref, rows), True).astype(bf16)
        pre_ref[rows, 2 * HEAD : 4 * HEAD] = value.astype(bf16)
    weight_part(qkv_part, slice(0, half))
    swap_qkv.start()
    qkv_parts[at.col] = qkv_part[at.col]
    bias = jnp.sum(pre_ref[...].astype(f32), axis=0, keepdims=True)
    bias_part[...] = jnp.broadcast_to(bias, bias_part.shape)
    swap_bias.start()
    biases[at.col] = bias_part[...]
    branch_rows.released()
    for first in firsts:
        rows = pl.ds(first, BLOCK)
        partial = dot_nt(pre_ref[rows, :], in_weight).astype(bf16)
        for part in range(BLOCK // PIECE):
            at_piece = first // PIECE + part
            normed_part_ref[at_piece // 2, at_piece % 2] = partial[
                part * PIECE : (part + 1) * PIECE, :
            ]

    normed_rows.start()
    swap_out.arrived()
    total = sum(out_parts[c].astype(f32) for c in range(at.cols))
    filled = jnp.zeros((feats, half - 2 * HEAD), f32)
    out_grad = jnp.concatenate([total[:, : 2 * HEAD], filled, total[:, 2 * HEAD :]], axis=1)
    out_grad_ref[...] = out_grad
    swap_up.arrived()
    up_grad = sum(up_parts[c].astype(f32) for c in range(at.cols))
    in_grad_ref[:, half:] = up_grad
    late = half // BLK
    for index in range(late, at.cols):
        first = (index - late) * BLK
        if first < half:
            direction(index, up_grad[:, first : first + BLK])
        else:
            direction(index, out_grad[:, first - half : first - half + BLK])
    swap_chunk.start(lambda to: to >= late)
    swap_qkv.arrived()
    qkv_grad = sum(qkv_parts[c].astype(f32) for c in range(at.cols))
    in_grad_ref[:, :half] = qkv_grad
    for index in range(late):
        direction(index, qkv_grad[:, index * BLK : (index + 1) * BLK])
    swap_chunk.start(lambda to: to < late)
    matrix_ref[at.col] = chunks[at.col]
    swap_bias.arrived()
    bias_grad_ref[...] = sum(biases[c] for c in range(at.cols))
    swap_chunk.arrived()

    strips = matrix_ref.shape[0]
    matrix = split(matrix_ref[...].reshape(strips * BLK, BLK))
    index = 0
    for i in range(strips):
        left = [m[i * BLK : (i + 1) * BLK, :] for m in matrix]
        right = [m[i * BLK :, :] for m in matrix]
        product = three(dot_nt, left, right)
        for j in range(strips - i):
            products[index] = product[:, j * BLK : (j + 1) * BLK]
            index += 1
    blocks = index // 2
    half_rows = blocks * BLK
    each = blocks // 2
    size = each * BLK // count

    def to_twin(group):
        return remote(
            products.at[pl.ds((1 - at.core) * blocks + group * each, each)],
            from_twin.at[pl.ds(group * each, each)],
            twin_send.at[group],
            twin_recv.at[group],
            at.twin,
        )

    def give(step, group):
        owner, device = member(step)
        return remote(
            half_sum.at[pl.ds(group * each * BLK + owner * size, size), :],
            slices.at[group, mine],
            sum_send.at[group * count + step],
            sum_recv.at[group * count + step],
            device,
        )

    def home(owner, group, core):
        first = core * half_rows + group * each * BLK + owner * size
        return gram_ref.at[pl.ds(first, size), :]

    def spread(step, group):
        slot = home(mine, group, at.core)
        sems_at = group * count + step
        return remote(slot, slot, all_send.at[sems_at], all_recv.at[sems_at], member(step)[1])

    def passing(step, group):
        slot = home(member(count - step)[0] if step else mine, group, at.core)
        sems_at = group * count + step
        return remote(slot, slot, pass_send.at[sems_at], pass_recv.at[sems_at], at.twin)

    for group in range(2):
        to_twin(group).start()
    for group in range(2):
        to_twin(group).wait_recv()
        for b in range(group * each, (group + 1) * each):
            half_sum[b * BLK : (b + 1) * BLK, :] = products[at.core * blocks + b] + from_twin[b]
        for step in range(1, count):
            give(step, group).start()
        slices[group, mine] = half_sum[pl.ds(group * each * BLK + mine * size, size), :]
    normed_rows.add_twin()
    for group in range(2):
        for step in range(1, count):
            came, device = member(count - step)
            slot = slices.at[group, came]
            sems_at = group * count + step
            remote(slot, slot, sum_send.at[sems_at], sum_recv.at[sems_at], device).wait_recv()
        total = slices[group, 0]
        for index in range(1, count):
            total = total + slices[group, index]
        first = at.core * half_rows + group * each * BLK + mine * size
        gram_ref[pl.ds(first, size), :] = total
        for step in range(1, count):
            spread(step, group).start()
        passing(0, group).start()
    for group in range(2):
        for step in range(1, count):
            came, device = member(count - step)
            slot = home(came, group, at.core)
            sems_at = group * count + step
            remote(slot, slot, all_send.at[sems_at], all_recv.at[sems_at], device).wait_recv()
            passing(step, group).start()
    for group in range(2):
        for step in range(count):
            slot = home(lax.rem(mine + count - step, count), group, 1 - at.core)
            sems_at = group * count + step
            remote(slot, slot, pass_send.at[sems_at], pass_recv.at[sems_at], at.twin).wait_recv()
            passing(step, group).wait_send()
    for group in range(2):
        to_twin(group).wait_send()
        for step in range(1, count):
            give(step, group).wait_send()
            spread(step, group).wait_send()
    branch_sum_ref[...] = branch_rows.finish().astype(bf16)
    branch_rows.sent()
    normed_rows.released()
    for moved in (last_tokens, last_cots, weights, rows_tokens, rows_cots):
        moved.sent()
    for moved in (swap_tokens, swap_cots, swap_vector):
        moved.sent()
    for moved in (swap_out, swap_up, swap_qkv, swap_bias, swap_chunk):
        moved.sent()


WIDE = 256


def poly_kernel(
    gram_ref,
    matrix_ref,
    twin_sums_ref,
    branch_ref,
    normalized_ref,
    inverse_std_ref,
    vector_ref,
    tokens_ref,
    cotangent_ref,
    pick_ref,
    pack_ref,
    update_ref,
    output_ref,
    input_grad_ref,
    vector_sum_ref,
    own_update,
    normed_ref,
    out_branch,
    in_branch,
    out_rows_branch,
    in_rows_branch,
    out_token,
    in_token,
    out_rows,
    in_rows,
    slots,
    *buffers,
):
    at = Place()
    sems, buffers = buffers[8:], buffers[:8]

    def block(ref):
        return lambda index: ref.at[index]

    swap_token = Swap(at, "col", block(out_token), block(in_token), sems[0:2])
    rows_token = Swap(at, "row", block(out_rows), block(in_rows), sems[2:4])
    feats = out_token.shape[2]
    swap_update = Swap(
        at,
        "col",
        lambda c: own_update.at[pl.ds(c * feats, feats), :],
        block(update_ref),
        sems[4:6],
    )
    swap_branch = Swap(at, "col", block(out_branch), block(in_branch), sems[6:8])
    rows_branch = Swap(at, "row", block(out_rows_branch), block(in_rows_branch), sems[8:10])
    normed_rows = RowSum(at, None, twin_sums_ref, slots, [None, None, *sems[10:12]])
    piece, capacity = normed_ref.shape[0], out_rows_branch.shape[1]
    lanes = [slice(f * feats, (f + 1) * feats) for f in range(at.cols)]
    for f in range(at.cols):
        out_branch[f] = branch_ref[:, lanes[f]]
    everyone = every_row(at) + col_peers(at)
    greet(everyone)

    def branch_back():
        swap_branch.arrived()
        pack_rows((pick_ref, capacity), flat(in_branch, piece), [out_rows_branch], feats)
        rows_branch.start()
        in_rows_branch[at.row] = out_rows_branch[at.row]

    def home(rows_ref, base_ref, shift, out_ref):
        values = flat(rows_ref, capacity)
        for first in range(0, out_ref.shape[0], BLOCK):
            rows = pl.ds(first, BLOCK)
            found = moved_rows(pack_ref[...], first, BLOCK, values)
            out_ref[rows, :] = found + base_ref[rows, :].astype(f32) + shift

    def branch_home():
        rows_branch.arrived()
        home(in_rows_branch, tokens_ref, vector_ref[at.col][2:3, :], output_ref)

    def extra(vectors):
        parts = [part.astype(f32) for vector in vectors for part in split(vector)]
        empty = jnp.zeros((EXTRA - len(parts), feats), f32)
        return jnp.concatenate([*parts, empty], axis=0).astype(bf16)

    def token_grads():
        normed_ref[...] = normed_rows.finish()
        width = at.cols * feats
        scaled = [normed_ref[:, lanes[f]] * vector_ref[f][0:1, :] for f in range(at.cols)]
        mean_first = sum(jnp.sum(part, axis=1, keepdims=True) for part in scaled) / width
        mean_second = (
            sum(
                jnp.sum(part * normalized_ref[:, lanes[f]], axis=1, keepdims=True)
                for f, part in enumerate(scaled)
            )
            / width
        )
        for f in range(at.cols):
            normalized, grad = normalized_ref[:, lanes[f]], normed_ref[:, lanes[f]]
            token_grad = inverse_std_ref[...] * (scaled[f] - mean_first - normalized * mean_second)
            out_token[f, :piece, :] = token_grad.astype(bf16)
            gain_grad = jnp.sum(grad * normalized, axis=0, keepdims=True)
            shift_grad = jnp.sum(grad, axis=0, keepdims=True)
            out_token[f, piece:, :] = extra([gain_grad, shift_grad])
        swap_token.start()
        in_token[at.col] = out_token[at.col]

    def token_back():
        cot_sum = jnp.sum(cotangent_ref[...].astype(f32), axis=0, keepdims=True)
        swap_token.arrived()
        pack_rows((pick_ref, capacity), flat(in_token, piece), [out_rows], feats)
        sums = sum(in_token[c, piece:, :].astype(f32) for c in range(at.cols))
        sums = extra([sums[0:1, :] + sums[1:2, :], sums[2:3, :] + sums[3:4, :], cot_sum])
        for row in range(at.rows):
            out_rows[row, capacity:, :] = sums
        rows_token.start()
        in_rows[at.row] = out_rows[at.row]

    first, second, third, thin = [buffers[2 * i : 2 * i + 2] for i in range(4)]
    strips = matrix_ref.shape[0]
    size = strips * BLK
    counts = range(size // WIDE)
    eye = lax.broadcasted_iota(jnp.int32, (BLK, BLK), 0) == lax.broadcasted_iota(
        jnp.int32, (BLK, BLK), 1
    )

    def put(pair, rows, lanes, value):
        high_part, low_part = split(value)
        pair[0][rows, lanes] = high_part
        pair[1][rows, lanes] = low_part

    def get(pair, rows, lanes):
        return pair[0][rows, lanes], pair[1][rows, lanes]

    places, index = [], 0
    for i in range(strips):
        for j in range(i, strips):
            places.append((i, j, index))
            index += 1
    trace = sum(
        jnp.sum(jnp.where(eye, gram_ref[spot * BLK : (spot + 1) * BLK, :], 0.0))
        for i, j, spot in places
        if i == j
    )
    shrink = 1.0 / (jnp.sqrt(jnp.full((1, 1), trace, f32)) + ortho_floor)
    for i, j, spot in places:
        block = gram_ref[spot * BLK : (spot + 1) * BLK, :] * (shrink * shrink)
        here, there = slice(i * BLK, (i + 1) * BLK), slice(j * BLK, (j + 1) * BLK)
        put(first, here, there, block)
        if j > i:
            put(first, there, here, block.T)
    everything = slice(0, size)
    for i in range(strips):
        put(thin, slice(i * BLK, (i + 1) * BLK), everything, matrix_ref[i] * shrink)

    meet(everyone)
    swap_branch.start()
    in_branch[at.col] = out_branch[at.col]
    normed_rows.spread()

    def product(left, right, out, finish=None):
        for i in counts:
            rows, rest = slice(i * WIDE, (i + 1) * WIDE), slice(i * WIDE, size)
            value = three(dot_nn, get(left, rows, everything), get(right, everything, rest))
            if finish is not None:
                value = finish(value, rows, rest)
            put(out, rows, rest, value)
            for j in range(i + 1, size // WIDE):
                part = value[:, (j - i) * WIDE : (j - i + 1) * WIDE]
                put(out, slice(j * WIDE, (j + 1) * WIDE), rows, part.T)

    def thin_product(left):
        right = get(thin, everything, everything)
        width = right[0].shape[1]
        both = jnp.concatenate(right, axis=1)
        found = []
        for i in counts:
            high_part, low_part = get(left, slice(i * WIDE, (i + 1) * WIDE), everything)
            value = dot_nn(high_part, both)
            found.append(value[:, :width] + (value[:, width:] + dot_nn(low_part, right[0])))
        return found

    def sweep(gram, poly, square, between=lambda: None):
        def finish(value, rows, rest):
            high_part, low_part = get(gram, rows, rest)
            value = poly_cubic * value + poly_square * (
                high_part.astype(f32) + low_part.astype(f32)
            )
            at_row = lax.broadcasted_iota(jnp.int32, value.shape, 0)
            at_lane = lax.broadcasted_iota(jnp.int32, value.shape, 1)
            return value + jnp.where(at_row == at_lane, poly_linear, 0.0)

        product(gram, gram, poly, finish)
        between()
        for i, value in zip(counts, thin_product(poly)):
            put(thin, slice(i * WIDE, (i + 1) * WIDE), everything, value)
        product(poly, poly, square)
        product(gram, square, poly)

    def two(step, carry):
        def early():
            @pl.when(step == 0)
            def _():
                branch_back()

            @pl.when(step == 1)
            def _():
                token_grads()

        def late():
            @pl.when(step == 1)
            def _():
                branch_home()

        sweep(first, second, third, early)

        @pl.when(step == 1)
        def _():
            token_back()

        sweep(second, first, third, late)
        return carry

    lax.fori_loop(0, 2, two, 0)
    once = thin_product(first)
    old = []
    for i in counts:
        rows = slice(i * WIDE, (i + 1) * WIDE)
        high_part, low_part = get(thin, rows, everything)
        old.append(high_part.astype(f32) + low_part.astype(f32))
    for i, value in zip(counts, once):
        put(thin, slice(i * WIDE, (i + 1) * WIDE), everything, value)
    for i, value in zip(counts, thin_product(first)):
        result = poly_linear * old[i] + poly_square * once[i] + poly_cubic * value
        own_update[i * WIDE : (i + 1) * WIDE, :] = result.astype(bf16)
    swap_update.start()
    update_ref[at.col] = own_update[pl.ds(at.col * feats, feats), :]

    rows_token.arrived()
    home(in_rows, cotangent_ref, 0.0, input_grad_ref)
    vector_sum_ref[...] = sum(
        in_rows[row, capacity:, :].astype(f32) for row in range(at.rows)
    )
    swap_update.arrived()
    for moved in (swap_token, rows_token, swap_update, swap_branch, rows_branch, normed_rows):
        moved.sent()


def orthogonalize(
    gram,
    matrix,
    twin_sums,
    branch_sum,
    normalized,
    inverse_std,
    vectors,
    tokens,
    cotangent,
    pick,
    pack,
    rows,
):
    cols, feats, width = matrix.shape
    size = cols * BLK
    piece, full = branch_sum.shape
    held = cotangent.shape[0]
    chips = rows // 2
    capacity = pack.shape[1] // rows
    shape = jax.ShapeDtypeStruct
    square, narrow = pltpu.VMEM((size, size), bf16), pltpu.VMEM((size, width), bf16)
    return remote_call(
        poly_kernel,
        3,
        (
            shape((cols, feats, width), bf16),
            shape((held, feats), f32),
            shape((held, feats), f32),
            shape((EXTRA, feats), f32),
        ),
        [VMEM_SPEC] * 11,
        [
            narrow,
            pltpu.VMEM((piece, full), f32),
            *([pltpu.VMEM((cols, piece, feats), bf16)] * 2),
            *([pltpu.VMEM((rows, capacity, feats), bf16)] * 2),
            *([pltpu.VMEM((cols, piece + EXTRA, feats), bf16)] * 2),
            *([pltpu.VMEM((rows, capacity + EXTRA, feats), bf16)] * 2),
            sum_scratch(piece, full, chips)[0],
            *([square] * 6),
            *([narrow] * 2),
            *swap_sems(cols),
            *swap_sems(rows),
            *(swap_sems(cols) * 2),
            *swap_sems(rows),
            *sum_scratch(piece, full, chips)[4:],
        ],
        60 * 10**9,
        "orthogonalize",
    )(
        *(gram, matrix, twin_sums, branch_sum, normalized),
        *(inverse_std, vectors, tokens, cotangent, pick, pack),
    )


def layer(tokens, cotangent, lengths, deal_order, vectors, bias, weights, momenta, rows, cols):
    held, feats = tokens.shape
    group = held * rows // cols
    piece, width, chips = group // rows, feats * cols, rows // 2
    in_width = bias.shape[1]
    up = in_width - 4 * HEAD
    branch = up + 2 * HEAD
    capacity = CAPACITY
    depth, tile = feats, 2 * up + branch
    blocks = cols * (cols + 1) // 2
    count = chips * 2
    half_rows = blocks * BLK // 2
    shape, vmem = jax.ShapeDtypeStruct, pltpu.VMEM
    dma = pltpu.SemaphoreType.DMA
    return remote_call(
        layer_kernel,
        0,
        (
            shape((1, cols * piece), jnp.int32),
            shape((1, rows * capacity), jnp.int32),
            shape((cols, 8, feats), f32),
            shape((piece, width), f32),
            shape((piece, 1), f32),
            shape((feats, in_width), f32),
            shape((feats, in_width), f32),
            shape((8, in_width), f32),
            shape((cols, feats, BLK), f32),
            shape((blocks * BLK, BLK), f32),
            shape((chips, piece, width), bf16),
            shape((piece, width), bf16),
        ),
        [VMEM_SPEC] * 14,
        [
            vmem((chips, 2, piece, width), bf16),
            vmem((1, held), jnp.int32),
            vmem((1, rows * capacity), jnp.int32),
            vmem((depth, tile), bf16),
            vmem((8, feats), f32),
            vmem((4 * ROT // 2, group), bf16),
            vmem((group, 1), jnp.int32),
            vmem((depth, 4 * up), f32),
            *([vmem((group, width), bf16)] * 2),
            vmem((depth * cols, tile), bf16),
            *([vmem((group, HEAD), bf16)] * 3),
            vmem((group, up), f32),
            vmem((group, branch), bf16),
            vmem((group, HEAD), bf16),
            vmem((group, 1), f32),
            vmem((cols, feats, branch), bf16),
            *([vmem((group, 2 * HEAD), f32)] * 2),
            *([vmem((rows, capacity, feats), bf16)] * 4),
            *([vmem((cols, piece, feats), bf16)] * 4),
            vmem((group, in_width), bf16),
            *([vmem((group, HEAD), f32)] * 2),
            vmem((cols, feats, branch), bf16),
            *([vmem((cols, feats, up), bf16)] * 4),
            vmem((8, in_width), f32),
            vmem((cols, 8, in_width), f32),
            vmem((cols, feats, BLK), f32),
            vmem((blocks, BLK, BLK), f32),
            vmem((blocks // 2, BLK, BLK), f32),
            vmem((half_rows, BLK), f32),
            vmem((2, count, half_rows // count // 2, BLK), f32),
            *sum_scratch(piece, width, chips)[:2],
            *(gather_sems() * 2),
            *(swap_sems(rows) * 2),
            *(swap_sems(cols) * 2),
            *hop_sems(),
            *swap_sems(cols),
            *sum_scratch(piece, width, chips)[2:],
            *(swap_sems(cols) * 5),
            *([dma((1,))] * 2),
            *([dma((2,))] * 2),
            *([dma((2 * count,))] * 6),
        ],
        150 * 10**9,
        "layer",
    )(tokens, cotangent, lengths, deal_order, vectors, bias, *weights, *momenta)


CAPACITY = 96


def column_sum(x):
    return jnp.sum(x.astype(f32), axis=0, keepdims=True).astype(jnp.int32)


def lane_sum(x):
    return jnp.sum(x.astype(f32), axis=1, keepdims=True).astype(jnp.int32)


class Plan:
    def __init__(self, at, lengths_ref, deal_ref, held):
        self.at, self.held = at, held
        total = held * at.rows
        self.group = total // at.cols
        self.piece = self.group // at.rows
        self.length_row = lengths_ref[...]
        slots = self.length_row.shape[1]
        self.slots = slots
        square = (slots, slots)
        below = lax.broadcasted_iota(jnp.int32, square, 1)
        above = lax.broadcasted_iota(jnp.int32, square, 0)
        self.same = below == above
        self.strict = jnp.where(below < above, 1.0, 0.0).astype(bf16)
        lengths = jnp.broadcast_to(self.length_row, square)
        self.starts = lane_sum(jnp.where(below < above, lengths, 0))
        self.ends = lane_sum(jnp.where(below <= above, lengths, 0))
        shape = deal_ref.shape
        position = lax.broadcasted_iota(jnp.int32, shape, 0) * shape[1]
        position = (position + lax.broadcasted_iota(jnp.int32, shape, 1)).astype(f32)
        deal = deal_ref[...]
        found = [
            jnp.sum(
                jnp.where(deal == self.starts[slot : slot + 1, :], position, 0.0),
                axis=0,
                keepdims=True,
            )
            for slot in range(slots)
        ]
        self.dealt = lane_sum(jnp.concatenate(found, axis=0))
        self.shift = self.dealt - self.starts

    def passed(self, x, to):
        rows = self.at.rows
        return (x + (rows - 1 - to)) >> int(math.log2(rows))

    def clipped(self, x, first):
        return jnp.minimum(jnp.maximum(x, first), first + self.held)

    def rank(self, token, holder, to):
        first = holder * self.held
        low = self.clipped(self.starts, first)
        high = jnp.maximum(self.clipped(jnp.minimum(self.ends, token), first), low)
        return column_sum(self.passed(high + self.shift, to) - self.passed(low + self.shift, to))

    def lanes(self, count):
        return lax.broadcasted_iota(jnp.int32, (1, count), 1)

    def take_back(self):
        token = self.at.row * self.held + self.lanes(self.held)
        holds = (self.starts <= token) & (token < self.ends)
        to = (token + column_sum(jnp.where(holds, self.shift, 0))) % self.at.rows
        return to * CAPACITY + self.rank(token, self.at.row, to)

    def in_dealt(self, position):
        lengths = self.ends - self.starts
        return (self.dealt <= position) & (position < self.dealt + lengths)

    def pick(self):
        at = self.at
        slot = self.lanes(at.cols * self.piece)
        position = (slot // self.piece) * self.group + (slot % self.piece) * at.rows + at.row
        inside = self.in_dealt(position)
        token = position - column_sum(jnp.where(inside, self.shift, 0))
        holder = token // self.held
        return holder * CAPACITY + self.rank(token, holder, at.row)

    def listed(self, holder_is_lane):
        at = self.at
        lane = self.lanes(at.rows * CAPACITY)
        which = sum(jnp.where(lane >= CAPACITY * row, 1, 0) for row in range(1, at.rows))
        slot = lane - CAPACITY * which
        holder, to = (which, at.row) if holder_is_lane else (at.row, which)
        first = holder * self.held
        begin = self.passed(self.clipped(self.starts, first) + self.shift, to)
        count = self.passed(self.clipped(self.ends, first) + self.shift, to) - begin
        before = dot_nn(self.strict, count.astype(f32).astype(bf16)).astype(jnp.int32)
        inside = slot - before
        found = (inside >= 0) & (inside < count)
        dealt = at.rows * (begin + inside) + to
        used = column_sum(jnp.where(found, 1, 0)) > 0
        if holder_is_lane:
            block = dealt // self.group
            rest = dealt % self.group
            value = block * self.piece + rest // at.rows
        else:
            value = dealt - self.shift - first
        return jnp.where(used, column_sum(jnp.where(found, value, 0)), -1)

    def block_starts(self):
        shape = (self.group, self.slots)
        first = self.at.col * self.group
        position = first + lax.broadcasted_iota(jnp.int32, shape, 0)
        dealt = column_sum(jnp.where(self.same, self.dealt, 0))
        inside = (dealt <= position) & (position < dealt + self.length_row)
        return lane_sum(jnp.where(inside, dealt - first, 0))

    def rotary(self):
        half_rot = ROT // 2
        lane = self.lanes(self.group)
        position = self.at.col * self.group + (lane % self.piece) * self.at.rows
        position = position + lane // self.piece
        inside = self.in_dealt(position)
        place = position - column_sum(jnp.where(inside, self.dealt, 0))
        entry = lax.broadcasted_iota(jnp.int32, (half_rot, 1), 0)
        inverse = sum(
            jnp.where(entry == index, 1.0 / 10000.0 ** (index * 2.0 / ROT), 0.0)
            for index in range(half_rot)
        )
        angles = inverse.astype(f32) * place.astype(f32)
        parts = split(jnp.concatenate([jnp.cos(angles), jnp.sin(angles)], axis=0))
        return jnp.concatenate(parts, axis=0)


def finish_kernel(
    in_grad_ref,
    out_grad_ref,
    update_ref,
    output_ref,
    input_grad_ref,
    vector_sum_ref,
    *refs,
):
    weights, momenta, norms, outs = refs[0:4], refs[4:8], refs[8:11], refs[11:]
    outs[0][...] = output_ref[...]
    outs[1][...] = input_grad_ref[...]
    wide = in_grad_ref.shape[1] // 2
    widths = (3 * D, FF, D, FF)
    for index in range(4):
        source = in_grad_ref if index < 2 else out_grad_ref
        first = (index % 2) * wide
        grad = source[:, first : first + wide]
        update = jnp.concatenate([update_ref[2 * index], update_ref[2 * index + 1]], axis=1)
        update = update.astype(f32)
        if index != 1:
            size = weights[index].shape[0]
            grad, update = grad.T[:size, :], update.T[:size, :]
        outs[2 + index][...] = grad
        outs[6 + index][...] = momentum * momenta[index][...] + grad
        outs[10 + index][...] = (
            weights[index][...] * (1.0 - rate_matrix * decay_matrix)
            - rate_matrix * 0.2 * math.sqrt(widths[index]) * update
        )
    sums = vector_sum_ref[...]
    grads = jnp.concatenate(
        [sums[2 * index : 2 * index + 1, :] + sums[2 * index + 1 : 2 * index + 2, :] for index in range(3)],
        axis=0,
    )
    for out_ref, value in zip(
        outs[14:], adam_step(norms[0][...], grads, norms[1][...], norms[2][...])
    ):
        out_ref[...] = value


def finish(in_grad, out_grad, update, output, input_grad, vector_sum, weights, momenta, norms):
    shape = jax.ShapeDtypeStruct
    matrices = [shape(weight.shape, f32) for weight in weights]
    return pl.pallas_call(
        finish_kernel,
        out_shape=(
            shape(output.shape, f32),
            shape(output.shape, f32),
            *(matrices * 3),
            *([shape(norms[0].shape, f32)] * 3),
        ),
        compiler_params=pltpu.CompilerParams(vmem_limit_bytes=VMEM_LIMIT),
        name="finish",
    )(in_grad, out_grad, update, output, input_grad, vector_sum, *weights, *momenta, *norms)


def adam_step(value, gradient, first_state, second_state):
    first_new = beta_first * first_state + (1.0 - beta_first) * gradient
    second_new = beta_second * second_state + (1.0 - beta_second) * gradient * gradient
    corrected = first_new / (1.0 - beta_first**STEP)
    root_term = jnp.sqrt(second_new / (1.0 - beta_second**STEP)) + adam_floor
    return (first_new, second_new, value - rate_vector * corrected / root_term)


def per_device(
    tokens,
    cotangent,
    lengths,
    deal_order,
    qkv_weight,
    up_weight,
    proj_weight,
    down_weight,
    norm_vectors,
    qkv_bias,
    mlp_bias,
    qkv_momentum,
    up_momentum,
    proj_momentum,
    down_momentum,
    norm_moment,
    norm_square,
    qkv_bias_moment,
    qkv_bias_square,
    mlp_bias_moment,
    mlp_bias_square,
):
    cols, rows = lax.axis_size("col"), lax.axis_size("row")
    qkv_width, up_width = qkv_weight.shape[1], up_weight.shape[1]
    bias = jnp.concatenate(
        [jnp.pad(qkv_bias, (0, up_width - qkv_width)), mlp_bias], axis=0
    ).reshape(1, 2 * up_width)
    weights = (qkv_weight.T, up_weight, proj_weight, down_weight)
    momenta = (qkv_momentum.T, up_momentum, proj_momentum, down_momentum)
    (
        pick,
        pack,
        vector_all,
        normalized,
        inverse_std,
        in_grad,
        out_grad,
        bias_rows,
        matrix,
        gram,
        twin_sums,
        branch_sum,
    ) = layer(
        tokens,
        cotangent,
        lengths.reshape(1, -1),
        deal_order.reshape(-1, 128),
        norm_vectors,
        bias,
        weights,
        momenta,
        rows,
        cols,
    )
    returned, output, input_grad, vector_sum = orthogonalize(
        gram,
        matrix,
        twin_sums,
        branch_sum,
        normalized,
        inverse_std,
        vector_all,
        tokens,
        cotangent,
        pick,
        pack,
        rows,
    )
    output, input_grad, *matrices = finish(
        in_grad,
        out_grad,
        returned,
        output,
        input_grad,
        vector_sum,
        weights,
        momenta,
        (norm_vectors, norm_moment, norm_square),
    )
    matrices, norms = matrices[:12], matrices[12:]
    for index in (0, 4, 8):
        matrices[index] = matrices[index].T
    in_bias_grad = bias_rows[0]
    qkv_first, qkv_second, qkv_bias_new = adam_step(
        qkv_bias, in_bias_grad[:qkv_width], qkv_bias_moment, qkv_bias_square
    )
    mlp_first, mlp_second, mlp_bias_new = adam_step(
        mlp_bias, in_bias_grad[up_width:], mlp_bias_moment, mlp_bias_square
    )
    return (
        output,
        input_grad,
        *matrices,
        *norms,
        qkv_first,
        qkv_second,
        qkv_bias_new,
        mlp_first,
        mlp_second,
        mlp_bias_new,
    )


def solution(mesh):
    over_both, over_flip = P("row", "col"), P("col", "row")
    features, hidden = P(None, "col"), P("row")
    return jax.shard_map(
        per_device,
        mesh=mesh,
        in_specs=(
            *(over_both, over_both, P(), P()),
            *(over_flip, over_flip, over_both, over_both),
            *(features, hidden, hidden),
            *(over_flip, over_flip, over_both, over_both),
            *(features, features, hidden, hidden, hidden, hidden),
        ),
        out_specs=(
            *(over_both, over_both),
            *(over_flip, over_flip, over_both, over_both) * 3,
            *(features,) * 3,
            *(hidden,) * 6,
        ),
        check_vma=False,
    )
```

```python
import functools
import math

import jax
import jax.numpy as jnp
from jax import lax
from jax.experimental import pallas as pl
from jax.experimental.pallas import tpu as pltpu
from jax.sharding import PartitionSpec as P

D = 1024
HEAD = 64
ROT = 16
FF = 4096
STEP = 10

poly_linear = 3.4445
poly_square = -4.775
poly_cubic = 2.0315
momentum = 0.95
rate_matrix = 0.15
decay_matrix = 0.1
beta_first = 0.9
beta_second = 0.95
rate_vector = 0.2
adam_floor = 1e-08
norm_floor = 1e-05
ortho_floor = 1e-07
masked_score = -1e30
f32 = jnp.float32
bf16 = jnp.bfloat16
BLOCK = 256
PIECE = 128
EXTRA = 16


def dot_nt(a, b, **kw):
    return lax.dot_general(a, b, (((1,), (1,)), ((), ())), preferred_element_type=f32, **kw)


def dot_tn(a, b, **kw):
    return lax.dot_general(a, b, (((0,), (0,)), ((), ())), preferred_element_type=f32, **kw)


def dot_nn(a, b, **kw):
    return lax.dot_general(a, b, (((1,), (0,)), ((), ())), preferred_element_type=f32, **kw)


def allowed_keys(start_ref, first, keys):
    shape = (BLOCK, keys)
    key_at = lax.broadcasted_iota(jnp.int32, shape, 1)
    query_at = first + lax.broadcasted_iota(jnp.int32, shape, 0)
    return (key_at >= start_ref[pl.ds(first, BLOCK), :]) & (key_at <= query_at)


def turning(table_ref, rows):
    lane = lax.broadcasted_iota(jnp.int32, (32, 2 * HEAD), 1) % HEAD
    entry = lax.broadcasted_iota(jnp.int32, (32, 2 * HEAD), 0) % 16
    half_rot = ROT // 2

    def spread(where, value):
        picks = jnp.where(where, value, 0.0).astype(bf16)
        return dot_tn(table_ref[:, rows], picks)

    cosine = spread((lane < ROT) & (entry == lane % half_rot), 1.0)
    cosine = cosine + jnp.where(lane[:1] < ROT, 0.0, 1.0)
    lower = spread((lane < half_rot) & (entry == lane + half_rot), -1.0)
    upper = spread((lane >= half_rot) & (lane < ROT) & (entry == lane), 1.0)
    return cosine, lower, upper


def turned(values, tables, back):
    cosine, lower, upper = tables
    half_rot = ROT // 2
    moved = (
        pltpu.roll(values, 2 * HEAD - half_rot, 1) * lower + pltpu.roll(values, half_rot, 1) * upper
    )
    return values * cosine - moved if back else values * cosine + moved


VMEM_LIMIT = 63 * 1024 * 1024


def remote_call(kernel, identity, out_shape, in_specs, scratch, flops, name):
    return pl.pallas_call(
        kernel,
        out_shape=out_shape,
        in_specs=in_specs,
        out_specs=(VMEM_SPEC,) * len(out_shape),
        scratch_shapes=scratch,
        compiler_params=pltpu.CompilerParams(
            collective_id=identity, has_side_effects=True, vmem_limit_bytes=VMEM_LIMIT
        ),
        cost_estimate=pl.CostEstimate(flops=flops, bytes_accessed=1 << 24, transcendentals=0),
        name=name,
    )


MESH = pl.DeviceIdType.MESH
VMEM_SPEC = pl.BlockSpec(memory_space=pltpu.VMEM)


def remote(src, dst, send, recv, device):
    return pltpu.make_async_remote_copy(
        src_ref=src, dst_ref=dst, send_sem=send, recv_sem=recv, device_id=device, device_id_type=MESH
    )


class Place:
    def __init__(self):
        self.row, self.col = lax.axis_index("row"), lax.axis_index("col")
        self.rows, self.cols = lax.axis_size("row"), lax.axis_size("col")
        self.chips = self.rows // 2
        self.chip, self.core = self.row // 2, self.row % 2
        self.twin = (self.chip * 2 + 1 - self.core, self.col)
        self.ring = self.chips // 2
        self.y, self.z = self.chip // self.ring, self.chip % self.ring

    def chip_at(self, step):
        return lax.rem(self.chip + step, self.chips)

    def chip_row(self, step):
        return self.chip_at(step) * 2 + self.core

    def col_at(self, step):
        return lax.rem(self.col + step, self.cols)


def greet(devices):
    barrier = pltpu.get_barrier_semaphore()
    for device in devices:
        pl.semaphore_signal(barrier, inc=1, device_id=device, device_id_type=MESH)


def meet(devices):
    pl.semaphore_wait(pltpu.get_barrier_semaphore(), len(devices))


class HopGather:
    OWN, PARTNER, BELOW, ABOVE, BELOW_PARTNER, ABOVE_PARTNER, FAR, FAR_PARTNER = range(8)

    def __init__(self, at, axis, slot, sems):
        self.at, self.axis, self.slot = at, axis, slot
        self.sems = sems
        index, ring = (at.chip, at.chips // 2) if axis == "row" else (at.col, at.cols // 2)
        side, step = index // ring, index % ring

        def place(other, hops):
            return (1 - side if other else side) * ring + lax.rem(step + hops, ring)

        self.places = [
            place(False, 0),
            place(True, 0),
            place(False, ring - 1),
            place(False, 1),
            place(True, ring - 1),
            place(True, 1),
            place(False, 2),
            place(True, 2),
        ]

    def index(self, which):
        return self.places[which] * 2 + self.at.core if self.axis == "row" else self.places[which]

    def device(self, which):
        at = self.at
        return (self.index(which), at.col) if self.axis == "row" else (at.row, self.index(which))

    def block(self, which):
        return self.slot(self.index(which))

    def part(self, which, upper):
        ref = self.block(which)
        half = ref.shape[0] // 2
        return ref.at[pl.ds(0 if upper else half, half), :]

    def hop(self, tag, src, dst, to):
        send, recv = self.sems[0], self.sems[1]
        return remote(src, dst, send.at[tag], recv.at[tag], self.device(to))

    def took(self, tag, ref):
        self.hop(tag, ref, ref, self.PARTNER).wait_recv()

    def passing(self, which, src=None):
        send, recv = self.sems[2], self.sems[3]
        ref = self.block(which)
        return remote(
            ref if src is None else src, ref, send.at[which], recv.at[which], self.at.twin
        )

    def hops(self):
        own, src = self.block(self.OWN), self.src
        partner = self.block(self.PARTNER)
        below, above = self.part(self.BELOW, True), self.part(self.ABOVE, False)
        far = self.block(self.FAR)
        return {
            "start": [
                (0, src, own, self.PARTNER),
                (1, src, own, self.ABOVE),
                (2, src, own, self.BELOW),
            ],
            "partner": [(3, partner, partner, self.ABOVE), (4, partner, partner, self.BELOW)],
            "below": [(5, below, below, self.ABOVE)],
            "above": [(6, above, above, self.BELOW)],
            "far": [(7, far, far, self.PARTNER)],
        }

    def go(self, stage):
        for hop in self.hops()[stage]:
            self.hop(*hop).start()

    def start(self, src):
        self.src = src
        self.go("start")
        if self.axis == "row":
            self.passing(self.OWN, src).start()

    def landed(self, which):
        if self.axis == "row":
            self.passing(which).start()

    def steps(self):
        def first():
            self.took(1, self.block(self.BELOW))
            self.go("below")
            self.took(2, self.block(self.ABOVE))
            self.go("above")
            self.landed(self.BELOW)
            self.landed(self.ABOVE)

        def second():
            self.took(0, self.block(self.PARTNER))
            self.go("partner")
            self.landed(self.PARTNER)

        def third():
            self.took(5, self.part(self.FAR, True))
            self.took(6, self.part(self.FAR, False))
            self.go("far")
            self.landed(self.FAR)

        def fourth():
            self.took(3, self.block(self.BELOW_PARTNER))
            self.landed(self.BELOW_PARTNER)
            self.took(4, self.block(self.ABOVE_PARTNER))
            self.landed(self.ABOVE_PARTNER)
            self.took(7, self.block(self.FAR_PARTNER))
            self.landed(self.FAR_PARTNER)

        return [first, second, third, fourth]

    def finish(self):
        send, recv = self.sems[2], self.sems[3]
        for which in range(8):
            slot = self.slot(self.places[which] * 2 + 1 - self.at.core)
            remote(slot, slot, send.at[which], recv.at[which], self.at.twin).wait_recv()

    def sent(self):
        for stage in self.hops().values():
            for hop in stage:
                self.hop(*hop).wait_send()
        if self.axis == "row":
            self.passing(self.OWN, self.src).wait_send()
            for which in range(1, 8):
                self.passing(which).wait_send()


class Swap:
    def __init__(self, at, axis, src, dst, sems):
        self.at, self.axis, self.src, self.dst = at, axis, src, dst
        self.send, self.recv = sems
        self.me, self.size = (at.row, at.rows) if axis == "row" else (at.col, at.cols)

    def to(self, step):
        return lax.rem(self.me + step, self.size)

    def device(self, index):
        return (index, self.at.col) if self.axis == "row" else (self.at.row, index)

    def outgoing(self, step):
        to = self.to(step)
        return remote(
            self.src(to),
            self.dst(self.me),
            self.send.at[step],
            self.recv.at[step],
            self.device(to),
        )

    def start(self, which=None):
        for step in range(1, self.size):
            if which is None:
                self.outgoing(step).start()
            else:

                @pl.when(which(self.to(step)))
                def _():
                    self.outgoing(step).start()

    def arrived(self):
        for step in range(1, self.size):
            came = self.to(self.size - step)
            slot = self.dst(came)
            remote(
                slot, slot, self.send.at[step], self.recv.at[step], self.device(came)
            ).wait_recv()

    def sent(self):
        for step in range(1, self.size):
            self.outgoing(step).wait_send()


class RowSum:
    SEMS = 4

    def __init__(self, at, part, pairs, slots, sems):
        self.at, self.part, self.pairs, self.slots = at, part, pairs, slots
        self.twin_send, self.twin_recv, self.send, self.recv = sems

    def to_twin(self):
        at = self.at
        return remote(
            self.part.at[:, 1 - at.core],
            self.pairs,
            self.twin_send.at[0],
            self.twin_recv.at[0],
            at.twin,
        )

    def outgoing(self, step):
        at = self.at
        return remote(
            self.pairs.at[at.chip_at(step)],
            self.slots.at[at.chip],
            self.send.at[step],
            self.recv.at[step],
            (at.chip_row(step), at.col),
        )

    def start(self):
        self.to_twin().start()

    def add_twin(self):
        at = self.at
        self.to_twin().wait_recv()
        for chip in range(at.chips):
            both = self.part[chip, at.core].astype(f32) + self.pairs[chip].astype(f32)
            self.pairs[chip] = both.astype(bf16)

    def spread(self):
        for step in (4, 1, 2, 3, 5, 6, 7):
            self.outgoing(step).start()

    def middle(self):
        self.add_twin()
        self.spread()

    def finish(self):
        at = self.at
        total = self.pairs[at.chip].astype(f32)
        for step in range(1, at.chips):
            chip = at.chip_at(at.chips - step)
            slot = self.slots.at[chip]
            remote(
                slot, slot, self.send.at[step], self.recv.at[step], (chip * 2 + at.core, at.col)
            ).wait_recv()
            total = total + self.slots[chip].astype(f32)
        return total

    def released(self):
        self.to_twin().wait_send()

    def sent(self):
        for step in range(1, self.at.chips):
            self.outgoing(step).wait_send()


def sum_scratch(piece, width, chips):
    dma = pltpu.SemaphoreType.DMA
    return [
        pltpu.VMEM((chips, piece, width), bf16),
        pltpu.VMEM((chips, piece, width), bf16),
        dma((1,)),
        dma((1,)),
        dma((chips,)),
        dma((chips,)),
    ]


def moved_rows(index_row, first, count, values):
    shape = (count, index_row.shape[1])
    here = first + lax.broadcasted_iota(jnp.int32, shape, 0) == index_row
    return dot_nn(jnp.where(here, 1.0, 0.0).astype(bf16), values)


def flat(ref, size):
    return jnp.concatenate([ref[index, :size, :] for index in range(ref.shape[0])], axis=0)


def pack_rows(index_ref, values, out_refs, lanes):
    blocks = out_refs[0].shape[0]
    size = index_ref[1]
    for first in range(0, blocks, 4):
        found = moved_rows(index_ref[0][...], first * size, 4 * size, values).astype(bf16)
        for index in range(4):
            part = found[index * size : (index + 1) * size, :]
            for which, out_ref in enumerate(out_refs):
                out_ref[first + index, :size, :] = part[:, which * lanes : (which + 1) * lanes]


def every_row(at):
    return [(lax.rem(at.row + step, at.rows), at.col) for step in range(1, at.rows)]


def row_peers(at):
    return [(at.chip_row(step), at.col) for step in range(1, at.chips)] + [at.twin]


def col_peers(at):
    return [(at.row, at.col_at(step)) for step in range(1, at.cols)]


def gather_sems():
    return [pltpu.SemaphoreType.DMA((count,)) for count in (8, 8, 8, 8)]


def hop_sems():
    return [pltpu.SemaphoreType.DMA((8,))] * 2


def swap_sems(cols):
    return [pltpu.SemaphoreType.DMA((cols,))] * 2


def split(x):
    high_part = x.astype(bf16)
    return high_part, (x - high_part.astype(f32)).astype(bf16)


def three(dot, left, right):
    return dot(left[0], right[0]) + (dot(left[0], right[1]) + dot(left[1], right[0]))


BLK = 128


def layer_kernel(
    tokens_ref,
    cotangent_ref,
    lengths_ref,
    deal_ref,
    norm_ref,
    bias_ref,
    qkv_weight_ref,
    up_weight_ref,
    proj_weight_ref,
    down_weight_ref,
    qkv_momentum_ref,
    up_momentum_ref,
    proj_momentum_ref,
    down_momentum_ref,
    pick_ref,
    pack_ref,
    vector_all_ref,
    normalized_ref,
    inverse_std_ref,
    in_grad_ref,
    out_grad_ref,
    bias_grad_ref,
    matrix_ref,
    gram_ref,
    normed_twins_ref,
    branch_sum_ref,
    normed_part_ref,
    take_back_ref,
    send_back_ref,
    weight_ref,
    vector_ref,
    table_ref,
    start_ref,
    momentum_ref,
    dealt_ref,
    cot_dealt_ref,
    weight_all_ref,
    q_ref,
    k_ref,
    v_ref,
    slope_ref,
    branch_ref,
    attended_ref,
    total_ref,
    out_part,
    pairs,
    values,
    out_rows_tokens,
    in_rows_tokens,
    out_rows_cots,
    in_rows_cots,
    out_tokens,
    in_tokens,
    out_cots,
    in_cots,
    pre_ref,
    dk_ref,
    dv_ref,
    out_parts,
    up_part,
    up_parts,
    qkv_part,
    qkv_parts,
    bias_part,
    biases,
    chunks,
    products,
    from_twin,
    half_sum,
    slices,
    twin_sums,
    slots,
    *sems,
):
    at = Place()
    held, feats = tokens_ref.shape
    piece = out_tokens.shape[1]
    capacity = out_rows_tokens.shape[1]
    depth = weight_ref.shape[0]
    sems = list(sems)

    def some(count):
        taken, sems[:count] = sems[:count], []
        return taken

    def block(ref):
        return lambda index: ref.at[index]

    def dealt_slot(ref):
        return lambda row: ref.at[pl.ds(row * piece, piece), :]

    last_tokens = HopGather(at, "row", dealt_slot(dealt_ref), some(4))
    last_cots = HopGather(at, "row", dealt_slot(cot_dealt_ref), some(4))
    rows_tokens = Swap(at, "row", block(out_rows_tokens), block(in_rows_tokens), some(2))
    rows_cots = Swap(at, "row", block(out_rows_cots), block(in_rows_cots), some(2))
    swap_tokens = Swap(at, "col", block(out_tokens), block(in_tokens), some(2))
    swap_cots = Swap(at, "col", block(out_cots), block(in_cots), some(2))
    weights = HopGather(
        at, "col", lambda c: weight_all_ref.at[pl.ds(c * depth, depth), :], some(2)
    )
    swap_vector = Swap(at, "col", lambda c: vector_ref, block(vector_all_ref), some(2))

    branch_rows = RowSum(at, normed_part_ref, twin_sums, slots, some(4))
    swap_out = Swap(at, "col", block(out_part), block(out_parts), some(2))
    swap_up = Swap(at, "col", block(up_part), block(up_parts), some(2))
    swap_qkv = Swap(at, "col", block(qkv_part), block(qkv_parts), some(2))
    swap_bias = Swap(at, "col", lambda c: bias_part, block(biases), some(2))
    swap_chunk = Swap(at, "col", block(chunks), block(matrix_ref), some(2))
    normed_rows = RowSum(at, normed_part_ref, normed_twins_ref, None, [*some(2), None, None])
    twin_send, twin_recv, sum_send, sum_recv, all_send, all_recv, pass_send, pass_recv = some(8)
    count = at.chips * 2
    mine = at.chip * 2 + at.col % 2
    first_col = at.col - at.col % 2

    def member(step):
        other = lax.rem(mine + step, count)
        return other, ((other // 2) * 2 + at.core, first_col + other % 2)

    peers = [member(step)[1] for step in range(1, count)]

    def pick(in_ref, out_ref):
        pack_rows((send_back_ref, piece), flat(in_ref, capacity), [out_ref], feats)

    everyone = every_row(at) + col_peers(at) + peers
    greet(everyone)
    plan = Plan(at, lengths_ref, deal_ref, held)
    take_back_ref[...] = plan.take_back()
    vector_ref[...] = jnp.zeros_like(vector_ref)
    vector_ref[: norm_ref.shape[0], :] = norm_ref[...]
    both = jnp.concatenate([tokens_ref[...], cotangent_ref[...]], axis=1)
    pack_rows((take_back_ref, capacity), both, [out_rows_tokens, out_rows_cots], feats)
    meet(everyone)
    rows_tokens.start()
    swap_vector.start()
    send_back_ref[...] = plan.listed(True)
    up = up_weight_ref.shape[1]
    weight_ref[...] = jnp.zeros_like(weight_ref)
    momentum_ref[...] = jnp.zeros_like(momentum_ref)
    for first, ref in (
        (0, qkv_weight_ref),
        (2 * up, proj_weight_ref),
        (2 * up + 2 * HEAD, down_weight_ref),
    ):
        weight_ref[:, first : first + ref.shape[0]] = ref[...].T.astype(bf16)
    weight_ref[:, up : 2 * up] = up_weight_ref[...].astype(bf16)
    weight_all_ref[pl.ds(at.col * depth, depth), :] = weight_ref[...]
    vector_all_ref[at.col] = vector_ref[...]
    in_rows_tokens[at.row] = out_rows_tokens[at.row]
    in_rows_cots[at.row] = out_rows_cots[at.row]

    rows_tokens.arrived()
    rows_cots.start()
    pick(in_rows_tokens, out_tokens)
    swap_tokens.start()
    in_tokens[at.col] = out_tokens[at.col]
    start_ref[...] = plan.block_starts()
    table_ref[...] = plan.rotary()

    swap_vector.arrived()
    swap_tokens.arrived()
    weights.start(weight_ref)
    width = at.cols * feats
    parts = [in_tokens[f].astype(f32) for f in range(at.cols)]
    mean = sum(jnp.sum(part, axis=1, keepdims=True) for part in parts) / width
    parts = [part - mean for part in parts]
    variance = sum(jnp.sum(part * part, axis=1, keepdims=True) for part in parts) / width
    inverse_std = lax.rsqrt(variance + norm_floor)
    inverse_std_ref[...] = inverse_std
    own = pl.ds(at.row * piece, piece)
    for f in range(at.cols):
        lanes = slice(f * feats, (f + 1) * feats)
        normalized = parts[f] * inverse_std
        normalized_ref[:, lanes] = normalized
        vectors = vector_all_ref[f]
        dealt_ref[own, lanes] = (normalized * vectors[0:1, :] + vectors[1:2, :]).astype(bf16)
    last_tokens.start(dealt_ref.at[own, :])
    token_steps, weight_steps = iter(last_tokens.steps()), iter(weights.steps())
    cot_steps = iter(last_cots.steps())
    rows_cots.arrived()
    pick(in_rows_cots, out_cots)
    swap_cots.start()
    in_cots[at.col] = out_cots[at.col]
    next(weight_steps)()
    next(token_steps)()
    next(weight_steps)()
    next(token_steps)()
    swap_cots.arrived()
    for f in range(at.cols):
        cot_dealt_ref[own, f * feats : (f + 1) * feats] = in_cots[f]
    last_cots.start(cot_dealt_ref.at[own, :])
    next(weight_steps)()
    next(token_steps)()
    next(weight_steps)()
    next(token_steps)()
    next(cot_steps)()
    last_tokens.finish()

    in_width = bias_ref.shape[1]
    tokens = dealt_ref.shape[0]
    rows_all = tokens // PIECE
    in_weight, out_weight = weight_all_ref[:, :in_width], weight_all_ref[:, in_width:]
    inner = math.sqrt(2.0 / math.pi)
    firsts = range(0, tokens, BLOCK)
    for first in firsts:
        if first == 4 * BLOCK:
            next(cot_steps)()
        rows = pl.ds(first, BLOCK)
        pre = dot_nn(dealt_ref[rows, :], in_weight) + bias_ref[...]
        pair = turned(pre[:, : 2 * HEAD], turning(table_ref, rows), False)
        for part in range(BLOCK // PIECE):
            these = slice(part * PIECE, (part + 1) * PIECE)
            spaced = pl.ds(first // PIECE + part, PIECE, stride=rows_all)
            pairs[spaced, :] = pair[these, :]
            values[spaced, :] = pre[these, 2 * HEAD : 4 * HEAD]
        up = pre[:, 4 * HEAD :]
        square = up * up
        bent = jnp.tanh(inner * (up + 0.044715 * square * up))
        branch_ref[rows, 2 * HEAD :] = (0.5 * up * (1.0 + bent)).astype(bf16)
        slope_ref[rows, :] = 0.5 * (1.0 + bent) + 0.5 * up * (1.0 - bent * bent) * (
            inner * (1.0 + 3.0 * 0.044715 * square)
        )
    for first in firsts:
        rows = pl.ds(first, BLOCK)
        pair = pairs[rows, :].astype(bf16)
        q_ref[rows, :] = (pair[:, :HEAD] * HEAD**-0.5).astype(bf16)
        k_ref[rows, :] = pair[:, HEAD:]
        v_ref[rows, :] = values[rows, :HEAD].astype(bf16)
    next(cot_steps)()
    for first in firsts:
        if first == 6 * BLOCK:
            next(cot_steps)()
        rows, keys = pl.ds(first, BLOCK), first + BLOCK
        scores = dot_nt(q_ref[rows, :], k_ref[:keys, :])
        scores = jnp.where(allowed_keys(start_ref, first, keys), scores, masked_score)
        top = jnp.max(scores, axis=1, keepdims=True)
        raw = jnp.exp(scores - top)
        total = jnp.sum(raw, axis=1, keepdims=True)
        attended = dot_nn(raw.astype(bf16), v_ref[:keys, :]) / total
        attended_ref[rows, :] = attended.astype(bf16)
        values[rows, :] = jnp.concatenate([attended, jnp.zeros_like(attended)], axis=1)
        total_ref[rows, :] = top + jnp.log(total)
    for first in firsts:
        rows = pl.ds(first, BLOCK)
        for part in range(BLOCK // PIECE):
            at_piece = first // PIECE + part
            branch_ref[at_piece * PIECE : (at_piece + 1) * PIECE, : 2 * HEAD] = values[
                pl.ds(at_piece, PIECE, stride=rows_all), :
            ].astype(bf16)
        partial = dot_nt(branch_ref[rows, :], out_weight).astype(bf16)
        for part in range(BLOCK // PIECE):
            at_piece = first // PIECE + part
            normed_part_ref[at_piece // 2, at_piece % 2] = partial[
                part * PIECE : (part + 1) * PIECE, :
            ]
    branch_rows.start()
    last_cots.finish()
    for first in range(0, cot_dealt_ref.shape[1], BLOCK):
        part = dot_tn(cot_dealt_ref[:, first : first + BLOCK], branch_ref[...]).astype(bf16)
        for index in range(BLOCK // feats):
            out_part[first // feats + index] = part[index * feats : (index + 1) * feats, :]
    swap_out.start()
    out_parts[at.col] = out_part[at.col]

    half = up_part.shape[2]

    def weight_part(ref, lanes):
        for first in range(0, dealt_ref.shape[1], BLOCK):
            part = dot_tn(dealt_ref[:, first : first + BLOCK], pre_ref[:, lanes])
            for index in range(BLOCK // feats):
                ref[first // feats + index] = part[
                    index * feats : (index + 1) * feats, :
                ].astype(bf16)

    def direction(index, grad):
        lanes = slice(index * BLK, (index + 1) * BLK)
        state = momentum * momentum_ref[:, lanes] + grad
        chunks[index] = grad + momentum * state

    for first in firsts:
        rows = pl.ds(first, BLOCK)
        branch_grad = dot_nn(cot_dealt_ref[rows, :], out_weight)
        for part in range(BLOCK // PIECE):
            these = slice(part * PIECE, (part + 1) * PIECE)
            spaced = pl.ds(first // PIECE + part, PIECE, stride=rows_all)
            values[spaced, :] = branch_grad[these, : 2 * HEAD]
        pre_ref[rows, 4 * HEAD :] = (branch_grad[:, 2 * HEAD :] * slope_ref[rows, :]).astype(bf16)
    weight_part(up_part, slice(half, 2 * half))
    swap_up.start()
    up_parts[at.col] = up_part[at.col]
    dk_ref[...] = jnp.zeros_like(dk_ref)
    dv_ref[...] = jnp.zeros_like(dv_ref)
    branch_rows.middle()
    for first in reversed(firsts):
        rows, keys = pl.ds(first, BLOCK), first + BLOCK
        query, grad = q_ref[rows, :], values[rows, :HEAD].astype(bf16)
        key, value = k_ref[:keys, :], v_ref[:keys, :]
        scores = dot_nt(query, key)
        allowed = allowed_keys(start_ref, first, keys)
        prob = jnp.where(allowed, jnp.exp(scores - total_ref[rows, :]), 0.0)
        delta = jnp.sum(
            grad.astype(f32) * attended_ref[rows, :].astype(f32), axis=1, keepdims=True
        )
        score_grad = (prob * (dot_nt(grad, value) - delta)).astype(bf16)
        dk_ref[:keys, :] += dot_tn(score_grad, query)
        dv_ref[:keys, :] += dot_tn(prob.astype(bf16), grad)
        pairs[rows, :] = jnp.concatenate(
            [dot_nn(score_grad, key) * HEAD**-0.5, dk_ref[rows, :]], axis=1
        )
        dv = dv_ref[rows, :]
        values[rows, :] = jnp.concatenate([dv, jnp.zeros_like(dv)], axis=1)
    for first in firsts:
        rows = pl.ds(first, BLOCK)
        pair, value = [
            jnp.concatenate(
                [
                    ref[pl.ds(first // PIECE + part, PIECE, stride=rows_all), :]
                    for part in range(BLOCK // PIECE)
                ],
                axis=0,
            )
            for ref in (pairs, values)
        ]
        pre_ref[rows, : 2 * HEAD] = turned(pair, turning(table_ref, rows), True).astype(bf16)
        pre_ref[rows, 2 * HEAD : 4 * HEAD] = value.astype(bf16)
    weight_part(qkv_part, slice(0, half))
    swap_qkv.start()
    qkv_parts[at.col] = qkv_part[at.col]
    bias = jnp.sum(pre_ref[...].astype(f32), axis=0, keepdims=True)
    bias_part[...] = jnp.broadcast_to(bias, bias_part.shape)
    swap_bias.start()
    biases[at.col] = bias_part[...]
    branch_rows.released()
    for first in firsts:
        rows = pl.ds(first, BLOCK)
        partial = dot_nt(pre_ref[rows, :], in_weight).astype(bf16)
        for part in range(BLOCK // PIECE):
            at_piece = first // PIECE + part
            normed_part_ref[at_piece // 2, at_piece % 2] = partial[
                part * PIECE : (part + 1) * PIECE, :
            ]

    normed_rows.start()
    for first, ref in (
        (0, qkv_momentum_ref),
        (2 * half, proj_momentum_ref),
        (3 * half, down_momentum_ref),
    ):
        momentum_ref[:, first : first + ref.shape[0]] = ref[...].T
    momentum_ref[:, half : 2 * half] = up_momentum_ref[...]
    swap_out.arrived()
    total = sum(out_parts[c].astype(f32) for c in range(at.cols))
    filled = jnp.zeros((feats, half - 2 * HEAD), f32)
    out_grad = jnp.concatenate([total[:, : 2 * HEAD], filled, total[:, 2 * HEAD :]], axis=1)
    out_grad_ref[...] = out_grad
    swap_up.arrived()
    up_grad = sum(up_parts[c].astype(f32) for c in range(at.cols))
    in_grad_ref[:, half:] = up_grad
    late = half // BLK
    for index in range(late, at.cols):
        first = (index - late) * BLK
        if first < half:
            direction(index, up_grad[:, first : first + BLK])
        else:
            direction(index, out_grad[:, first - half : first - half + BLK])
    swap_chunk.start(lambda to: to >= late)
    swap_qkv.arrived()
    qkv_grad = sum(qkv_parts[c].astype(f32) for c in range(at.cols))
    in_grad_ref[:, :half] = qkv_grad
    for index in range(late):
        direction(index, qkv_grad[:, index * BLK : (index + 1) * BLK])
    swap_chunk.start(lambda to: to < late)
    matrix_ref[at.col] = chunks[at.col]
    swap_bias.arrived()
    bias_grad_ref[...] = sum(biases[c] for c in range(at.cols))
    swap_chunk.arrived()

    strips = matrix_ref.shape[0]
    matrix = split(matrix_ref[...].reshape(strips * BLK, BLK))
    index = 0
    for i in range(strips):
        left = [m[i * BLK : (i + 1) * BLK, :] for m in matrix]
        right = [m[i * BLK :, :] for m in matrix]
        product = three(dot_nt, left, right)
        for j in range(strips - i):
            products[index] = product[:, j * BLK : (j + 1) * BLK]
            index += 1
    blocks = index // 2
    half_rows = blocks * BLK
    each = blocks // 2
    size = each * BLK // count

    def to_twin(group):
        return remote(
            products.at[pl.ds((1 - at.core) * blocks + group * each, each)],
            from_twin.at[pl.ds(group * each, each)],
            twin_send.at[group],
            twin_recv.at[group],
            at.twin,
        )

    def give(step, group):
        owner, device = member(step)
        return remote(
            half_sum.at[pl.ds(group * each * BLK + owner * size, size), :],
            slices.at[group, mine],
            sum_send.at[group * count + step],
            sum_recv.at[group * count + step],
            device,
        )

    def home(owner, group, core):
        first = core * half_rows + group * each * BLK + owner * size
        return gram_ref.at[pl.ds(first, size), :]

    def spread(step, group):
        slot = home(mine, group, at.core)
        sems_at = group * count + step
        return remote(slot, slot, all_send.at[sems_at], all_recv.at[sems_at], member(step)[1])

    def passing(step, group):
        slot = home(member(count - step)[0] if step else mine, group, at.core)
        sems_at = group * count + step
        return remote(slot, slot, pass_send.at[sems_at], pass_recv.at[sems_at], at.twin)

    for group in range(2):
        to_twin(group).start()
    for group in range(2):
        to_twin(group).wait_recv()
        for b in range(group * each, (group + 1) * each):
            half_sum[b * BLK : (b + 1) * BLK, :] = products[at.core * blocks + b] + from_twin[b]
        for step in range(1, count):
            give(step, group).start()
        slices[group, mine] = half_sum[pl.ds(group * each * BLK + mine * size, size), :]
    normed_rows.add_twin()
    pick_ref[...] = plan.pick()
    pack_ref[...] = plan.listed(False)
    for group in range(2):
        for step in range(1, count):
            came, device = member(count - step)
            slot = slices.at[group, came]
            sems_at = group * count + step
            remote(slot, slot, sum_send.at[sems_at], sum_recv.at[sems_at], device).wait_recv()
        total = slices[group, 0]
        for index in range(1, count):
            total = total + slices[group, index]
        first = at.core * half_rows + group * each * BLK + mine * size
        gram_ref[pl.ds(first, size), :] = total
        for step in range(1, count):
            spread(step, group).start()
        passing(0, group).start()
    for group in range(2):
        for step in range(1, count):
            came, device = member(count - step)
            slot = home(came, group, at.core)
            sems_at = group * count + step
            remote(slot, slot, all_send.at[sems_at], all_recv.at[sems_at], device).wait_recv()
            passing(step, group).start()
    for group in range(2):
        for step in range(count):
            slot = home(lax.rem(mine + count - step, count), group, 1 - at.core)
            sems_at = group * count + step
            remote(slot, slot, pass_send.at[sems_at], pass_recv.at[sems_at], at.twin).wait_recv()
            passing(step, group).wait_send()
    for group in range(2):
        to_twin(group).wait_send()
        for step in range(1, count):
            give(step, group).wait_send()
            spread(step, group).wait_send()
    branch_sum_ref[...] = branch_rows.finish().astype(bf16)
    branch_rows.sent()
    normed_rows.released()
    for moved in (last_tokens, last_cots, weights, rows_tokens, rows_cots):
        moved.sent()
    for moved in (swap_tokens, swap_cots, swap_vector):
        moved.sent()
    for moved in (swap_out, swap_up, swap_qkv, swap_bias, swap_chunk):
        moved.sent()


WIDE = 256


def poly_kernel(
    gram_ref,
    matrix_ref,
    twin_sums_ref,
    branch_ref,
    normalized_ref,
    inverse_std_ref,
    vector_ref,
    tokens_ref,
    cotangent_ref,
    pick_ref,
    pack_ref,
    update_ref,
    output_ref,
    input_grad_ref,
    vector_sum_ref,
    own_update,
    normed_ref,
    out_branch,
    in_branch,
    out_rows_branch,
    in_rows_branch,
    out_token,
    in_token,
    out_rows,
    in_rows,
    slots,
    *buffers,
):
    at = Place()
    sems, buffers = buffers[8:], buffers[:8]

    def block(ref):
        return lambda index: ref.at[index]

    swap_token = Swap(at, "col", block(out_token), block(in_token), sems[0:2])
    rows_token = Swap(at, "row", block(out_rows), block(in_rows), sems[2:4])
    feats = out_token.shape[2]
    swap_update = Swap(
        at,
        "col",
        lambda c: own_update.at[pl.ds(c * feats, feats), :],
        block(update_ref),
        sems[4:6],
    )
    swap_branch = Swap(at, "col", block(out_branch), block(in_branch), sems[6:8])
    rows_branch = Swap(at, "row", block(out_rows_branch), block(in_rows_branch), sems[8:10])
    normed_rows = RowSum(at, None, twin_sums_ref, slots, [None, None, *sems[10:12]])
    piece, capacity = normed_ref.shape[0], out_rows_branch.shape[1]
    lanes = [slice(f * feats, (f + 1) * feats) for f in range(at.cols)]
    for f in range(at.cols):
        out_branch[f] = branch_ref[:, lanes[f]]
    everyone = every_row(at) + col_peers(at)
    greet(everyone)

    def branch_back():
        swap_branch.arrived()
        pack_rows((pick_ref, capacity), flat(in_branch, piece), [out_rows_branch], feats)
        rows_branch.start()
        in_rows_branch[at.row] = out_rows_branch[at.row]

    def home(rows_ref, base_ref, shift, out_ref):
        values = flat(rows_ref, capacity)
        for first in range(0, out_ref.shape[0], BLOCK):
            rows = pl.ds(first, BLOCK)
            found = moved_rows(pack_ref[...], first, BLOCK, values)
            out_ref[rows, :] = found + base_ref[rows, :].astype(f32) + shift

    def branch_home():
        rows_branch.arrived()
        home(in_rows_branch, tokens_ref, vector_ref[at.col][2:3, :], output_ref)

    def extra(vectors):
        parts = [part.astype(f32) for vector in vectors for part in split(vector)]
        empty = jnp.zeros((EXTRA - len(parts), feats), f32)
        return jnp.concatenate([*parts, empty], axis=0).astype(bf16)

    def token_grads():
        normed_ref[...] = normed_rows.finish()
        width = at.cols * feats
        scaled = [normed_ref[:, lanes[f]] * vector_ref[f][0:1, :] for f in range(at.cols)]
        mean_first = sum(jnp.sum(part, axis=1, keepdims=True) for part in scaled) / width
        mean_second = (
            sum(
                jnp.sum(part * normalized_ref[:, lanes[f]], axis=1, keepdims=True)
                for f, part in enumerate(scaled)
            )
            / width
        )
        for f in range(at.cols):
            normalized, grad = normalized_ref[:, lanes[f]], normed_ref[:, lanes[f]]
            token_grad = inverse_std_ref[...] * (scaled[f] - mean_first - normalized * mean_second)
            out_token[f, :piece, :] = token_grad.astype(bf16)
            gain_grad = jnp.sum(grad * normalized, axis=0, keepdims=True)
            shift_grad = jnp.sum(grad, axis=0, keepdims=True)
            out_token[f, piece:, :] = extra([gain_grad, shift_grad])
        swap_token.start()
        in_token[at.col] = out_token[at.col]

    def token_back():
        cot_sum = jnp.sum(cotangent_ref[...].astype(f32), axis=0, keepdims=True)
        swap_token.arrived()
        pack_rows((pick_ref, capacity), flat(in_token, piece), [out_rows], feats)
        sums = sum(in_token[c, piece:, :].astype(f32) for c in range(at.cols))
        sums = extra([sums[0:1, :] + sums[1:2, :], sums[2:3, :] + sums[3:4, :], cot_sum])
        for row in range(at.rows):
            out_rows[row, capacity:, :] = sums
        rows_token.start()
        in_rows[at.row] = out_rows[at.row]

    first, second, third, thin = [buffers[2 * i : 2 * i + 2] for i in range(4)]
    strips = matrix_ref.shape[0]
    size = strips * BLK
    counts = range(size // WIDE)
    eye = lax.broadcasted_iota(jnp.int32, (BLK, BLK), 0) == lax.broadcasted_iota(
        jnp.int32, (BLK, BLK), 1
    )

    def put(pair, rows, lanes, value):
        high_part, low_part = split(value)
        pair[0][rows, lanes] = high_part
        pair[1][rows, lanes] = low_part

    def get(pair, rows, lanes):
        return pair[0][rows, lanes], pair[1][rows, lanes]

    places, index = [], 0
    for i in range(strips):
        for j in range(i, strips):
            places.append((i, j, index))
            index += 1
    trace = sum(
        jnp.sum(jnp.where(eye, gram_ref[spot * BLK : (spot + 1) * BLK, :], 0.0))
        for i, j, spot in places
        if i == j
    )
    shrink = 1.0 / (jnp.sqrt(jnp.full((1, 1), trace, f32)) + ortho_floor)
    for i, j, spot in places:
        block = gram_ref[spot * BLK : (spot + 1) * BLK, :] * (shrink * shrink)
        here, there = slice(i * BLK, (i + 1) * BLK), slice(j * BLK, (j + 1) * BLK)
        put(first, here, there, block)
        if j > i:
            put(first, there, here, block.T)
    everything = slice(0, size)
    for i in range(strips):
        put(thin, slice(i * BLK, (i + 1) * BLK), everything, matrix_ref[i] * shrink)

    meet(everyone)
    swap_branch.start()
    in_branch[at.col] = out_branch[at.col]
    normed_rows.spread()

    def product(left, right, out, finish=None):
        for i in counts:
            rows, rest = slice(i * WIDE, (i + 1) * WIDE), slice(i * WIDE, size)
            value = three(dot_nn, get(left, rows, everything), get(right, everything, rest))
            if finish is not None:
                value = finish(value, rows, rest)
            put(out, rows, rest, value)
            for j in range(i + 1, size // WIDE):
                part = value[:, (j - i) * WIDE : (j - i + 1) * WIDE]
                put(out, slice(j * WIDE, (j + 1) * WIDE), rows, part.T)

    def thin_product(left):
        right = get(thin, everything, everything)
        width = right[0].shape[1]
        both = jnp.concatenate(right, axis=1)
        found = []
        for i in counts:
            high_part, low_part = get(left, slice(i * WIDE, (i + 1) * WIDE), everything)
            value = dot_nn(high_part, both)
            found.append(value[:, :width] + (value[:, width:] + dot_nn(low_part, right[0])))
        return found

    def sweep(gram, poly, square, between=lambda: None):
        def finish(value, rows, rest):
            high_part, low_part = get(gram, rows, rest)
            value = poly_cubic * value + poly_square * (
                high_part.astype(f32) + low_part.astype(f32)
            )
            at_row = lax.broadcasted_iota(jnp.int32, value.shape, 0)
            at_lane = lax.broadcasted_iota(jnp.int32, value.shape, 1)
            return value + jnp.where(at_row == at_lane, poly_linear, 0.0)

        product(gram, gram, poly, finish)
        between()
        for i, value in zip(counts, thin_product(poly)):
            put(thin, slice(i * WIDE, (i + 1) * WIDE), everything, value)
        product(poly, poly, square)
        product(gram, square, poly)

    def two(step, carry):
        def early():
            @pl.when(step == 0)
            def _():
                branch_back()

            @pl.when(step == 1)
            def _():
                token_grads()

        def late():
            @pl.when(step == 1)
            def _():
                branch_home()

        sweep(first, second, third, early)

        @pl.when(step == 1)
        def _():
            token_back()

        sweep(second, first, third, late)
        return carry

    lax.fori_loop(0, 2, two, 0)
    once = thin_product(first)
    old = []
    for i in counts:
        rows = slice(i * WIDE, (i + 1) * WIDE)
        high_part, low_part = get(thin, rows, everything)
        old.append(high_part.astype(f32) + low_part.astype(f32))
    for i, value in zip(counts, once):
        put(thin, slice(i * WIDE, (i + 1) * WIDE), everything, value)
    for i, value in zip(counts, thin_product(first)):
        result = poly_linear * old[i] + poly_square * once[i] + poly_cubic * value
        own_update[i * WIDE : (i + 1) * WIDE, :] = result.astype(bf16)
    swap_update.start()
    update_ref[at.col] = own_update[pl.ds(at.col * feats, feats), :]

    rows_token.arrived()
    home(in_rows, cotangent_ref, 0.0, input_grad_ref)
    vector_sum_ref[...] = sum(
        in_rows[row, capacity:, :].astype(f32) for row in range(at.rows)
    )
    swap_update.arrived()
    for moved in (swap_token, rows_token, swap_update, swap_branch, rows_branch, normed_rows):
        moved.sent()


def orthogonalize(
    gram,
    matrix,
    twin_sums,
    branch_sum,
    normalized,
    inverse_std,
    vectors,
    tokens,
    cotangent,
    pick,
    pack,
    rows,
):
    cols, feats, width = matrix.shape
    size = cols * BLK
    piece, full = branch_sum.shape
    held = cotangent.shape[0]
    chips = rows // 2
    capacity = pack.shape[1] // rows
    shape = jax.ShapeDtypeStruct
    square, narrow = pltpu.VMEM((size, size), bf16), pltpu.VMEM((size, width), bf16)
    return remote_call(
        poly_kernel,
        3,
        (
            shape((cols, feats, width), bf16),
            shape((held, feats), f32),
            shape((held, feats), f32),
            shape((EXTRA, feats), f32),
        ),
        [VMEM_SPEC] * 11,
        [
            narrow,
            pltpu.VMEM((piece, full), f32),
            *([pltpu.VMEM((cols, piece, feats), bf16)] * 2),
            *([pltpu.VMEM((rows, capacity, feats), bf16)] * 2),
            *([pltpu.VMEM((cols, piece + EXTRA, feats), bf16)] * 2),
            *([pltpu.VMEM((rows, capacity + EXTRA, feats), bf16)] * 2),
            sum_scratch(piece, full, chips)[0],
            *([square] * 6),
            *([narrow] * 2),
            *swap_sems(cols),
            *swap_sems(rows),
            *(swap_sems(cols) * 2),
            *swap_sems(rows),
            *sum_scratch(piece, full, chips)[4:],
        ],
        60 * 10**9,
        "orthogonalize",
    )(
        *(gram, matrix, twin_sums, branch_sum, normalized),
        *(inverse_std, vectors, tokens, cotangent, pick, pack),
    )


def layer(tokens, cotangent, lengths, deal_order, vectors, bias, weights, momenta, rows, cols):
    held, feats = tokens.shape
    group = held * rows // cols
    piece, width, chips = group // rows, feats * cols, rows // 2
    in_width = bias.shape[1]
    up = in_width - 4 * HEAD
    branch = up + 2 * HEAD
    capacity = CAPACITY
    depth, tile = feats, 2 * up + branch
    blocks = cols * (cols + 1) // 2
    count = chips * 2
    half_rows = blocks * BLK // 2
    shape, vmem = jax.ShapeDtypeStruct, pltpu.VMEM
    dma = pltpu.SemaphoreType.DMA
    return remote_call(
        layer_kernel,
        0,
        (
            shape((1, cols * piece), jnp.int32),
            shape((1, rows * capacity), jnp.int32),
            shape((cols, 8, feats), f32),
            shape((piece, width), f32),
            shape((piece, 1), f32),
            shape((feats, in_width), f32),
            shape((feats, in_width), f32),
            shape((8, in_width), f32),
            shape((cols, feats, BLK), f32),
            shape((blocks * BLK, BLK), f32),
            shape((chips, piece, width), bf16),
            shape((piece, width), bf16),
        ),
        [VMEM_SPEC] * 14,
        [
            vmem((chips, 2, piece, width), bf16),
            vmem((1, held), jnp.int32),
            vmem((1, rows * capacity), jnp.int32),
            vmem((depth, tile), bf16),
            vmem((8, feats), f32),
            vmem((4 * ROT // 2, group), bf16),
            vmem((group, 1), jnp.int32),
            vmem((depth, 4 * up), f32),
            *([vmem((group, width), bf16)] * 2),
            vmem((depth * cols, tile), bf16),
            *([vmem((group, HEAD), bf16)] * 3),
            vmem((group, up), f32),
            vmem((group, branch), bf16),
            vmem((group, HEAD), bf16),
            vmem((group, 1), f32),
            vmem((cols, feats, branch), bf16),
            *([vmem((group, 2 * HEAD), f32)] * 2),
            *([vmem((rows, capacity, feats), bf16)] * 4),
            *([vmem((cols, piece, feats), bf16)] * 4),
            vmem((group, in_width), bf16),
            *([vmem((group, HEAD), f32)] * 2),
            vmem((cols, feats, branch), bf16),
            *([vmem((cols, feats, up), bf16)] * 4),
            vmem((8, in_width), f32),
            vmem((cols, 8, in_width), f32),
            vmem((cols, feats, BLK), f32),
            vmem((blocks, BLK, BLK), f32),
            vmem((blocks // 2, BLK, BLK), f32),
            vmem((half_rows, BLK), f32),
            vmem((2, count, half_rows // count // 2, BLK), f32),
            *sum_scratch(piece, width, chips)[:2],
            *(gather_sems() * 2),
            *(swap_sems(rows) * 2),
            *(swap_sems(cols) * 2),
            *hop_sems(),
            *swap_sems(cols),
            *sum_scratch(piece, width, chips)[2:],
            *(swap_sems(cols) * 5),
            *([dma((1,))] * 2),
            *([dma((2,))] * 2),
            *([dma((2 * count,))] * 6),
        ],
        150 * 10**9,
        "layer",
    )(tokens, cotangent, lengths, deal_order, vectors, bias, *weights, *momenta)


CAPACITY = 96


def column_sum(x):
    return jnp.sum(x.astype(f32), axis=0, keepdims=True).astype(jnp.int32)


def lane_sum(x):
    return jnp.sum(x.astype(f32), axis=1, keepdims=True).astype(jnp.int32)


class Plan:
    def __init__(self, at, lengths_ref, deal_ref, held):
        self.at, self.held = at, held
        total = held * at.rows
        self.group = total // at.cols
        self.piece = self.group // at.rows
        self.length_row = lengths_ref[...]
        slots = self.length_row.shape[1]
        self.slots = slots
        square = (slots, slots)
        below = lax.broadcasted_iota(jnp.int32, square, 1)
        above = lax.broadcasted_iota(jnp.int32, square, 0)
        self.same = below == above
        self.strict = jnp.where(below < above, 1.0, 0.0).astype(bf16)
        lengths = jnp.broadcast_to(self.length_row, square)
        self.starts = lane_sum(jnp.where(below < above, lengths, 0))
        self.ends = lane_sum(jnp.where(below <= above, lengths, 0))
        shape = deal_ref.shape
        position = lax.broadcasted_iota(jnp.int32, shape, 0) * shape[1]
        position = (position + lax.broadcasted_iota(jnp.int32, shape, 1)).astype(f32)
        deal = deal_ref[...]
        found = [
            jnp.sum(
                jnp.where(deal == self.starts[slot : slot + 1, :], position, 0.0),
                axis=0,
                keepdims=True,
            )
            for slot in range(slots)
        ]
        self.dealt = lane_sum(jnp.concatenate(found, axis=0))
        self.shift = self.dealt - self.starts

    def passed(self, x, to):
        rows = self.at.rows
        return (x + (rows - 1 - to)) >> int(math.log2(rows))

    def clipped(self, x, first):
        return jnp.minimum(jnp.maximum(x, first), first + self.held)

    def rank(self, token, holder, to):
        first = holder * self.held
        low = self.clipped(self.starts, first)
        high = jnp.maximum(self.clipped(jnp.minimum(self.ends, token), first), low)
        return column_sum(self.passed(high + self.shift, to) - self.passed(low + self.shift, to))

    def lanes(self, count):
        return lax.broadcasted_iota(jnp.int32, (1, count), 1)

    def take_back(self):
        token = self.at.row * self.held + self.lanes(self.held)
        holds = (self.starts <= token) & (token < self.ends)
        to = (token + column_sum(jnp.where(holds, self.shift, 0))) % self.at.rows
        return to * CAPACITY + self.rank(token, self.at.row, to)

    def in_dealt(self, position):
        lengths = self.ends - self.starts
        return (self.dealt <= position) & (position < self.dealt + lengths)

    def pick(self):
        at = self.at
        slot = self.lanes(at.cols * self.piece)
        position = (slot // self.piece) * self.group + (slot % self.piece) * at.rows + at.row
        inside = self.in_dealt(position)
        token = position - column_sum(jnp.where(inside, self.shift, 0))
        holder = token // self.held
        return holder * CAPACITY + self.rank(token, holder, at.row)

    def listed(self, holder_is_lane):
        at = self.at
        lane = self.lanes(at.rows * CAPACITY)
        which = sum(jnp.where(lane >= CAPACITY * row, 1, 0) for row in range(1, at.rows))
        slot = lane - CAPACITY * which
        holder, to = (which, at.row) if holder_is_lane else (at.row, which)
        first = holder * self.held
        begin = self.passed(self.clipped(self.starts, first) + self.shift, to)
        count = self.passed(self.clipped(self.ends, first) + self.shift, to) - begin
        before = dot_nn(self.strict, count.astype(f32).astype(bf16)).astype(jnp.int32)
        inside = slot - before
        found = (inside >= 0) & (inside < count)
        dealt = at.rows * (begin + inside) + to
        used = column_sum(jnp.where(found, 1, 0)) > 0
        if holder_is_lane:
            block = dealt // self.group
            rest = dealt % self.group
            value = block * self.piece + rest // at.rows
        else:
            value = dealt - self.shift - first
        return jnp.where(used, column_sum(jnp.where(found, value, 0)), -1)

    def block_starts(self):
        shape = (self.group, self.slots)
        first = self.at.col * self.group
        position = first + lax.broadcasted_iota(jnp.int32, shape, 0)
        dealt = column_sum(jnp.where(self.same, self.dealt, 0))
        inside = (dealt <= position) & (position < dealt + self.length_row)
        return lane_sum(jnp.where(inside, dealt - first, 0))

    def rotary(self):
        half_rot = ROT // 2
        lane = self.lanes(self.group)
        position = self.at.col * self.group + (lane % self.piece) * self.at.rows
        position = position + lane // self.piece
        inside = self.in_dealt(position)
        place = position - column_sum(jnp.where(inside, self.dealt, 0))
        entry = lax.broadcasted_iota(jnp.int32, (half_rot, 1), 0)
        inverse = sum(
            jnp.where(entry == index, 1.0 / 10000.0 ** (index * 2.0 / ROT), 0.0)
            for index in range(half_rot)
        )
        angles = inverse.astype(f32) * place.astype(f32)
        parts = split(jnp.concatenate([jnp.cos(angles), jnp.sin(angles)], axis=0))
        return jnp.concatenate(parts, axis=0)


def finish_kernel(
    in_grad_ref,
    out_grad_ref,
    update_ref,
    output_ref,
    input_grad_ref,
    vector_sum_ref,
    *refs,
):
    weights, momenta, norms, outs = refs[0:4], refs[4:8], refs[8:11], refs[11:]
    outs[0][...] = output_ref[...]
    outs[1][...] = input_grad_ref[...]
    wide = in_grad_ref.shape[1] // 2
    widths = (3 * D, FF, D, FF)
    for index in range(4):
        source = in_grad_ref if index < 2 else out_grad_ref
        first = (index % 2) * wide
        grad = source[:, first : first + wide]
        update = jnp.concatenate([update_ref[2 * index], update_ref[2 * index + 1]], axis=1)
        update = update.astype(f32)
        if index != 1:
            size = weights[index].shape[0]
            grad, update = grad.T[:size, :], update.T[:size, :]
        outs[2 + index][...] = grad
        outs[6 + index][...] = momentum * momenta[index][...] + grad
        outs[10 + index][...] = (
            weights[index][...] * (1.0 - rate_matrix * decay_matrix)
            - rate_matrix * 0.2 * math.sqrt(widths[index]) * update
        )
    sums = vector_sum_ref[...]
    grads = jnp.concatenate(
        [sums[2 * index : 2 * index + 1, :] + sums[2 * index + 1 : 2 * index + 2, :] for index in range(3)],
        axis=0,
    )
    for out_ref, value in zip(
        outs[14:], adam_step(norms[0][...], grads, norms[1][...], norms[2][...])
    ):
        out_ref[...] = value


def finish(in_grad, out_grad, update, output, input_grad, vector_sum, weights, momenta, norms):
    shape = jax.ShapeDtypeStruct
    matrices = [shape(weight.shape, f32) for weight in weights]
    return pl.pallas_call(
        finish_kernel,
        out_shape=(
            shape(output.shape, f32),
            shape(output.shape, f32),
            *(matrices * 3),
            *([shape(norms[0].shape, f32)] * 3),
        ),
        compiler_params=pltpu.CompilerParams(vmem_limit_bytes=VMEM_LIMIT),
        name="finish",
    )(in_grad, out_grad, update, output, input_grad, vector_sum, *weights, *momenta, *norms)


def adam_step(value, gradient, first_state, second_state):
    first_new = beta_first * first_state + (1.0 - beta_first) * gradient
    second_new = beta_second * second_state + (1.0 - beta_second) * gradient * gradient
    corrected = first_new / (1.0 - beta_first**STEP)
    root_term = jnp.sqrt(second_new / (1.0 - beta_second**STEP)) + adam_floor
    return (first_new, second_new, value - rate_vector * corrected / root_term)


def per_device(
    tokens,
    cotangent,
    lengths,
    deal_order,
    qkv_weight,
    up_weight,
    proj_weight,
    down_weight,
    norm_vectors,
    qkv_bias,
    mlp_bias,
    qkv_momentum,
    up_momentum,
    proj_momentum,
    down_momentum,
    norm_moment,
    norm_square,
    qkv_bias_moment,
    qkv_bias_square,
    mlp_bias_moment,
    mlp_bias_square,
):
    cols, rows = lax.axis_size("col"), lax.axis_size("row")
    qkv_width, up_width = qkv_weight.shape[1], up_weight.shape[1]
    bias = jnp.concatenate(
        [jnp.pad(qkv_bias, (0, up_width - qkv_width)), mlp_bias], axis=0
    ).reshape(1, 2 * up_width)
    weights = (qkv_weight.T, up_weight, proj_weight, down_weight)
    momenta = (qkv_momentum.T, up_momentum, proj_momentum, down_momentum)
    (
        pick,
        pack,
        vector_all,
        normalized,
        inverse_std,
        in_grad,
        out_grad,
        bias_rows,
        matrix,
        gram,
        twin_sums,
        branch_sum,
    ) = layer(
        tokens,
        cotangent,
        lengths.reshape(1, -1),
        deal_order.reshape(-1, 128),
        norm_vectors,
        bias,
        weights,
        momenta,
        rows,
        cols,
    )
    returned, output, input_grad, vector_sum = orthogonalize(
        gram,
        matrix,
        twin_sums,
        branch_sum,
        normalized,
        inverse_std,
        vector_all,
        tokens,
        cotangent,
        pick,
        pack,
        rows,
    )
    output, input_grad, *matrices = finish(
        in_grad,
        out_grad,
        returned,
        output,
        input_grad,
        vector_sum,
        weights,
        momenta,
        (norm_vectors, norm_moment, norm_square),
    )
    matrices, norms = matrices[:12], matrices[12:]
    for index in (0, 4, 8):
        matrices[index] = matrices[index].T
    in_bias_grad = bias_rows[0]
    qkv_first, qkv_second, qkv_bias_new = adam_step(
        qkv_bias, in_bias_grad[:qkv_width], qkv_bias_moment, qkv_bias_square
    )
    mlp_first, mlp_second, mlp_bias_new = adam_step(
        mlp_bias, in_bias_grad[up_width:], mlp_bias_moment, mlp_bias_square
    )
    return (
        output,
        input_grad,
        *matrices,
        *norms,
        qkv_first,
        qkv_second,
        qkv_bias_new,
        mlp_first,
        mlp_second,
        mlp_bias_new,
    )


def solution(mesh):
    over_both, over_flip = P("row", "col"), P("col", "row")
    features, hidden = P(None, "col"), P("row")
    return jax.shard_map(
        per_device,
        mesh=mesh,
        in_specs=(
            *(over_both, over_both, P(), P()),
            *(over_flip, over_flip, over_both, over_both),
            *(features, hidden, hidden),
            *(over_flip, over_flip, over_both, over_both),
            *(features, features, hidden, hidden, hidden, hidden),
        ),
        out_specs=(
            *(over_both, over_both),
            *(over_flip, over_flip, over_both, over_both) * 3,
            *(features,) * 3,
            *(hidden,) * 6,
        ),
        check_vma=False,
    )
```
